32 devices in a mesh: seq: 2 (over x), exp: 16 (over z, y, core).
Axes of the slice: x: 2, y: 2, z: 4, core: 2. Of those that a mesh axis runs over, the one named last changes fastest.
Arguments:
- tokens: bfloat16 [4096, 4096], P(('seq', 'exp')), may hold values from -6 to 6
- cotangent: bfloat16 [4096, 4096], P(('seq', 'exp')), may hold values from -3 to 3
- factors: bfloat16 [16, 3, 4, 1024, 128], P('exp', None, None, 'seq'), may hold values from -0.09375 to 0.09375
- mix: float32 [16, 3, 4, 4, 4], P('exp'), may hold values from -3 to 3
- selection: int32 [16, 4, 64], P('exp', 'seq'), may hold values from 0 to 1023, as said below
- scores: int32 [16, 4, 64], P('exp', 'seq'), may hold values from -192 to 191
Outputs:
- token_grad: bfloat16 [4096, 4096], P(('seq', 'exp'))
- factor_grad: float32 [16, 3, 4, 1024, 128], P('exp', None, None, 'seq')
- mix_grad: float32 [16, 3, 4, 4, 4], P('exp')
- gate_grad: float32 [16, 4, 64], P('exp', 'seq')
The draws below stay inside these ranges and needn't reach their ends.
Inputs may be any that keep to these rules, and one draw needn't show every extreme that they name: `selection`: for every expert and block the 64 positions are distinct and ascending; at most 12 of them lie among the 128 positions of one device (aligned runs of 128), and for every expert and block some device holds exactly 12 of them.
All inputs are finite; a program needn't handle non-finite values.
Results may differ from the reference program's by a relative error of at most 0.015.
Values may be sent and summed in bfloat16 or wider, within the bound.
No kernel may reach another device: no remote copies, remote signals or barrier semaphores. Data moves between devices by JAX's collectives and lax.ppermute only.
A program may use at most 64 MiB of HBM per device.

```python
import jax
import jax.numpy as jnp
from jax import lax

D = 4096
FF = 512
NPHM = 4
C = 64
TOK_DEV = 128
EXPERTS = 16
BLOCK = 1024
CAP = 12
GROUPS = 2
BLOCKS = 4
ROWS = 128
TOKENS = 4096


def draw_selection(key, part):
    key_rank = jax.random.fold_in(key, 11)
    key_favour = jax.random.fold_in(key, 12)
    key_forced = jax.random.fold_in(key, 13)
    key_jitter = jax.random.fold_in(key, 14)
    owner_total = BLOCK // TOK_DEV
    rank_keys = jax.random.randint(key_rank, (EXPERTS, BLOCKS, owner_total, TOK_DEV), 0, 1 << 20)
    local_idx = jnp.arange(TOK_DEV, dtype=jnp.int32)
    rank_keys = rank_keys * TOK_DEV + local_idx
    run_order = jnp.argsort(jnp.argsort(rank_keys, axis=-1), axis=-1)
    allowed = run_order < CAP
    favour = jax.random.randint(key_favour, (1, BLOCKS, owner_total, 1), 0, 4)
    forced_owner = jax.random.randint(key_forced, (EXPERTS, BLOCKS, 1, 1), 0, owner_total)
    jitter = jax.random.randint(key_jitter, (EXPERTS, BLOCKS, owner_total, TOK_DEV), 0, 1024)
    owner_ids = jnp.arange(owner_total, dtype=jnp.int32)[None, None, :, None]
    priority = 1 + favour * 1024 + jitter + (owner_ids == forced_owner).astype(jnp.int32) * 8192
    priority = jnp.where(allowed, priority, 0)
    ranked = priority.reshape(EXPERTS, BLOCKS, BLOCK) * BLOCK + jnp.arange(BLOCK, dtype=jnp.int32)
    ignored, picked = lax.top_k(ranked, C)
    return jnp.sort(picked, axis=-1).astype(jnp.int32)


def set_ends(values, rng, least, top_value):
    shape = values.shape
    place = [jax.random.randint(jax.random.fold_in(rng, axis), (), 0, shape[axis]) for axis in range(len(shape))]
    values = values.at[tuple(place)].set(least)
    longest = shape.index(max(shape))
    place[longest] = (place[longest] + 1) % shape[longest]
    return values.at[tuple(place)].set(top_value)


def block_scale(own_key, extent, cuts, low, high):
    loudness, own = 1.0, jax.random.fold_in(own_key, 6)
    for position, parts in cuts:
        steps = jnp.exp(jax.random.uniform(jax.random.fold_in(own, position), (parts,), jnp.float32, low / len(cuts), high / len(cuts)))
        loudness = loudness * jnp.repeat(steps, extent[position] // parts).reshape([-1 if axis == position else 1 for axis in range(len(extent))])
    return loudness


def gaussian(key, dims, width, most, shards=(), held_as=jnp.bfloat16):
    factor_of = block_scale(key, dims, shards, -0.22, 0.18) if shards else 1.0
    entries = jax.random.normal(key, dims, jnp.float32) * width * factor_of
    return jnp.minimum(jnp.maximum(entries, -most), most).astype(held_as)


def setup_inputs(seed: int = 0) -> dict:
    key_list = jax.random.split(jax.random.key(seed), 7)
    return {
        "tokens": gaussian(key_list[0], (TOKENS, D), 1.0, 6.0, ((0, 32),)),
        "cotangent": gaussian(key_list[1], (TOKENS, D), 0.5, 3.0, ((0, 32),)),
        "factors": gaussian(key_list[2], (EXPERTS, 3, NPHM, D // NPHM, FF // NPHM), D ** -0.5, 0.09375, ((0, 16), (3, 2))),
        "mix": gaussian(key_list[3], (EXPERTS, 3, NPHM, NPHM, NPHM), 0.5, 3.0, ((0, 16),), jnp.float32),
        "selection": draw_selection(jax.random.fold_in(key_list[6], 71), 0),
        "scores": set_ends(jax.random.randint(key_list[5], (EXPERTS, BLOCKS, C), -192, 192), jax.random.fold_in(key_list[5], 1), -192, 191).astype(jnp.int32),
    }


PRECISE = lax.Precision.HIGHEST


def expand(mixing, factor_set):
    shape_set = factor_set.shape
    expanded = jnp.einsum("iab,ipq->apbq", mixing, factor_set.astype(jnp.float32), precision=PRECISE)
    return expanded.reshape(shape_set[0] * shape_set[1], shape_set[0] * shape_set[2])


def project(mixing, factor_set, kernel_grad):
    shape_set = factor_set.shape
    block_view = kernel_grad.reshape(shape_set[0], shape_set[1], shape_set[0], shape_set[2])
    factor_out = jnp.einsum("iab,apbq->ipq", mixing, block_view, precision=PRECISE)
    mixing_out = jnp.einsum("apbq,ipq->iab", block_view, factor_set.astype(jnp.float32), precision=PRECISE)
    return factor_out, mixing_out


def silu_parts(preact):
    sigmoid_val = jax.nn.sigmoid(preact)
    return preact * sigmoid_val, sigmoid_val + preact * sigmoid_val * (1.0 - sigmoid_val)


def contract(left, right):
    return lax.dot_general(left, right, (((0,), (0,)), ((), ())), preferred_element_type=jnp.float32)


def transposed(left, kernel):
    return lax.dot_general(left, kernel, (((1,), (1,)), ((), ())), preferred_element_type=jnp.float32)


def expert_core(sel_rows, sel_grads, gate_val, kernels):
    pre_gate = jnp.dot(sel_rows, kernels[0], preferred_element_type=jnp.float32)
    pre_up = jnp.dot(sel_rows, kernels[1], preferred_element_type=jnp.float32)
    gate_act, gate_slope = silu_parts(pre_gate)
    hidden = (gate_act * pre_up).astype(jnp.bfloat16)
    expert_out = transposed(hidden, kernels[2])
    gate_in = jnp.sum(sel_grads.astype(jnp.float32) * expert_out, axis=1)
    gate_grad = gate_in * gate_val * (1.0 - gate_val)
    out_grad = (gate_val[:, None] * sel_grads.astype(jnp.float32)).astype(jnp.bfloat16)
    hidden_grad = jnp.dot(out_grad, kernels[2], preferred_element_type=jnp.float32)
    gate_pre = (hidden_grad * pre_up * gate_slope).astype(jnp.bfloat16)
    up_pre = (hidden_grad * gate_act).astype(jnp.bfloat16)
    row_grad = (transposed(gate_pre, kernels[0]) + transposed(up_pre, kernels[1])).astype(jnp.bfloat16)
    return gate_grad, row_grad, gate_pre, up_pre, out_grad, hidden


def reference(tokens, cotangent, factors, mix, selection, scores):
    def one_expert(running, inputs):
        chosen, score_set, factor_e, mix_e = inputs
        kernels = [expand(mix_e[number], factor_e[number]).astype(jnp.bfloat16) for number in range(3)]
        token_index = (jnp.arange(BLOCKS, dtype=jnp.int32)[:, None] * BLOCK + chosen).reshape(-1).astype(jnp.int32)
        sel_rows = jnp.take(tokens, token_index, axis=0)
        sel_grads = jnp.take(cotangent, token_index, axis=0)
        gate_val = jax.nn.sigmoid(score_set.reshape(-1).astype(jnp.float32) / 64.0)
        gate_grad, row_grad, gate_pre, up_pre, out_grad, hidden = expert_core(sel_rows, sel_grads, gate_val, kernels)
        running = running.at[token_index].add(row_grad.astype(jnp.float32))

        def group_part(pieces):
            rows_g, gate_g, up_g, out_g, hidden_g = pieces
            kernel_grads = [contract(rows_g, gate_g), contract(rows_g, up_g), contract(out_g, hidden_g)]
            projected = [project(mix_e[number], factor_e[number], kernel_grads[number]) for number in range(3)]
            factor_part = jnp.stack([item[0] for item in projected]).astype(jnp.bfloat16)
            mix_part = jnp.stack([item[1] for item in projected])
            return factor_part, mix_part

        grouped = tuple(array.reshape(GROUPS, ROWS, array.shape[-1]) for array in (sel_rows, gate_pre, up_pre, out_grad, hidden))
        factor_parts, mix_parts = lax.map(group_part, grouped)
        factor_parts = lax.optimization_barrier(factor_parts)
        factor_grad = jnp.sum(factor_parts.astype(jnp.float32), axis=0)
        mix_grad = jnp.sum(mix_parts, axis=0)
        return running, (factor_grad, mix_grad, gate_grad.reshape(BLOCKS, C))

    initial = jnp.zeros((TOKENS, D), jnp.float32)
    token_grad, stacked = lax.scan(one_expert, initial, (selection, scores, factors, mix))
    return token_grad.astype(jnp.bfloat16), stacked[0], stacked[1], stacked[2]
```

```python
import functools

import jax
import jax.numpy as jnp
from jax import lax
from jax.experimental import pallas as pl
from jax.experimental.pallas import tpu as pltpu
from jax.sharding import PartitionSpec as P

SELECTED = 64
NPHM = 4
VMEM_LIMIT = 32 * 1024 * 1024
F32 = jnp.float32
BF16 = jnp.bfloat16


def iota(shape, dim):
    return lax.broadcasted_iota(jnp.int32, shape, dim)


def dot(left, right):
    return jnp.dot(left, right, preferred_element_type=F32)


def dot_tn(left, right):
    return lax.dot_general(left, right, (((0,), (0,)), ((), ())), preferred_element_type=F32)


def dot_nt(left, right):
    return lax.dot_general(left, right, (((1,), (1,)), ((), ())), preferred_element_type=F32)


def call(body, outs, ins, name, flops, scratch=(), smem=(), **extra):
    vmem = pl.BlockSpec(memory_space=pltpu.VMEM)
    scalar = pl.BlockSpec(memory_space=pltpu.SMEM)
    single = not isinstance(outs, (list, tuple))
    moved = sum(x.size * x.dtype.itemsize for x in ins)
    moved += sum(x.size * x.dtype.itemsize for x in ([outs] if single else outs))
    return pl.pallas_call(
        body,
        out_shape=outs,
        in_specs=[scalar if n in smem else vmem for n in range(len(ins))],
        out_specs=vmem if single else [vmem] * len(outs),
        scratch_shapes=list(scratch),
        compiler_params=pltpu.CompilerParams(vmem_limit_bytes=VMEM_LIMIT),
        cost_estimate=pl.CostEstimate(flops=flops, bytes_accessed=moved, transcendentals=0),
        name=name,
        **extra,
    )(*ins)


def shaped(shape, dtype):
    return jax.ShapeDtypeStruct(shape, dtype)


def index_body(cap, pieces, own_rows, block_len, chosen_ref, wanted_ref, slot_ref):
    peers, lanes = wanted_ref.shape
    rows = slot_ref.shape[1]
    position = jnp.concatenate(
        [chosen_ref[b : b + 1, :] + b * block_len for b in range(chosen_ref.shape[0])], axis=1
    )
    owner = lax.shift_right_logical(position, own_rows.bit_length() - 1)
    local = position & (own_rows - 1)
    peer = iota((peers, rows), 0)
    mine = (peer == owner).astype(F32)
    count = jnp.sum(mine, axis=1, keepdims=True)
    earlier = jnp.sum(jnp.where(peer < owner, count, 0.0), axis=0, keepdims=True).astype(jnp.int32)
    rank = iota((1, rows), 1) - earlier
    slot_ref[...] = owner * (cap * pieces) + rank
    lane = iota((lanes, rows), 0)
    hit = jnp.zeros((lanes, rows), F32)
    for j in range(pieces):
        hit = hit + (lane == rank + j * cap).astype(F32)
    marked = mine * (local + 1).astype(F32)
    wanted_ref[...] = dot_nt(marked.astype(BF16), hit.astype(BF16)).astype(jnp.int32)


def pick_matrix(cap, pieces, own_rows, requested):
    peers, lanes = requested.shape
    group = cap * pieces
    slots = peers * group
    peer = iota((peers, group, peers), 0).reshape(slots, peers)
    spread = dot(
        (peer == iota((slots, peers), 1)).astype(BF16), requested.astype(F32).astype(BF16)
    )
    place = iota((peers, group, lanes), 1).reshape(slots, lanes)
    row = jnp.sum(
        jnp.where(place == iota((slots, lanes), 1), spread, 0.0), axis=1, keepdims=True
    ).astype(jnp.int32)
    piece = iota((peers, group, 1), 1).reshape(slots, 1)
    shift = jnp.zeros((slots, 1), jnp.int32)
    for j in range(1, pieces):
        shift = shift + jnp.where(piece >= j * cap, own_rows, 0)
    target = jnp.where(row > 0, row - 1 + shift, -1)
    return (target == iota((slots, pieces * own_rows), 1)).astype(BF16)


def pick_body(cap, pieces, own_rows, requested_ref, *refs):
    columns, out_ref, pick_ref = refs[:pieces], refs[pieces], refs[pieces + 1]

    @pl.when(pl.program_id(0) == 0)
    def _():
        pick_ref[...] = pick_matrix(cap, pieces, own_rows, requested_ref[...])

    stacked = jnp.concatenate([ref[...] for ref in columns], axis=0)
    out_ref[...] = dot(pick_ref[...], stacked).astype(BF16)


def pick_rows(cap, pieces, requested, source, name):
    own_rows, width = source.shape
    part = width // pieces
    chunk = min(part, 512)
    steps = part // chunk
    slots = requested.shape[0] * cap * pieces
    specs = [
        pl.BlockSpec((own_rows, chunk), functools.partial(lambda j, c: (0, j * steps + c), j))
        for j in range(pieces)
    ]
    return pl.pallas_call(
        functools.partial(pick_body, cap, pieces, own_rows),
        out_shape=shaped((slots, part), BF16),
        grid=(steps,),
        in_specs=[pl.BlockSpec(requested.shape, lambda c: (0, 0))] + specs,
        out_specs=pl.BlockSpec((slots, chunk), lambda c: (0, c)),
        scratch_shapes=[pltpu.VMEM((slots, pieces * own_rows), BF16)],
        compiler_params=pltpu.CompilerParams(vmem_limit_bytes=VMEM_LIMIT),
        cost_estimate=pl.CostEstimate(
            flops=2 * slots * pieces * own_rows * part,
            bytes_accessed=4 * slots * part,
            transcendentals=0,
        ),
        name=name,
    )(requested, *([source] * pieces))


def place_body(cap, pieces, own_rows, requested_ref, returned_ref, out_ref, pick_ref):
    @pl.when(pl.program_id(0) == 0)
    def _():
        pick_ref[...] = pick_matrix(cap, pieces, own_rows, requested_ref[...])

    total = dot_tn(pick_ref[...], returned_ref[...]).astype(BF16)
    for j in range(pieces):
        out_ref[:, j, :] = total[j * own_rows : (j + 1) * own_rows]


def sum_rows(cap, pieces, own_rows, requested, returned):
    slots, part = returned.shape

    def body(requested_ref, returned_ref, out_ref):
        pick = pick_matrix(cap, pieces, own_rows, requested_ref[...])
        chunk = min(part, 512)
        for c in range(part // chunk):
            total = dot_tn(pick, returned_ref[:, c * chunk : (c + 1) * chunk]).astype(BF16)
            for j in range(pieces):
                start = j * part + c * chunk
                out_ref[:, start : start + chunk] = total[j * own_rows : (j + 1) * own_rows]

    return call(
        body,
        shaped((own_rows, part * pieces), BF16),
        [requested, returned],
        "sum_rows",
        2 * slots * pieces * own_rows * part,
    )


def assemble_body(order_ref, *refs):
    parts, out_ref = refs[:-1], refs[-1]
    for n, part in enumerate(parts):
        weights, count, rows, cols = part.shape
        start = pl.multiple_of(order_ref[n] * rows, rows)
        for m in range(weights):
            for i in range(count):
                out_ref[m, pl.ds(start, rows), i * cols : (i + 1) * cols] = part[m, i]


def place_matrix(cap, pieces, slots, slot):
    wide = jnp.concatenate([slot + j * cap for j in range(pieces)], axis=1)
    return (iota((slots, wide.shape[1]), 0) == wide).astype(BF16)


def stack_rows(pieces, place, got_ref, out_ref):
    part = got_ref.shape[1]
    rows, depth = out_ref.shape[0] // NPHM, out_ref.shape[1]
    chunk = min(part, 512)
    for c in range(part // chunk):
        block = dot_tn(place, got_ref[:, c * chunk : (c + 1) * chunk]).astype(BF16)
        for j in range(pieces):
            column = j * part + c * chunk
            a, start = column // depth, column % depth
            out_ref[a * rows : (a + 1) * rows, start : start + chunk] = block[
                j * rows : (j + 1) * rows
            ]


STRIP = 32


def mix_in(mix_ref, m, y_ref, emit):
    rows, cols = y_ref.shape[0] // NPHM, y_ref.shape[1] // NPHM

    def strip(n, carry):
        start = pl.multiple_of(n * STRIP, STRIP)
        total = [jnp.zeros((STRIP, cols), F32)] * NPHM
        for a in range(NPHM):
            for i in range(NPHM):
                block = y_ref[pl.ds(a * rows + start, STRIP), i * cols : (i + 1) * cols]
                for b in range(NPHM):
                    total[b] = total[b] + mix_ref[m * 64 + i * 16 + a * 4 + b] * block
        emit(start, total)
        return carry

    lax.fori_loop(0, rows // STRIP, strip, 0)


def mix_out(mix_ref, m, d_ref, z_ref):
    rows, cols = d_ref.shape[0], d_ref.shape[1] // NPHM

    def strip(n, carry):
        start = pl.multiple_of(n * STRIP, STRIP)
        blocks = [
            d_ref[pl.ds(start, STRIP), b * cols : (b + 1) * cols].astype(F32) for b in range(NPHM)
        ]
        for a in range(NPHM):
            for i in range(NPHM):
                total = mix_ref[m * 64 + i * 16 + a * 4] * blocks[0]
                for b in range(1, NPHM):
                    total = total + mix_ref[m * 64 + i * 16 + a * 4 + b] * blocks[b]
                z_ref[pl.ds(a * rows + start, STRIP), i * cols : (i + 1) * cols] = total.astype(
                    z_ref.dtype
                )
        return carry

    lax.fori_loop(0, rows // STRIP, strip, 0)


def forward_body(
    cap, pieces, slot_ref, mix_ref, got_ref, factor_ref, x_ref, yg_ref, yu_ref, act_ref, slope_ref, hid_ref, pre_ref
):
    place = place_matrix(cap, pieces, got_ref.shape[0], slot_ref[...])
    stack_rows(pieces, place, got_ref, x_ref)
    yg_ref[...] = dot(x_ref[...], factor_ref[0])
    yu_ref[...] = dot(x_ref[...], factor_ref[1])
    cols = yg_ref.shape[1] // NPHM

    def keep(start, total):
        for b in range(NPHM):
            pre_ref[pl.ds(start, STRIP), b * cols : (b + 1) * cols] = total[b]

    def finish(start, total):
        for b in range(NPHM):
            at = (pl.ds(start, STRIP), slice(b * cols, (b + 1) * cols))
            gate = pre_ref[at]
            sig = jax.nn.sigmoid(gate)
            act = gate * sig
            act_ref[at] = act
            slope_ref[at] = total[b] * (sig + act * (1.0 - sig))
            hid_ref[at] = act * total[b]

    mix_in(mix_ref, 0, yg_ref, keep)
    mix_in(mix_ref, 1, yu_ref, finish)


def backward_body(
    cap, pieces, slot_ref, mix_ref, got_ref, factor_ref, act_ref, slope_ref, hid_ref, gate_ref,
    back_ref, x_ref, y_ref, dg_ref, du_ref, dd_ref, zg_ref, zu_ref, part_ref, grad_ref,
):
    place = place_matrix(cap, pieces, got_ref.shape[0], slot_ref[...])
    stack_rows(pieces, place, got_ref, x_ref)
    y_ref[...] = dot(x_ref[...], factor_ref[2])
    cols = y_ref.shape[1] // NPHM

    def finish(start, total):
        gate = gate_ref[pl.ds(start, STRIP), :]
        inner = jnp.zeros((STRIP, cols), F32)
        for b in range(NPHM):
            at = (pl.ds(start, STRIP), slice(b * cols, (b + 1) * cols))
            hidden = hid_ref[at]
            inner = inner + hidden * total[b]
            hidden_grad = gate * total[b]
            dg_ref[at] = (hidden_grad * slope_ref[at]).astype(dg_ref.dtype)
            du_ref[at] = (hidden_grad * act_ref[at]).astype(du_ref.dtype)
            dd_ref[at] = (hidden * gate).astype(dd_ref.dtype)
        part_ref[pl.ds(start, STRIP), :] = inner

    mix_in(mix_ref, 2, y_ref, finish)
    mix_out(mix_ref, 0, dg_ref, zg_ref)
    mix_out(mix_ref, 1, du_ref, zu_ref)
    grad = dot_nt(zg_ref[...], factor_ref[0]) + dot_nt(zu_ref[...], factor_ref[1])
    grad_ref[...] = grad.astype(BF16)
    part = back_ref.shape[1]
    rows, depth = x_ref.shape[0] // NPHM, x_ref.shape[1]
    chunk = min(part, 512)
    for c in range(part // chunk):
        blocks = []
        for j in range(pieces):
            column = j * part + c * chunk
            a, start = column // depth, column % depth
            blocks.append(grad_ref[a * rows : (a + 1) * rows, start : start + chunk])
        back_ref[:, c * chunk : (c + 1) * chunk] = dot(
            place, jnp.concatenate(blocks, axis=0)
        ).astype(BF16)


def factor_body(swap, order_ref, mix_ref, xr_ref, xg_ref, zg_ref, zu_ref, dd_ref, *refs):
    zd_ref = refs[-1]
    mix_out(mix_ref, 2, dd_ref, zd_ref)
    pairs = ((xr_ref, zg_ref), (xr_ref, zu_ref), (xg_ref, zd_ref))
    if swap:
        other_ref, own_ref = refs[0], refs[1]
        half = own_ref.shape[1]
        for ref, n in ((other_ref, 1), (own_ref, 0)):
            start = pl.multiple_of(order_ref[n] * half, half)
            for m, (x_ref, z_ref) in enumerate(pairs):
                ref[m] = dot_tn(x_ref[:, pl.ds(start, half)], z_ref[...]).astype(ref.dtype)
    else:
        for m, (x_ref, z_ref) in enumerate(pairs):
            refs[0][m] = dot_tn(x_ref[...], z_ref[...]).astype(BF16)


def mix_grad_body(yg_ref, yu_ref, yd_ref, dg_ref, du_ref, dd_ref, out_ref):
    rows, cols = dg_ref.shape[0], dg_ref.shape[1] // NPHM
    for m, (y_ref, d_ref) in enumerate(((yg_ref, dg_ref), (yu_ref, du_ref), (yd_ref, dd_ref))):
        for a in range(NPHM):
            for i in range(NPHM):
                block = y_ref[a * rows : (a + 1) * rows, i * cols : (i + 1) * cols]
                for b in range(NPHM):
                    at = m * 64 + i * 16 + a * 4 + b
                    other = d_ref[:, b * cols : (b + 1) * cols].astype(F32)
                    out_ref[at : at + 1, :] = jnp.sum(block * other, axis=0, keepdims=True)


def combine_body(*refs):
    parts, out_ref = refs[:-1], refs[-1]
    weights, count, _, cols = out_ref.shape
    for m in range(weights):
        for i in range(count):
            at = slice(i * cols, (i + 1) * cols)
            out_ref[m, i] = sum(part[m, :, at].astype(F32) for part in parts)


def shards(tokens, cotangent, factors, mix, selection, scores):
    peers = lax.axis_size("exp")
    groups = lax.axis_size("seq")
    group = lax.axis_index("seq")
    own_rows, width = tokens.shape
    _, weights, count, depth_own, cols = factors.shape
    depth = depth_own * groups
    hidden = count * cols
    cap = 3 * own_rows // (2 * peers)
    pieces = 1
    while (cap * pieces) % 8:
        pieces *= 2
    lanes = 128
    slots = peers * cap * pieces
    part = width // pieces
    block_len = peers * SELECTED
    rows = selection.shape[1] * selection.shape[2]
    swap = groups == 2
    pair = [(0, 1), (1, 0)]
    mixing = mix.reshape(-1)
    order = jnp.stack([group, 1 - group]).astype(jnp.int32)

    if swap:
        factor_parts = [factors[0], lax.ppermute(factors, "seq", pair)[0]]
    else:
        factor_parts = [lax.all_gather(factors, "seq", axis=3, tiled=True)[0]]

    wanted, slot = call(
        functools.partial(index_body, cap, pieces, own_rows, block_len),
        [shaped((peers, lanes), jnp.int32), shaped((1, rows), jnp.int32)],
        [selection[0]],
        "wanted_rows",
        1 << 20,
    )
    requested = lax.all_to_all(wanted, "exp", split_axis=0, concat_axis=0, tiled=True)

    def exchange(array):
        array = array.reshape(peers, cap * pieces, part)
        array = lax.all_to_all(array, "exp", split_axis=0, concat_axis=0, tiled=True)
        return array.reshape(slots, part)

    got_rows = exchange(pick_rows(cap, pieces, requested, tokens, "pick_tokens"))
    got_grads = exchange(pick_rows(cap, pieces, requested, cotangent, "pick_cotangent"))

    factor_order = order if swap else jnp.zeros((2,), jnp.int32)
    side = call(
        assemble_body,
        shaped((weights, depth, hidden), BF16),
        [factor_order] + factor_parts,
        "assemble_factors",
        1 << 20,
        smem=(0,),
    )
    gate = jax.nn.sigmoid(scores[0].reshape(-1).astype(F32) / 64.0)
    gate_wide = jnp.broadcast_to(gate[:, None], (rows, cols))

    product = 2 * count * rows * depth * hidden
    stack = shaped((count * rows, depth), BF16)
    mixed = shaped((count * rows, hidden), F32)
    mixed_low = shaped((count * rows, hidden), BF16)
    flat = shaped((rows, hidden), F32)
    flat_low = shaped((rows, hidden), BF16)
    x_rows, y_gate, y_up, act, slope, hid = call(
        functools.partial(forward_body, cap, pieces),
        [stack, mixed, mixed, flat, flat, flat],
        [slot, mixing, got_rows, side],
        "forward",
        2 * product,
        scratch=[pltpu.VMEM((rows, hidden), F32)],
        smem=(1,),
    )
    back, x_grads, y_down, d_gate, d_up, d_down, z_gate, z_up, inner = call(
        functools.partial(backward_body, cap, pieces),
        [shaped((slots, part), BF16), stack, mixed, flat_low, flat_low, flat_low, mixed_low, mixed_low]
        + [shaped((rows, cols), F32)],
        [slot, mixing, got_grads, side, act, slope, hid, gate_wide],
        "backward",
        3 * product,
        scratch=[pltpu.VMEM((count * rows, depth), BF16)],
        smem=(1,),
    )
    returned = exchange(back)

    if swap:
        outs = [shaped((weights, depth_own, hidden), BF16), shaped((weights, depth_own, hidden), F32)]
    else:
        outs = [shaped((weights, depth, hidden), BF16)]
    partial = call(
        functools.partial(factor_body, swap),
        outs,
        [order, mixing, x_rows, x_grads, z_gate, z_up, d_down],
        "factor_partials",
        3 * product,
        scratch=[pltpu.VMEM((count * rows, hidden), BF16)],
        smem=(0, 1),
    )
    mix_rows = call(
        mix_grad_body,
        shaped((mixing.size, cols), F32),
        [y_gate, y_up, y_down, d_gate, d_up, d_down],
        "mix_partials",
        weights * 64 * 2 * rows * cols,
    )
    mix_part = jnp.sum(mix_rows, axis=1).reshape(mix.shape)
    if swap:
        halves = [partial[1], lax.ppermute(partial[0], "seq", pair)]
        mix_grad = mix_part + lax.ppermute(mix_part, "seq", pair)
    else:
        halves = [lax.psum_scatter(partial[0], "seq", scatter_dimension=1, tiled=True)]
        mix_grad = lax.psum(mix_part, "seq")
    gate_grad = (jnp.sum(inner, axis=1) * gate * (1.0 - gate)).reshape(selection.shape)
    factor_grad = call(
        combine_body,
        shaped((weights, count, depth_own, cols), F32),
        halves,
        "factor_grad",
        1 << 20,
    )[None]
    token_grad = sum_rows(cap, pieces, own_rows, requested, returned)
    return token_grad, factor_grad, mix_grad, gate_grad


def solution(mesh):
    return jax.shard_map(
        shards,
        mesh=mesh,
        in_specs=(
            P(("seq", "exp"), None),
            P(("seq", "exp"), None),
            P("exp", None, None, "seq", None),
            P("exp", None, None, None, None),
            P("exp", "seq", None),
            P("exp", "seq", None),
        ),
        out_specs=(
            P(("seq", "exp"), None),
            P("exp", None, None, "seq", None),
            P("exp", None, None, None, None),
            P("exp", "seq", None),
        ),
        check_vma=False,
    )
```

```python
import functools

import jax
import jax.numpy as jnp
from jax import lax
from jax.experimental import pallas as pl
from jax.experimental.pallas import tpu as pltpu
from jax.sharding import PartitionSpec as P

SELECTED = 64
NPHM = 4
VMEM_LIMIT = 32 * 1024 * 1024
F32 = jnp.float32
BF16 = jnp.bfloat16


def iota(shape, dim):
    return lax.broadcasted_iota(jnp.int32, shape, dim)


def dot(left, right):
    return jnp.dot(left, right, preferred_element_type=F32)


def dot_tn(left, right):
    return lax.dot_general(left, right, (((0,), (0,)), ((), ())), preferred_element_type=F32)


def dot_nt(left, right):
    return lax.dot_general(left, right, (((1,), (1,)), ((), ())), preferred_element_type=F32)


HBM = pl.BlockSpec(memory_space=pltpu.HBM)
VMEM = pl.BlockSpec(memory_space=pltpu.VMEM)
SMEM = pl.BlockSpec(memory_space=pltpu.SMEM)


def call(body, outs, ins, name, flops, scratch=()):
    moved = sum(x.size * x.dtype.itemsize for x, _ in list(ins) + list(outs))
    return pl.pallas_call(
        body,
        out_shape=[x for x, _ in outs],
        in_specs=[place for _, place in ins],
        out_specs=[place for _, place in outs],
        scratch_shapes=list(scratch),
        compiler_params=pltpu.CompilerParams(vmem_limit_bytes=VMEM_LIMIT),
        cost_estimate=pl.CostEstimate(flops=flops, bytes_accessed=moved, transcendentals=0),
        name=name,
    )(*[x for x, _ in ins])


def begin(source, target, sem):
    copy = pltpu.make_async_copy(source, target, sem)
    copy.start()
    return copy


def shaped(shape, dtype):
    return jax.ShapeDtypeStruct(shape, dtype)


def scratch_like(shape, dtype):
    return pltpu.VMEM(shape, dtype)


def chunks_of(part):
    chunk = min(part, 512)
    return [slice(c * chunk, (c + 1) * chunk) for c in range(part // chunk)]


def index_body(cap, pieces, own_rows, block_len, chosen_ref, wanted_ref, slot_ref):
    peers, lanes = wanted_ref.shape
    rows = slot_ref.shape[1]
    position = jnp.concatenate(
        [chosen_ref[b : b + 1, :] + b * block_len for b in range(chosen_ref.shape[0])], axis=1
    )
    owner = lax.shift_right_logical(position, own_rows.bit_length() - 1)
    local = position & (own_rows - 1)
    peer = iota((peers, rows), 0)
    mine = (peer == owner).astype(F32)
    count = jnp.sum(mine, axis=1, keepdims=True)
    earlier = jnp.sum(jnp.where(peer < owner, count, 0.0), axis=0, keepdims=True).astype(jnp.int32)
    rank = iota((1, rows), 1) - earlier
    slot_ref[...] = owner * (cap * pieces) + rank
    lane = iota((lanes, rows), 0)
    hit = jnp.zeros((lanes, rows), F32)
    for j in range(pieces):
        hit = hit + (lane == rank + j * cap).astype(F32)
    marked = mine * (local + 1).astype(F32)
    wanted_ref[...] = dot_nt(marked.astype(BF16), hit.astype(BF16)).astype(jnp.int32)


def pick_matrix(cap, pieces, own_rows, requested):
    peers, lanes = requested.shape
    group = cap * pieces
    slots = peers * group
    peer = iota((peers, group, peers), 0).reshape(slots, peers)
    spread = dot(
        (peer == iota((slots, peers), 1)).astype(BF16), requested.astype(F32).astype(BF16)
    )
    place = iota((peers, group, lanes), 1).reshape(slots, lanes)
    row = jnp.sum(
        jnp.where(place == iota((slots, lanes), 1), spread, 0.0), axis=1, keepdims=True
    ).astype(jnp.int32)
    piece = iota((peers, group, 1), 1).reshape(slots, 1)
    shift = jnp.zeros((slots, 1), jnp.int32)
    for j in range(1, pieces):
        shift = shift + jnp.where(piece >= j * cap, own_rows, 0)
    target = jnp.where(row > 0, row - 1 + shift, -1)
    return (target == iota((slots, pieces * own_rows), 1)).astype(BF16)


def pick_rows(cap, pieces, requested, source, after, name):
    own_rows, width = source.shape
    part = width // pieces
    slots = requested.shape[0] * cap * pieces
    columns = chunks_of(part)

    def body(requested_ref, source_ref, *refs):
        out_ref, rows_ref, sent_ref, in_sem, out_sem = refs[len(after) :]
        loads = []
        for n, at in enumerate(columns):
            for j in range(pieces):
                wide = slice(j * part + at.start, j * part + at.stop)
                target = rows_ref.at[j * own_rows : (j + 1) * own_rows, at]
                loads.append(begin(source_ref.at[:, wide], target, in_sem.at[n, j]))
        pick = pick_matrix(cap, pieces, own_rows, requested_ref[...])
        stores = []
        for n, at in enumerate(columns):
            for load in loads[n * pieces : (n + 1) * pieces]:
                load.wait()
            sent_ref[:, at] = dot(pick, rows_ref[:, at]).astype(BF16)
            stores.append(begin(sent_ref.at[:, at], out_ref.at[:, at], out_sem.at[n]))
        for store in stores:
            store.wait()

    return call(
        body,
        [(shaped((slots, part), BF16), HBM)],
        [(requested, VMEM), (source, HBM)] + [(x, HBM) for x in after],
        name,
        2 * slots * pieces * own_rows * part,
        [
            scratch_like((pieces * own_rows, part), BF16),
            scratch_like((slots, part), BF16),
            pltpu.SemaphoreType.DMA((len(columns), pieces)),
            pltpu.SemaphoreType.DMA((len(columns),)),
        ],
    )[0]


def sum_rows(cap, pieces, own_rows, requested, returned):
    slots, part = returned.shape
    columns = chunks_of(part)

    def body(requested_ref, returned_ref, out_ref, got_ref, sum_ref, in_sem, out_sem):
        loads = [
            begin(returned_ref.at[:, at], got_ref.at[:, at], in_sem.at[n])
            for n, at in enumerate(columns)
        ]
        pick = pick_matrix(cap, pieces, own_rows, requested_ref[...])
        stores = []
        for n, at in enumerate(columns):
            loads[n].wait()
            total = dot_tn(pick, got_ref[:, at]).astype(BF16)
            for j in range(pieces):
                wide = slice(j * part + at.start, j * part + at.stop)
                sum_ref[:, wide] = total[j * own_rows : (j + 1) * own_rows]
                stores.append(
                    begin(sum_ref.at[:, wide], out_ref.at[:, wide], out_sem.at[n, j])
                )
        for store in stores:
            store.wait()

    return call(
        body,
        [(shaped((own_rows, part * pieces), BF16), HBM)],
        [(requested, VMEM), (returned, HBM)],
        "sum_rows",
        2 * slots * pieces * own_rows * part,
        [
            scratch_like((slots, part), BF16),
            scratch_like((own_rows, part * pieces), BF16),
            pltpu.SemaphoreType.DMA((len(columns),)),
            pltpu.SemaphoreType.DMA((len(columns), pieces)),
        ],
    )[0]


def load_factor(order_ref, parts, m, target, sems):
    copies = []
    for n, part in enumerate(parts):
        _, count, rows, cols = part.shape
        start = pl.multiple_of(order_ref[n] * rows, rows)
        for i in range(count):
            at = target.at[pl.ds(start, rows), i * cols : (i + 1) * cols]
            copies.append(begin(part.at[m, i], at, sems.at[n, i]))
    return copies


def wait_all(copies):
    for copy in copies:
        copy.wait()


def place_matrix(cap, pieces, slots, slot):
    wide = jnp.concatenate([slot + j * cap for j in range(pieces)], axis=1)
    return (iota((slots, wide.shape[1]), 0) == wide).astype(BF16)


def load_rows(got_hbm, got_ref, sems):
    return [
        begin(got_hbm.at[:, at], got_ref.at[:, at], sems.at[n])
        for n, at in enumerate(chunks_of(got_ref.shape[1]))
    ]


def stack_rows(pieces, place, loads, got_ref, out_ref):
    part = got_ref.shape[1]
    rows, depth = out_ref.shape[0] // NPHM, out_ref.shape[1]
    for load, at in zip(loads, chunks_of(part)):
        load.wait()
        block = dot_tn(place, got_ref[:, at]).astype(BF16)
        for j in range(pieces):
            column = j * part + at.start
            a, start = column // depth, column % depth
            out_ref[a * rows : (a + 1) * rows, start : start + at.stop - at.start] = block[
                j * rows : (j + 1) * rows
            ]


def store_parts(order_ref, source_ref, outs, sems):
    copies = []
    for n, out in enumerate(outs):
        size = out.shape[1]
        start = pl.multiple_of(order_ref[n] * size, size)
        copies.append(begin(source_ref.at[:, pl.ds(start, size)], out, sems.at[n]))
    return copies


STRIP = 32


def mix_in(mix_ref, m, y_ref, emit):
    rows, cols = y_ref.shape[0] // NPHM, y_ref.shape[1] // NPHM

    def strip(n, carry):
        start = pl.multiple_of(n * STRIP, STRIP)
        total = [jnp.zeros((STRIP, cols), F32)] * NPHM
        for a in range(NPHM):
            for i in range(NPHM):
                block = y_ref[pl.ds(a * rows + start, STRIP), i * cols : (i + 1) * cols]
                for b in range(NPHM):
                    total[b] = total[b] + mix_ref[m * 64 + i * 16 + a * 4 + b] * block
        emit(start, total)
        return carry

    lax.fori_loop(0, rows // STRIP, strip, 0)


def mix_out(mix_ref, m, d_ref, z_ref):
    rows, cols = d_ref.shape[0], d_ref.shape[1] // NPHM

    def strip(n, carry):
        start = pl.multiple_of(n * STRIP, STRIP)
        blocks = [
            d_ref[pl.ds(start, STRIP), b * cols : (b + 1) * cols].astype(F32) for b in range(NPHM)
        ]
        for a in range(NPHM):
            for i in range(NPHM):
                total = mix_ref[m * 64 + i * 16 + a * 4] * blocks[0]
                for b in range(1, NPHM):
                    total = total + mix_ref[m * 64 + i * 16 + a * 4 + b] * blocks[b]
                z_ref[pl.ds(a * rows + start, STRIP), i * cols : (i + 1) * cols] = total.astype(
                    z_ref.dtype
                )
        return carry

    lax.fori_loop(0, rows // STRIP, strip, 0)


def forward_body(
    cap, pieces, sides, slot_ref, mix_ref, order_ref, got_hbm, *refs
):
    parts, refs = refs[:sides], refs[sides:]
    x_outs, refs = refs[:sides], refs[sides:]
    yg_hbm, yu_hbm, act_hbm, slope_hbm, hid_hbm = refs[:5]
    got_ref, side_ref, x_ref, yg_ref, yu_ref, pre_ref, act_ref, slope_ref, hid_ref = refs[5:14]
    got_sem, side_sem, out_sem = refs[14:]
    loads = load_rows(got_hbm, got_ref, got_sem)
    sides_in = [
        load_factor(order_ref, parts, m, side_ref.at[m], side_sem.at[m]) for m in range(2)
    ]
    place = place_matrix(cap, pieces, got_ref.shape[0], slot_ref[...])
    stack_rows(pieces, place, loads, got_ref, x_ref)
    stores = store_parts(order_ref, x_ref, x_outs, out_sem)
    wait_all(sides_in[0])
    yg_ref[...] = dot(x_ref[...], side_ref[0])
    stores.append(begin(yg_ref, yg_hbm, out_sem.at[2]))
    wait_all(sides_in[1])
    yu_ref[...] = dot(x_ref[...], side_ref[1])
    stores.append(begin(yu_ref, yu_hbm, out_sem.at[3]))
    cols = yg_ref.shape[1] // NPHM

    def keep(start, total):
        for b in range(NPHM):
            pre_ref[pl.ds(start, STRIP), b * cols : (b + 1) * cols] = total[b]

    def finish(start, total):
        for b in range(NPHM):
            at = (pl.ds(start, STRIP), slice(b * cols, (b + 1) * cols))
            gate = pre_ref[at]
            sig = jax.nn.sigmoid(gate)
            act = gate * sig
            act_ref[at] = act
            slope_ref[at] = total[b] * (sig + act * (1.0 - sig))
            hid_ref[at] = act * total[b]

    mix_in(mix_ref, 0, yg_ref, keep)
    mix_in(mix_ref, 1, yu_ref, finish)
    stores.append(begin(act_ref, act_hbm, out_sem.at[4]))
    stores.append(begin(slope_ref, slope_hbm, out_sem.at[5]))
    stores.append(begin(hid_ref, hid_hbm, out_sem.at[6]))
    wait_all(stores)


def backward_body(
    cap, pieces, sides, after, slot_ref, mix_ref, order_ref, gate_ref, got_hbm, act_hbm, slope_hbm, hid_hbm,
    *refs,
):
    parts, refs = refs[:sides], refs[sides + after :]
    back_hbm, x_outs, refs = refs[0], refs[1 : 1 + sides], refs[1 + sides :]
    y_hbm, d_hbm, inner_ref = refs[:3]
    (
        got_ref, side_ref, x_ref, y_ref, d_ref, act_ref, slope_ref, hid_ref, zg_ref, zu_ref, grad_ref,
        back_ref, got_sem, side_sem, in_sem, out_sem,
    ) = refs[3:]
    loads = load_rows(got_hbm, got_ref, got_sem)
    down_in = load_factor(order_ref, parts, 2, side_ref.at[2], side_sem.at[2])
    flat_in = [
        begin(source, target, in_sem.at[n])
        for n, (source, target) in enumerate(
            ((act_hbm, act_ref), (slope_hbm, slope_ref), (hid_hbm, hid_ref))
        )
    ]
    sides_in = [
        load_factor(order_ref, parts, m, side_ref.at[m], side_sem.at[m]) for m in range(2)
    ]
    place = place_matrix(cap, pieces, got_ref.shape[0], slot_ref[...])
    stack_rows(pieces, place, loads, got_ref, x_ref)
    stores = store_parts(order_ref, x_ref, x_outs, out_sem)
    wait_all(down_in)
    y_ref[...] = dot(x_ref[...], side_ref[2])
    stores.append(begin(y_ref, y_hbm, out_sem.at[2]))
    cols = y_ref.shape[1] // NPHM
    wait_all(flat_in)

    def finish(start, total):
        gate = gate_ref[pl.ds(start, STRIP), :]
        inner = jnp.zeros((STRIP, cols), F32)
        for b in range(NPHM):
            at = (pl.ds(start, STRIP), slice(b * cols, (b + 1) * cols))
            hidden = hid_ref[at]
            inner = inner + hidden * total[b]
            hidden_grad = gate * total[b]
            d_ref[(0,) + at] = (hidden_grad * slope_ref[at]).astype(BF16)
            d_ref[(1,) + at] = (hidden_grad * act_ref[at]).astype(BF16)
            d_ref[(2,) + at] = (hidden * gate).astype(BF16)
        inner_ref[pl.ds(start, STRIP), :] = inner

    mix_in(mix_ref, 2, y_ref, finish)
    stores.append(begin(d_ref, d_hbm, out_sem.at[3]))
    mix_out(mix_ref, 0, d_ref.at[0], zg_ref)
    mix_out(mix_ref, 1, d_ref.at[1], zu_ref)
    wait_all(sides_in[0])
    wait_all(sides_in[1])
    grad = dot_nt(zg_ref[...], side_ref[0]) + dot_nt(zu_ref[...], side_ref[1])
    grad_ref[...] = grad.astype(BF16)
    part = back_ref.shape[1]
    rows, depth = x_ref.shape[0] // NPHM, x_ref.shape[1]
    for n, at in enumerate(chunks_of(part)):
        blocks = []
        for j in range(pieces):
            column = j * part + at.start
            a, start = column // depth, column % depth
            blocks.append(
                grad_ref[a * rows : (a + 1) * rows, start : start + at.stop - at.start]
            )
        back_ref[:, at] = dot(place, jnp.concatenate(blocks, axis=0)).astype(BF16)
        stores.append(begin(back_ref.at[:, at], back_hbm.at[:, at], out_sem.at[4 + n]))
    wait_all(stores)


def factor_body(count_groups, mix_ref, *refs):
    rows_in, refs = refs[: 3 * count_groups], refs[3 * count_groups :]
    out_hbm, x_ref, g_ref, d_ref, z_ref, sum_ref, in_sem, out_sem = refs
    loads = []
    for n in range(count_groups):
        for k, target in enumerate((x_ref, g_ref, d_ref)):
            loads.append(begin(rows_in[3 * n + k], target.at[n], in_sem.at[n, k]))
    stores = []
    cols = out_hbm.shape[3]
    wait_all(loads)
    for m in (2, 0, 1):
        for n in range(count_groups):
            mix_out(mix_ref, m, d_ref.at[n, m], z_ref.at[n])
        left = g_ref if m == 2 else x_ref
        sum_ref[m] = sum(dot_tn(left[n], z_ref[n]) for n in range(count_groups))
        for i in range(NPHM):
            at = sum_ref.at[m, :, i * cols : (i + 1) * cols]
            stores.append(begin(at, out_hbm.at[m, i], out_sem.at[m, i]))
    wait_all(stores)


def mix_grad_body(yg_hbm, yu_hbm, yd_hbm, d_hbm, out_ref, y_ref, d_ref, sems):
    loads = [begin(d_hbm, d_ref, sems.at[3])]
    for m, source in enumerate((yg_hbm, yu_hbm, yd_hbm)):
        loads.append(begin(source, y_ref.at[m], sems.at[m]))
    wait_all(loads)
    rows, cols = d_ref.shape[1], d_ref.shape[2] // NPHM
    for m in range(3):
        for a in range(NPHM):
            for i in range(NPHM):
                block = y_ref[m, a * rows : (a + 1) * rows, i * cols : (i + 1) * cols]
                for b in range(NPHM):
                    at = m * 64 + i * 16 + a * 4 + b
                    other = d_ref[m, :, b * cols : (b + 1) * cols].astype(F32)
                    out_ref[at : at + 1, :] = jnp.sum(block * other, axis=0, keepdims=True)


def shards(tokens, cotangent, factors, mix, selection, scores):
    peers = lax.axis_size("exp")
    groups = lax.axis_size("seq")
    group = lax.axis_index("seq")
    own_rows, width = tokens.shape
    _, weights, count, depth_own, cols = factors.shape
    depth = depth_own * groups
    hidden = count * cols
    cap = 3 * own_rows // (2 * peers)
    pieces = 1
    while (cap * pieces) % 8:
        pieces *= 2
    lanes = 128
    slots = peers * cap * pieces
    part = width // pieces
    steps = len(chunks_of(part))
    block_len = peers * SELECTED
    rows = selection.shape[1] * selection.shape[2]
    stacked = count * rows
    swap = groups == 2
    pair = [(0, 1), (1, 0)]
    mixing = mix.reshape(-1)
    dma = pltpu.SemaphoreType.DMA

    def across(array):
        return lax.ppermute(array, "seq", pair)

    if swap:
        factor_parts = [factors[0], across(factors)[0]]
        order = jnp.stack([group, 1 - group]).astype(jnp.int32)
    else:
        factor_parts = [lax.all_gather(factors, "seq", axis=3, tiled=True)[0]]
        order = jnp.zeros((2,), jnp.int32)
    sides = len(factor_parts)
    sides_in = [(x, HBM) for x in factor_parts]

    wanted, slot = call(
        functools.partial(index_body, cap, pieces, own_rows, block_len),
        [(shaped((peers, lanes), jnp.int32), VMEM), (shaped((1, rows), jnp.int32), VMEM)],
        [(selection[0], VMEM)],
        "wanted_rows",
        1 << 20,
    )
    requested = lax.all_to_all(wanted, "exp", split_axis=0, concat_axis=0, tiled=True)

    def exchange(array):
        array = array.reshape(peers, cap * pieces, part)
        array = lax.all_to_all(array, "exp", split_axis=0, concat_axis=0, tiled=True)
        return array.reshape(slots, part)

    got_rows = exchange(pick_rows(cap, pieces, requested, tokens, [], "pick_tokens"))
    got_grads = exchange(
        pick_rows(cap, pieces, requested, cotangent, factor_parts[1:], "pick_cotangent")
    )

    gate = jax.nn.sigmoid(scores[0].reshape(-1).astype(F32) / 64.0)
    gate_wide = jnp.broadcast_to(gate[:, None], (rows, cols))

    product = 2 * stacked * depth * hidden
    split = [(shaped((stacked, depth // sides), BF16), HBM)] * sides
    mixed = (shaped((stacked, hidden), F32), HBM)
    flat = (shaped((rows, hidden), F32), HBM)
    got_scratch = scratch_like((slots, part), BF16)
    stack_scratch = scratch_like((stacked, depth), BF16)
    mixed_scratch = scratch_like((stacked, hidden), F32)
    low_scratch = scratch_like((stacked, hidden), BF16)
    flat_scratch = scratch_like((rows, hidden), F32)
    outs = call(
        functools.partial(forward_body, cap, pieces, sides),
        split + [mixed, mixed, flat, flat, flat],
        [(slot, VMEM), (mixing, SMEM), (order, SMEM), (got_rows, HBM)] + sides_in,
        "forward",
        2 * product,
        [got_scratch, scratch_like((2, depth, hidden), BF16), stack_scratch, mixed_scratch, mixed_scratch]
        + [flat_scratch] * 4
        + [dma((steps,)), dma((2, sides, count)), dma((7,))],
    )
    x_parts, (y_gate, y_up, act, slope, hid) = outs[:sides], outs[sides:]
    x_rows = [x_parts[0]] + [across(x) for x in x_parts[1:]]
    after = x_rows[1:]
    outs = call(
        functools.partial(backward_body, cap, pieces, sides, len(after)),
        [(shaped((slots, part), BF16), HBM)]
        + split
        + [mixed, (shaped((weights, rows, hidden), BF16), HBM), (shaped((rows, cols), F32), VMEM)],
        [(slot, VMEM), (mixing, SMEM), (order, SMEM), (gate_wide, VMEM), (got_grads, HBM)]
        + [(x, HBM) for x in (act, slope, hid)]
        + sides_in
        + [(x, HBM) for x in after],
        "backward",
        3 * product,
        [got_scratch, scratch_like((weights, depth, hidden), BF16), stack_scratch, mixed_scratch]
        + [scratch_like((weights, rows, hidden), BF16)]
        + [flat_scratch] * 3
        + [low_scratch] * 2
        + [stack_scratch, got_scratch]
        + [dma((steps,)), dma((weights, sides, count)), dma((3,)), dma((4 + steps,))],
    )
    back, g_parts, (y_down, d_own, inner) = outs[0], outs[1 : 1 + sides], outs[1 + sides :]
    returned = exchange(back)

    d_rows = [d_own] + [across(d_own) for _ in x_parts[1:]]
    g_rows = [g_parts[0]] + [across(x) for x in g_parts[1:]]
    depth_here = depth // sides
    factor_grad = call(
        functools.partial(factor_body, sides),
        [(shaped((weights, count, depth_here, cols), F32), HBM)],
        [(mixing, SMEM)]
        + [(x, HBM) for n in range(sides) for x in (x_rows[n], g_rows[n], d_rows[n])],
        "factor_grad",
        3 * product,
        [scratch_like((sides, stacked, depth_here), BF16)] * 2
        + [
            scratch_like((sides, weights, rows, hidden), BF16),
            scratch_like((sides, stacked, hidden), BF16),
            scratch_like((weights, depth_here, hidden), F32),
            dma((sides, 3)),
            dma((weights, count)),
        ],
    )[0]
    mix_rows = call(
        mix_grad_body,
        [(shaped((mixing.size, cols), F32), VMEM)],
        [(x, HBM) for x in (y_gate, y_up, y_down, d_own)],
        "mix_partials",
        weights * 64 * 2 * rows * cols,
        [
            scratch_like((weights, stacked, hidden), F32),
            scratch_like((weights, rows, hidden), BF16),
            dma((4,)),
        ],
    )[0]
    mix_part = jnp.sum(mix_rows, axis=1).reshape(mix.shape)
    if swap:
        mix_grad = mix_part + across(mix_part)
    else:
        factor_grad = lax.psum_scatter(
            factor_grad.astype(BF16), "seq", scatter_dimension=2, tiled=True
        ).astype(F32)
        mix_grad = lax.psum(mix_part, "seq")
    gate_grad = (jnp.sum(inner, axis=1) * gate * (1.0 - gate)).reshape(selection.shape)
    token_grad = sum_rows(cap, pieces, own_rows, requested, returned)
    return token_grad, factor_grad[None], mix_grad, gate_grad


def solution(mesh):
    return jax.shard_map(
        shards,
        mesh=mesh,
        in_specs=(
            P(("seq", "exp"), None),
            P(("seq", "exp"), None),
            P("exp", None, None, "seq", None),
            P("exp", None, None, None, None),
            P("exp", "seq", None),
            P("exp", "seq", None),
        ),
        out_specs=(
            P(("seq", "exp"), None),
            P("exp", None, None, "seq", None),
            P("exp", None, None, None, None),
            P("exp", "seq", None),
        ),
        check_vma=False,
    )
```

```python
import functools

import jax
import jax.numpy as jnp
from jax import lax
from jax.experimental import pallas as pl
from jax.experimental.pallas import tpu as pltpu
from jax.sharding import PartitionSpec as P

SELECTED = 64
NPHM = 4
VMEM_LIMIT = 63 * 1024 * 1024
F32 = jnp.float32
BF16 = jnp.bfloat16


def iota(shape, dim):
    return lax.broadcasted_iota(jnp.int32, shape, dim)


def dot(left, right):
    return jnp.dot(left, right, preferred_element_type=F32)


def dot_tn(left, right):
    return lax.dot_general(left, right, (((0,), (0,)), ((), ())), preferred_element_type=F32)


def dot_nt(left, right):
    return lax.dot_general(left, right, (((1,), (1,)), ((), ())), preferred_element_type=F32)


HBM = pl.BlockSpec(memory_space=pltpu.HBM)
VMEM = pl.BlockSpec(memory_space=pltpu.VMEM)
SMEM = pl.BlockSpec(memory_space=pltpu.SMEM)


def call(body, outs, ins, name, flops, scratch=()):
    moved = sum(x.size * x.dtype.itemsize for x, _ in list(ins) + list(outs))
    return pl.pallas_call(
        body,
        out_shape=[x for x, _ in outs],
        in_specs=[place for _, place in ins],
        out_specs=[place for _, place in outs],
        scratch_shapes=list(scratch),
        compiler_params=pltpu.CompilerParams(vmem_limit_bytes=VMEM_LIMIT),
        cost_estimate=pl.CostEstimate(flops=flops, bytes_accessed=moved, transcendentals=0),
        name=name,
    )(*[x for x, _ in ins])


def begin(source, target, sem):
    copy = pltpu.make_async_copy(source, target, sem)
    copy.start()
    return copy


def shaped(shape, dtype):
    return jax.ShapeDtypeStruct(shape, dtype)


def scratch_like(shape, dtype):
    return pltpu.VMEM(shape, dtype)


def chunks_of(part):
    chunk = min(part, 512)
    return [slice(c * chunk, (c + 1) * chunk) for c in range(part // chunk)]


def index_body(cap, pieces, own_rows, block_len, chosen_ref, wanted_ref, slot_ref):
    peers, lanes = wanted_ref.shape
    rows = slot_ref.shape[1]
    position = jnp.concatenate(
        [chosen_ref[b : b + 1, :] + b * block_len for b in range(chosen_ref.shape[0])], axis=1
    )
    owner = lax.shift_right_logical(position, own_rows.bit_length() - 1)
    local = position & (own_rows - 1)
    peer = iota((peers, rows), 0)
    mine = (peer == owner).astype(F32)
    count = jnp.sum(mine, axis=1, keepdims=True)
    earlier = jnp.sum(jnp.where(peer < owner, count, 0.0), axis=0, keepdims=True).astype(jnp.int32)
    rank = iota((1, rows), 1) - earlier
    slot_ref[...] = owner * (cap * pieces) + rank
    lane = iota((lanes, rows), 0)
    hit = jnp.zeros((lanes, rows), F32)
    for j in range(pieces):
        hit = hit + (lane == rank + j * cap).astype(F32)
    marked = mine * (local + 1).astype(F32)
    wanted_ref[...] = dot_nt(marked.astype(BF16), hit.astype(BF16)).astype(jnp.int32)


def pick_matrix(cap, pieces, own_rows, requested):
    peers, lanes = requested.shape
    group = cap * pieces
    slots = peers * group
    peer = iota((peers, group, peers), 0).reshape(slots, peers)
    spread = dot(
        (peer == iota((slots, peers), 1)).astype(BF16), requested.astype(F32).astype(BF16)
    )
    place = iota((peers, group, lanes), 1).reshape(slots, lanes)
    row = jnp.sum(
        jnp.where(place == iota((slots, lanes), 1), spread, 0.0), axis=1, keepdims=True
    ).astype(jnp.int32)
    piece = iota((peers, group, 1), 1).reshape(slots, 1)
    shift = jnp.zeros((slots, 1), jnp.int32)
    for j in range(1, pieces):
        shift = shift + jnp.where(piece >= j * cap, own_rows, 0)
    target = jnp.where(row > 0, row - 1 + shift, -1)
    return (target == iota((slots, pieces * own_rows), 1)).astype(BF16)


def pick_rows(cap, pieces, requested, source, after, name):
    own_rows, width = source.shape
    part = width // pieces
    slots = requested.shape[0] * cap * pieces
    columns = chunks_of(part)

    def body(requested_ref, source_ref, *refs):
        out_ref, rows_ref, sent_ref, in_sem, out_sem = refs[len(after) :]
        loads = []
        for n, at in enumerate(columns):
            for j in range(pieces):
                wide = slice(j * part + at.start, j * part + at.stop)
                target = rows_ref.at[j * own_rows : (j + 1) * own_rows, at]
                loads.append(begin(source_ref.at[:, wide], target, in_sem.at[n, j]))
        pick = pick_matrix(cap, pieces, own_rows, requested_ref[...])
        stores = []
        for n, at in enumerate(columns):
            for load in loads[n * pieces : (n + 1) * pieces]:
                load.wait()
            sent_ref[:, at] = dot(pick, rows_ref[:, at]).astype(BF16)
            stores.append(begin(sent_ref.at[:, at], out_ref.at[:, at], out_sem.at[n]))
        for store in stores:
            store.wait()

    return call(
        body,
        [(shaped((slots, part), BF16), HBM)],
        [(requested, VMEM), (source, HBM)] + [(x, HBM) for x in after],
        name,
        2 * slots * pieces * own_rows * part,
        [
            scratch_like((pieces * own_rows, part), BF16),
            scratch_like((slots, part), BF16),
            pltpu.SemaphoreType.DMA((len(columns), pieces)),
            pltpu.SemaphoreType.DMA((len(columns),)),
        ],
    )[0]


def sum_rows(cap, pieces, own_rows, requested, returned):
    slots, part = returned.shape
    columns = chunks_of(part)

    def body(requested_ref, returned_ref, out_ref, got_ref, sum_ref, in_sem, out_sem):
        loads = [
            begin(returned_ref.at[:, at], got_ref.at[:, at], in_sem.at[n])
            for n, at in enumerate(columns)
        ]
        pick = pick_matrix(cap, pieces, own_rows, requested_ref[...])
        stores = []
        for n, at in enumerate(columns):
            loads[n].wait()
            total = dot_tn(pick, got_ref[:, at]).astype(BF16)
            for j in range(pieces):
                wide = slice(j * part + at.start, j * part + at.stop)
                sum_ref[:, wide] = total[j * own_rows : (j + 1) * own_rows]
                stores.append(
                    begin(sum_ref.at[:, wide], out_ref.at[:, wide], out_sem.at[n, j])
                )
        for store in stores:
            store.wait()

    return call(
        body,
        [(shaped((own_rows, part * pieces), BF16), HBM)],
        [(requested, VMEM), (returned, HBM)],
        "sum_rows",
        2 * slots * pieces * own_rows * part,
        [
            scratch_like((slots, part), BF16),
            scratch_like((own_rows, part * pieces), BF16),
            pltpu.SemaphoreType.DMA((len(columns),)),
            pltpu.SemaphoreType.DMA((len(columns), pieces)),
        ],
    )[0]


def load_factor(order_ref, parts, m, target, sems):
    copies = []
    for n, side in enumerate(parts):
        held = m
        for part in side:
            if held < part.shape[0]:
                break
            held -= part.shape[0]
        _, count, rows, cols = part.shape
        start = pl.multiple_of(order_ref[n] * rows, rows)
        for i in range(count):
            at = target.at[pl.ds(start, rows), i * cols : (i + 1) * cols]
            copies.append(begin(part.at[held, i], at, sems.at[n, i]))
    return copies


def sides_of(sides, refs):
    if sides == 1:
        return [refs[:1]], refs[1:]
    return [refs[:1], refs[1:3]], refs[3:]


def wait_all(copies):
    for copy in copies:
        copy.wait()


def place_matrix(cap, pieces, slots, slot):
    wide = jnp.concatenate([slot + j * cap for j in range(pieces)], axis=1)
    return (iota((slots, wide.shape[1]), 0) == wide).astype(BF16)


def load_rows(got_hbm, got_ref, sems):
    return [
        begin(got_hbm.at[:, at], got_ref.at[:, at], sems.at[n])
        for n, at in enumerate(chunks_of(got_ref.shape[1]))
    ]


def stack_rows(pieces, place, loads, got_ref, out_ref):
    part = got_ref.shape[1]
    rows, depth = out_ref.shape[0] // NPHM, out_ref.shape[1]
    for load, at in zip(loads, chunks_of(part)):
        load.wait()
        block = dot_tn(place, got_ref[:, at]).astype(BF16)
        for j in range(pieces):
            column = j * part + at.start
            a, start = column // depth, column % depth
            out_ref[a * rows : (a + 1) * rows, start : start + at.stop - at.start] = block[
                j * rows : (j + 1) * rows
            ]


def store_parts(order_ref, source_ref, outs, sems):
    copies = []
    for n, out in enumerate(outs):
        size = out.shape[1]
        start = pl.multiple_of(order_ref[n] * size, size)
        copies.append(begin(source_ref.at[:, pl.ds(start, size)], out, sems.at[n]))
    return copies


STRIP = 32


def mix_in(mix_ref, m, y_ref, emit):
    rows, cols = y_ref.shape[0] // NPHM, y_ref.shape[1] // NPHM

    def strip(n, carry):
        start = pl.multiple_of(n * STRIP, STRIP)
        total = [jnp.zeros((STRIP, cols), F32)] * NPHM
        for a in range(NPHM):
            for i in range(NPHM):
                block = y_ref[pl.ds(a * rows + start, STRIP), i * cols : (i + 1) * cols]
                for b in range(NPHM):
                    total[b] = total[b] + mix_ref[m * 64 + i * 16 + a * 4 + b] * block
        emit(start, total)
        return carry

    lax.fori_loop(0, rows // STRIP, strip, 0)


def mix_out(mix_ref, m, d_ref, z_ref):
    rows, cols = d_ref.shape[0], d_ref.shape[1] // NPHM

    def strip(n, carry):
        start = pl.multiple_of(n * STRIP, STRIP)
        blocks = [
            d_ref[pl.ds(start, STRIP), b * cols : (b + 1) * cols].astype(F32) for b in range(NPHM)
        ]
        for a in range(NPHM):
            for i in range(NPHM):
                total = mix_ref[m * 64 + i * 16 + a * 4] * blocks[0]
                for b in range(1, NPHM):
                    total = total + mix_ref[m * 64 + i * 16 + a * 4 + b] * blocks[b]
                z_ref[pl.ds(a * rows + start, STRIP), i * cols : (i + 1) * cols] = total.astype(
                    z_ref.dtype
                )
        return carry

    lax.fori_loop(0, rows // STRIP, strip, 0)


def forward_body(
    cap, pieces, sides, slot_ref, mix_ref, order_ref, got_hbm, *refs
):
    parts, refs = sides_of(sides, refs)
    x_outs, refs = refs[:sides], refs[sides:]
    yg_hbm, yu_hbm, act_hbm, slope_hbm, hid_hbm = refs[:5]
    got_ref, side_ref, x_ref, yg_ref, yu_ref, pre_ref, act_ref, slope_ref, hid_ref = refs[5:14]
    got_sem, side_sem, out_sem = refs[14:]
    loads = load_rows(got_hbm, got_ref, got_sem)
    sides_in = [
        load_factor(order_ref, parts, m, side_ref.at[m], side_sem.at[m]) for m in range(2)
    ]
    place = place_matrix(cap, pieces, got_ref.shape[0], slot_ref[...])
    stack_rows(pieces, place, loads, got_ref, x_ref)
    stores = store_parts(order_ref, x_ref, x_outs, out_sem)
    wait_all(sides_in[0])
    yg_ref[...] = dot(x_ref[...], side_ref[0])
    stores.append(begin(yg_ref, yg_hbm, out_sem.at[2]))
    wait_all(sides_in[1])
    yu_ref[...] = dot(x_ref[...], side_ref[1])
    stores.append(begin(yu_ref, yu_hbm, out_sem.at[3]))
    cols = yg_ref.shape[1] // NPHM

    def keep(start, total):
        for b in range(NPHM):
            pre_ref[pl.ds(start, STRIP), b * cols : (b + 1) * cols] = total[b]

    def finish(start, total):
        for b in range(NPHM):
            at = (pl.ds(start, STRIP), slice(b * cols, (b + 1) * cols))
            gate = pre_ref[at]
            sig = jax.nn.sigmoid(gate)
            act = gate * sig
            act_ref[at] = act
            slope_ref[at] = total[b] * (sig + act * (1.0 - sig))
            hid_ref[at] = act * total[b]

    mix_in(mix_ref, 0, yg_ref, keep)
    mix_in(mix_ref, 1, yu_ref, finish)
    stores.append(begin(act_ref, act_hbm, out_sem.at[4]))
    stores.append(begin(slope_ref, slope_hbm, out_sem.at[5]))
    stores.append(begin(hid_ref, hid_hbm, out_sem.at[6]))
    wait_all(stores)


def backward_body(
    cap, pieces, sides, after, slot_ref, mix_ref, order_ref, gate_ref, got_hbm, act_hbm, slope_hbm, hid_hbm,
    *refs,
):
    parts, refs = sides_of(sides, refs)
    refs = refs[after:]
    back_hbm, x_outs, refs = refs[0], refs[1 : 1 + sides], refs[1 + sides :]
    y_hbm, d_hbm, inner_ref = refs[:3]
    (
        got_ref, side_ref, x_ref, y_ref, d_ref, act_ref, slope_ref, hid_ref, zg_ref, zu_ref, grad_ref,
        back_ref, got_sem, side_sem, in_sem, out_sem,
    ) = refs[3:]
    loads = load_rows(got_hbm, got_ref, got_sem)
    down_in = load_factor(order_ref, parts, 2, side_ref.at[2], side_sem.at[2])
    flat_in = [
        begin(source, target, in_sem.at[n])
        for n, (source, target) in enumerate(
            ((act_hbm, act_ref), (slope_hbm, slope_ref), (hid_hbm, hid_ref))
        )
    ]
    sides_in = [
        load_factor(order_ref, parts, m, side_ref.at[m], side_sem.at[m]) for m in range(2)
    ]
    place = place_matrix(cap, pieces, got_ref.shape[0], slot_ref[...])
    stack_rows(pieces, place, loads, got_ref, x_ref)
    stores = store_parts(order_ref, x_ref, x_outs, out_sem)
    wait_all(down_in)
    y_ref[...] = dot(x_ref[...], side_ref[2])
    stores.append(begin(y_ref, y_hbm, out_sem.at[2]))
    cols = y_ref.shape[1] // NPHM
    wait_all(flat_in)

    def finish(start, total):
        gate = gate_ref[pl.ds(start, STRIP), :]
        inner = jnp.zeros((STRIP, cols), F32)
        for b in range(NPHM):
            at = (pl.ds(start, STRIP), slice(b * cols, (b + 1) * cols))
            hidden = hid_ref[at]
            inner = inner + hidden * total[b]
            hidden_grad = gate * total[b]
            d_ref[(0,) + at] = (hidden_grad * slope_ref[at]).astype(BF16)
            d_ref[(1,) + at] = (hidden_grad * act_ref[at]).astype(BF16)
            d_ref[(2,) + at] = (hidden * gate).astype(BF16)
        inner_ref[pl.ds(start, STRIP), :] = inner

    mix_in(mix_ref, 2, y_ref, finish)
    stores.append(begin(d_ref, d_hbm, out_sem.at[3]))
    mix_out(mix_ref, 0, d_ref.at[0], zg_ref)
    mix_out(mix_ref, 1, d_ref.at[1], zu_ref)
    wait_all(sides_in[0])
    wait_all(sides_in[1])
    grad = dot_nt(zg_ref[...], side_ref[0]) + dot_nt(zu_ref[...], side_ref[1])
    grad_ref[...] = grad.astype(BF16)
    part = back_ref.shape[1]
    rows, depth = x_ref.shape[0] // NPHM, x_ref.shape[1]
    for n, at in enumerate(chunks_of(part)):
        blocks = []
        for j in range(pieces):
            column = j * part + at.start
            a, start = column // depth, column % depth
            blocks.append(
                grad_ref[a * rows : (a + 1) * rows, start : start + at.stop - at.start]
            )
        back_ref[:, at] = dot(place, jnp.concatenate(blocks, axis=0)).astype(BF16)
        stores.append(begin(back_ref.at[:, at], back_hbm.at[:, at], out_sem.at[4 + n]))
    wait_all(stores)


def factor_body(count_groups, mix_ref, *refs):
    rows_in, refs = refs[: 3 * count_groups], refs[3 * count_groups :]
    out_hbm, x_ref, g_ref, d_ref, z_ref, sum_ref, in_sem, out_sem = refs
    loads = []
    for n in range(count_groups):
        for k, target in enumerate((x_ref, g_ref, d_ref)):
            loads.append(begin(rows_in[3 * n + k], target.at[n], in_sem.at[n, k]))
    stores = []
    cols = out_hbm.shape[3]
    wait_all(loads)
    for m in (2, 0, 1):
        for n in range(count_groups):
            mix_out(mix_ref, m, d_ref.at[n, m], z_ref.at[n])
        left = g_ref if m == 2 else x_ref
        sum_ref[m] = sum(dot_tn(left[n], z_ref[n]) for n in range(count_groups))
        for i in range(NPHM):
            at = sum_ref.at[m, :, i * cols : (i + 1) * cols]
            stores.append(begin(at, out_hbm.at[m, i], out_sem.at[m, i]))
    wait_all(stores)


def mix_grad_body(yg_hbm, yu_hbm, yd_hbm, d_hbm, out_ref, y_ref, d_ref, sems):
    loads = [begin(d_hbm, d_ref, sems.at[3])]
    for m, source in enumerate((yg_hbm, yu_hbm, yd_hbm)):
        loads.append(begin(source, y_ref.at[m], sems.at[m]))
    wait_all(loads)
    rows, cols = d_ref.shape[1], d_ref.shape[2] // NPHM
    for m in range(3):
        for a in range(NPHM):
            for i in range(NPHM):
                block = y_ref[m, a * rows : (a + 1) * rows, i * cols : (i + 1) * cols]
                for b in range(NPHM):
                    at = m * 64 + i * 16 + a * 4 + b
                    other = d_ref[m, :, b * cols : (b + 1) * cols].astype(F32)
                    out_ref[at : at + 1, :] = jnp.sum(block * other, axis=0, keepdims=True)


def shards(tokens, cotangent, factors, mix, selection, scores):
    peers = lax.axis_size("exp")
    groups = lax.axis_size("seq")
    group = lax.axis_index("seq")
    own_rows, width = tokens.shape
    _, weights, count, depth_own, cols = factors.shape
    depth = depth_own * groups
    hidden = count * cols
    cap = 3 * own_rows // (2 * peers)
    pieces = 1
    while (cap * pieces) % 8:
        pieces *= 2
    lanes = 128
    slots = peers * cap * pieces
    part = width // pieces
    steps = len(chunks_of(part))
    block_len = peers * SELECTED
    rows = selection.shape[1] * selection.shape[2]
    stacked = count * rows
    swap = groups == 2
    pair = [(0, 1), (1, 0)]
    mixing = mix.reshape(-1)
    dma = pltpu.SemaphoreType.DMA

    def across(array):
        return lax.ppermute(array, "seq", pair)

    if swap:
        early, late = across(factors[0, :1]), across(factors[0, 1:])
        factor_parts = [[factors[0]], [early, late]]
        order = jnp.stack([group, 1 - group]).astype(jnp.int32)
    else:
        early = late = None
        factor_parts = [[lax.all_gather(factors, "seq", axis=3, tiled=True)[0]]]
        order = jnp.zeros((2,), jnp.int32)
    sides = len(factor_parts)
    sides_in = [(x, HBM) for side in factor_parts for x in side]

    wanted, slot = call(
        functools.partial(index_body, cap, pieces, own_rows, block_len),
        [(shaped((peers, lanes), jnp.int32), VMEM), (shaped((1, rows), jnp.int32), VMEM)],
        [(selection[0], VMEM)],
        "wanted_rows",
        1 << 20,
    )
    requested = lax.all_to_all(wanted, "exp", split_axis=0, concat_axis=0, tiled=True)

    def exchange(array):
        array = array.reshape(peers, cap * pieces, part)
        array = lax.all_to_all(array, "exp", split_axis=0, concat_axis=0, tiled=True)
        return array.reshape(slots, part)

    got_rows = exchange(pick_rows(cap, pieces, requested, tokens, [early] if swap else [], "pick_tokens"))
    got_grads = exchange(
        pick_rows(cap, pieces, requested, cotangent, [late] if swap else [], "pick_cotangent")
    )

    gate = jax.nn.sigmoid(scores[0].reshape(-1).astype(F32) / 64.0)
    gate_wide = jnp.broadcast_to(gate[:, None], (rows, cols))

    product = 2 * stacked * depth * hidden
    split = [(shaped((stacked, depth // sides), BF16), HBM)] * sides
    mixed = (shaped((stacked, hidden), F32), HBM)
    flat = (shaped((rows, hidden), F32), HBM)
    got_scratch = scratch_like((slots, part), BF16)
    stack_scratch = scratch_like((stacked, depth), BF16)
    mixed_scratch = scratch_like((stacked, hidden), F32)
    low_scratch = scratch_like((stacked, hidden), BF16)
    flat_scratch = scratch_like((rows, hidden), F32)
    outs = call(
        functools.partial(forward_body, cap, pieces, sides),
        split + [mixed, mixed, flat, flat, flat],
        [(slot, VMEM), (mixing, SMEM), (order, SMEM), (got_rows, HBM)] + sides_in,
        "forward",
        2 * product,
        [got_scratch, scratch_like((2, depth, hidden), BF16), stack_scratch, mixed_scratch, mixed_scratch]
        + [flat_scratch] * 4
        + [dma((steps,)), dma((2, sides, count)), dma((7,))],
    )
    x_parts, (y_gate, y_up, act, slope, hid) = outs[:sides], outs[sides:]
    x_rows = [x_parts[0]] + [across(x) for x in x_parts[1:]]
    after = x_rows[1:]
    outs = call(
        functools.partial(backward_body, cap, pieces, sides, len(after)),
        [(shaped((slots, part), BF16), HBM)]
        + split
        + [mixed, (shaped((weights, rows, hidden), BF16), HBM), (shaped((rows, cols), F32), VMEM)],
        [(slot, VMEM), (mixing, SMEM), (order, SMEM), (gate_wide, VMEM), (got_grads, HBM)]
        + [(x, HBM) for x in (act, slope, hid)]
        + sides_in
        + [(x, HBM) for x in after],
        "backward",
        3 * product,
        [got_scratch, scratch_like((weights, depth, hidden), BF16), stack_scratch, mixed_scratch]
        + [scratch_like((weights, rows, hidden), BF16)]
        + [flat_scratch] * 3
        + [low_scratch] * 2
        + [stack_scratch, got_scratch]
        + [dma((steps,)), dma((weights, sides, count)), dma((3,)), dma((4 + steps,))],
    )
    back, g_parts, (y_down, d_own, inner) = outs[0], outs[1 : 1 + sides], outs[1 + sides :]
    returned = exchange(back)

    d_rows = [d_own] + [across(d_own) for _ in x_parts[1:]]
    g_rows = [g_parts[0]] + [across(x) for x in g_parts[1:]]
    depth_here = depth // sides
    factor_grad = call(
        functools.partial(factor_body, sides),
        [(shaped((weights, count, depth_here, cols), F32), HBM)],
        [(mixing, SMEM)]
        + [(x, HBM) for n in range(sides) for x in (x_rows[n], g_rows[n], d_rows[n])],
        "factor_grad",
        3 * product,
        [scratch_like((sides, stacked, depth_here), BF16)] * 2
        + [
            scratch_like((sides, weights, rows, hidden), BF16),
            scratch_like((sides, stacked, hidden), BF16),
            scratch_like((weights, depth_here, hidden), F32),
            dma((sides, 3)),
            dma((weights, count)),
        ],
    )[0]
    mix_rows = call(
        mix_grad_body,
        [(shaped((mixing.size, cols), F32), VMEM)],
        [(x, HBM) for x in (y_gate, y_up, y_down, d_own)],
        "mix_partials",
        weights * 64 * 2 * rows * cols,
        [
            scratch_like((weights, stacked, hidden), F32),
            scratch_like((weights, rows, hidden), BF16),
            dma((4,)),
        ],
    )[0]
    mix_part = jnp.sum(mix_rows, axis=1).reshape(mix.shape)
    if swap:
        mix_grad = mix_part + across(mix_part)
    else:
        factor_grad = lax.psum_scatter(
            factor_grad.astype(BF16), "seq", scatter_dimension=2, tiled=True
        ).astype(F32)
        mix_grad = lax.psum(mix_part, "seq")
    gate_grad = (jnp.sum(inner, axis=1) * gate * (1.0 - gate)).reshape(selection.shape)
    token_grad = sum_rows(cap, pieces, own_rows, requested, returned)
    return token_grad, factor_grad[None], mix_grad, gate_grad


def solution(mesh):
    return jax.shard_map(
        shards,
        mesh=mesh,
        in_specs=(
            P(("seq", "exp"), None),
            P(("seq", "exp"), None),
            P("exp", None, None, "seq", None),
            P("exp", None, None, None, None),
            P("exp", "seq", None),
            P("exp", "seq", None),
        ),
        out_specs=(
            P(("seq", "exp"), None),
            P("exp", None, None, "seq", None),
            P("exp", None, None, None, None),
            P("exp", "seq", None),
        ),
        check_vma=False,
    )
```

```python
import functools

import jax
import jax.numpy as jnp
from jax import lax
from jax.experimental import pallas as pl
from jax.experimental.pallas import tpu as pltpu
from jax.sharding import PartitionSpec as P

SELECTED = 64
NPHM = 4
VMEM_LIMIT = 63 * 1024 * 1024
F32 = jnp.float32
BF16 = jnp.bfloat16


def iota(shape, dim):
    return lax.broadcasted_iota(jnp.int32, shape, dim)


def dot(left, right):
    return jnp.dot(left, right, preferred_element_type=F32)


def dot_tn(left, right):
    return lax.dot_general(left, right, (((0,), (0,)), ((), ())), preferred_element_type=F32)


def dot_nt(left, right):
    return lax.dot_general(left, right, (((1,), (1,)), ((), ())), preferred_element_type=F32)


HBM = pl.BlockSpec(memory_space=pltpu.HBM)
VMEM = pl.BlockSpec(memory_space=pltpu.VMEM)
SMEM = pl.BlockSpec(memory_space=pltpu.SMEM)


def call(body, outs, ins, name, flops, scratch=()):
    moved = sum(x.size * x.dtype.itemsize for x, _ in list(ins) + list(outs))
    return pl.pallas_call(
        body,
        out_shape=[x for x, _ in outs],
        in_specs=[place for _, place in ins],
        out_specs=[place for _, place in outs],
        scratch_shapes=list(scratch),
        compiler_params=pltpu.CompilerParams(vmem_limit_bytes=VMEM_LIMIT),
        cost_estimate=pl.CostEstimate(flops=flops, bytes_accessed=moved, transcendentals=0),
        name=name,
    )(*[x for x, _ in ins])


def begin(source, target, sem):
    copy = pltpu.make_async_copy(source, target, sem)
    copy.start()
    return copy


def shaped(shape, dtype):
    return jax.ShapeDtypeStruct(shape, dtype)


def scratch_like(shape, dtype):
    return pltpu.VMEM(shape, dtype)


def chunks_of(part):
    chunk = min(part, 512)
    return [slice(c * chunk, (c + 1) * chunk) for c in range(part // chunk)]


def index_body(cap, pieces, own_rows, block_len, me_ref, chosen_ref, wanted_ref, slot_ref):
    peers, lanes = wanted_ref.shape
    rows = slot_ref.shape[1]
    position = jnp.concatenate(
        [chosen_ref[b : b + 1, :] + b * block_len for b in range(chosen_ref.shape[0])], axis=1
    )
    owner = lax.shift_right_logical(position, own_rows.bit_length() - 1)
    local = position & (own_rows - 1)
    peer = iota((peers, rows), 0)
    mine = (peer == owner).astype(F32)
    count = jnp.sum(mine, axis=1, keepdims=True)
    earlier = jnp.sum(jnp.where(peer < owner, count, 0.0), axis=0, keepdims=True).astype(jnp.int32)
    rank = iota((1, rows), 1) - earlier
    slot_ref[...] = (owner ^ me_ref[0]) * (cap * pieces) + rank
    lane = iota((lanes, rows), 0)
    hit = jnp.zeros((lanes, rows), F32)
    for j in range(pieces):
        hit = hit + (lane == rank + j * cap).astype(F32)
    marked = mine * (local + 1).astype(F32)
    wanted_ref[...] = dot_nt(marked.astype(BF16), hit.astype(BF16)).astype(jnp.int32)


def pick_matrix(cap, pieces, own_rows, me, requested):
    peers, lanes = requested.shape
    group = cap * pieces
    slots = peers * group
    peer = iota((peers, group, peers), 0).reshape(slots, peers) ^ me
    spread = dot(
        (peer == iota((slots, peers), 1)).astype(BF16), requested.astype(F32).astype(BF16)
    )
    place = iota((peers, group, lanes), 1).reshape(slots, lanes)
    row = jnp.sum(
        jnp.where(place == iota((slots, lanes), 1), spread, 0.0), axis=1, keepdims=True
    ).astype(jnp.int32)
    piece = iota((peers, group, 1), 1).reshape(slots, 1)
    shift = jnp.zeros((slots, 1), jnp.int32)
    for j in range(1, pieces):
        shift = shift + jnp.where(piece >= j * cap, own_rows, 0)
    target = jnp.where(row > 0, row - 1 + shift, -1)
    return (target == iota((slots, pieces * own_rows), 1)).astype(BF16)


def slab_specs(count, slots, part):
    return [(shaped((slots // count, part), BF16), HBM)] * count


def store_slabs(source_ref, at, outs, sems):
    size = outs[0].shape[0]
    return [
        begin(source_ref.at[k * size : (k + 1) * size, at], out.at[:, at], sems.at[k])
        for k, out in enumerate(outs)
    ]


def load_slabs(slabs, target_ref, sems):
    size = slabs[0].shape[0]
    return [
        begin(slab, target_ref.at[k * size : (k + 1) * size], sems.at[k])
        for k, slab in enumerate(slabs)
    ]


def pick_rows(cap, pieces, count, me, requested, source, name):
    own_rows, width = source.shape
    part = width // pieces
    slots = requested.shape[0] * cap * pieces
    columns = chunks_of(part)

    def body(me_ref, requested_ref, source_ref, *refs):
        outs, (rows_ref, sent_ref, in_sem, out_sem) = refs[:count], refs[count:]
        loads = []
        for n, at in enumerate(columns):
            for j in range(pieces):
                wide = slice(j * part + at.start, j * part + at.stop)
                target = rows_ref.at[j * own_rows : (j + 1) * own_rows, at]
                loads.append(begin(source_ref.at[:, wide], target, in_sem.at[n, j]))
        pick = pick_matrix(cap, pieces, own_rows, me_ref[0], requested_ref[...])
        stores = []
        for n, at in enumerate(columns):
            wait_all(loads[n * pieces : (n + 1) * pieces])
            sent_ref[:, at] = dot(pick, rows_ref[:, at]).astype(BF16)
            stores += store_slabs(sent_ref, at, outs, out_sem.at[n])
        wait_all(stores)

    return call(
        body,
        slab_specs(count, slots, part),
        [(me, SMEM), (requested, VMEM), (source, HBM)],
        name,
        2 * slots * pieces * own_rows * part,
        [
            scratch_like((pieces * own_rows, part), BF16),
            scratch_like((slots, part), BF16),
            pltpu.SemaphoreType.DMA((len(columns), pieces)),
            pltpu.SemaphoreType.DMA((len(columns), count)),
        ],
    )


def sum_rows(cap, pieces, own_rows, me, requested, returned):
    count, part = len(returned), returned[0].shape[1]
    slots = count * returned[0].shape[0]
    columns = chunks_of(part)

    def body(me_ref, requested_ref, *refs):
        slabs, (out_ref, got_ref, sum_ref, in_sem, out_sem) = refs[:count], refs[count:]
        loads = load_slabs(slabs, got_ref, in_sem)
        pick = pick_matrix(cap, pieces, own_rows, me_ref[0], requested_ref[...])
        wait_all(loads)
        stores = []
        for n, at in enumerate(columns):
            total = dot_tn(pick, got_ref[:, at]).astype(BF16)
            for j in range(pieces):
                wide = slice(j * part + at.start, j * part + at.stop)
                sum_ref[:, wide] = total[j * own_rows : (j + 1) * own_rows]
                stores.append(
                    begin(sum_ref.at[:, wide], out_ref.at[:, wide], out_sem.at[n, j])
                )
        wait_all(stores)

    return call(
        body,
        [(shaped((own_rows, part * pieces), BF16), HBM)],
        [(me, SMEM), (requested, VMEM)] + [(x, HBM) for x in returned],
        "sum_rows",
        2 * slots * pieces * own_rows * part,
        [
            scratch_like((slots, part), BF16),
            scratch_like((own_rows, part * pieces), BF16),
            pltpu.SemaphoreType.DMA((count,)),
            pltpu.SemaphoreType.DMA((len(columns), pieces)),
        ],
    )[0]


def load_factor(order_ref, parts, m, target, sems):
    copies = []
    for n, side in enumerate(parts):
        held = m
        for part in side:
            if held < part.shape[0]:
                break
            held -= part.shape[0]
        _, count, rows, cols = part.shape
        start = pl.multiple_of(order_ref[n] * rows, rows)
        for i in range(count):
            at = target.at[pl.ds(start, rows), i * cols : (i + 1) * cols]
            copies.append(begin(part.at[held, i], at, sems.at[n, i]))
    return copies


def sides_of(sides, refs):
    if sides == 1:
        return [refs[:1]], refs[1:]
    return [refs[:1], refs[1:2]], refs[2:]


def wait_all(copies):
    for copy in copies:
        copy.wait()


def place_matrix(cap, pieces, slots, slot):
    wide = jnp.concatenate([slot + j * cap for j in range(pieces)], axis=1)
    return (iota((slots, wide.shape[1]), 0) == wide).astype(BF16)


def stack_rows(pieces, place, got_ref, out_ref):
    part = got_ref.shape[1]
    rows, depth = out_ref.shape[0] // NPHM, out_ref.shape[1]
    for at in chunks_of(part):
        block = dot_tn(place, got_ref[:, at]).astype(BF16)
        for j in range(pieces):
            column = j * part + at.start
            a, start = column // depth, column % depth
            out_ref[a * rows : (a + 1) * rows, start : start + at.stop - at.start] = block[
                j * rows : (j + 1) * rows
            ]


def store_parts(order_ref, source_ref, outs, sems):
    copies = []
    for n, out in enumerate(outs):
        size = out.shape[1]
        start = pl.multiple_of(order_ref[n] * size, size)
        copies.append(begin(source_ref.at[:, pl.ds(start, size)], out, sems.at[n]))
    return copies


STRIP = 32


def mix_in(mix_ref, m, y_ref, emit):
    rows, cols = y_ref.shape[0] // NPHM, y_ref.shape[1] // NPHM

    def strip(n, carry):
        start = pl.multiple_of(n * STRIP, STRIP)
        total = [jnp.zeros((STRIP, cols), F32)] * NPHM
        for a in range(NPHM):
            for i in range(NPHM):
                block = y_ref[pl.ds(a * rows + start, STRIP), i * cols : (i + 1) * cols]
                for b in range(NPHM):
                    total[b] = total[b] + mix_ref[m * 64 + i * 16 + a * 4 + b] * block
        emit(start, total)
        return carry

    lax.fori_loop(0, rows // STRIP, strip, 0)


def mix_out(mix_ref, m, d_ref, z_ref):
    rows, cols = d_ref.shape[0], d_ref.shape[1] // NPHM

    def strip(n, carry):
        start = pl.multiple_of(n * STRIP, STRIP)
        blocks = [
            d_ref[pl.ds(start, STRIP), b * cols : (b + 1) * cols].astype(F32) for b in range(NPHM)
        ]
        for a in range(NPHM):
            for i in range(NPHM):
                total = mix_ref[m * 64 + i * 16 + a * 4] * blocks[0]
                for b in range(1, NPHM):
                    total = total + mix_ref[m * 64 + i * 16 + a * 4 + b] * blocks[b]
                z_ref[pl.ds(a * rows + start, STRIP), i * cols : (i + 1) * cols] = total.astype(
                    z_ref.dtype
                )
        return carry

    lax.fori_loop(0, rows // STRIP, strip, 0)


def forward_body(
    cap, pieces, sides, count, slot_ref, mix_ref, order_ref, *refs
):
    slabs, refs = refs[:count], refs[count:]
    parts, refs = sides_of(sides, refs)
    x_outs, refs = refs[:sides], refs[sides:]
    yg_hbm, yu_hbm, act_hbm, slope_hbm, hid_hbm = refs[:5]
    got_ref, side_ref, x_ref, yg_ref, yu_ref, pre_ref, act_ref, slope_ref, hid_ref = refs[5:14]
    got_sem, side_sem, out_sem = refs[14:]
    loads = load_slabs(slabs, got_ref, got_sem)
    sides_in = [
        load_factor(order_ref, parts, m, side_ref.at[m], side_sem.at[m]) for m in range(2)
    ]
    place = place_matrix(cap, pieces, got_ref.shape[0], slot_ref[...])
    wait_all(loads)
    stack_rows(pieces, place, got_ref, x_ref)
    stores = store_parts(order_ref, x_ref, x_outs, out_sem)
    wait_all(sides_in[0])
    yg_ref[...] = dot(x_ref[...], side_ref[0])
    stores.append(begin(yg_ref, yg_hbm, out_sem.at[2]))
    wait_all(sides_in[1])
    yu_ref[...] = dot(x_ref[...], side_ref[1])
    stores.append(begin(yu_ref, yu_hbm, out_sem.at[3]))
    cols = yg_ref.shape[1] // NPHM

    def keep(start, total):
        for b in range(NPHM):
            pre_ref[pl.ds(start, STRIP), b * cols : (b + 1) * cols] = total[b]

    def finish(start, total):
        for b in range(NPHM):
            at = (pl.ds(start, STRIP), slice(b * cols, (b + 1) * cols))
            gate = pre_ref[at]
            sig = jax.nn.sigmoid(gate)
            act = gate * sig
            act_ref[at] = act
            slope_ref[at] = total[b] * (sig + act * (1.0 - sig))
            hid_ref[at] = act * total[b]

    mix_in(mix_ref, 0, yg_ref, keep)
    mix_in(mix_ref, 1, yu_ref, finish)
    stores.append(begin(act_ref, act_hbm, out_sem.at[4]))
    stores.append(begin(slope_ref, slope_hbm, out_sem.at[5]))
    stores.append(begin(hid_ref, hid_hbm, out_sem.at[6]))
    wait_all(stores)


def backward_body(
    cap, pieces, sides, after, count, slot_ref, mix_ref, order_ref, gate_ref, act_hbm, slope_hbm, hid_hbm,
    *refs,
):
    slabs, refs = refs[:count], refs[count:]
    parts, refs = sides_of(sides, refs)
    refs = refs[after:]
    backs, refs = refs[:count], refs[count:]
    x_outs, refs = refs[:sides], refs[sides:]
    y_hbm, d_hbm, inner_ref = refs[:3]
    (
        got_ref, side_ref, x_ref, y_ref, d_ref, act_ref, slope_ref, hid_ref, zg_ref, zu_ref, grad_ref,
        back_ref, got_sem, side_sem, in_sem, out_sem, back_sem,
    ) = refs[3:]
    loads = load_slabs(slabs, got_ref, got_sem)
    down_in = load_factor(order_ref, parts, 2, side_ref.at[2], side_sem.at[2])
    flat_in = [
        begin(source, target, in_sem.at[n])
        for n, (source, target) in enumerate(
            ((act_hbm, act_ref), (slope_hbm, slope_ref), (hid_hbm, hid_ref))
        )
    ]
    sides_in = [
        load_factor(order_ref, parts, m, side_ref.at[m], side_sem.at[m]) for m in range(2)
    ]
    place = place_matrix(cap, pieces, got_ref.shape[0], slot_ref[...])
    wait_all(loads)
    stack_rows(pieces, place, got_ref, x_ref)
    stores = store_parts(order_ref, x_ref, x_outs, out_sem)
    wait_all(down_in)
    y_ref[...] = dot(x_ref[...], side_ref[2])
    stores.append(begin(y_ref, y_hbm, out_sem.at[2]))
    cols = y_ref.shape[1] // NPHM
    wait_all(flat_in)

    def finish(start, total):
        gate = gate_ref[pl.ds(start, STRIP), :]
        inner = jnp.zeros((STRIP, cols), F32)
        for b in range(NPHM):
            at = (pl.ds(start, STRIP), slice(b * cols, (b + 1) * cols))
            hidden = hid_ref[at]
            inner = inner + hidden * total[b]
            hidden_grad = gate * total[b]
            d_ref[(0,) + at] = (hidden_grad * slope_ref[at]).astype(BF16)
            d_ref[(1,) + at] = (hidden_grad * act_ref[at]).astype(BF16)
            d_ref[(2,) + at] = (hidden * gate).astype(BF16)
        inner_ref[pl.ds(start, STRIP), :] = inner

    mix_in(mix_ref, 2, y_ref, finish)
    stores.append(begin(d_ref, d_hbm, out_sem.at[3]))
    mix_out(mix_ref, 0, d_ref.at[0], zg_ref)
    mix_out(mix_ref, 1, d_ref.at[1], zu_ref)
    wait_all(sides_in[0])
    wait_all(sides_in[1])
    grad = dot_nt(zg_ref[...], side_ref[0]) + dot_nt(zu_ref[...], side_ref[1])
    grad_ref[...] = grad.astype(BF16)
    part = back_ref.shape[1]
    rows, depth = x_ref.shape[0] // NPHM, x_ref.shape[1]
    for n, at in enumerate(chunks_of(part)):
        blocks = []
        for j in range(pieces):
            column = j * part + at.start
            a, start = column // depth, column % depth
            blocks.append(
                grad_ref[a * rows : (a + 1) * rows, start : start + at.stop - at.start]
            )
        back_ref[:, at] = dot(place, jnp.concatenate(blocks, axis=0)).astype(BF16)
        stores += store_slabs(back_ref, at, backs, back_sem.at[n])
    wait_all(stores)


def factor_body(count_groups, mix_ref, *refs):
    rows_in, refs = refs[: 3 * count_groups], refs[3 * count_groups :]
    out_hbm, x_ref, g_ref, d_ref, z_ref, sum_ref, in_sem, out_sem = refs
    loads = []
    for n in range(count_groups):
        for k, target in enumerate((x_ref, g_ref, d_ref)):
            loads.append(begin(rows_in[3 * n + k], target.at[n], in_sem.at[n, k]))
    stores = []
    cols = out_hbm.shape[3]
    wait_all(loads)
    for m in (2, 0, 1):
        for n in range(count_groups):
            mix_out(mix_ref, m, d_ref.at[n, m], z_ref.at[n])
        left = g_ref if m == 2 else x_ref
        sum_ref[m] = sum(dot_tn(left[n], z_ref[n]) for n in range(count_groups))
        for i in range(NPHM):
            at = sum_ref.at[m, :, i * cols : (i + 1) * cols]
            stores.append(begin(at, out_hbm.at[m, i], out_sem.at[m, i]))
    wait_all(stores)


def mix_grad_body(yg_hbm, yu_hbm, yd_hbm, d_hbm, out_ref, y_ref, d_ref, sems):
    loads = [begin(d_hbm, d_ref, sems.at[3])]
    for m, source in enumerate((yg_hbm, yu_hbm, yd_hbm)):
        loads.append(begin(source, y_ref.at[m], sems.at[m]))
    wait_all(loads)
    rows, cols = d_ref.shape[1], d_ref.shape[2] // NPHM
    for m in range(3):
        for a in range(NPHM):
            for i in range(NPHM):
                block = y_ref[m, a * rows : (a + 1) * rows, i * cols : (i + 1) * cols]
                for b in range(NPHM):
                    at = m * 64 + i * 16 + a * 4 + b
                    other = d_ref[m, :, b * cols : (b + 1) * cols].astype(F32)
                    out_ref[at : at + 1, :] = jnp.sum(block * other, axis=0, keepdims=True)


def shards(tokens, cotangent, factors, mix, selection, scores):
    peers = lax.axis_size("exp")
    groups = lax.axis_size("seq")
    group = lax.axis_index("seq")
    own_rows, width = tokens.shape
    _, weights, count, depth_own, cols = factors.shape
    depth = depth_own * groups
    hidden = count * cols
    cap = 3 * own_rows // (2 * peers)
    pieces = 1
    while (cap * pieces) % 16:
        pieces *= 2
    lanes = 128
    slots = peers * cap * pieces
    part = width // pieces
    steps = len(chunks_of(part))
    block_len = peers * SELECTED
    rows = selection.shape[1] * selection.shape[2]
    stacked = count * rows
    swap = groups == 2
    pair = [(0, 1), (1, 0)]
    mixing = mix.reshape(-1)
    dma = pltpu.SemaphoreType.DMA

    def across(array):
        return lax.ppermute(array, "seq", pair)

    if swap:
        factor_parts = [[factors[0]], [across(factors)[0]]]
        order = jnp.stack([group, 1 - group]).astype(jnp.int32)
    else:
        factor_parts = [[lax.all_gather(factors, "seq", axis=3, tiled=True)[0]]]
        order = jnp.zeros((2,), jnp.int32)
    sides = len(factor_parts)
    direct = peers <= 16
    count_slabs = peers if direct else 1
    me = lax.axis_index("exp").astype(jnp.int32) if direct else jnp.int32(0)
    me = me.reshape(1)
    sides_in = [(x, HBM) for side in factor_parts for x in side]

    wanted, slot = call(
        functools.partial(index_body, cap, pieces, own_rows, block_len),
        [(shaped((peers, lanes), jnp.int32), VMEM), (shaped((1, rows), jnp.int32), VMEM)],
        [(me, SMEM), (selection[0], VMEM)],
        "wanted_rows",
        1 << 20,
    )
    requested = lax.all_to_all(wanted, "exp", split_axis=0, concat_axis=0, tiled=True)

    def exchange(slabs):
        if direct:
            return [slabs[0]] + [
                lax.ppermute(slabs[k], "exp", [(n, n ^ k) for n in range(peers)])
                for k in range(1, peers)
            ]
        array = slabs[0].reshape(peers, cap * pieces, part)
        array = lax.all_to_all(array, "exp", split_axis=0, concat_axis=0, tiled=True)
        return [array.reshape(slots, part)]

    def picked(source, name):
        return pick_rows(cap, pieces, count_slabs, me, requested, source, name)

    got_rows = exchange(picked(tokens, "pick_tokens"))
    got_grads = exchange(picked(cotangent, "pick_cotangent"))

    gate = jax.nn.sigmoid(scores[0].reshape(-1).astype(F32) / 64.0)
    gate_wide = jnp.broadcast_to(gate[:, None], (rows, cols))

    product = 2 * stacked * depth * hidden
    split = [(shaped((stacked, depth // sides), BF16), HBM)] * sides
    mixed = (shaped((stacked, hidden), F32), HBM)
    flat = (shaped((rows, hidden), F32), HBM)
    got_scratch = scratch_like((slots, part), BF16)
    stack_scratch = scratch_like((stacked, depth), BF16)
    mixed_scratch = scratch_like((stacked, hidden), F32)
    low_scratch = scratch_like((stacked, hidden), BF16)
    flat_scratch = scratch_like((rows, hidden), F32)
    outs = call(
        functools.partial(forward_body, cap, pieces, sides, count_slabs),
        split + [mixed, mixed, flat, flat, flat],
        [(slot, VMEM), (mixing, SMEM), (order, SMEM)]
        + [(x, HBM) for x in got_rows]
        + sides_in,
        "forward",
        2 * product,
        [got_scratch, scratch_like((2, depth, hidden), BF16), stack_scratch, mixed_scratch, mixed_scratch]
        + [flat_scratch] * 4
        + [dma((count_slabs,)), dma((2, sides, count)), dma((7,))],
    )
    x_parts, (y_gate, y_up, act, slope, hid) = outs[:sides], outs[sides:]
    x_rows = [x_parts[0]] + [across(x) for x in x_parts[1:]]
    after = x_rows[1:]
    outs = call(
        functools.partial(backward_body, cap, pieces, sides, len(after), count_slabs),
        slab_specs(count_slabs, slots, part)
        + split
        + [mixed, (shaped((weights, rows, hidden), BF16), HBM), (shaped((rows, cols), F32), VMEM)],
        [(slot, VMEM), (mixing, SMEM), (order, SMEM), (gate_wide, VMEM)]
        + [(x, HBM) for x in [act, slope, hid] + got_grads]
        + sides_in
        + [(x, HBM) for x in after],
        "backward",
        3 * product,
        [got_scratch, scratch_like((weights, depth, hidden), BF16), stack_scratch, mixed_scratch]
        + [scratch_like((weights, rows, hidden), BF16)]
        + [flat_scratch] * 3
        + [low_scratch] * 2
        + [stack_scratch, got_scratch]
        + [dma((count_slabs,)), dma((weights, sides, count)), dma((3,)), dma((4,))]
        + [dma((steps, count_slabs))],
    )
    back, outs = outs[:count_slabs], outs[count_slabs:]
    g_parts, (y_down, d_own, inner) = outs[:sides], outs[sides:]
    returned = exchange(back)

    d_rows = [d_own] + [across(d_own) for _ in x_parts[1:]]
    g_rows = [g_parts[0]] + [across(x) for x in g_parts[1:]]
    depth_here = depth // sides
    factor_grad = call(
        functools.partial(factor_body, sides),
        [(shaped((weights, count, depth_here, cols), F32), HBM)],
        [(mixing, SMEM)]
        + [(x, HBM) for n in range(sides) for x in (x_rows[n], g_rows[n], d_rows[n])],
        "factor_grad",
        3 * product,
        [scratch_like((sides, stacked, depth_here), BF16)] * 2
        + [
            scratch_like((sides, weights, rows, hidden), BF16),
            scratch_like((sides, stacked, hidden), BF16),
            scratch_like((weights, depth_here, hidden), F32),
            dma((sides, 3)),
            dma((weights, count)),
        ],
    )[0]
    mix_rows = call(
        mix_grad_body,
        [(shaped((mixing.size, cols), F32), VMEM)],
        [(x, HBM) for x in (y_gate, y_up, y_down, d_own)],
        "mix_partials",
        weights * 64 * 2 * rows * cols,
        [
            scratch_like((weights, stacked, hidden), F32),
            scratch_like((weights, rows, hidden), BF16),
            dma((4,)),
        ],
    )[0]
    mix_part = jnp.sum(mix_rows, axis=1).reshape(mix.shape)
    if swap:
        mix_grad = mix_part + across(mix_part)
    else:
        factor_grad = lax.psum_scatter(
            factor_grad.astype(BF16), "seq", scatter_dimension=2, tiled=True
        ).astype(F32)
        mix_grad = lax.psum(mix_part, "seq")
    gate_grad = (jnp.sum(inner, axis=1) * gate * (1.0 - gate)).reshape(selection.shape)
    token_grad = sum_rows(cap, pieces, own_rows, me, requested, returned)
    return token_grad, factor_grad[None], mix_grad, gate_grad


def solution(mesh):
    return jax.shard_map(
        shards,
        mesh=mesh,
        in_specs=(
            P(("seq", "exp"), None),
            P(("seq", "exp"), None),
            P("exp", None, None, "seq", None),
            P("exp", None, None, None, None),
            P("exp", "seq", None),
            P("exp", "seq", None),
        ),
        out_specs=(
            P(("seq", "exp"), None),
            P("exp", None, None, "seq", None),
            P("exp", None, None, None, None),
            P("exp", "seq", None),
        ),
        check_vma=False,
    )
```

```python
import functools

import jax
import jax.numpy as jnp
from jax import lax
from jax.experimental import pallas as pl
from jax.experimental.pallas import tpu as pltpu
from jax.sharding import PartitionSpec as P

SELECTED = 64
NPHM = 4
VMEM_LIMIT = 63 * 1024 * 1024
F32 = jnp.float32
BF16 = jnp.bfloat16


def iota(shape, dim):
    return lax.broadcasted_iota(jnp.int32, shape, dim)


def dot(left, right):
    return jnp.dot(left, right, preferred_element_type=F32)


def dot_tn(left, right):
    return lax.dot_general(left, right, (((0,), (0,)), ((), ())), preferred_element_type=F32)


def dot_nt(left, right):
    return lax.dot_general(left, right, (((1,), (1,)), ((), ())), preferred_element_type=F32)


HBM = pl.BlockSpec(memory_space=pltpu.HBM)
VMEM = pl.BlockSpec(memory_space=pltpu.VMEM)
SMEM = pl.BlockSpec(memory_space=pltpu.SMEM)


def call(body, outs, ins, name, flops, scratch=()):
    moved = sum(x.size * x.dtype.itemsize for x, _ in list(ins) + list(outs))
    return pl.pallas_call(
        body,
        out_shape=[x for x, _ in outs],
        in_specs=[place for _, place in ins],
        out_specs=[place for _, place in outs],
        scratch_shapes=list(scratch),
        compiler_params=pltpu.CompilerParams(vmem_limit_bytes=VMEM_LIMIT),
        cost_estimate=pl.CostEstimate(flops=flops, bytes_accessed=moved, transcendentals=0),
        name=name,
    )(*[x for x, _ in ins])


def begin(source, target, sem):
    copy = pltpu.make_async_copy(source, target, sem)
    copy.start()
    return copy


def shaped(shape, dtype):
    return jax.ShapeDtypeStruct(shape, dtype)


def scratch_like(shape, dtype):
    return pltpu.VMEM(shape, dtype)


def chunks_of(part):
    chunk = min(part, 512)
    return [slice(c * chunk, (c + 1) * chunk) for c in range(part // chunk)]


def position_of(peers, direct, me, peer):
    if not direct:
        return peer
    half = peers // 2
    apart = peer ^ me
    return jnp.where(apart < half, peer & (half - 1), apart)


def index_body(cap, pieces, own_rows, block_len, direct, me_ref, chosen_ref, wanted_ref, slot_ref):
    peers, lanes = wanted_ref.shape
    rows = slot_ref.shape[1]
    position = jnp.concatenate(
        [chosen_ref[b : b + 1, :] + b * block_len for b in range(chosen_ref.shape[0])], axis=1
    )
    owner = lax.shift_right_logical(position, own_rows.bit_length() - 1)
    local = position & (own_rows - 1)
    peer = iota((peers, rows), 0)
    mine = (peer == owner).astype(F32)
    count = jnp.sum(mine, axis=1, keepdims=True)
    earlier = jnp.sum(jnp.where(peer < owner, count, 0.0), axis=0, keepdims=True).astype(jnp.int32)
    rank = iota((1, rows), 1) - earlier
    place = position_of(peers, direct, me_ref[0], owner)
    slot_ref[...] = place * (cap * pieces) + rank
    lane = iota((lanes, rows), 0)
    hit = jnp.zeros((lanes, rows), F32)
    for j in range(pieces):
        hit = hit + (lane == rank + j * cap).astype(F32)
    marked = mine * (local + 1).astype(F32)
    wanted_ref[...] = dot_nt(marked.astype(BF16), hit.astype(BF16)).astype(jnp.int32)


def pick_matrix(cap, pieces, own_rows, direct, me, requested, first, count):
    peers, lanes = requested.shape
    group = cap * pieces
    slots = count * group
    place = iota((count, group, peers), 0).reshape(slots, peers) + first
    peer = position_of(peers, direct, me, iota((slots, peers), 1))
    spread = dot((peer == place).astype(BF16), requested.astype(F32).astype(BF16))
    rank = iota((count, group, lanes), 1).reshape(slots, lanes)
    row = jnp.sum(
        jnp.where(rank == iota((slots, lanes), 1), spread, 0.0), axis=1, keepdims=True
    ).astype(jnp.int32)
    piece = iota((count, group, 1), 1).reshape(slots, 1)
    shift = jnp.zeros((slots, 1), jnp.int32)
    for j in range(1, pieces):
        shift = shift + jnp.where(piece >= j * cap, own_rows, 0)
    target = jnp.where(row > 0, row - 1 + shift, -1)
    return (target == iota((slots, pieces * own_rows), 1)).astype(BF16)


def slab_specs(sizes, part):
    return [(shaped((size, part), BF16), HBM) for size in sizes]


def store_slabs(source_ref, at, outs, sems):
    copies, start = [], 0
    for k, out in enumerate(outs):
        stop = start + out.shape[0]
        copies.append(begin(source_ref.at[start:stop, at], out.at[:, at], sems.at[k]))
        start = stop
    return copies


def load_slabs(slabs, target_ref, sems):
    copies, start = [], 0
    for k, slab in enumerate(slabs):
        stop = start + slab.shape[0]
        copies.append(begin(slab, target_ref.at[start:stop], sems.at[k]))
        start = stop
    return copies


def pick_rows(cap, pieces, direct, first, sizes, me, requested, source, after, name):
    own_rows, width = source.shape
    part = width // pieces
    slots = sum(sizes)
    peers = slots // (cap * pieces)
    columns = chunks_of(part)

    def body(me_ref, requested_ref, source_ref, *refs):
        refs = refs[len(after) :]
        outs, (rows_ref, sent_ref, in_sem, out_sem) = refs[: len(sizes)], refs[len(sizes) :]
        loads = []
        for n, at in enumerate(columns):
            for j in range(pieces):
                wide = slice(j * part + at.start, j * part + at.stop)
                target = rows_ref.at[j * own_rows : (j + 1) * own_rows, at]
                loads.append(begin(source_ref.at[:, wide], target, in_sem.at[n, j]))
        pick = pick_matrix(
            cap, pieces, own_rows, direct, me_ref[0], requested_ref[...], first, peers
        )
        stores = []
        for n, at in enumerate(columns):
            wait_all(loads[n * pieces : (n + 1) * pieces])
            sent_ref[:, at] = dot(pick, rows_ref[:, at]).astype(BF16)
            stores += store_slabs(sent_ref, at, outs, out_sem.at[n])
        wait_all(stores)

    return call(
        body,
        slab_specs(sizes, part),
        [(me, SMEM), (requested, VMEM), (source, HBM)] + [(x, HBM) for x in after],
        name,
        2 * slots * pieces * own_rows * part,
        [
            scratch_like((pieces * own_rows, part), BF16),
            scratch_like((slots, part), BF16),
            pltpu.SemaphoreType.DMA((len(columns), pieces)),
            pltpu.SemaphoreType.DMA((len(columns), len(sizes))),
        ],
    )


def sum_rows(cap, pieces, own_rows, direct, me, requested, returned):
    count, part = len(returned), returned[0].shape[1]
    slots = sum(x.shape[0] for x in returned)
    peers = slots // (cap * pieces)
    columns = chunks_of(part)

    def body(me_ref, requested_ref, *refs):
        slabs, (out_ref, got_ref, sum_ref, in_sem, out_sem) = refs[:count], refs[count:]
        loads = load_slabs(slabs, got_ref, in_sem)
        pick = pick_matrix(cap, pieces, own_rows, direct, me_ref[0], requested_ref[...], 0, peers)
        wait_all(loads)
        stores = []
        for n, at in enumerate(columns):
            total = dot_tn(pick, got_ref[:, at]).astype(BF16)
            for j in range(pieces):
                wide = slice(j * part + at.start, j * part + at.stop)
                sum_ref[:, wide] = total[j * own_rows : (j + 1) * own_rows]
                stores.append(
                    begin(sum_ref.at[:, wide], out_ref.at[:, wide], out_sem.at[n, j])
                )
        wait_all(stores)

    return call(
        body,
        [(shaped((own_rows, part * pieces), BF16), HBM)],
        [(me, SMEM), (requested, VMEM)] + [(x, HBM) for x in returned],
        "sum_rows",
        2 * slots * pieces * own_rows * part,
        [
            scratch_like((slots, part), BF16),
            scratch_like((own_rows, part * pieces), BF16),
            pltpu.SemaphoreType.DMA((count,)),
            pltpu.SemaphoreType.DMA((len(columns), pieces)),
        ],
    )[0]


def load_factor(order_ref, parts, m, target, sems):
    copies = []
    for n, side in enumerate(parts):
        held = m
        for part in side:
            if held < part.shape[0]:
                break
            held -= part.shape[0]
        _, count, rows, cols = part.shape
        start = pl.multiple_of(order_ref[n] * rows, rows)
        for i in range(count):
            at = target.at[pl.ds(start, rows), i * cols : (i + 1) * cols]
            copies.append(begin(part.at[held, i], at, sems.at[n, i]))
    return copies


def sides_of(sides, refs):
    if sides == 1:
        return [refs[:1]], refs[1:]
    return [refs[:1], refs[1:2]], refs[2:]


def wait_all(copies):
    for copy in copies:
        copy.wait()


def place_matrix(cap, pieces, slots, slot):
    wide = jnp.concatenate([slot + j * cap for j in range(pieces)], axis=1)
    return (iota((slots, wide.shape[1]), 0) == wide).astype(BF16)


def stack_rows(pieces, place, got_ref, out_ref):
    part = got_ref.shape[1]
    rows, depth = out_ref.shape[0] // NPHM, out_ref.shape[1]
    for at in chunks_of(part):
        block = dot_tn(place, got_ref[:, at]).astype(BF16)
        for j in range(pieces):
            column = j * part + at.start
            a, start = column // depth, column % depth
            out_ref[a * rows : (a + 1) * rows, start : start + at.stop - at.start] = block[
                j * rows : (j + 1) * rows
            ]


def store_parts(order_ref, source_ref, outs, sems):
    copies = []
    for n, out in enumerate(outs):
        size = out.shape[1]
        start = pl.multiple_of(order_ref[n] * size, size)
        copies.append(begin(source_ref.at[:, pl.ds(start, size)], out, sems.at[n]))
    return copies


STRIP = 32


def mix_in(mix_ref, m, y_ref, emit):
    rows, cols = y_ref.shape[0] // NPHM, y_ref.shape[1] // NPHM

    def strip(n, carry):
        start = pl.multiple_of(n * STRIP, STRIP)
        total = [jnp.zeros((STRIP, cols), F32)] * NPHM
        for a in range(NPHM):
            for i in range(NPHM):
                block = y_ref[pl.ds(a * rows + start, STRIP), i * cols : (i + 1) * cols]
                for b in range(NPHM):
                    total[b] = total[b] + mix_ref[m * 64 + i * 16 + a * 4 + b] * block
        emit(start, total)
        return carry

    lax.fori_loop(0, rows // STRIP, strip, 0)


def mix_out(mix_ref, m, d_ref, z_ref):
    rows, cols = d_ref.shape[0], d_ref.shape[1] // NPHM

    def strip(n, carry):
        start = pl.multiple_of(n * STRIP, STRIP)
        blocks = [
            d_ref[pl.ds(start, STRIP), b * cols : (b + 1) * cols].astype(F32) for b in range(NPHM)
        ]
        for a in range(NPHM):
            for i in range(NPHM):
                total = mix_ref[m * 64 + i * 16 + a * 4] * blocks[0]
                for b in range(1, NPHM):
                    total = total + mix_ref[m * 64 + i * 16 + a * 4 + b] * blocks[b]
                z_ref[pl.ds(a * rows + start, STRIP), i * cols : (i + 1) * cols] = total.astype(
                    z_ref.dtype
                )
        return carry

    lax.fori_loop(0, rows // STRIP, strip, 0)


def forward_body(
    cap, pieces, sides, after, count, slot_ref, mix_ref, order_ref, *refs
):
    slabs, refs = refs[:count], refs[count:]
    parts, refs = sides_of(sides, refs)
    refs = refs[after:]
    x_outs, refs = refs[:sides], refs[sides:]
    yg_hbm, yu_hbm, act_hbm, slope_hbm, hid_hbm = refs[:5]
    got_ref, side_ref, x_ref, yg_ref, yu_ref, pre_ref, act_ref, slope_ref, hid_ref = refs[5:14]
    got_sem, side_sem, out_sem = refs[14:]
    loads = load_slabs(slabs, got_ref, got_sem)
    sides_in = [
        load_factor(order_ref, parts, m, side_ref.at[m], side_sem.at[m]) for m in range(2)
    ]
    place = place_matrix(cap, pieces, got_ref.shape[0], slot_ref[...])
    wait_all(loads)
    stack_rows(pieces, place, got_ref, x_ref)
    stores = store_parts(order_ref, x_ref, x_outs, out_sem)
    wait_all(sides_in[0])
    yg_ref[...] = dot(x_ref[...], side_ref[0])
    stores.append(begin(yg_ref, yg_hbm, out_sem.at[2]))
    wait_all(sides_in[1])
    yu_ref[...] = dot(x_ref[...], side_ref[1])
    stores.append(begin(yu_ref, yu_hbm, out_sem.at[3]))
    cols = yg_ref.shape[1] // NPHM

    def keep(start, total):
        for b in range(NPHM):
            pre_ref[pl.ds(start, STRIP), b * cols : (b + 1) * cols] = total[b]

    def finish(start, total):
        for b in range(NPHM):
            at = (pl.ds(start, STRIP), slice(b * cols, (b + 1) * cols))
            gate = pre_ref[at]
            sig = jax.nn.sigmoid(gate)
            act = gate * sig
            act_ref[at] = act
            slope_ref[at] = total[b] * (sig + act * (1.0 - sig))
            hid_ref[at] = act * total[b]

    mix_in(mix_ref, 0, yg_ref, keep)
    mix_in(mix_ref, 1, yu_ref, finish)
    stores.append(begin(act_ref, act_hbm, out_sem.at[4]))
    stores.append(begin(slope_ref, slope_hbm, out_sem.at[5]))
    stores.append(begin(hid_ref, hid_hbm, out_sem.at[6]))
    wait_all(stores)


def backward_body(
    cap, pieces, sides, after, count, slot_ref, mix_ref, order_ref, gate_ref, act_hbm, slope_hbm, hid_hbm,
    *refs,
):
    slabs, refs = refs[:count], refs[count:]
    parts, refs = sides_of(sides, refs)
    refs = refs[after:]
    backs, refs = refs[:count], refs[count:]
    x_outs, refs = refs[:sides], refs[sides:]
    y_hbm, d_hbm, inner_ref = refs[:3]
    (
        got_ref, side_ref, x_ref, y_ref, d_ref, act_ref, slope_ref, hid_ref, zg_ref, zu_ref, grad_ref,
        back_ref, got_sem, side_sem, in_sem, out_sem, back_sem,
    ) = refs[3:]
    loads = load_slabs(slabs, got_ref, got_sem)
    down_in = load_factor(order_ref, parts, 2, side_ref.at[2], side_sem.at[2])
    flat_in = [
        begin(source, target, in_sem.at[n])
        for n, (source, target) in enumerate(
            ((act_hbm, act_ref), (slope_hbm, slope_ref), (hid_hbm, hid_ref))
        )
    ]
    sides_in = [
        load_factor(order_ref, parts, m, side_ref.at[m], side_sem.at[m]) for m in range(2)
    ]
    place = place_matrix(cap, pieces, got_ref.shape[0], slot_ref[...])
    wait_all(loads)
    stack_rows(pieces, place, got_ref, x_ref)
    stores = store_parts(order_ref, x_ref, x_outs, out_sem)
    wait_all(down_in)
    y_ref[...] = dot(x_ref[...], side_ref[2])
    stores.append(begin(y_ref, y_hbm, out_sem.at[2]))
    cols = y_ref.shape[1] // NPHM
    wait_all(flat_in)

    def finish(start, total):
        gate = gate_ref[pl.ds(start, STRIP), :]
        inner = jnp.zeros((STRIP, cols), F32)
        for b in range(NPHM):
            at = (pl.ds(start, STRIP), slice(b * cols, (b + 1) * cols))
            hidden = hid_ref[at]
            inner = inner + hidden * total[b]
            hidden_grad = gate * total[b]
            d_ref[(0,) + at] = (hidden_grad * slope_ref[at]).astype(BF16)
            d_ref[(1,) + at] = (hidden_grad * act_ref[at]).astype(BF16)
            d_ref[(2,) + at] = (hidden * gate).astype(BF16)
        inner_ref[pl.ds(start, STRIP), :] = inner

    mix_in(mix_ref, 2, y_ref, finish)
    stores.append(begin(d_ref, d_hbm, out_sem.at[3]))
    mix_out(mix_ref, 0, d_ref.at[0], zg_ref)
    mix_out(mix_ref, 1, d_ref.at[1], zu_ref)
    wait_all(sides_in[0])
    wait_all(sides_in[1])
    grad = dot_nt(zg_ref[...], side_ref[0]) + dot_nt(zu_ref[...], side_ref[1])
    grad_ref[...] = grad.astype(BF16)
    part = back_ref.shape[1]
    rows, depth = x_ref.shape[0] // NPHM, x_ref.shape[1]
    for n, at in enumerate(chunks_of(part)):
        blocks = []
        for j in range(pieces):
            column = j * part + at.start
            a, start = column // depth, column % depth
            blocks.append(
                grad_ref[a * rows : (a + 1) * rows, start : start + at.stop - at.start]
            )
        back_ref[:, at] = dot(place, jnp.concatenate(blocks, axis=0)).astype(BF16)
        stores += store_slabs(back_ref, at, backs, back_sem.at[n])
    wait_all(stores)


def factor_body(count_groups, mix_ref, *refs):
    rows_in, refs = refs[: 3 * count_groups], refs[3 * count_groups :]
    out_hbm, x_ref, g_ref, d_ref, z_ref, sum_ref, in_sem, out_sem = refs
    loads = []
    for n in range(count_groups):
        for k, target in enumerate((x_ref, g_ref, d_ref)):
            loads.append(begin(rows_in[3 * n + k], target.at[n], in_sem.at[n, k]))
    stores = []
    cols = out_hbm.shape[3]
    wait_all(loads)
    for m in (2, 0, 1):
        for n in range(count_groups):
            mix_out(mix_ref, m, d_ref.at[n, m], z_ref.at[n])
        left = g_ref if m == 2 else x_ref
        sum_ref[m] = sum(dot_tn(left[n], z_ref[n]) for n in range(count_groups))
        for i in range(NPHM):
            at = sum_ref.at[m, :, i * cols : (i + 1) * cols]
            stores.append(begin(at, out_hbm.at[m, i], out_sem.at[m, i]))
    wait_all(stores)


def mix_grad_body(yg_hbm, yu_hbm, yd_hbm, d_hbm, out_ref, y_ref, d_ref, sems):
    loads = [begin(d_hbm, d_ref, sems.at[3])]
    for m, source in enumerate((yg_hbm, yu_hbm, yd_hbm)):
        loads.append(begin(source, y_ref.at[m], sems.at[m]))
    wait_all(loads)
    rows, cols = d_ref.shape[1], d_ref.shape[2] // NPHM
    for m in range(3):
        for a in range(NPHM):
            for i in range(NPHM):
                block = y_ref[m, a * rows : (a + 1) * rows, i * cols : (i + 1) * cols]
                for b in range(NPHM):
                    at = m * 64 + i * 16 + a * 4 + b
                    other = d_ref[m, :, b * cols : (b + 1) * cols].astype(F32)
                    out_ref[at : at + 1, :] = jnp.sum(block * other, axis=0, keepdims=True)


def shards(tokens, cotangent, factors, mix, selection, scores):
    peers = lax.axis_size("exp")
    groups = lax.axis_size("seq")
    group = lax.axis_index("seq")
    own_rows, width = tokens.shape
    _, weights, count, depth_own, cols = factors.shape
    depth = depth_own * groups
    hidden = count * cols
    cap = 3 * own_rows // (2 * peers)
    pieces = 1
    while (cap * pieces) % 16:
        pieces *= 2
    lanes = 128
    slots = peers * cap * pieces
    part = width // pieces
    steps = len(chunks_of(part))
    block_len = peers * SELECTED
    rows = selection.shape[1] * selection.shape[2]
    stacked = count * rows
    swap = groups == 2
    pair = [(0, 1), (1, 0)]
    mixing = mix.reshape(-1)
    dma = pltpu.SemaphoreType.DMA

    def across(array):
        return lax.ppermute(array, "seq", pair)

    if swap:
        factor_parts = [[factors[0]], [across(factors)[0]]]
        order = jnp.stack([group, 1 - group]).astype(jnp.int32)
    else:
        factor_parts = [[lax.all_gather(factors, "seq", axis=3, tiled=True)[0]]]
        order = jnp.zeros((2,), jnp.int32)
    sides = len(factor_parts)
    direct = peers == 16
    half, slab = peers // 2, cap * pieces
    near, far = (half, half) if direct else (peers, 0)
    sizes = [near * slab] + [slab] * far
    count_slabs = len(sizes)
    me = lax.axis_index("exp").astype(jnp.int32) if direct else jnp.int32(0)
    me = me.reshape(1)
    sides_in = [(x, HBM) for side in factor_parts for x in side]

    wanted, slot = call(
        functools.partial(index_body, cap, pieces, own_rows, block_len, direct),
        [(shaped((peers, lanes), jnp.int32), VMEM), (shaped((1, rows), jnp.int32), VMEM)],
        [(me, SMEM), (selection[0], VMEM)],
        "wanted_rows",
        1 << 20,
    )
    requested = lax.all_to_all(wanted, "exp", split_axis=0, concat_axis=0, tiled=True)

    halves = [list(range(half)), list(range(half, peers))] if direct else None

    def exchange_near(array):
        array = array.reshape(near, slab, part)
        array = lax.all_to_all(
            array, "exp", split_axis=0, concat_axis=0, axis_index_groups=halves, tiled=True
        )
        return array.reshape(near * slab, part)

    def exchange_far(slabs):
        return [
            lax.ppermute(x, "exp", [(n, n ^ (half + k)) for n in range(peers)])
            for k, x in enumerate(slabs)
        ]

    if direct:
        far_sizes = [slab] * far
        pick_of = functools.partial(pick_rows, cap, pieces, direct)
        far_rows = exchange_far(
            pick_of(half, far_sizes, me, requested, tokens, [], "pick_tokens_far")
        )
        near_rows = pick_of(0, sizes[:1], me, requested, tokens, far_rows[:1], "pick_tokens_near")
        got_rows = [exchange_near(near_rows[0])] + far_rows
        far_grads = exchange_far(
            pick_of(half, far_sizes, me, requested, cotangent, far_rows[1:2], "pick_cotangent_far")
        )
        near_grads = pick_of(
            0, sizes[:1], me, requested, cotangent, far_rows[4:5], "pick_cotangent_near"
        )
        got_grads = [exchange_near(near_grads[0])] + far_grads
        before_forward = far_grads[:4]
    else:
        got_rows, got_grads = [
            [
                exchange_near(
                    pick_rows(cap, pieces, direct, 0, sizes, me, requested, source, [], name)[0]
                )
            ]
            for source, name in ((tokens, "pick_tokens"), (cotangent, "pick_cotangent"))
        ]
        before_forward = []

    gate = jax.nn.sigmoid(scores[0].reshape(-1).astype(F32) / 64.0)
    gate_wide = jnp.broadcast_to(gate[:, None], (rows, cols))

    product = 2 * stacked * depth * hidden
    split = [(shaped((stacked, depth // sides), BF16), HBM)] * sides
    mixed = (shaped((stacked, hidden), F32), HBM)
    flat = (shaped((rows, hidden), F32), HBM)
    got_scratch = scratch_like((slots, part), BF16)
    stack_scratch = scratch_like((stacked, depth), BF16)
    mixed_scratch = scratch_like((stacked, hidden), F32)
    low_scratch = scratch_like((stacked, hidden), BF16)
    flat_scratch = scratch_like((rows, hidden), F32)
    outs = call(
        functools.partial(forward_body, cap, pieces, sides, len(before_forward), count_slabs),
        split + [mixed, mixed, flat, flat, flat],
        [(slot, VMEM), (mixing, SMEM), (order, SMEM)]
        + [(x, HBM) for x in got_rows]
        + sides_in
        + [(x, HBM) for x in before_forward],
        "forward",
        2 * product,
        [got_scratch, scratch_like((2, depth, hidden), BF16), stack_scratch, mixed_scratch, mixed_scratch]
        + [flat_scratch] * 4
        + [dma((count_slabs,)), dma((2, sides, count)), dma((7,))],
    )
    x_parts, (y_gate, y_up, act, slope, hid) = outs[:sides], outs[sides:]
    x_rows = [x_parts[0]] + [across(x) for x in x_parts[1:]]
    after = x_rows[1:]
    outs = call(
        functools.partial(backward_body, cap, pieces, sides, len(after), count_slabs),
        slab_specs(sizes, part)
        + split
        + [mixed, (shaped((weights, rows, hidden), BF16), HBM), (shaped((rows, cols), F32), VMEM)],
        [(slot, VMEM), (mixing, SMEM), (order, SMEM), (gate_wide, VMEM)]
        + [(x, HBM) for x in [act, slope, hid] + got_grads]
        + sides_in
        + [(x, HBM) for x in after],
        "backward",
        3 * product,
        [got_scratch, scratch_like((weights, depth, hidden), BF16), stack_scratch, mixed_scratch]
        + [scratch_like((weights, rows, hidden), BF16)]
        + [flat_scratch] * 3
        + [low_scratch] * 2
        + [stack_scratch, got_scratch]
        + [dma((count_slabs,)), dma((weights, sides, count)), dma((3,)), dma((4,))]
        + [dma((steps, count_slabs))],
    )
    back, outs = outs[:count_slabs], outs[count_slabs:]
    g_parts, (y_down, d_own, inner) = outs[:sides], outs[sides:]
    returned = [exchange_near(back[0])] + exchange_far(back[1:])

    d_rows = [d_own] + [across(d_own) for _ in x_parts[1:]]
    g_rows = [g_parts[0]] + [across(x) for x in g_parts[1:]]
    depth_here = depth // sides
    factor_grad = call(
        functools.partial(factor_body, sides),
        [(shaped((weights, count, depth_here, cols), F32), HBM)],
        [(mixing, SMEM)]
        + [(x, HBM) for n in range(sides) for x in (x_rows[n], g_rows[n], d_rows[n])],
        "factor_grad",
        3 * product,
        [scratch_like((sides, stacked, depth_here), BF16)] * 2
        + [
            scratch_like((sides, weights, rows, hidden), BF16),
            scratch_like((sides, stacked, hidden), BF16),
            scratch_like((weights, depth_here, hidden), F32),
            dma((sides, 3)),
            dma((weights, count)),
        ],
    )[0]
    mix_rows = call(
        mix_grad_body,
        [(shaped((mixing.size, cols), F32), VMEM)],
        [(x, HBM) for x in (y_gate, y_up, y_down, d_own)],
        "mix_partials",
        weights * 64 * 2 * rows * cols,
        [
            scratch_like((weights, stacked, hidden), F32),
            scratch_like((weights, rows, hidden), BF16),
            dma((4,)),
        ],
    )[0]
    mix_part = jnp.sum(mix_rows, axis=1).reshape(mix.shape)
    if swap:
        mix_grad = mix_part + across(mix_part)
    else:
        factor_grad = lax.psum_scatter(
            factor_grad.astype(BF16), "seq", scatter_dimension=2, tiled=True
        ).astype(F32)
        mix_grad = lax.psum(mix_part, "seq")
    gate_grad = (jnp.sum(inner, axis=1) * gate * (1.0 - gate)).reshape(selection.shape)
    token_grad = sum_rows(cap, pieces, own_rows, direct, me, requested, returned)
    return token_grad, factor_grad[None], mix_grad, gate_grad


def solution(mesh):
    return jax.shard_map(
        shards,
        mesh=mesh,
        in_specs=(
            P(("seq", "exp"), None),
            P(("seq", "exp"), None),
            P("exp", None, None, "seq", None),
            P("exp", None, None, None, None),
            P("exp", "seq", None),
            P("exp", "seq", None),
        ),
        out_specs=(
            P(("seq", "exp"), None),
            P("exp", None, None, "seq", None),
            P("exp", None, None, None, None),
            P("exp", "seq", None),
        ),
        check_vma=False,
    )
```

```python
import functools

import jax
import jax.numpy as jnp
from jax import lax
from jax.experimental import pallas as pl
from jax.experimental.pallas import tpu as pltpu
from jax.sharding import PartitionSpec as P

SELECTED = 64
NPHM = 4
VMEM_LIMIT = 63 * 1024 * 1024
F32 = jnp.float32
BF16 = jnp.bfloat16


def iota(shape, dim):
    return lax.broadcasted_iota(jnp.int32, shape, dim)


def dot(left, right):
    return jnp.dot(left, right, preferred_element_type=F32)


def dot_tn(left, right):
    return lax.dot_general(left, right, (((0,), (0,)), ((), ())), preferred_element_type=F32)


def dot_nt(left, right):
    return lax.dot_general(left, right, (((1,), (1,)), ((), ())), preferred_element_type=F32)


HBM = pl.BlockSpec(memory_space=pltpu.HBM)
VMEM = pl.BlockSpec(memory_space=pltpu.VMEM)
SMEM = pl.BlockSpec(memory_space=pltpu.SMEM)


def call(body, outs, ins, name, flops, scratch=()):
    moved = sum(x.size * x.dtype.itemsize for x, _ in list(ins) + list(outs))
    return pl.pallas_call(
        body,
        out_shape=[x for x, _ in outs],
        in_specs=[place for _, place in ins],
        out_specs=[place for _, place in outs],
        scratch_shapes=list(scratch),
        compiler_params=pltpu.CompilerParams(vmem_limit_bytes=VMEM_LIMIT),
        cost_estimate=pl.CostEstimate(flops=flops, bytes_accessed=moved, transcendentals=0),
        name=name,
    )(*[x for x, _ in ins])


def begin(source, target, sem):
    copy = pltpu.make_async_copy(source, target, sem)
    copy.start()
    return copy


def shaped(shape, dtype):
    return jax.ShapeDtypeStruct(shape, dtype)


def scratch_like(shape, dtype):
    return pltpu.VMEM(shape, dtype)


def chunks_of(part):
    chunk = min(part, 512)
    return [slice(c * chunk, (c + 1) * chunk) for c in range(part // chunk)]


def start_all(pairs, sems):
    return [begin(source, target, sems.at[n]) for n, (source, target) in enumerate(pairs)]


def spread_columns(places, source, half, direct, name):
    own_rows, width = source.shape
    part = width // half

    def body(places_ref, source_ref, *refs):
        outs, sems = refs[:-1], refs[-1]
        copies = []
        for k in range(half):
            share = places_ref[1] ^ k if direct else k
            at = source_ref.at[:, pl.ds(pl.multiple_of(share * part, part), part)]
            out = outs[k] if direct else outs[0].at[k * own_rows : (k + 1) * own_rows]
            copies.append(begin(at, out, sems.at[k]))
        wait_all(copies)

    if direct:
        outs = [(shaped((own_rows, part), BF16), HBM)] * half
    else:
        outs = [(shaped((half * own_rows, part), BF16), HBM)]
    ins = [(places, SMEM), (source, HBM)]
    return call(body, outs, ins, name, 0, [pltpu.SemaphoreType.DMA((half,))])


def pick_rows(places, chosen, shares, own_rows, name):
    peers, _, picks = chosen.shape
    part = shares[0].shape[1]
    block = sum(x.shape[0] for x in shares)
    batch = min(peers, 16)

    def body(places_ref, chosen_ref, *refs):
        parts, (out_ref, rows_ref, pick_ref, sent_ref, in_sem, out_sem) = (
            refs[: len(shares)],
            refs[len(shares) :],
        )
        loads = []
        for k, share in enumerate(parts):
            size = share.shape[0]
            start = pl.multiple_of((places_ref[1] ^ k) * size if len(parts) > 1 else 0, 16)
            loads.append(begin(share, rows_ref.at[pl.ds(start, size)], in_sem.at[k]))
        stores = []
        for first in range(0, peers, batch):
            for e in range(batch):
                wanted = chosen_ref[first + e, pl.ds(places_ref[2], 1), :]
                same = iota((picks, picks), 0) == iota((picks, picks), 1)
                column = jnp.sum(jnp.where(same, wanted, 0), axis=1, keepdims=True)
                pick_ref[e * picks : (e + 1) * picks] = (
                    column == iota((picks, block), 1)
                ).astype(BF16)
            if first == 0:
                wait_all(loads)
            at = slice(first * picks, (first + batch) * picks)
            sent_ref[at] = dot(pick_ref[...], rows_ref[...]).astype(BF16)
            stores.append(begin(sent_ref.at[at], out_ref.at[at], out_sem.at[first // batch]))
        wait_all(stores)

    return call(
        body,
        [(shaped((peers * picks, part), BF16), HBM)],
        [(places, SMEM), (chosen, VMEM)] + [(x, HBM) for x in shares],
        name,
        2 * peers * picks * block * part,
        [
            scratch_like((block, part), BF16),
            scratch_like((batch * picks, block), BF16),
            scratch_like((peers * picks, part), BF16),
            pltpu.SemaphoreType.DMA((len(shares),)),
            pltpu.SemaphoreType.DMA((peers // batch,)),
        ],
    )[0]


def slot_body(cap, pieces, own_rows, block_len, chosen_ref, slot_ref):
    rows = slot_ref.shape[1]
    position = jnp.concatenate(
        [chosen_ref[b : b + 1, :] + b * block_len for b in range(chosen_ref.shape[0])], axis=1
    )
    owner = lax.shift_right_logical(position, own_rows.bit_length() - 1)
    peers = chosen_ref.shape[0] * block_len // own_rows
    peer = iota((peers, rows), 0)
    count = jnp.sum((peer == owner).astype(F32), axis=1, keepdims=True)
    earlier = jnp.sum(jnp.where(peer < owner, count, 0.0), axis=0, keepdims=True).astype(jnp.int32)
    slot_ref[...] = owner * (cap * pieces) + iota((1, rows), 1) - earlier


def sum_rows(cap, pieces, own_rows, places, chosen, returned):
    slots, part = returned.shape
    peers, _, picks = chosen.shape
    group = cap * pieces
    columns = chunks_of(part)

    def body(places_ref, chosen_ref, returned_ref, out_ref, got_ref, pick_ref, sum_ref, in_sem, out_sem):
        loads = [
            begin(returned_ref.at[:, at], got_ref.at[:, at], in_sem.at[n])
            for n, at in enumerate(columns)
        ]
        for e in range(peers):
            local = chosen_ref[e, pl.ds(places_ref[2], 1), :] - places_ref[1] * own_rows
            before = jnp.sum((local < 0).astype(F32), axis=1, keepdims=True).astype(jnp.int32)
            rank = iota((1, picks), 1) - before
            mine = jnp.where((local >= 0) & (local < own_rows), local + 1, 0)
            place = iota((group, picks), 0)
            column = jnp.zeros((group, 1), jnp.int32)
            for j in range(pieces):
                hit = jnp.where((place == rank + j * cap) & (rank >= 0) & (rank < cap), mine, 0)
                row = jnp.sum(hit, axis=1, keepdims=True)
                column = column + jnp.where(row > 0, row + j * own_rows, 0)
            pick_ref[e * group : (e + 1) * group] = (
                column == iota((group, pieces * own_rows), 1) + 1
            ).astype(F32)
        pick = pick_ref[...].astype(BF16)
        stores = []
        for n, at in enumerate(columns):
            loads[n].wait()
            total = dot_tn(pick, got_ref[:, at]).astype(BF16)
            for j in range(pieces):
                wide = slice(j * part + at.start, j * part + at.stop)
                sum_ref[:, wide] = total[j * own_rows : (j + 1) * own_rows]
                stores.append(
                    begin(sum_ref.at[:, wide], out_ref.at[:, wide], out_sem.at[n, j])
                )
        wait_all(stores)

    return call(
        body,
        [(shaped((own_rows, part * pieces), BF16), HBM)],
        [(places, SMEM), (chosen, VMEM), (returned, HBM)],
        "sum_rows",
        2 * slots * pieces * own_rows * part,
        [
            scratch_like((slots, part), BF16),
            scratch_like((slots, pieces * own_rows), F32),
            scratch_like((own_rows, part * pieces), BF16),
            pltpu.SemaphoreType.DMA((len(columns),)),
            pltpu.SemaphoreType.DMA((len(columns), pieces)),
        ],
    )[0]


def load_factor(order_ref, parts, m, target, sems):
    copies = []
    for n, side in enumerate(parts):
        _, count, rows, cols = side.shape
        start = pl.multiple_of(order_ref[3 + n] * rows, rows)
        for i in range(count):
            at = target.at[pl.ds(start, rows), i * cols : (i + 1) * cols]
            copies.append(begin(side.at[m, i], at, sems.at[n, i]))
    return copies


def wait_all(copies):
    for copy in copies:
        copy.wait()


def place_matrix(cap, pieces, slots, slot):
    wide = jnp.concatenate([slot + j * cap for j in range(pieces)], axis=1)
    return (iota((slots, wide.shape[1]), 0) == wide).astype(BF16)


def load_rows(got_hbm, x_ref, sems):
    rows, depth = x_ref.shape[0] // NPHM, x_ref.shape[1]
    part = got_hbm.shape[1]
    shares = NPHM * depth // part
    picks = got_hbm.shape[0] * part // (NPHM * depth) // (rows // SELECTED)
    copies = []
    for n in range(got_hbm.shape[0] // picks):
        block, share = divmod(n, shares)
        a, start = share * part // depth, share * part % depth
        first = a * rows + block * picks
        at = x_ref.at[first : first + picks, start : start + part]
        copies.append(begin(got_hbm.at[n * picks : (n + 1) * picks], at, sems.at[n]))
    return copies


def store_parts(order_ref, source_ref, outs, sems):
    copies = []
    for n, out in enumerate(outs):
        size = out.shape[1]
        start = pl.multiple_of(order_ref[3 + n] * size, size)
        copies.append(begin(source_ref.at[:, pl.ds(start, size)], out, sems.at[n]))
    return copies


STRIP = 32


def mix_in(mix_ref, m, y_ref, emit):
    rows, cols = y_ref.shape[0] // NPHM, y_ref.shape[1] // NPHM

    def strip(n, carry):
        start = pl.multiple_of(n * STRIP, STRIP)
        total = [jnp.zeros((STRIP, cols), F32)] * NPHM
        for a in range(NPHM):
            for i in range(NPHM):
                block = y_ref[pl.ds(a * rows + start, STRIP), i * cols : (i + 1) * cols]
                for b in range(NPHM):
                    total[b] = total[b] + mix_ref[m * 64 + i * 16 + a * 4 + b] * block
        emit(start, total)
        return carry

    lax.fori_loop(0, rows // STRIP, strip, 0)


def mix_out(mix_ref, m, d_ref, z_ref):
    rows, cols = d_ref.shape[0], d_ref.shape[1] // NPHM

    def strip(n, carry):
        start = pl.multiple_of(n * STRIP, STRIP)
        blocks = [
            d_ref[pl.ds(start, STRIP), b * cols : (b + 1) * cols].astype(F32) for b in range(NPHM)
        ]
        for a in range(NPHM):
            for i in range(NPHM):
                total = mix_ref[m * 64 + i * 16 + a * 4] * blocks[0]
                for b in range(1, NPHM):
                    total = total + mix_ref[m * 64 + i * 16 + a * 4 + b] * blocks[b]
                z_ref[pl.ds(a * rows + start, STRIP), i * cols : (i + 1) * cols] = total.astype(
                    z_ref.dtype
                )
        return carry

    lax.fori_loop(0, rows // STRIP, strip, 0)


def forward_body(
    sides, order_ref, mix_ref, got_hbm, *refs
):
    parts, refs = refs[:sides], refs[sides:]
    x_outs, refs = refs[:sides], refs[sides:]
    yg_hbm, yu_hbm, act_hbm, slope_hbm, hid_hbm = refs[:5]
    side_ref, x_ref, yg_ref, yu_ref, pre_ref, act_ref, slope_ref, hid_ref = refs[5:13]
    got_sem, side_sem, out_sem = refs[13:]
    loads = load_rows(got_hbm, x_ref, got_sem)
    sides_in = [
        load_factor(order_ref, parts, m, side_ref.at[m], side_sem.at[m]) for m in range(2)
    ]
    wait_all(loads)
    stores = store_parts(order_ref, x_ref, x_outs, out_sem)
    wait_all(sides_in[0])
    yg_ref[...] = dot(x_ref[...], side_ref[0])
    stores.append(begin(yg_ref, yg_hbm, out_sem.at[2]))
    wait_all(sides_in[1])
    yu_ref[...] = dot(x_ref[...], side_ref[1])
    stores.append(begin(yu_ref, yu_hbm, out_sem.at[3]))
    cols = yg_ref.shape[1] // NPHM

    def keep(start, total):
        for b in range(NPHM):
            pre_ref[pl.ds(start, STRIP), b * cols : (b + 1) * cols] = total[b]

    def finish(start, total):
        for b in range(NPHM):
            at = (pl.ds(start, STRIP), slice(b * cols, (b + 1) * cols))
            gate = pre_ref[at]
            sig = jax.nn.sigmoid(gate)
            act = gate * sig
            act_ref[at] = act
            slope_ref[at] = total[b] * (sig + act * (1.0 - sig))
            hid_ref[at] = act * total[b]

    mix_in(mix_ref, 0, yg_ref, keep)
    mix_in(mix_ref, 1, yu_ref, finish)
    stores.append(begin(act_ref, act_hbm, out_sem.at[4]))
    stores.append(begin(slope_ref, slope_hbm, out_sem.at[5]))
    stores.append(begin(hid_ref, hid_hbm, out_sem.at[6]))
    wait_all(stores)


def backward_body(
    cap, pieces, sides, after, order_ref, mix_ref, slot_ref, gate_ref, got_hbm, act_hbm, slope_hbm, hid_hbm,
    *refs,
):
    parts, refs = refs[:sides], refs[sides + after :]
    back_hbm, x_outs, refs = refs[0], refs[1 : 1 + sides], refs[1 + sides :]
    y_hbm, d_hbm, inner_ref = refs[:3]
    (
        side_ref, x_ref, y_ref, d_ref, act_ref, slope_ref, hid_ref, zg_ref, zu_ref, grad_ref,
        back_ref, got_sem, side_sem, in_sem, out_sem,
    ) = refs[3:]
    loads = load_rows(got_hbm, x_ref, got_sem)
    down_in = load_factor(order_ref, parts, 2, side_ref.at[2], side_sem.at[2])
    flat_in = [
        begin(source, target, in_sem.at[n])
        for n, (source, target) in enumerate(
            ((act_hbm, act_ref), (slope_hbm, slope_ref), (hid_hbm, hid_ref))
        )
    ]
    sides_in = [
        load_factor(order_ref, parts, m, side_ref.at[m], side_sem.at[m]) for m in range(2)
    ]
    wait_all(loads)
    stores = store_parts(order_ref, x_ref, x_outs, out_sem)
    wait_all(down_in)
    y_ref[...] = dot(x_ref[...], side_ref[2])
    stores.append(begin(y_ref, y_hbm, out_sem.at[2]))
    cols = y_ref.shape[1] // NPHM
    wait_all(flat_in)

    def finish(start, total):
        gate = gate_ref[pl.ds(start, STRIP), :]
        inner = jnp.zeros((STRIP, cols), F32)
        for b in range(NPHM):
            at = (pl.ds(start, STRIP), slice(b * cols, (b + 1) * cols))
            hidden = hid_ref[at]
            inner = inner + hidden * total[b]
            hidden_grad = gate * total[b]
            d_ref[(0,) + at] = (hidden_grad * slope_ref[at]).astype(BF16)
            d_ref[(1,) + at] = (hidden_grad * act_ref[at]).astype(BF16)
            d_ref[(2,) + at] = (hidden * gate).astype(BF16)
        inner_ref[pl.ds(start, STRIP), :] = inner

    mix_in(mix_ref, 2, y_ref, finish)
    stores.append(begin(d_ref, d_hbm, out_sem.at[3]))
    mix_out(mix_ref, 0, d_ref.at[0], zg_ref)
    mix_out(mix_ref, 1, d_ref.at[1], zu_ref)
    wait_all(sides_in[0])
    wait_all(sides_in[1])
    grad = dot_nt(zg_ref[...], side_ref[0]) + dot_nt(zu_ref[...], side_ref[1])
    grad_ref[...] = grad.astype(BF16)
    place = place_matrix(cap, pieces, back_ref.shape[0], slot_ref[...])
    part = back_ref.shape[1]
    rows, depth = x_ref.shape[0] // NPHM, x_ref.shape[1]
    for n, at in enumerate(chunks_of(part)):
        blocks = []
        for j in range(pieces):
            column = j * part + at.start
            a, start = column // depth, column % depth
            blocks.append(
                grad_ref[a * rows : (a + 1) * rows, start : start + at.stop - at.start]
            )
        back_ref[:, at] = dot(place, jnp.concatenate(blocks, axis=0)).astype(BF16)
        stores.append(begin(back_ref.at[:, at], back_hbm.at[:, at], out_sem.at[4 + n]))
    wait_all(stores)


def factor_body(count_groups, mix_ref, *refs):
    rows_in, refs = refs[: 3 * count_groups], refs[3 * count_groups :]
    out_hbm, x_ref, g_ref, d_ref, z_ref, sum_ref, in_sem, out_sem = refs
    loads = []
    for n in range(count_groups):
        for k, target in enumerate((x_ref, g_ref, d_ref)):
            loads.append(begin(rows_in[3 * n + k], target.at[n], in_sem.at[n, k]))
    stores = []
    cols = out_hbm.shape[3]
    wait_all(loads)
    for m in (2, 0, 1):
        for n in range(count_groups):
            mix_out(mix_ref, m, d_ref.at[n, m], z_ref.at[n])
        left = g_ref if m == 2 else x_ref
        sum_ref[m] = sum(dot_tn(left[n], z_ref[n]) for n in range(count_groups))
        for i in range(NPHM):
            at = sum_ref.at[m, :, i * cols : (i + 1) * cols]
            stores.append(begin(at, out_hbm.at[m, i], out_sem.at[m, i]))
    wait_all(stores)


def mix_grad_body(yg_hbm, yu_hbm, yd_hbm, d_hbm, out_ref, y_ref, d_ref, sems):
    loads = [begin(d_hbm, d_ref, sems.at[3])]
    for m, source in enumerate((yg_hbm, yu_hbm, yd_hbm)):
        loads.append(begin(source, y_ref.at[m], sems.at[m]))
    wait_all(loads)
    rows, cols = d_ref.shape[1], d_ref.shape[2] // NPHM
    for m in range(3):
        for a in range(NPHM):
            for i in range(NPHM):
                block = y_ref[m, a * rows : (a + 1) * rows, i * cols : (i + 1) * cols]
                for b in range(NPHM):
                    at = m * 64 + i * 16 + a * 4 + b
                    other = d_ref[m, :, b * cols : (b + 1) * cols].astype(F32)
                    out_ref[at : at + 1, :] = jnp.sum(block * other, axis=0, keepdims=True)


def shards(tokens, cotangent, factors, mix, selection, scores):
    peers = lax.axis_size("exp")
    groups = lax.axis_size("seq")
    group = lax.axis_index("seq")
    own_rows, width = tokens.shape
    _, weights, count, depth_own, cols = factors.shape
    depth = depth_own * groups
    hidden = count * cols
    cap = 3 * own_rows // (2 * peers)
    pieces = 1
    while (cap * pieces) % 8:
        pieces *= 2
    slots = peers * cap * pieces
    part = width // pieces
    steps = len(chunks_of(part))
    block_len = peers * SELECTED
    rows = selection.shape[1] * selection.shape[2]
    stacked = count * rows
    swap = groups == 2
    pair = [(0, 1), (1, 0)]
    mixing = mix.reshape(-1)
    dma = pltpu.SemaphoreType.DMA

    def across(array):
        return lax.ppermute(array, "seq", pair)

    if swap:
        factor_parts = [factors[0], across(factors)[0]]
    else:
        factor_parts = [lax.all_gather(factors, "seq", axis=3, tiled=True)[0]]
    sides = len(factor_parts)
    sides_in = [(x, HBM) for x in factor_parts]

    half = peers // selection.shape[1]
    direct = half == 8
    me = lax.axis_index("exp")
    first = group if swap else 0
    places = jnp.stack([me, me % half, me // half, first, 1 - first]).astype(jnp.int32)
    chosen = lax.all_gather(selection[0], "exp")
    halves = [list(range(h, h + half)) for h in range(0, peers, half)]

    def to_peers(array):
        array = array.reshape(peers, -1, array.shape[1])
        array = lax.all_to_all(array, "exp", split_axis=0, concat_axis=0, tiled=True)
        return array.reshape(-1, array.shape[2])

    def collect(source, name):
        shares = spread_columns(places, source, half, direct, "spread_" + name)
        if direct:
            shares = [shares[0]] + [
                lax.ppermute(shares[k], "exp", [(n, n ^ k) for n in range(peers)])
                for k in range(1, half)
            ]
        else:
            array = shares[0].reshape(half, own_rows, -1)
            array = lax.all_to_all(
                array, "exp", split_axis=0, concat_axis=0, axis_index_groups=halves, tiled=True
            )
            shares = [array.reshape(half * own_rows, -1)]
        return to_peers(pick_rows(places, chosen, shares, own_rows, "pick_" + name))

    got_rows = collect(tokens, "tokens")
    got_grads = collect(cotangent, "cotangent")
    slot = call(
        functools.partial(slot_body, cap, pieces, own_rows, block_len),
        [(shaped((1, rows), jnp.int32), VMEM)],
        [(selection[0], VMEM)],
        "row_slots",
        1 << 16,
    )[0]

    gate = jax.nn.sigmoid(scores[0].reshape(-1).astype(F32) / 64.0)
    gate_wide = jnp.broadcast_to(gate[:, None], (rows, cols))

    product = 2 * stacked * depth * hidden
    split = [(shaped((stacked, depth // sides), BF16), HBM)] * sides
    mixed = (shaped((stacked, hidden), F32), HBM)
    flat = (shaped((rows, hidden), F32), HBM)
    back_scratch = scratch_like((slots, part), BF16)
    pieces_in = got_rows.shape[0] // SELECTED
    stack_scratch = scratch_like((stacked, depth), BF16)
    mixed_scratch = scratch_like((stacked, hidden), F32)
    low_scratch = scratch_like((stacked, hidden), BF16)
    flat_scratch = scratch_like((rows, hidden), F32)
    outs = call(
        functools.partial(forward_body, sides),
        split + [mixed, mixed, flat, flat, flat],
        [(places, SMEM), (mixing, SMEM), (got_rows, HBM)] + sides_in,
        "forward",
        2 * product,
        [scratch_like((2, depth, hidden), BF16), stack_scratch, mixed_scratch, mixed_scratch]
        + [flat_scratch] * 4
        + [dma((pieces_in,)), dma((2, sides, count)), dma((7,))],
    )
    x_parts, (y_gate, y_up, act, slope, hid) = outs[:sides], outs[sides:]
    x_rows = [x_parts[0]] + [across(x) for x in x_parts[1:]]
    after = x_rows[1:]
    outs = call(
        functools.partial(backward_body, cap, pieces, sides, len(after)),
        [(shaped((slots, part), BF16), HBM)]
        + split
        + [mixed, (shaped((weights, rows, hidden), BF16), HBM), (shaped((rows, cols), F32), VMEM)],
        [(places, SMEM), (mixing, SMEM), (slot, VMEM), (gate_wide, VMEM), (got_grads, HBM)]
        + [(x, HBM) for x in (act, slope, hid)]
        + sides_in
        + [(x, HBM) for x in after],
        "backward",
        3 * product,
        [scratch_like((weights, depth, hidden), BF16), stack_scratch, mixed_scratch]
        + [scratch_like((weights, rows, hidden), BF16)]
        + [flat_scratch] * 3
        + [low_scratch] * 2
        + [stack_scratch, back_scratch]
        + [dma((pieces_in,)), dma((weights, sides, count)), dma((3,)), dma((4 + steps,))],
    )
    back, g_parts, (y_down, d_own, inner) = outs[0], outs[1 : 1 + sides], outs[1 + sides :]
    returned = to_peers(back)

    d_rows = [d_own] + [across(d_own) for _ in x_parts[1:]]
    g_rows = [g_parts[0]] + [across(x) for x in g_parts[1:]]
    depth_here = depth // sides
    factor_grad = call(
        functools.partial(factor_body, sides),
        [(shaped((weights, count, depth_here, cols), F32), HBM)],
        [(mixing, SMEM)]
        + [(x, HBM) for n in range(sides) for x in (x_rows[n], g_rows[n], d_rows[n])],
        "factor_grad",
        3 * product,
        [scratch_like((sides, stacked, depth_here), BF16)] * 2
        + [
            scratch_like((sides, weights, rows, hidden), BF16),
            scratch_like((sides, stacked, hidden), BF16),
            scratch_like((weights, depth_here, hidden), F32),
            dma((sides, 3)),
            dma((weights, count)),
        ],
    )[0]
    mix_rows = call(
        mix_grad_body,
        [(shaped((mixing.size, cols), F32), VMEM)],
        [(x, HBM) for x in (y_gate, y_up, y_down, d_own)],
        "mix_partials",
        weights * 64 * 2 * rows * cols,
        [
            scratch_like((weights, stacked, hidden), F32),
            scratch_like((weights, rows, hidden), BF16),
            dma((4,)),
        ],
    )[0]
    mix_part = jnp.sum(mix_rows, axis=1).reshape(mix.shape)
    if swap:
        mix_grad = mix_part + across(mix_part)
    else:
        factor_grad = lax.psum_scatter(
            factor_grad.astype(BF16), "seq", scatter_dimension=2, tiled=True
        ).astype(F32)
        mix_grad = lax.psum(mix_part, "seq")
    gate_grad = (jnp.sum(inner, axis=1) * gate * (1.0 - gate)).reshape(selection.shape)
    token_grad = sum_rows(cap, pieces, own_rows, places, chosen, returned)
    return token_grad, factor_grad[None], mix_grad, gate_grad


def solution(mesh):
    return jax.shard_map(
        shards,
        mesh=mesh,
        in_specs=(
            P(("seq", "exp"), None),
            P(("seq", "exp"), None),
            P("exp", None, None, "seq", None),
            P("exp", None, None, None, None),
            P("exp", "seq", None),
            P("exp", "seq", None),
        ),
        out_specs=(
            P(("seq", "exp"), None),
            P("exp", None, None, "seq", None),
            P("exp", None, None, None, None),
            P("exp", "seq", None),
        ),
        check_vma=False,
    )
```

```python
import functools

import jax
import jax.numpy as jnp
from jax import lax
from jax.experimental import pallas as pl
from jax.experimental.pallas import tpu as pltpu
from jax.sharding import PartitionSpec as P

SELECTED = 64
NPHM = 4
VMEM_LIMIT = 63 * 1024 * 1024
F32 = jnp.float32
BF16 = jnp.bfloat16


def iota(shape, dim):
    return lax.broadcasted_iota(jnp.int32, shape, dim)


def dot(left, right):
    return jnp.dot(left, right, preferred_element_type=F32)


def dot_tn(left, right):
    return lax.dot_general(left, right, (((0,), (0,)), ((), ())), preferred_element_type=F32)


def dot_nt(left, right):
    return lax.dot_general(left, right, (((1,), (1,)), ((), ())), preferred_element_type=F32)


HBM = pl.BlockSpec(memory_space=pltpu.HBM)
VMEM = pl.BlockSpec(memory_space=pltpu.VMEM)
SMEM = pl.BlockSpec(memory_space=pltpu.SMEM)


def call(body, outs, ins, name, flops, scratch=()):
    moved = sum(x.size * x.dtype.itemsize for x, _ in list(ins) + list(outs))
    return pl.pallas_call(
        body,
        out_shape=[x for x, _ in outs],
        in_specs=[place for _, place in ins],
        out_specs=[place for _, place in outs],
        scratch_shapes=list(scratch),
        compiler_params=pltpu.CompilerParams(vmem_limit_bytes=VMEM_LIMIT),
        cost_estimate=pl.CostEstimate(flops=flops, bytes_accessed=moved, transcendentals=0),
        name=name,
    )(*[x for x, _ in ins])


def begin(source, target, sem):
    copy = pltpu.make_async_copy(source, target, sem)
    copy.start()
    return copy


def shaped(shape, dtype):
    return jax.ShapeDtypeStruct(shape, dtype)


def scratch_like(shape, dtype):
    return pltpu.VMEM(shape, dtype)


def chunks_of(part):
    chunk = min(part, 512)
    return [slice(c * chunk, (c + 1) * chunk) for c in range(part // chunk)]


def start_all(pairs, sems):
    return [begin(source, target, sems.at[n]) for n, (source, target) in enumerate(pairs)]


def spread_columns(me, source, half, direct, name, more=(), selection=None, cuts=None):
    own_rows, width = source.shape
    part = width // half
    count = half if direct else 1
    ahead = [] if cuts is None else [(selection, VMEM), (cuts, HBM)]

    def body(me_ref, source_ref, *refs):
        held_ref, sems = refs[-2:]
        refs = refs[:-2]
        load = begin(source_ref, held_ref.at[0], sems.at[0])
        if ahead:
            chosen_ref, cuts_ref, refs = refs[0], refs[1], refs[2:]
            wanted_ref, pieces, refs = refs[0], refs[1 : 1 + cuts.shape[0]], refs[1 + cuts.shape[0] :]
        outs, scratch = refs[:count], refs[count:]
        copies = []
        if ahead:
            cut_ref, cut_sems = scratch
            cuts_in = [
                begin(cuts_ref.at[m], cut_ref.at[m], cut_sems.at[0, m])
                for m in range(cuts.shape[0])
            ]
            row = jnp.concatenate([chosen_ref[b : b + 1, :] for b in range(chosen_ref.shape[0])], axis=1)
            wanted_ref[...] = jnp.broadcast_to(row, wanted_ref.shape)
        load.wait()
        low = me_ref[0] & (half - 1)
        for k in range(half):
            share = low ^ k if direct else k
            at = held_ref.at[0, :, pl.ds(pl.multiple_of(share * part, part), part)]
            out = outs[k] if direct else outs[0].at[k * own_rows : (k + 1) * own_rows]
            copies.append(begin(at, out, sems.at[1 + k]))
        if ahead:
            for m, copy in enumerate(cuts_in):
                copy.wait()
                copies.append(begin(cut_ref.at[m], pieces[m], cut_sems.at[1, m]))
        wait_all(copies)

    if direct:
        outs = [(shaped((own_rows, part), BF16), HBM)] * half
    else:
        outs = [(shaped((half * own_rows, part), BF16), HBM)]
    scratch = []
    if ahead:
        wanted = shaped((more[0], selection.size), jnp.int32)
        outs = [(wanted, VMEM)] + [(shaped(cuts.shape[1:], BF16), HBM)] * cuts.shape[0] + outs
        scratch = [scratch_like(cuts.shape, BF16), pltpu.SemaphoreType.DMA((2, cuts.shape[0]))]
    scratch += [scratch_like((1, own_rows, width), BF16), pltpu.SemaphoreType.DMA((1 + half,))]
    return call(body, outs, [(me, SMEM), (source, HBM)] + ahead, name, 0, scratch)


def pick_rows(me, half, chosen, shares, after, name):
    peers, total = chosen.shape
    picks = total * half // peers
    part = shares[0].shape[1]
    block = sum(x.shape[0] for x in shares)
    batch = min(peers, 8)

    def body(me_ref, chosen_ref, *refs):
        refs = refs[len(after) :]
        parts, (out_ref, rows_ref, pick_ref, sent_ref, in_sem, out_sem) = (
            refs[: len(shares)],
            refs[len(shares) :],
        )
        loads = []
        for k, share in enumerate(parts):
            size = share.shape[0]
            place = (me_ref[0] & (half - 1)) ^ k if len(parts) > 1 else 0
            start = pl.multiple_of(place * size, 16)
            loads.append(begin(share, rows_ref.at[pl.ds(start, size)], in_sem.at[k]))
        block_at = lax.shift_right_logical(me_ref[0], half.bit_length() - 1)
        same = iota((picks, total), 0) + block_at * picks == iota((picks, total), 1)
        stores = []
        for first in range(0, peers, batch):
            for e in range(batch):
                wanted = chosen_ref[first + e : first + e + 1, :]
                column = jnp.sum(jnp.where(same, wanted, 0), axis=1, keepdims=True)
                pick_ref[first // batch % 2, e * picks : (e + 1) * picks] = (
                    column == iota((picks, block), 1)
                ).astype(BF16)
            if first == 0:
                wait_all(loads)
            at = slice(first * picks, (first + batch) * picks)
            sent_ref[at] = dot(pick_ref[first // batch % 2], rows_ref[...]).astype(BF16)
            stores.append(begin(sent_ref.at[at], out_ref.at[at], out_sem.at[first // batch]))
        wait_all(stores)

    return call(
        body,
        [(shaped((peers * picks, part), BF16), HBM)],
        [(me, SMEM), (chosen, VMEM)] + [(x, HBM) for x in list(after) + list(shares)],
        name,
        2 * peers * picks * block * part,
        [
            scratch_like((block, part), BF16),
            scratch_like((2, batch * picks, block), BF16),
            scratch_like((peers * picks, part), BF16),
            pltpu.SemaphoreType.DMA((len(shares),)),
            pltpu.SemaphoreType.DMA((peers // batch,)),
        ],
    )[0]


def slot_body(cap, pieces, own_rows, block_len, chosen_ref, slot_ref):
    rows = slot_ref.shape[1]
    position = jnp.concatenate(
        [chosen_ref[b : b + 1, :] + b * block_len for b in range(chosen_ref.shape[0])], axis=1
    )
    owner = lax.shift_right_logical(position, own_rows.bit_length() - 1)
    peers = chosen_ref.shape[0] * block_len // own_rows
    peer = iota((peers, rows), 0)
    count = jnp.sum((peer == owner).astype(F32), axis=1, keepdims=True)
    earlier = jnp.sum(jnp.where(peer < owner, count, 0.0), axis=0, keepdims=True).astype(jnp.int32)
    slot_ref[...] = owner * (cap * pieces) + iota((1, rows), 1) - earlier


def sum_rows(cap, pieces, own_rows, me, half, chosen, returned):
    slots, part = returned.shape
    peers, total = chosen.shape
    picks = total * half // peers
    group = cap * pieces
    columns = chunks_of(part)

    def body(me_ref, chosen_ref, returned_ref, out_ref, got_ref, pick_ref, sum_ref, in_sem, out_sem):
        loads = [
            begin(returned_ref.at[:, at], got_ref.at[:, at], in_sem.at[n])
            for n, at in enumerate(columns)
        ]
        low = me_ref[0] & (half - 1)
        block_at = lax.shift_right_logical(me_ref[0], half.bit_length() - 1)
        lane = iota((peers, total), 1) - block_at * picks
        here = (lane >= 0) & (lane < picks)
        local = jnp.where(here, chosen_ref[...] - low * own_rows, own_rows)
        before = jnp.sum((local < 0).astype(F32), axis=1, keepdims=True).astype(jnp.int32)
        ranks = lane - before
        owned = jnp.where((local >= 0) & (local < own_rows), local + 1, 0)
        place = iota((group, total), 0)
        for e in range(peers):
            rank, mine = ranks[e : e + 1], owned[e : e + 1]
            column = jnp.zeros((group, 1), jnp.int32)
            for j in range(pieces):
                hit = jnp.where((place == rank + j * cap) & (rank >= 0) & (rank < cap), mine, 0)
                row = jnp.sum(hit, axis=1, keepdims=True)
                column = column + jnp.where(row > 0, row + j * own_rows, 0)
            pick_ref[e * group : (e + 1) * group] = (
                column == iota((group, pieces * own_rows), 1) + 1
            ).astype(F32)
        pick = pick_ref[...].astype(BF16)
        stores = []
        for n, at in enumerate(columns):
            loads[n].wait()
            summed = dot_tn(pick, got_ref[:, at]).astype(BF16)
            for j in range(pieces):
                wide = slice(j * part + at.start, j * part + at.stop)
                sum_ref[:, wide] = summed[j * own_rows : (j + 1) * own_rows]
                stores.append(
                    begin(sum_ref.at[:, wide], out_ref.at[:, wide], out_sem.at[n, j])
                )
        wait_all(stores)

    return call(
        body,
        [(shaped((own_rows, part * pieces), BF16), HBM)],
        [(me, SMEM), (chosen, VMEM), (returned, HBM)],
        "sum_rows",
        2 * slots * pieces * own_rows * part,
        [
            scratch_like((slots, part), BF16),
            scratch_like((slots, pieces * own_rows), F32),
            scratch_like((own_rows, part * pieces), BF16),
            pltpu.SemaphoreType.DMA((len(columns),)),
            pltpu.SemaphoreType.DMA((len(columns), pieces)),
        ],
    )[0]


def load_factor(order_ref, parts, m, target, sems):
    copies = []
    for n, side in enumerate((parts[0].at[m], parts[1 + m]) if len(parts) > 1 else (parts[0].at[m],)):
        count, rows, cols = side.shape
        place = order_ref[0] ^ n if len(parts) > 1 else 0
        start = pl.multiple_of(place * rows, rows)
        for i in range(count):
            at = target.at[pl.ds(start, rows), i * cols : (i + 1) * cols]
            copies.append(begin(side.at[i], at, sems.at[n, i]))
    return copies


def wait_all(copies):
    for copy in copies:
        copy.wait()


def place_matrix(cap, pieces, slots, slot):
    wide = jnp.concatenate([slot + j * cap for j in range(pieces)], axis=1)
    return (iota((slots, wide.shape[1]), 0) == wide).astype(BF16)


def load_rows(got_hbm, x_ref, sems):
    rows, depth = x_ref.shape[0] // NPHM, x_ref.shape[1]
    part = got_hbm.shape[1]
    shares = NPHM * depth // part
    picks = got_hbm.shape[0] * part // (NPHM * depth) // (rows // SELECTED)
    copies = []
    for n in range(got_hbm.shape[0] // picks):
        block, share = divmod(n, shares)
        a, start = share * part // depth, share * part % depth
        first = a * rows + block * picks
        at = x_ref.at[first : first + picks, start : start + part]
        copies.append(begin(got_hbm.at[n * picks : (n + 1) * picks], at, sems.at[n]))
    return copies


def store_parts(order_ref, source_ref, outs, sems):
    copies = []
    for n, out in enumerate(outs):
        size = out.shape[1]
        start = pl.multiple_of((order_ref[0] ^ n) * size if len(outs) > 1 else 0, size)
        copies.append(begin(source_ref.at[:, pl.ds(start, size)], out, sems.at[n]))
    return copies


STRIP = 32


def mix_in(mix_ref, m, y_ref, emit):
    rows, cols = y_ref.shape[0] // NPHM, y_ref.shape[1] // NPHM

    def strip(n, carry):
        start = pl.multiple_of(n * STRIP, STRIP)
        total = [jnp.zeros((STRIP, cols), F32)] * NPHM
        for a in range(NPHM):
            for i in range(NPHM):
                block = y_ref[pl.ds(a * rows + start, STRIP), i * cols : (i + 1) * cols]
                for b in range(NPHM):
                    total[b] = total[b] + mix_ref[m * 64 + i * 16 + a * 4 + b] * block
        emit(start, total)
        return carry

    lax.fori_loop(0, rows // STRIP, strip, 0)


def mix_out(mix_ref, m, d_ref, z_ref):
    rows, cols = d_ref.shape[0], d_ref.shape[1] // NPHM

    def strip(n, carry):
        start = pl.multiple_of(n * STRIP, STRIP)
        blocks = [
            d_ref[pl.ds(start, STRIP), b * cols : (b + 1) * cols].astype(F32) for b in range(NPHM)
        ]
        for a in range(NPHM):
            for i in range(NPHM):
                total = mix_ref[m * 64 + i * 16 + a * 4] * blocks[0]
                for b in range(1, NPHM):
                    total = total + mix_ref[m * 64 + i * 16 + a * 4 + b] * blocks[b]
                z_ref[pl.ds(a * rows + start, STRIP), i * cols : (i + 1) * cols] = total.astype(
                    z_ref.dtype
                )
        return carry

    lax.fori_loop(0, rows // STRIP, strip, 0)


def forward_body(
    sides, order_ref, mix_ref, got_hbm, *refs
):
    held = 3 if sides > 1 else 1
    parts, refs = refs[:held], refs[held:]
    x_outs, refs = refs[:sides], refs[sides:]
    yg_hbm, yu_hbm, act_hbm, slope_hbm, hid_hbm = refs[:5]
    side_ref, x_ref, yg_ref, yu_ref, pre_ref, act_ref, slope_ref, hid_ref = refs[5:13]
    got_sem, side_sem, out_sem = refs[13:]
    loads = load_rows(got_hbm, x_ref, got_sem)
    sides_in = [
        load_factor(order_ref, parts, m, side_ref.at[m], side_sem.at[m]) for m in range(2)
    ]
    wait_all(loads)
    stores = store_parts(order_ref, x_ref, x_outs, out_sem)
    wait_all(sides_in[0])
    yg_ref[...] = dot(x_ref[...], side_ref[0])
    stores.append(begin(yg_ref, yg_hbm, out_sem.at[2]))
    wait_all(sides_in[1])
    yu_ref[...] = dot(x_ref[...], side_ref[1])
    stores.append(begin(yu_ref, yu_hbm, out_sem.at[3]))
    cols = yg_ref.shape[1] // NPHM

    def keep(start, total):
        for b in range(NPHM):
            pre_ref[pl.ds(start, STRIP), b * cols : (b + 1) * cols] = total[b]

    def finish(start, total):
        for b in range(NPHM):
            at = (pl.ds(start, STRIP), slice(b * cols, (b + 1) * cols))
            gate = pre_ref[at]
            sig = jax.nn.sigmoid(gate)
            act = gate * sig
            act_ref[at] = act
            slope_ref[at] = total[b] * (sig + act * (1.0 - sig))
            hid_ref[at] = act * total[b]

    mix_in(mix_ref, 0, yg_ref, keep)
    mix_in(mix_ref, 1, yu_ref, finish)
    stores.append(begin(act_ref, act_hbm, out_sem.at[4]))
    stores.append(begin(slope_ref, slope_hbm, out_sem.at[5]))
    stores.append(begin(hid_ref, hid_hbm, out_sem.at[6]))
    wait_all(stores)


def backward_body(
    cap, pieces, sides, after, order_ref, mix_ref, slot_ref, gate_ref, got_hbm, act_hbm, slope_hbm, hid_hbm,
    *refs,
):
    held = 4 if sides > 1 else 1
    parts, refs = refs[:held], refs[held + after :]
    back_hbm, x_outs, refs = refs[0], refs[1 : 1 + sides], refs[1 + sides :]
    y_hbm, d_hbm, inner_ref = refs[:3]
    (
        side_ref, x_ref, y_ref, d_ref, act_ref, slope_ref, hid_ref, zg_ref, zu_ref, grad_ref,
        back_ref, got_sem, side_sem, in_sem, out_sem,
    ) = refs[3:]
    loads = load_rows(got_hbm, x_ref, got_sem)
    down_in = load_factor(order_ref, parts, 2, side_ref.at[2], side_sem.at[2])
    flat_in = [
        begin(source, target, in_sem.at[n])
        for n, (source, target) in enumerate(
            ((act_hbm, act_ref), (slope_hbm, slope_ref), (hid_hbm, hid_ref))
        )
    ]
    sides_in = [
        load_factor(order_ref, parts, m, side_ref.at[m], side_sem.at[m]) for m in range(2)
    ]
    wait_all(loads)
    stores = store_parts(order_ref, x_ref, x_outs, out_sem)
    wait_all(down_in)
    y_ref[...] = dot(x_ref[...], side_ref[2])
    stores.append(begin(y_ref, y_hbm, out_sem.at[2]))
    cols = y_ref.shape[1] // NPHM
    wait_all(flat_in)

    def finish(start, total):
        gate = gate_ref[pl.ds(start, STRIP), :]
        inner = jnp.zeros((STRIP, cols), F32)
        for b in range(NPHM):
            at = (pl.ds(start, STRIP), slice(b * cols, (b + 1) * cols))
            hidden = hid_ref[at]
            inner = inner + hidden * total[b]
            hidden_grad = gate * total[b]
            d_ref[(0,) + at] = (hidden_grad * slope_ref[at]).astype(BF16)
            d_ref[(1,) + at] = (hidden_grad * act_ref[at]).astype(BF16)
            d_ref[(2,) + at] = (hidden * gate).astype(BF16)
        inner_ref[pl.ds(start, STRIP), :] = inner

    mix_in(mix_ref, 2, y_ref, finish)
    stores.append(begin(d_ref, d_hbm, out_sem.at[3]))
    mix_out(mix_ref, 0, d_ref.at[0], zg_ref)
    mix_out(mix_ref, 1, d_ref.at[1], zu_ref)
    wait_all(sides_in[0])
    wait_all(sides_in[1])
    grad = dot_nt(zg_ref[...], side_ref[0]) + dot_nt(zu_ref[...], side_ref[1])
    grad_ref[...] = grad.astype(BF16)
    place = place_matrix(cap, pieces, back_ref.shape[0], slot_ref[...])
    part = back_ref.shape[1]
    rows, depth = x_ref.shape[0] // NPHM, x_ref.shape[1]
    for n, at in enumerate(chunks_of(part)):
        blocks = []
        for j in range(pieces):
            column = j * part + at.start
            a, start = column // depth, column % depth
            blocks.append(
                grad_ref[a * rows : (a + 1) * rows, start : start + at.stop - at.start]
            )
        back_ref[:, at] = dot(place, jnp.concatenate(blocks, axis=0)).astype(BF16)
        stores.append(begin(back_ref.at[:, at], back_hbm.at[:, at], out_sem.at[4 + n]))
    wait_all(stores)


def factor_body(count_groups, mix_ref, *refs):
    rows_in, refs = refs[: 3 * count_groups], refs[3 * count_groups :]
    out_hbm, x_ref, g_ref, d_ref, z_ref, sum_ref, in_sem, out_sem = refs
    loads = []
    for n in range(count_groups):
        for k, target in enumerate((x_ref, g_ref, d_ref)):
            loads.append(begin(rows_in[3 * n + k], target.at[n], in_sem.at[n, k]))
    stores = []
    cols = out_hbm.shape[3]
    wait_all(loads)
    for m in (2, 0, 1):
        for n in range(count_groups):
            mix_out(mix_ref, m, d_ref.at[n, m], z_ref.at[n])
        left = g_ref if m == 2 else x_ref
        sum_ref[m] = sum(dot_tn(left[n], z_ref[n]) for n in range(count_groups))
        for i in range(NPHM):
            at = sum_ref.at[m, :, i * cols : (i + 1) * cols]
            stores.append(begin(at, out_hbm.at[m, i], out_sem.at[m, i]))
    wait_all(stores)


def mix_grad_body(yg_hbm, yu_hbm, yd_hbm, d_hbm, out_ref, y_ref, d_ref, sems):
    loads = [begin(d_hbm, d_ref, sems.at[3])]
    for m, source in enumerate((yg_hbm, yu_hbm, yd_hbm)):
        loads.append(begin(source, y_ref.at[m], sems.at[m]))
    wait_all(loads)
    rows, cols = d_ref.shape[1], d_ref.shape[2] // NPHM
    for m in range(3):
        for a in range(NPHM):
            for i in range(NPHM):
                block = y_ref[m, a * rows : (a + 1) * rows, i * cols : (i + 1) * cols]
                for b in range(NPHM):
                    at = m * 64 + i * 16 + a * 4 + b
                    other = d_ref[m, :, b * cols : (b + 1) * cols].astype(F32)
                    out_ref[at : at + 1, :] = jnp.sum(block * other, axis=0, keepdims=True)


def shards(tokens, cotangent, factors, mix, selection, scores):
    peers = lax.axis_size("exp")
    groups = lax.axis_size("seq")
    own_rows, width = tokens.shape
    _, weights, count, depth_own, cols = factors.shape
    depth = depth_own * groups
    hidden = count * cols
    cap = 3 * own_rows // (2 * peers)
    pieces = 1
    while (cap * pieces) % 8:
        pieces *= 2
    slots = peers * cap * pieces
    part = width // pieces
    steps = len(chunks_of(part))
    block_len = peers * SELECTED
    rows = selection.shape[1] * selection.shape[2]
    stacked = count * rows
    swap = groups == 2
    pair = [(0, 1), (1, 0)]
    mixing = mix.reshape(-1)
    dma = pltpu.SemaphoreType.DMA

    def across(array):
        return lax.ppermute(array, "seq", pair)

    half = peers // selection.shape[1]
    direct = half == 8
    me = lax.axis_index("exp").astype(jnp.int32).reshape(1)
    group = lax.axis_index("seq").astype(jnp.int32).reshape(1)
    halves = [list(range(h, h + half)) for h in range(0, peers, half)]
    near = [k for k in range(1, half) if k >= 4] + [k for k in range(1, half) if k < 4]

    outs = spread_columns(
        me, tokens, half, direct, "spread_tokens", (peers,), selection[0], factors[0]
    )
    wanted, cuts, token_shares = outs[0], outs[1 : 1 + weights], outs[1 + weights :]
    if swap:
        cuts = [across(x) for x in cuts]
        factor_parts = [factors[0]] + cuts
        sides = 2
    else:
        cuts = []
        factor_parts = [lax.all_gather(factors, "seq", axis=3, tiled=True)[0]]
        sides = 1
    sides_in = [(x, HBM) for x in factor_parts]
    chosen = lax.all_to_all(wanted, "exp", split_axis=0, concat_axis=0, tiled=True)

    def to_peers(array):
        array = array.reshape(peers, -1, array.shape[1])
        array = lax.all_to_all(array, "exp", split_axis=0, concat_axis=0, tiled=True)
        return array.reshape(-1, array.shape[2])

    def collect(shares):
        if direct:
            moved = {
                k: lax.ppermute(shares[k], "exp", [(n, n ^ k) for n in range(peers)]) for k in near
            }
            return [shares[0]] + [moved[k] for k in range(1, half)]
        array = shares[0].reshape(half, own_rows, -1)
        array = lax.all_to_all(
            array, "exp", split_axis=0, concat_axis=0, axis_index_groups=halves, tiled=True
        )
        return [array.reshape(half * own_rows, -1)]

    got_rows = to_peers(
        pick_rows(me, half, chosen, collect(token_shares), cuts[:1], "pick_tokens")
    )
    grad_shares = spread_columns(me, cotangent, half, direct, "spread_cotangent")
    got_grads = to_peers(
        pick_rows(me, half, chosen, collect(grad_shares), cuts[1:2], "pick_cotangent")
    )
    slot = call(
        functools.partial(slot_body, cap, pieces, own_rows, block_len),
        [(shaped((1, rows), jnp.int32), VMEM)],
        [(selection[0], VMEM)],
        "row_slots",
        1 << 16,
    )[0]

    gate = jax.nn.sigmoid(scores[0].reshape(-1).astype(F32) / 64.0)
    gate_wide = jnp.broadcast_to(gate[:, None], (rows, cols))

    product = 2 * stacked * depth * hidden
    split = [(shaped((stacked, depth // sides), BF16), HBM)] * sides
    mixed = (shaped((stacked, hidden), F32), HBM)
    flat = (shaped((rows, hidden), F32), HBM)
    back_scratch = scratch_like((slots, part), BF16)
    pieces_in = got_rows.shape[0] // SELECTED
    stack_scratch = scratch_like((stacked, depth), BF16)
    mixed_scratch = scratch_like((stacked, hidden), F32)
    low_scratch = scratch_like((stacked, hidden), BF16)
    flat_scratch = scratch_like((rows, hidden), F32)
    outs = call(
        functools.partial(forward_body, sides),
        split + [mixed, mixed, flat, flat, flat],
        [(group, SMEM), (mixing, SMEM), (got_rows, HBM)] + sides_in[:3],
        "forward",
        2 * product,
        [scratch_like((2, depth, hidden), BF16), stack_scratch, mixed_scratch, mixed_scratch]
        + [flat_scratch] * 4
        + [dma((pieces_in,)), dma((2, sides, count)), dma((7,))],
    )
    x_parts, (y_gate, y_up, act, slope, hid) = outs[:sides], outs[sides:]
    x_rows = [x_parts[0]] + [across(x) for x in x_parts[1:]]
    after = x_rows[1:]
    outs = call(
        functools.partial(backward_body, cap, pieces, sides, len(after)),
        [(shaped((slots, part), BF16), HBM)]
        + split
        + [mixed, (shaped((weights, rows, hidden), BF16), HBM), (shaped((rows, cols), F32), VMEM)],
        [(group, SMEM), (mixing, SMEM), (slot, VMEM), (gate_wide, VMEM), (got_grads, HBM)]
        + [(x, HBM) for x in (act, slope, hid)]
        + sides_in
        + [(x, HBM) for x in after],
        "backward",
        3 * product,
        [scratch_like((weights, depth, hidden), BF16), stack_scratch, mixed_scratch]
        + [scratch_like((weights, rows, hidden), BF16)]
        + [flat_scratch] * 3
        + [low_scratch] * 2
        + [stack_scratch, back_scratch]
        + [dma((pieces_in,)), dma((weights, sides, count)), dma((3,)), dma((4 + steps,))],
    )
    back, g_parts, (y_down, d_own, inner) = outs[0], outs[1 : 1 + sides], outs[1 + sides :]
    returned = to_peers(back)

    d_rows = [d_own] + [across(d_own) for _ in x_parts[1:]]
    g_rows = [g_parts[0]] + [across(x) for x in g_parts[1:]]
    depth_here = depth // sides
    factor_grad = call(
        functools.partial(factor_body, sides),
        [(shaped((weights, count, depth_here, cols), F32), HBM)],
        [(mixing, SMEM)]
        + [(x, HBM) for n in range(sides) for x in (x_rows[n], g_rows[n], d_rows[n])],
        "factor_grad",
        3 * product,
        [scratch_like((sides, stacked, depth_here), BF16)] * 2
        + [
            scratch_like((sides, weights, rows, hidden), BF16),
            scratch_like((sides, stacked, hidden), BF16),
            scratch_like((weights, depth_here, hidden), F32),
            dma((sides, 3)),
            dma((weights, count)),
        ],
    )[0]
    mix_rows = call(
        mix_grad_body,
        [(shaped((mixing.size, cols), F32), VMEM)],
        [(x, HBM) for x in (y_gate, y_up, y_down, d_own)],
        "mix_partials",
        weights * 64 * 2 * rows * cols,
        [
            scratch_like((weights, stacked, hidden), F32),
            scratch_like((weights, rows, hidden), BF16),
            dma((4,)),
        ],
    )[0]
    mix_part = jnp.sum(mix_rows, axis=1).reshape(mix.shape)
    if swap:
        mix_grad = mix_part + across(mix_part)
    else:
        factor_grad = lax.psum_scatter(
            factor_grad.astype(BF16), "seq", scatter_dimension=2, tiled=True
        ).astype(F32)
        mix_grad = lax.psum(mix_part, "seq")
    gate_grad = (jnp.sum(inner, axis=1) * gate * (1.0 - gate)).reshape(selection.shape)
    token_grad = sum_rows(cap, pieces, own_rows, me, half, chosen, returned)
    return token_grad, factor_grad[None], mix_grad, gate_grad


def solution(mesh):
    return jax.shard_map(
        shards,
        mesh=mesh,
        in_specs=(
            P(("seq", "exp"), None),
            P(("seq", "exp"), None),
            P("exp", None, None, "seq", None),
            P("exp", None, None, None, None),
            P("exp", "seq", None),
            P("exp", "seq", None),
        ),
        out_specs=(
            P(("seq", "exp"), None),
            P("exp", None, None, "seq", None),
            P("exp", None, None, None, None),
            P("exp", "seq", None),
        ),
        check_vma=False,
    )
```

```python
import functools

import jax
import jax.numpy as jnp
from jax import lax
from jax.experimental import pallas as pl
from jax.experimental.pallas import tpu as pltpu
from jax.sharding import PartitionSpec as P

SELECTED = 64
NPHM = 4
VMEM_LIMIT = 63 * 1024 * 1024
F32 = jnp.float32
BF16 = jnp.bfloat16


def iota(shape, dim):
    return lax.broadcasted_iota(jnp.int32, shape, dim)


def dot(left, right):
    return jnp.dot(left, right, preferred_element_type=F32)


def dot_tn(left, right):
    return lax.dot_general(left, right, (((0,), (0,)), ((), ())), preferred_element_type=F32)


def dot_nt(left, right):
    return lax.dot_general(left, right, (((1,), (1,)), ((), ())), preferred_element_type=F32)


HBM = pl.BlockSpec(memory_space=pltpu.HBM)
VMEM = pl.BlockSpec(memory_space=pltpu.VMEM)
SMEM = pl.BlockSpec(memory_space=pltpu.SMEM)


def call(body, outs, ins, name, flops, scratch=()):
    moved = sum(x.size * x.dtype.itemsize for x, _ in list(ins) + list(outs))
    return pl.pallas_call(
        body,
        out_shape=[x for x, _ in outs],
        in_specs=[place for _, place in ins],
        out_specs=[place for _, place in outs],
        scratch_shapes=list(scratch),
        compiler_params=pltpu.CompilerParams(vmem_limit_bytes=VMEM_LIMIT),
        cost_estimate=pl.CostEstimate(flops=flops, bytes_accessed=moved, transcendentals=0),
        name=name,
    )(*[x for x, _ in ins])


def begin(source, target, sem):
    copy = pltpu.make_async_copy(source, target, sem)
    copy.start()
    return copy


def shaped(shape, dtype):
    return jax.ShapeDtypeStruct(shape, dtype)


def scratch_like(shape, dtype):
    return pltpu.VMEM(shape, dtype)


def chunks_of(part):
    chunk = min(part, 512)
    return [slice(c * chunk, (c + 1) * chunk) for c in range(part // chunk)]


def start_all(pairs, sems):
    return [begin(source, target, sems.at[n]) for n, (source, target) in enumerate(pairs)]


def spread_columns(me, sources, half, direct, name):
    own_rows, width = sources[0].shape
    count = len(sources)
    part = width // half
    tall = count * own_rows

    def body(me_ref, *refs):
        ins, outs = refs[:count], refs[count : -3]
        held_ref, in_sem, out_sem = refs[-3:]
        loads = [begin(ref, held_ref.at[n], in_sem.at[n]) for n, ref in enumerate(ins)]
        low = me_ref[0] & (half - 1)
        copies = []
        for n, load in enumerate(loads):
            load.wait()
            for k in range(half):
                share = low ^ k if direct else k
                at = held_ref.at[n, :, pl.ds(pl.multiple_of(share * part, part), part)]
                out, first = (outs[k], 0) if direct else (outs[0], k * tall)
                rows = pl.ds(first + n * own_rows, own_rows)
                copies.append(begin(at, out.at[rows], out_sem.at[n, k]))
        wait_all(copies)

    if direct:
        outs = [(shaped((tall, part), BF16), HBM)] * half
    else:
        outs = [(shaped((half * tall, part), BF16), HBM)]
    scratch = [
        scratch_like((count, own_rows, width), BF16),
        pltpu.SemaphoreType.DMA((count,)),
        pltpu.SemaphoreType.DMA((count, half)),
    ]
    return call(body, outs, [(me, SMEM)] + [(x, HBM) for x in sources], name, 0, scratch)


def share_selection(chosen, peers):
    def body(chosen_ref, out_ref):
        blocks = [chosen_ref[b : b + 1, :] for b in range(chosen_ref.shape[0])]
        out_ref[...] = jnp.broadcast_to(jnp.concatenate(blocks, axis=1), out_ref.shape)

    out = (shaped((peers, chosen.size), jnp.int32), VMEM)
    return call(body, [out], [(chosen, VMEM)], "share_selection", 0)[0]


def cut_factors(factors):
    weights = factors.shape[0]

    def body(factors_ref, *refs):
        outs, (held_ref, sems) = refs[:weights], refs[weights:]
        loads = [
            begin(factors_ref.at[m], held_ref.at[m], sems.at[0, m]) for m in range(weights)
        ]
        copies = []
        for m, load in enumerate(loads):
            load.wait()
            copies.append(begin(held_ref.at[m], outs[m], sems.at[1, m]))
        wait_all(copies)

    outs = [(shaped(factors.shape[1:], BF16), HBM)] * weights
    scratch = [scratch_like(factors.shape, BF16), pltpu.SemaphoreType.DMA((2, weights))]
    return call(body, outs, [(factors, HBM)], "cut_factors", 0, scratch)


def pick_rows(me, half, own_rows, which, chosen, shares, after, name):
    peers, total = chosen.shape
    picks = total * half // peers
    part = shares[0].shape[1]
    block = half * own_rows
    tall = sum(x.shape[0] for x in shares) // half
    batch = min(peers, 8)

    def body(me_ref, chosen_ref, *refs):
        refs = refs[len(after) :]
        parts, (out_ref, rows_ref, pick_ref, sent_ref, in_sem, out_sem) = (
            refs[: len(shares)],
            refs[len(shares) :],
        )
        loads = []
        for k in range(half):
            place = (me_ref[0] & (half - 1)) ^ k if len(parts) > 1 else k
            share, first = (parts[k], 0) if len(parts) > 1 else (parts[0], k * tall)
            first += which * own_rows
            target = rows_ref.at[pl.ds(pl.multiple_of(place * own_rows, own_rows), own_rows)]
            loads.append(begin(share.at[first : first + own_rows], target, in_sem.at[k]))
        block_at = lax.shift_right_logical(me_ref[0], half.bit_length() - 1)
        same = iota((picks, total), 0) + block_at * picks == iota((picks, total), 1)
        stores = []
        for first in range(0, peers, batch):
            for e in range(batch):
                wanted = chosen_ref[first + e : first + e + 1, :]
                column = jnp.sum(jnp.where(same, wanted, 0), axis=1, keepdims=True)
                pick_ref[first // batch % 2, e * picks : (e + 1) * picks] = (
                    column == iota((picks, block), 1)
                ).astype(BF16)
            if first == 0:
                wait_all(loads)
            at = slice(first * picks, (first + batch) * picks)
            sent_ref[at] = dot(pick_ref[first // batch % 2], rows_ref[...]).astype(BF16)
            stores.append(begin(sent_ref.at[at], out_ref.at[at], out_sem.at[first // batch]))
        wait_all(stores)

    return call(
        body,
        [(shaped((peers * picks, part), BF16), HBM)],
        [(me, SMEM), (chosen, VMEM)] + [(x, HBM) for x in list(after) + list(shares)],
        name,
        2 * peers * picks * block * part,
        [
            scratch_like((block, part), BF16),
            scratch_like((2, batch * picks, block), BF16),
            scratch_like((peers * picks, part), BF16),
            pltpu.SemaphoreType.DMA((half,)),
            pltpu.SemaphoreType.DMA((peers // batch,)),
        ],
    )[0]


def slot_body(cap, pieces, own_rows, block_len, chosen_ref, slot_ref):
    rows = slot_ref.shape[1]
    position = jnp.concatenate(
        [chosen_ref[b : b + 1, :] + b * block_len for b in range(chosen_ref.shape[0])], axis=1
    )
    owner = lax.shift_right_logical(position, own_rows.bit_length() - 1)
    peers = chosen_ref.shape[0] * block_len // own_rows
    peer = iota((peers, rows), 0)
    count = jnp.sum((peer == owner).astype(F32), axis=1, keepdims=True)
    earlier = jnp.sum(jnp.where(peer < owner, count, 0.0), axis=0, keepdims=True).astype(jnp.int32)
    slot_ref[...] = owner * (cap * pieces) + iota((1, rows), 1) - earlier


def place_rows(cap, pieces, own_rows, me, half, chosen):
    peers, total = chosen.shape
    picks = total * half // peers
    group = cap * pieces

    def body(me_ref, chosen_ref, out_ref, pick_ref):
        low = me_ref[0] & (half - 1)
        block_at = lax.shift_right_logical(me_ref[0], half.bit_length() - 1)
        lane = iota((peers, total), 1) - block_at * picks
        here = (lane >= 0) & (lane < picks)
        local = jnp.where(here, chosen_ref[...] - low * own_rows, own_rows)
        before = jnp.sum((local < 0).astype(F32), axis=1, keepdims=True).astype(jnp.int32)
        ranks = lane - before
        owned = jnp.where((local >= 0) & (local < own_rows), local + 1, 0)
        place = iota((group, total), 0)
        for e in range(peers):
            rank, mine = ranks[e : e + 1], owned[e : e + 1]
            column = jnp.zeros((group, 1), jnp.int32)
            for j in range(pieces):
                hit = jnp.where((place == rank + j * cap) & (rank >= 0) & (rank < cap), mine, 0)
                row = jnp.sum(hit, axis=1, keepdims=True)
                column = column + jnp.where(row > 0, row + j * own_rows, 0)
            pick_ref[e * group : (e + 1) * group] = (
                column == iota((group, pieces * own_rows), 1) + 1
            ).astype(F32)
        out_ref[...] = jnp.transpose(pick_ref[...]).astype(BF16)

    return call(
        body,
        [(shaped((pieces * own_rows, peers * group), BF16), VMEM)],
        [(me, SMEM), (chosen, VMEM)],
        "place_rows",
        1 << 20,
        [scratch_like((peers * group, pieces * own_rows), F32)],
    )[0]


def sum_rows(pieces, placed, returned):
    slots, part = returned.shape
    own_rows = placed.shape[0] // pieces
    columns = chunks_of(part)

    def body(placed_hbm, returned_ref, out_ref, place_ref, got_ref, sum_ref, in_sem, out_sem):
        first = begin(placed_hbm, place_ref, in_sem.at[len(columns)])
        loads = [
            begin(returned_ref.at[:, at], got_ref.at[:, at], in_sem.at[n])
            for n, at in enumerate(columns)
        ]
        first.wait()
        stores = []
        for n, at in enumerate(columns):
            loads[n].wait()
            summed = dot(place_ref[...], got_ref[:, at]).astype(BF16)
            for j in range(pieces):
                wide = slice(j * part + at.start, j * part + at.stop)
                sum_ref[:, wide] = summed[j * own_rows : (j + 1) * own_rows]
                stores.append(
                    begin(sum_ref.at[:, wide], out_ref.at[:, wide], out_sem.at[n, j])
                )
        wait_all(stores)

    return call(
        body,
        [(shaped((own_rows, part * pieces), BF16), HBM)],
        [(placed, HBM), (returned, HBM)],
        "sum_rows",
        2 * slots * pieces * own_rows * part,
        [
            scratch_like(placed.shape, BF16),
            scratch_like((slots, part), BF16),
            scratch_like((own_rows, part * pieces), BF16),
            pltpu.SemaphoreType.DMA((len(columns) + 1,)),
            pltpu.SemaphoreType.DMA((len(columns), pieces)),
        ],
    )[0]


def load_factor(order_ref, parts, m, target, sems):
    copies = []
    for n, side in enumerate((parts[0].at[m], parts[1 + m]) if len(parts) > 1 else (parts[0].at[m],)):
        count, rows, cols = side.shape
        place = order_ref[0] ^ n if len(parts) > 1 else 0
        start = pl.multiple_of(place * rows, rows)
        for i in range(count):
            at = target.at[pl.ds(start, rows), i * cols : (i + 1) * cols]
            copies.append(begin(side.at[i], at, sems.at[n, i]))
    return copies


def wait_all(copies):
    for copy in copies:
        copy.wait()


def place_matrix(cap, pieces, slots, slot):
    wide = jnp.concatenate([slot + j * cap for j in range(pieces)], axis=1)
    return (iota((slots, wide.shape[1]), 0) == wide).astype(BF16)


def load_rows(got_hbm, x_ref, sems):
    rows, depth = x_ref.shape[0] // NPHM, x_ref.shape[1]
    part = got_hbm.shape[1]
    shares = NPHM * depth // part
    picks = got_hbm.shape[0] * part // (NPHM * depth) // (rows // SELECTED)
    copies = []
    for n in range(got_hbm.shape[0] // picks):
        block, share = divmod(n, shares)
        a, start = share * part // depth, share * part % depth
        first = a * rows + block * picks
        at = x_ref.at[first : first + picks, start : start + part]
        copies.append(begin(got_hbm.at[n * picks : (n + 1) * picks], at, sems.at[n]))
    return copies


def store_parts(order_ref, source_ref, outs, sems):
    copies = []
    for n, out in enumerate(outs):
        size = out.shape[1]
        start = pl.multiple_of((order_ref[0] ^ n) * size if len(outs) > 1 else 0, size)
        copies.append(begin(source_ref.at[:, pl.ds(start, size)], out, sems.at[n]))
    return copies


STRIP = 32


def mix_in(mix_ref, m, y_ref, emit):
    rows, cols = y_ref.shape[0] // NPHM, y_ref.shape[1] // NPHM

    def strip(n, carry):
        start = pl.multiple_of(n * STRIP, STRIP)
        total = [jnp.zeros((STRIP, cols), F32)] * NPHM
        for a in range(NPHM):
            for i in range(NPHM):
                block = y_ref[pl.ds(a * rows + start, STRIP), i * cols : (i + 1) * cols]
                for b in range(NPHM):
                    total[b] = total[b] + mix_ref[m * 64 + i * 16 + a * 4 + b] * block
        emit(start, total)
        return carry

    lax.fori_loop(0, rows // STRIP, strip, 0)


def mix_out(mix_ref, m, d_ref, z_ref):
    rows, cols = d_ref.shape[0], d_ref.shape[1] // NPHM

    def strip(n, carry):
        start = pl.multiple_of(n * STRIP, STRIP)
        blocks = [
            d_ref[pl.ds(start, STRIP), b * cols : (b + 1) * cols].astype(F32) for b in range(NPHM)
        ]
        for a in range(NPHM):
            for i in range(NPHM):
                total = mix_ref[m * 64 + i * 16 + a * 4] * blocks[0]
                for b in range(1, NPHM):
                    total = total + mix_ref[m * 64 + i * 16 + a * 4 + b] * blocks[b]
                z_ref[pl.ds(a * rows + start, STRIP), i * cols : (i + 1) * cols] = total.astype(
                    z_ref.dtype
                )
        return carry

    lax.fori_loop(0, rows // STRIP, strip, 0)


def forward_body(
    sides, order_ref, mix_ref, got_hbm, *refs
):
    held = 3 if sides > 1 else 1
    parts, refs = refs[:held], refs[held:]
    x_outs, refs = refs[:sides], refs[sides:]
    yg_hbm, yu_hbm, act_hbm, slope_hbm, hid_hbm = refs[:5]
    side_ref, x_ref, yg_ref, yu_ref, pre_ref, act_ref, slope_ref, hid_ref = refs[5:13]
    got_sem, side_sem, out_sem = refs[13:]
    loads = load_rows(got_hbm, x_ref, got_sem)
    sides_in = [
        load_factor(order_ref, parts, m, side_ref.at[m], side_sem.at[m]) for m in range(2)
    ]
    wait_all(loads)
    stores = store_parts(order_ref, x_ref, x_outs, out_sem)
    wait_all(sides_in[0])
    yg_ref[...] = dot(x_ref[...], side_ref[0])
    stores.append(begin(yg_ref, yg_hbm, out_sem.at[2]))
    wait_all(sides_in[1])
    yu_ref[...] = dot(x_ref[...], side_ref[1])
    stores.append(begin(yu_ref, yu_hbm, out_sem.at[3]))
    cols = yg_ref.shape[1] // NPHM

    def keep(start, total):
        for b in range(NPHM):
            pre_ref[pl.ds(start, STRIP), b * cols : (b + 1) * cols] = total[b]

    def finish(start, total):
        for b in range(NPHM):
            at = (pl.ds(start, STRIP), slice(b * cols, (b + 1) * cols))
            gate = pre_ref[at]
            sig = jax.nn.sigmoid(gate)
            act = gate * sig
            act_ref[at] = act
            slope_ref[at] = total[b] * (sig + act * (1.0 - sig))
            hid_ref[at] = act * total[b]

    mix_in(mix_ref, 0, yg_ref, keep)
    mix_in(mix_ref, 1, yu_ref, finish)
    stores.append(begin(act_ref, act_hbm, out_sem.at[4]))
    stores.append(begin(slope_ref, slope_hbm, out_sem.at[5]))
    stores.append(begin(hid_ref, hid_hbm, out_sem.at[6]))
    wait_all(stores)


def backward_body(
    cap, pieces, sides, after, order_ref, mix_ref, slot_ref, score_ref, got_hbm, act_hbm, slope_hbm, hid_hbm,
    *refs,
):
    held = 4 if sides > 1 else 1
    parts, refs = refs[:held], refs[held + after :]
    back_hbm, x_outs, refs = refs[0], refs[1 : 1 + sides], refs[1 + sides :]
    y_hbm, d_hbm, inner_ref = refs[:3]
    (
        side_ref, x_ref, y_ref, d_ref, act_ref, slope_ref, hid_ref, zg_ref, zu_ref, grad_ref,
        back_ref, gate_ref, got_sem, side_sem, in_sem, out_sem,
    ) = refs[3:]
    loads = load_rows(got_hbm, x_ref, got_sem)
    down_in = load_factor(order_ref, parts, 2, side_ref.at[2], side_sem.at[2])
    flat_in = [
        begin(source, target, in_sem.at[n])
        for n, (source, target) in enumerate(
            ((act_hbm, act_ref), (slope_hbm, slope_ref), (hid_hbm, hid_ref))
        )
    ]
    sides_in = [
        load_factor(order_ref, parts, m, side_ref.at[m], side_sem.at[m]) for m in range(2)
    ]
    score = jnp.concatenate([score_ref[b : b + 1, :] for b in range(score_ref.shape[0])], axis=1)
    rows = score.shape[1]
    same = iota((rows, rows), 0) == iota((rows, rows), 1)
    score = jnp.sum(jnp.where(same, score.astype(F32), 0.0), axis=1, keepdims=True)
    gate_ref[...] = jnp.broadcast_to(jax.nn.sigmoid(score / 64.0), gate_ref.shape)
    wait_all(loads)
    stores = store_parts(order_ref, x_ref, x_outs, out_sem)
    wait_all(down_in)
    y_ref[...] = dot(x_ref[...], side_ref[2])
    stores.append(begin(y_ref, y_hbm, out_sem.at[2]))
    cols = y_ref.shape[1] // NPHM
    wait_all(flat_in)

    def finish(start, total):
        gate = gate_ref[pl.ds(start, STRIP), :]
        inner = jnp.zeros((STRIP, cols), F32)
        for b in range(NPHM):
            at = (pl.ds(start, STRIP), slice(b * cols, (b + 1) * cols))
            hidden = hid_ref[at]
            inner = inner + hidden * total[b]
            hidden_grad = gate * total[b]
            d_ref[(0,) + at] = (hidden_grad * slope_ref[at]).astype(BF16)
            d_ref[(1,) + at] = (hidden_grad * act_ref[at]).astype(BF16)
            d_ref[(2,) + at] = (hidden * gate).astype(BF16)
        inner_ref[pl.ds(start, STRIP), :] = inner

    mix_in(mix_ref, 2, y_ref, finish)
    stores.append(begin(d_ref, d_hbm, out_sem.at[3]))
    mix_out(mix_ref, 0, d_ref.at[0], zg_ref)
    mix_out(mix_ref, 1, d_ref.at[1], zu_ref)
    wait_all(sides_in[0])
    wait_all(sides_in[1])
    grad = dot_nt(zg_ref[...], side_ref[0]) + dot_nt(zu_ref[...], side_ref[1])
    grad_ref[...] = grad.astype(BF16)
    place = place_matrix(cap, pieces, back_ref.shape[0], slot_ref[...])
    part = back_ref.shape[1]
    rows, depth = x_ref.shape[0] // NPHM, x_ref.shape[1]
    for n, at in enumerate(chunks_of(part)):
        blocks = []
        for j in range(pieces):
            column = j * part + at.start
            a, start = column // depth, column % depth
            blocks.append(
                grad_ref[a * rows : (a + 1) * rows, start : start + at.stop - at.start]
            )
        back_ref[:, at] = dot(place, jnp.concatenate(blocks, axis=0)).astype(BF16)
        stores.append(begin(back_ref.at[:, at], back_hbm.at[:, at], out_sem.at[4 + n]))
    wait_all(stores)


def factor_body(count_groups, mix_ref, *refs):
    rows_in, refs = refs[: 3 * count_groups], refs[3 * count_groups :]
    out_hbm, x_ref, g_ref, d_ref, z_ref, sum_ref, in_sem, out_sem = refs
    loads = []
    for n in range(count_groups):
        for k, target in enumerate((x_ref, g_ref, d_ref)):
            loads.append(begin(rows_in[3 * n + k], target.at[n], in_sem.at[n, k]))
    stores = []
    cols = out_hbm.shape[3]
    wait_all(loads)
    for m in (2, 0, 1):
        for n in range(count_groups):
            mix_out(mix_ref, m, d_ref.at[n, m], z_ref.at[n])
        left = g_ref if m == 2 else x_ref
        sum_ref[m] = sum(dot_tn(left[n], z_ref[n]) for n in range(count_groups))
        for i in range(NPHM):
            at = sum_ref.at[m, :, i * cols : (i + 1) * cols]
            stores.append(begin(at, out_hbm.at[m, i], out_sem.at[m, i]))
    wait_all(stores)


def mix_grad_body(yg_hbm, yu_hbm, yd_hbm, d_hbm, out_ref, y_ref, d_ref, sems):
    loads = [begin(d_hbm, d_ref, sems.at[3])]
    for m, source in enumerate((yg_hbm, yu_hbm, yd_hbm)):
        loads.append(begin(source, y_ref.at[m], sems.at[m]))
    wait_all(loads)
    rows, cols = d_ref.shape[1], d_ref.shape[2] // NPHM
    for m in range(3):
        for a in range(NPHM):
            for i in range(NPHM):
                block = y_ref[m, a * rows : (a + 1) * rows, i * cols : (i + 1) * cols]
                for b in range(NPHM):
                    at = m * 64 + i * 16 + a * 4 + b
                    other = d_ref[m, :, b * cols : (b + 1) * cols].astype(F32)
                    out_ref[at : at + 1, :] = jnp.sum(block * other, axis=0, keepdims=True)


def shards(tokens, cotangent, factors, mix, selection, scores):
    peers = lax.axis_size("exp")
    groups = lax.axis_size("seq")
    own_rows, width = tokens.shape
    _, weights, count, depth_own, cols = factors.shape
    depth = depth_own * groups
    hidden = count * cols
    cap = 3 * own_rows // (2 * peers)
    pieces = 1
    while (cap * pieces) % 8:
        pieces *= 2
    slots = peers * cap * pieces
    part = width // pieces
    steps = len(chunks_of(part))
    block_len = peers * SELECTED
    rows = selection.shape[1] * selection.shape[2]
    stacked = count * rows
    swap = groups == 2
    pair = [(0, 1), (1, 0)]
    mixing = mix.reshape(-1)
    dma = pltpu.SemaphoreType.DMA

    def across(array):
        return lax.ppermute(array, "seq", pair)

    half = peers // selection.shape[1]
    direct = half == 8
    me = lax.axis_index("exp").astype(jnp.int32).reshape(1)
    group = lax.axis_index("seq").astype(jnp.int32).reshape(1)
    halves = [list(range(h, h + half)) for h in range(0, peers, half)]
    near = [k for k in range(1, half) if k >= 4] + [k for k in range(1, half) if k < 4]

    shares = spread_columns(me, [tokens, cotangent], half, direct, "spread_columns")
    cuts = cut_factors(factors[0])
    wanted = share_selection(selection[0], peers)
    if swap:
        cuts = [across(x) for x in cuts]
        factor_parts = [factors[0]] + cuts
        sides = 2
    else:
        cuts = []
        factor_parts = [lax.all_gather(factors, "seq", axis=3, tiled=True)[0]]
        sides = 1
    sides_in = [(x, HBM) for x in factor_parts]
    chosen = lax.all_to_all(wanted, "exp", split_axis=0, concat_axis=0, tiled=True)

    def to_peers(array):
        array = array.reshape(peers, -1, array.shape[1])
        array = lax.all_to_all(array, "exp", split_axis=0, concat_axis=0, tiled=True)
        return array.reshape(-1, array.shape[2])

    def collect(shares):
        if direct:
            moved = {
                k: lax.ppermute(shares[k], "exp", [(n, n ^ k) for n in range(peers)]) for k in near
            }
            return [shares[0]] + [moved[k] for k in range(1, half)]
        array = shares[0].reshape(half, -1, shares[0].shape[1])
        array = lax.all_to_all(
            array, "exp", split_axis=0, concat_axis=0, axis_index_groups=halves, tiled=True
        )
        return [array.reshape(shares[0].shape)]

    shares = collect(shares)
    pick = functools.partial(pick_rows, me, half, own_rows)
    got_rows = to_peers(pick(0, chosen, shares, cuts[:1], "pick_tokens"))
    got_grads = to_peers(pick(1, chosen, shares, cuts[1:2], "pick_cotangent"))
    placed = place_rows(cap, pieces, own_rows, me, half, chosen)
    slot = call(
        functools.partial(slot_body, cap, pieces, own_rows, block_len),
        [(shaped((1, rows), jnp.int32), VMEM)],
        [(selection[0], VMEM)],
        "row_slots",
        1 << 16,
    )[0]

    gate = jax.nn.sigmoid(scores[0].reshape(-1).astype(F32) / 64.0)

    product = 2 * stacked * depth * hidden
    split = [(shaped((stacked, depth // sides), BF16), HBM)] * sides
    mixed = (shaped((stacked, hidden), F32), HBM)
    flat = (shaped((rows, hidden), F32), HBM)
    back_scratch = scratch_like((slots, part), BF16)
    pieces_in = got_rows.shape[0] // SELECTED
    stack_scratch = scratch_like((stacked, depth), BF16)
    mixed_scratch = scratch_like((stacked, hidden), F32)
    low_scratch = scratch_like((stacked, hidden), BF16)
    flat_scratch = scratch_like((rows, hidden), F32)
    outs = call(
        functools.partial(forward_body, sides),
        split + [mixed, mixed, flat, flat, flat],
        [(group, SMEM), (mixing, SMEM), (got_rows, HBM)] + sides_in[:3],
        "forward",
        2 * product,
        [scratch_like((2, depth, hidden), BF16), stack_scratch, mixed_scratch, mixed_scratch]
        + [flat_scratch] * 4
        + [dma((pieces_in,)), dma((2, sides, count)), dma((7,))],
    )
    x_parts, (y_gate, y_up, act, slope, hid) = outs[:sides], outs[sides:]
    x_rows = [x_parts[0]] + [across(x) for x in x_parts[1:]]
    after = x_rows[1:]
    outs = call(
        functools.partial(backward_body, cap, pieces, sides, len(after)),
        [(shaped((slots, part), BF16), HBM)]
        + split
        + [mixed, (shaped((weights, rows, hidden), BF16), HBM), (shaped((rows, cols), F32), VMEM)],
        [(group, SMEM), (mixing, SMEM), (slot, VMEM), (scores[0], VMEM), (got_grads, HBM)]
        + [(x, HBM) for x in (act, slope, hid)]
        + sides_in
        + [(x, HBM) for x in after],
        "backward",
        3 * product,
        [scratch_like((weights, depth, hidden), BF16), stack_scratch, mixed_scratch]
        + [scratch_like((weights, rows, hidden), BF16)]
        + [flat_scratch] * 3
        + [low_scratch] * 2
        + [stack_scratch, back_scratch, scratch_like((rows, cols), F32)]
        + [dma((pieces_in,)), dma((weights, sides, count)), dma((3,)), dma((4 + steps,))],
    )
    back, g_parts, (y_down, d_own, inner) = outs[0], outs[1 : 1 + sides], outs[1 + sides :]
    returned = to_peers(back)

    d_rows = [d_own] + [across(d_own) for _ in x_parts[1:]]
    g_rows = [g_parts[0]] + [across(x) for x in g_parts[1:]]
    depth_here = depth // sides
    factor_grad = call(
        functools.partial(factor_body, sides),
        [(shaped((weights, count, depth_here, cols), F32), HBM)],
        [(mixing, SMEM)]
        + [(x, HBM) for n in range(sides) for x in (x_rows[n], g_rows[n], d_rows[n])],
        "factor_grad",
        3 * product,
        [scratch_like((sides, stacked, depth_here), BF16)] * 2
        + [
            scratch_like((sides, weights, rows, hidden), BF16),
            scratch_like((sides, stacked, hidden), BF16),
            scratch_like((weights, depth_here, hidden), F32),
            dma((sides, 3)),
            dma((weights, count)),
        ],
    )[0]
    mix_rows = call(
        mix_grad_body,
        [(shaped((mixing.size, cols), F32), VMEM)],
        [(x, HBM) for x in (y_gate, y_up, y_down, d_own)],
        "mix_partials",
        weights * 64 * 2 * rows * cols,
        [
            scratch_like((weights, stacked, hidden), F32),
            scratch_like((weights, rows, hidden), BF16),
            dma((4,)),
        ],
    )[0]
    mix_part = jnp.sum(mix_rows, axis=1).reshape(mix.shape)
    if swap:
        mix_grad = mix_part + across(mix_part)
    else:
        factor_grad = lax.psum_scatter(
            factor_grad.astype(BF16), "seq", scatter_dimension=2, tiled=True
        ).astype(F32)
        mix_grad = lax.psum(mix_part, "seq")
    gate_grad = (jnp.sum(inner, axis=1) * gate * (1.0 - gate)).reshape(selection.shape)
    token_grad = sum_rows(pieces, placed, returned)
    return token_grad, factor_grad[None], mix_grad, gate_grad


def solution(mesh):
    return jax.shard_map(
        shards,
        mesh=mesh,
        in_specs=(
            P(("seq", "exp"), None),
            P(("seq", "exp"), None),
            P("exp", None, None, "seq", None),
            P("exp", None, None, None, None),
            P("exp", "seq", None),
            P("exp", "seq", None),
        ),
        out_specs=(
            P(("seq", "exp"), None),
            P("exp", None, None, "seq", None),
            P("exp", None, None, None, None),
            P("exp", "seq", None),
        ),
        check_vma=False,
    )
```

```python
import functools

import jax
import jax.numpy as jnp
from jax import lax
from jax.experimental import pallas as pl
from jax.experimental.pallas import tpu as pltpu
from jax.sharding import PartitionSpec as P

SELECTED = 64
NPHM = 4
VMEM_LIMIT = 63 * 1024 * 1024
F32 = jnp.float32
BF16 = jnp.bfloat16


def iota(shape, dim):
    return lax.broadcasted_iota(jnp.int32, shape, dim)


def dot(left, right):
    return jnp.dot(left, right, preferred_element_type=F32)


def dot_tn(left, right):
    return lax.dot_general(left, right, (((0,), (0,)), ((), ())), preferred_element_type=F32)


def dot_nt(left, right):
    return lax.dot_general(left, right, (((1,), (1,)), ((), ())), preferred_element_type=F32)


HBM = pl.BlockSpec(memory_space=pltpu.HBM)
VMEM = pl.BlockSpec(memory_space=pltpu.VMEM)
SMEM = pl.BlockSpec(memory_space=pltpu.SMEM)


def call(body, outs, ins, name, flops, scratch=()):
    moved = sum(x.size * x.dtype.itemsize for x, _ in list(ins) + list(outs))
    return pl.pallas_call(
        body,
        out_shape=[x for x, _ in outs],
        in_specs=[place for _, place in ins],
        out_specs=[place for _, place in outs],
        scratch_shapes=list(scratch),
        compiler_params=pltpu.CompilerParams(vmem_limit_bytes=VMEM_LIMIT),
        cost_estimate=pl.CostEstimate(flops=flops, bytes_accessed=moved, transcendentals=0),
        name=name,
    )(*[x for x, _ in ins])


def begin(source, target, sem):
    copy = pltpu.make_async_copy(source, target, sem)
    copy.start()
    return copy


def shaped(shape, dtype):
    return jax.ShapeDtypeStruct(shape, dtype)


def scratch_like(shape, dtype):
    return pltpu.VMEM(shape, dtype)


def chunks_of(part):
    chunk = min(part, 512)
    return [slice(c * chunk, (c + 1) * chunk) for c in range(part // chunk)]


def index_body(cap, pieces, own_rows, block_len, chosen_ref, told_ref, slot_ref):
    peers, rows = told_ref.shape[0] // 2, slot_ref.shape[1]
    blocks = [chosen_ref[b : b + 1, :] for b in range(chosen_ref.shape[0])]
    position = jnp.concatenate([x + b * block_len for b, x in enumerate(blocks)], axis=1)
    owner = lax.shift_right_logical(position, own_rows.bit_length() - 1)
    local = position & (own_rows - 1)
    peer = iota((peers, rows), 0)
    mine = (peer == owner).astype(F32)
    count = jnp.sum(mine, axis=1, keepdims=True)
    earlier = jnp.sum(jnp.where(peer < owner, count, 0.0), axis=0, keepdims=True).astype(jnp.int32)
    rank = iota((1, rows), 1) - earlier
    slot_ref[...] = owner * (cap * pieces) + rank
    lane = iota((rows, rows), 0)
    hit = jnp.zeros((rows, rows), F32)
    for j in range(pieces):
        hit = hit + (lane == rank + j * cap).astype(F32)
    twice = iota((2 * peers, rows), 0)
    marked = jnp.where(twice == 2 * owner, local + 1, 0).astype(F32)
    asked = dot_nt(marked.astype(BF16), hit.astype(BF16)).astype(jnp.int32)
    told_ref[...] = jnp.where((twice & 1) == 1, jnp.concatenate(blocks, axis=1), asked)


def pick_matrix(cap, pieces, own_rows, requested):
    told, lanes = requested.shape
    peers = told // 2
    group = cap * pieces
    slots = peers * group
    peer = 2 * iota((peers, group, told), 0).reshape(slots, told)
    spread = dot(
        (peer == iota((slots, told), 1)).astype(BF16), requested.astype(F32).astype(BF16)
    )
    place = iota((peers, group, lanes), 1).reshape(slots, lanes)
    row = jnp.sum(
        jnp.where(place == iota((slots, lanes), 1), spread, 0.0), axis=1, keepdims=True
    ).astype(jnp.int32)
    piece = iota((peers, group, 1), 1).reshape(slots, 1)
    shift = jnp.zeros((slots, 1), jnp.int32)
    for j in range(1, pieces):
        shift = shift + jnp.where(piece >= j * cap, own_rows, 0)
    target = jnp.where(row > 0, row - 1 + shift, -1)
    return (target == iota((slots, pieces * own_rows), 1)).astype(BF16)


def pick_slots(cap, pieces, requested, source, name):
    own_rows, width = source.shape
    part = width // pieces
    slots = requested.shape[0] // 2 * cap * pieces
    columns = chunks_of(part)

    def body(requested_ref, source_ref, *refs):
        out_ref, rows_ref, sent_ref, in_sem, out_sem = refs
        loads = []
        for n, at in enumerate(columns):
            for j in range(pieces):
                wide = slice(j * part + at.start, j * part + at.stop)
                target = rows_ref.at[j * own_rows : (j + 1) * own_rows, at]
                loads.append(begin(source_ref.at[:, wide], target, in_sem.at[n, j]))
        pick = pick_matrix(cap, pieces, own_rows, requested_ref[...])
        stores = []
        for n, at in enumerate(columns):
            for load in loads[n * pieces : (n + 1) * pieces]:
                load.wait()
            sent_ref[:, at] = dot(pick, rows_ref[:, at]).astype(BF16)
            stores.append(begin(sent_ref.at[:, at], out_ref.at[:, at], out_sem.at[n]))
        for store in stores:
            store.wait()

    return call(
        body,
        [(shaped((slots, part), BF16), HBM)],
        [(requested, VMEM), (source, HBM)],
        name,
        2 * slots * pieces * own_rows * part,
        [
            scratch_like((pieces * own_rows, part), BF16),
            scratch_like((slots, part), BF16),
            pltpu.SemaphoreType.DMA((len(columns), pieces)),
            pltpu.SemaphoreType.DMA((len(columns),)),
        ],
    )[0]


def spread_columns(me, sources, half, direct, name):
    own_rows, width = sources[0].shape
    count = len(sources)
    part = width // half
    tall = count * own_rows

    def body(me_ref, *refs):
        ins, outs = refs[:count], refs[count : -3]
        held_ref, in_sem, out_sem = refs[-3:]
        loads = [begin(ref, held_ref.at[n], in_sem.at[n]) for n, ref in enumerate(ins)]
        low = me_ref[0] & (half - 1)
        copies = []
        for n, load in enumerate(loads):
            load.wait()
            for k in range(half):
                share = low ^ k if direct else k
                at = held_ref.at[n, :, pl.ds(pl.multiple_of(share * part, part), part)]
                out, first = (outs[k], 0) if direct else (outs[0], k * tall)
                rows = pl.ds(first + n * own_rows, own_rows)
                copies.append(begin(at, out.at[rows], out_sem.at[n, k]))
        wait_all(copies)

    if direct:
        outs = [(shaped((tall, part), BF16), HBM)] * half
    else:
        outs = [(shaped((half * tall, part), BF16), HBM)]
    scratch = [
        scratch_like((count, own_rows, width), BF16),
        pltpu.SemaphoreType.DMA((count,)),
        pltpu.SemaphoreType.DMA((count, half)),
    ]
    return call(body, outs, [(me, SMEM)] + [(x, HBM) for x in sources], name, 0, scratch)


def cut_factors(factors, first):
    cuts = (slice(0, first), slice(first, factors.shape[0]))

    def body(factors_ref, *refs):
        outs, (held_ref, sems) = refs[:2], refs[2:]
        loads = [
            begin(factors_ref.at[at], held_ref.at[at], sems.at[0, n]) for n, at in enumerate(cuts)
        ]
        copies = []
        for n, at in enumerate(cuts):
            loads[n].wait()
            copies.append(begin(held_ref.at[at], outs[n], sems.at[1, n]))
        wait_all(copies)

    outs = [
        (shaped((at.stop - at.start,) + factors.shape[1:], BF16), HBM) for at in cuts
    ]
    scratch = [scratch_like(factors.shape, BF16), pltpu.SemaphoreType.DMA((2, 2))]
    return call(body, outs, [(factors, HBM)], "cut_factors", 0, scratch)


def pick_rows(me, half, own_rows, which, chosen, shares, after, name):
    peers, total = chosen.shape[0] // 2, chosen.shape[1]
    picks = total * half // peers
    part = shares[0].shape[1]
    block = half * own_rows
    tall = sum(x.shape[0] for x in shares) // half
    batch = min(peers, 8)

    def body(me_ref, chosen_ref, *refs):
        refs = refs[len(after) :]
        parts, (out_ref, rows_ref, pick_ref, sent_ref, in_sem, out_sem) = (
            refs[: len(shares)],
            refs[len(shares) :],
        )
        loads = []
        for k in range(half):
            place = (me_ref[0] & (half - 1)) ^ k if len(parts) > 1 else k
            share, first = (parts[k], 0) if len(parts) > 1 else (parts[0], k * tall)
            first += which * own_rows
            target = rows_ref.at[pl.ds(pl.multiple_of(place * own_rows, own_rows), own_rows)]
            loads.append(begin(share.at[first : first + own_rows], target, in_sem.at[k]))
        block_at = lax.shift_right_logical(me_ref[0], half.bit_length() - 1)
        same = iota((picks, total), 0) + block_at * picks == iota((picks, total), 1)
        stores = []
        for first in range(0, peers, batch):
            for e in range(batch):
                wanted = chosen_ref[2 * (first + e) + 1 : 2 * (first + e) + 2, :]
                column = jnp.sum(jnp.where(same, wanted, 0), axis=1, keepdims=True)
                pick_ref[first // batch % 2, e * picks : (e + 1) * picks] = (
                    column == iota((picks, block), 1)
                ).astype(BF16)
            if first == 0:
                wait_all(loads)
            at = slice(first * picks, (first + batch) * picks)
            sent_ref[at] = dot(pick_ref[first // batch % 2], rows_ref[...]).astype(BF16)
            stores.append(begin(sent_ref.at[at], out_ref.at[at], out_sem.at[first // batch]))
        wait_all(stores)

    return call(
        body,
        [(shaped((peers * picks, part), BF16), HBM)],
        [(me, SMEM), (chosen, VMEM)] + [(x, HBM) for x in list(after) + list(shares)],
        name,
        2 * peers * picks * block * part,
        [
            scratch_like((block, part), BF16),
            scratch_like((2, batch * picks, block), BF16),
            scratch_like((peers * picks, part), BF16),
            pltpu.SemaphoreType.DMA((half,)),
            pltpu.SemaphoreType.DMA((peers // batch,)),
        ],
    )[0]


def place_rows(cap, pieces, own_rows, me, half, chosen):
    peers, total = chosen.shape[0] // 2, chosen.shape[1]
    picks = total * half // peers
    group = cap * pieces

    def body(me_ref, chosen_ref, out_ref, pick_ref):
        low = me_ref[0] & (half - 1)
        block_at = lax.shift_right_logical(me_ref[0], half.bit_length() - 1)
        lane = iota((2 * peers, total), 1) - block_at * picks
        here = (lane >= 0) & (lane < picks)
        local = jnp.where(here, chosen_ref[...] - low * own_rows, own_rows)
        before = jnp.sum((local < 0).astype(F32), axis=1, keepdims=True).astype(jnp.int32)
        ranks = lane - before
        owned = jnp.where((local >= 0) & (local < own_rows), local + 1, 0)
        place = iota((group, total), 0)
        for e in range(peers):
            at = slice(2 * e + 1, 2 * e + 2)
            rank, mine = ranks[at], owned[at]
            column = jnp.zeros((group, 1), jnp.int32)
            for j in range(pieces):
                hit = jnp.where((place == rank + j * cap) & (rank >= 0) & (rank < cap), mine, 0)
                row = jnp.sum(hit, axis=1, keepdims=True)
                column = column + jnp.where(row > 0, row + j * own_rows, 0)
            pick_ref[e * group : (e + 1) * group] = (
                column == iota((group, pieces * own_rows), 1) + 1
            ).astype(F32)
        out_ref[...] = jnp.transpose(pick_ref[...]).astype(BF16)

    return call(
        body,
        [(shaped((pieces * own_rows, peers * group), BF16), VMEM)],
        [(me, SMEM), (chosen, VMEM)],
        "place_rows",
        1 << 20,
        [scratch_like((peers * group, pieces * own_rows), F32)],
    )[0]


def sum_rows(pieces, placed, returned):
    slots, part = returned.shape
    own_rows = placed.shape[0] // pieces
    columns = chunks_of(part)

    def body(placed_hbm, returned_ref, out_ref, place_ref, got_ref, sum_ref, in_sem, out_sem):
        first = begin(placed_hbm, place_ref, in_sem.at[len(columns)])
        loads = [
            begin(returned_ref.at[:, at], got_ref.at[:, at], in_sem.at[n])
            for n, at in enumerate(columns)
        ]
        first.wait()
        stores = []
        for n, at in enumerate(columns):
            loads[n].wait()
            summed = dot(place_ref[...], got_ref[:, at]).astype(BF16)
            for j in range(pieces):
                wide = slice(j * part + at.start, j * part + at.stop)
                sum_ref[:, wide] = summed[j * own_rows : (j + 1) * own_rows]
                stores.append(
                    begin(sum_ref.at[:, wide], out_ref.at[:, wide], out_sem.at[n, j])
                )
        wait_all(stores)

    return call(
        body,
        [(shaped((own_rows, part * pieces), BF16), HBM)],
        [(placed, HBM), (returned, HBM)],
        "sum_rows",
        2 * slots * pieces * own_rows * part,
        [
            scratch_like(placed.shape, BF16),
            scratch_like((slots, part), BF16),
            scratch_like((own_rows, part * pieces), BF16),
            pltpu.SemaphoreType.DMA((len(columns) + 1,)),
            pltpu.SemaphoreType.DMA((len(columns), pieces)),
        ],
    )[0]


def load_factor(order_ref, parts, m, target, sems):
    copies = []
    sides = [parts[0].at[m]]
    if len(parts) > 1:
        first = parts[1].shape[0]
        sides.append(parts[1].at[m] if m < first else parts[2].at[m - first])
    for n, side in enumerate(sides):
        count, rows, cols = side.shape
        place = order_ref[0] ^ n if len(parts) > 1 else 0
        start = pl.multiple_of(place * rows, rows)
        for i in range(count):
            at = target.at[pl.ds(start, rows), i * cols : (i + 1) * cols]
            copies.append(begin(side.at[i], at, sems.at[n, i]))
    return copies


def wait_all(copies):
    for copy in copies:
        copy.wait()


def place_matrix(cap, pieces, slots, slot):
    wide = jnp.concatenate([slot + j * cap for j in range(pieces)], axis=1)
    return (iota((slots, wide.shape[1]), 0) == wide).astype(BF16)


def load_rows(got_hbm, x_ref, sems):
    rows, depth = x_ref.shape[0] // NPHM, x_ref.shape[1]
    part = got_hbm.shape[1]
    shares = NPHM * depth // part
    picks = got_hbm.shape[0] * part // (NPHM * depth) // (rows // SELECTED)
    copies = []
    for n in range(got_hbm.shape[0] // picks):
        block, share = divmod(n, shares)
        a, start = share * part // depth, share * part % depth
        first = a * rows + block * picks
        at = x_ref.at[first : first + picks, start : start + part]
        copies.append(begin(got_hbm.at[n * picks : (n + 1) * picks], at, sems.at[n]))
    return copies


def load_slots(got_hbm, got_ref, sems):
    return [
        begin(got_hbm.at[:, at], got_ref.at[:, at], sems.at[n])
        for n, at in enumerate(chunks_of(got_ref.shape[1]))
    ]


def stack_rows(pieces, place, loads, got_ref, out_ref):
    part = got_ref.shape[1]
    rows, depth = out_ref.shape[0] // NPHM, out_ref.shape[1]
    for load, at in zip(loads, chunks_of(part)):
        load.wait()
        block = dot_tn(place, got_ref[:, at]).astype(BF16)
        for j in range(pieces):
            column = j * part + at.start
            a, start = column // depth, column % depth
            out_ref[a * rows : (a + 1) * rows, start : start + at.stop - at.start] = block[
                j * rows : (j + 1) * rows
            ]


def store_parts(order_ref, source_ref, outs, sems):
    copies = []
    for n, out in enumerate(outs):
        size = out.shape[1]
        start = pl.multiple_of((order_ref[0] ^ n) * size if len(outs) > 1 else 0, size)
        copies.append(begin(source_ref.at[:, pl.ds(start, size)], out, sems.at[n]))
    return copies


STRIP = 32


def mix_in(mix_ref, m, y_ref, emit):
    rows, cols = y_ref.shape[0] // NPHM, y_ref.shape[1] // NPHM

    def strip(n, carry):
        start = pl.multiple_of(n * STRIP, STRIP)
        total = [jnp.zeros((STRIP, cols), F32)] * NPHM
        for a in range(NPHM):
            for i in range(NPHM):
                block = y_ref[pl.ds(a * rows + start, STRIP), i * cols : (i + 1) * cols]
                for b in range(NPHM):
                    total[b] = total[b] + mix_ref[m * 64 + i * 16 + a * 4 + b] * block
        emit(start, total)
        return carry

    lax.fori_loop(0, rows // STRIP, strip, 0)


def mix_out(mix_ref, m, d_ref, z_ref):
    rows, cols = d_ref.shape[0], d_ref.shape[1] // NPHM

    def strip(n, carry):
        start = pl.multiple_of(n * STRIP, STRIP)
        blocks = [
            d_ref[pl.ds(start, STRIP), b * cols : (b + 1) * cols].astype(F32) for b in range(NPHM)
        ]
        for a in range(NPHM):
            for i in range(NPHM):
                total = mix_ref[m * 64 + i * 16 + a * 4] * blocks[0]
                for b in range(1, NPHM):
                    total = total + mix_ref[m * 64 + i * 16 + a * 4 + b] * blocks[b]
                z_ref[pl.ds(a * rows + start, STRIP), i * cols : (i + 1) * cols] = total.astype(
                    z_ref.dtype
                )
        return carry

    lax.fori_loop(0, rows // STRIP, strip, 0)


def forward_body(
    cap, pieces, sides, order_ref, mix_ref, slot_ref, got_hbm, *refs
):
    held = 2 if sides > 1 else 1
    parts, refs = refs[:held], refs[held:]
    x_outs, refs = refs[:sides], refs[sides:]
    yg_hbm, yu_hbm, act_hbm, slope_hbm, hid_hbm = refs[:5]
    got_ref, side_ref, x_ref, yg_ref, yu_ref, pre_ref, act_ref, slope_ref, hid_ref = refs[5:14]
    got_sem, side_sem, out_sem = refs[14:]
    loads = load_slots(got_hbm, got_ref, got_sem)
    sides_in = [
        load_factor(order_ref, parts, m, side_ref.at[m], side_sem.at[m]) for m in range(2)
    ]
    place = place_matrix(cap, pieces, got_ref.shape[0], slot_ref[...])
    stack_rows(pieces, place, loads, got_ref, x_ref)
    stores = store_parts(order_ref, x_ref, x_outs, out_sem)
    wait_all(sides_in[0])
    yg_ref[...] = dot(x_ref[...], side_ref[0])
    stores.append(begin(yg_ref, yg_hbm, out_sem.at[2]))
    wait_all(sides_in[1])
    yu_ref[...] = dot(x_ref[...], side_ref[1])
    stores.append(begin(yu_ref, yu_hbm, out_sem.at[3]))
    cols = yg_ref.shape[1] // NPHM

    def keep(start, total):
        for b in range(NPHM):
            pre_ref[pl.ds(start, STRIP), b * cols : (b + 1) * cols] = total[b]

    def finish(start, total):
        for b in range(NPHM):
            at = (pl.ds(start, STRIP), slice(b * cols, (b + 1) * cols))
            gate = pre_ref[at]
            sig = jax.nn.sigmoid(gate)
            act = gate * sig
            act_ref[at] = act
            slope_ref[at] = total[b] * (sig + act * (1.0 - sig))
            hid_ref[at] = act * total[b]

    mix_in(mix_ref, 0, yg_ref, keep)
    mix_in(mix_ref, 1, yu_ref, finish)
    stores.append(begin(act_ref, act_hbm, out_sem.at[4]))
    stores.append(begin(slope_ref, slope_hbm, out_sem.at[5]))
    stores.append(begin(hid_ref, hid_hbm, out_sem.at[6]))
    wait_all(stores)


def backward_body(
    cap, pieces, sides, after, order_ref, mix_ref, slot_ref, score_ref, got_hbm, act_hbm, slope_hbm, hid_hbm,
    *refs,
):
    held = 3 if sides > 1 else 1
    parts, refs = refs[:held], refs[held + after :]
    back_hbm, x_outs, refs = refs[0], refs[1 : 1 + sides], refs[1 + sides :]
    y_hbm, d_hbm, inner_ref = refs[:3]
    (
        side_ref, x_ref, y_ref, d_ref, act_ref, slope_ref, hid_ref, zg_ref, zu_ref, grad_ref,
        back_ref, gate_ref, got_sem, side_sem, in_sem, out_sem,
    ) = refs[3:]
    loads = load_rows(got_hbm, x_ref, got_sem)
    down_in = load_factor(order_ref, parts, 2, side_ref.at[2], side_sem.at[2])
    flat_in = [
        begin(source, target, in_sem.at[n])
        for n, (source, target) in enumerate(
            ((act_hbm, act_ref), (slope_hbm, slope_ref), (hid_hbm, hid_ref))
        )
    ]
    sides_in = [
        load_factor(order_ref, parts, m, side_ref.at[m], side_sem.at[m]) for m in range(2)
    ]
    score = jnp.concatenate([score_ref[b : b + 1, :] for b in range(score_ref.shape[0])], axis=1)
    rows = score.shape[1]
    same = iota((rows, rows), 0) == iota((rows, rows), 1)
    score = jnp.sum(jnp.where(same, score.astype(F32), 0.0), axis=1, keepdims=True)
    gate_ref[...] = jnp.broadcast_to(jax.nn.sigmoid(score / 64.0), gate_ref.shape)
    wait_all(loads)
    stores = store_parts(order_ref, x_ref, x_outs, out_sem)
    wait_all(down_in)
    y_ref[...] = dot(x_ref[...], side_ref[2])
    stores.append(begin(y_ref, y_hbm, out_sem.at[2]))
    cols = y_ref.shape[1] // NPHM
    wait_all(flat_in)

    def finish(start, total):
        gate = gate_ref[pl.ds(start, STRIP), :]
        inner = jnp.zeros((STRIP, cols), F32)
        for b in range(NPHM):
            at = (pl.ds(start, STRIP), slice(b * cols, (b + 1) * cols))
            hidden = hid_ref[at]
            inner = inner + hidden * total[b]
            hidden_grad = gate * total[b]
            d_ref[(0,) + at] = (hidden_grad * slope_ref[at]).astype(BF16)
            d_ref[(1,) + at] = (hidden_grad * act_ref[at]).astype(BF16)
            d_ref[(2,) + at] = (hidden * gate).astype(BF16)
        inner_ref[pl.ds(start, STRIP), :] = inner

    mix_in(mix_ref, 2, y_ref, finish)
    stores.append(begin(d_ref, d_hbm, out_sem.at[3]))
    mix_out(mix_ref, 0, d_ref.at[0], zg_ref)
    mix_out(mix_ref, 1, d_ref.at[1], zu_ref)
    wait_all(sides_in[0])
    wait_all(sides_in[1])
    grad = dot_nt(zg_ref[...], side_ref[0]) + dot_nt(zu_ref[...], side_ref[1])
    grad_ref[...] = grad.astype(BF16)
    place = place_matrix(cap, pieces, back_ref.shape[0], slot_ref[...])
    part = back_ref.shape[1]
    rows, depth = x_ref.shape[0] // NPHM, x_ref.shape[1]
    for n, at in enumerate(chunks_of(part)):
        blocks = []
        for j in range(pieces):
            column = j * part + at.start
            a, start = column // depth, column % depth
            blocks.append(
                grad_ref[a * rows : (a + 1) * rows, start : start + at.stop - at.start]
            )
        back_ref[:, at] = dot(place, jnp.concatenate(blocks, axis=0)).astype(BF16)
        stores.append(begin(back_ref.at[:, at], back_hbm.at[:, at], out_sem.at[4 + n]))
    wait_all(stores)


def factor_body(count_groups, mix_ref, *refs):
    rows_in, refs = refs[: 3 * count_groups], refs[3 * count_groups :]
    out_hbm, x_ref, g_ref, d_ref, z_ref, sum_ref, in_sem, out_sem = refs
    loads = []
    for n in range(count_groups):
        for k, target in enumerate((x_ref, g_ref, d_ref)):
            loads.append(begin(rows_in[3 * n + k], target.at[n], in_sem.at[n, k]))
    stores = []
    cols = out_hbm.shape[3]
    wait_all(loads)
    for m in (2, 0, 1):
        for n in range(count_groups):
            mix_out(mix_ref, m, d_ref.at[n, m], z_ref.at[n])
        left = g_ref if m == 2 else x_ref
        sum_ref[m] = sum(dot_tn(left[n], z_ref[n]) for n in range(count_groups))
        for i in range(NPHM):
            at = sum_ref.at[m, :, i * cols : (i + 1) * cols]
            stores.append(begin(at, out_hbm.at[m, i], out_sem.at[m, i]))
    wait_all(stores)


def mix_grad_body(yg_hbm, yu_hbm, yd_hbm, d_hbm, out_ref, y_ref, d_ref, sems):
    loads = [begin(d_hbm, d_ref, sems.at[3])]
    for m, source in enumerate((yg_hbm, yu_hbm, yd_hbm)):
        loads.append(begin(source, y_ref.at[m], sems.at[m]))
    wait_all(loads)
    rows, cols = d_ref.shape[1], d_ref.shape[2] // NPHM
    for m in range(3):
        for a in range(NPHM):
            for i in range(NPHM):
                block = y_ref[m, a * rows : (a + 1) * rows, i * cols : (i + 1) * cols]
                for b in range(NPHM):
                    at = m * 64 + i * 16 + a * 4 + b
                    other = d_ref[m, :, b * cols : (b + 1) * cols].astype(F32)
                    out_ref[at : at + 1, :] = jnp.sum(block * other, axis=0, keepdims=True)


def shards(tokens, cotangent, factors, mix, selection, scores):
    peers = lax.axis_size("exp")
    groups = lax.axis_size("seq")
    own_rows, width = tokens.shape
    _, weights, count, depth_own, cols = factors.shape
    depth = depth_own * groups
    hidden = count * cols
    cap = 3 * own_rows // (2 * peers)
    pieces = 1
    while (cap * pieces) % 8:
        pieces *= 2
    slots = peers * cap * pieces
    part = width // pieces
    steps = len(chunks_of(part))
    block_len = peers * SELECTED
    rows = selection.shape[1] * selection.shape[2]
    stacked = count * rows
    swap = groups == 2
    pair = [(0, 1), (1, 0)]
    mixing = mix.reshape(-1)
    dma = pltpu.SemaphoreType.DMA

    def across(array):
        return lax.ppermute(array, "seq", pair)

    half = peers // selection.shape[1]
    direct = half == 8
    me = lax.axis_index("exp").astype(jnp.int32).reshape(1)
    group = lax.axis_index("seq").astype(jnp.int32).reshape(1)
    halves = [list(range(h, h + half)) for h in range(0, peers, half)]
    near = [k for k in range(1, half) if k >= 4] + [k for k in range(1, half) if k < 4]

    if swap:
        cuts = [across(x) for x in cut_factors(factors[0], 2)]
        factor_parts = [factors[0]] + cuts
        sides = 2
    else:
        cuts = []
        factor_parts = [lax.all_gather(factors, "seq", axis=3, tiled=True)[0]]
        sides = 1
    sides_in = [(x, HBM) for x in factor_parts]
    told, slot = call(
        functools.partial(index_body, cap, pieces, own_rows, block_len),
        [(shaped((2 * peers, rows), jnp.int32), VMEM), (shaped((1, rows), jnp.int32), VMEM)],
        [(selection[0], VMEM)],
        "wanted_rows",
        1 << 20,
    )
    chosen = lax.all_to_all(told, "exp", split_axis=0, concat_axis=0, tiled=True)

    def to_peers(array):
        array = array.reshape(peers, -1, array.shape[1])
        array = lax.all_to_all(array, "exp", split_axis=0, concat_axis=0, tiled=True)
        return array.reshape(-1, array.shape[2])

    def collect(shares):
        if direct:
            moved = {
                k: lax.ppermute(shares[k], "exp", [(n, n ^ k) for n in range(peers)]) for k in near
            }
            return [shares[0]] + [moved[k] for k in range(1, half)]
        array = shares[0].reshape(half, -1, shares[0].shape[1])
        array = lax.all_to_all(
            array, "exp", split_axis=0, concat_axis=0, axis_index_groups=halves, tiled=True
        )
        return [array.reshape(shares[0].shape)]

    got_rows = to_peers(pick_slots(cap, pieces, chosen, tokens, "pick_tokens"))
    shares = collect(spread_columns(me, [cotangent], half, direct, "spread_cotangent"))
    picked = pick_rows(me, half, own_rows, 0, chosen, shares, cuts[:1], "pick_cotangent")
    got_grads = to_peers(picked)
    placed = place_rows(cap, pieces, own_rows, me, half, chosen)
    gate = jax.nn.sigmoid(scores[0].reshape(-1).astype(F32) / 64.0)

    product = 2 * stacked * depth * hidden
    split = [(shaped((stacked, depth // sides), BF16), HBM)] * sides
    mixed = (shaped((stacked, hidden), F32), HBM)
    flat = (shaped((rows, hidden), F32), HBM)
    back_scratch = scratch_like((slots, part), BF16)
    pieces_in = got_grads.shape[0] // SELECTED
    stack_scratch = scratch_like((stacked, depth), BF16)
    mixed_scratch = scratch_like((stacked, hidden), F32)
    low_scratch = scratch_like((stacked, hidden), BF16)
    flat_scratch = scratch_like((rows, hidden), F32)
    outs = call(
        functools.partial(forward_body, cap, pieces, sides),
        split + [mixed, mixed, flat, flat, flat],
        [(group, SMEM), (mixing, SMEM), (slot, VMEM), (got_rows, HBM)] + sides_in[:2],
        "forward",
        2 * product,
        [back_scratch, scratch_like((2, depth, hidden), BF16), stack_scratch, mixed_scratch, mixed_scratch]
        + [flat_scratch] * 4
        + [dma((steps,)), dma((2, sides, count)), dma((7,))],
    )
    x_parts, (y_gate, y_up, act, slope, hid) = outs[:sides], outs[sides:]
    x_rows = [x_parts[0]] + [across(x) for x in x_parts[1:]]
    after = x_rows[1:]
    outs = call(
        functools.partial(backward_body, cap, pieces, sides, len(after)),
        [(shaped((slots, part), BF16), HBM)]
        + split
        + [mixed, (shaped((weights, rows, hidden), BF16), HBM), (shaped((rows, cols), F32), VMEM)],
        [(group, SMEM), (mixing, SMEM), (slot, VMEM), (scores[0], VMEM), (got_grads, HBM)]
        + [(x, HBM) for x in (act, slope, hid)]
        + sides_in
        + [(x, HBM) for x in after],
        "backward",
        3 * product,
        [scratch_like((weights, depth, hidden), BF16), stack_scratch, mixed_scratch]
        + [scratch_like((weights, rows, hidden), BF16)]
        + [flat_scratch] * 3
        + [low_scratch] * 2
        + [stack_scratch, back_scratch, scratch_like((rows, cols), F32)]
        + [dma((pieces_in,)), dma((weights, sides, count)), dma((3,)), dma((4 + steps,))],
    )
    back, g_parts, (y_down, d_own, inner) = outs[0], outs[1 : 1 + sides], outs[1 + sides :]
    returned = to_peers(back)

    d_rows = [d_own] + [across(d_own) for _ in x_parts[1:]]
    g_rows = [g_parts[0]] + [across(x) for x in g_parts[1:]]
    depth_here = depth // sides
    factor_grad = call(
        functools.partial(factor_body, sides),
        [(shaped((weights, count, depth_here, cols), F32), HBM)],
        [(mixing, SMEM)]
        + [(x, HBM) for n in range(sides) for x in (x_rows[n], g_rows[n], d_rows[n])],
        "factor_grad",
        3 * product,
        [scratch_like((sides, stacked, depth_here), BF16)] * 2
        + [
            scratch_like((sides, weights, rows, hidden), BF16),
            scratch_like((sides, stacked, hidden), BF16),
            scratch_like((weights, depth_here, hidden), F32),
            dma((sides, 3)),
            dma((weights, count)),
        ],
    )[0]
    mix_rows = call(
        mix_grad_body,
        [(shaped((mixing.size, cols), F32), VMEM)],
        [(x, HBM) for x in (y_gate, y_up, y_down, d_own)],
        "mix_partials",
        weights * 64 * 2 * rows * cols,
        [
            scratch_like((weights, stacked, hidden), F32),
            scratch_like((weights, rows, hidden), BF16),
            dma((4,)),
        ],
    )[0]
    mix_part = jnp.sum(mix_rows, axis=1).reshape(mix.shape)
    if swap:
        mix_grad = mix_part + across(mix_part)
    else:
        factor_grad = lax.psum_scatter(
            factor_grad.astype(BF16), "seq", scatter_dimension=2, tiled=True
        ).astype(F32)
        mix_grad = lax.psum(mix_part, "seq")
    gate_grad = (jnp.sum(inner, axis=1) * gate * (1.0 - gate)).reshape(selection.shape)
    token_grad = sum_rows(pieces, placed, returned)
    return token_grad, factor_grad[None], mix_grad, gate_grad


def solution(mesh):
    return jax.shard_map(
        shards,
        mesh=mesh,
        in_specs=(
            P(("seq", "exp"), None),
            P(("seq", "exp"), None),
            P("exp", None, None, "seq", None),
            P("exp", None, None, None, None),
            P("exp", "seq", None),
            P("exp", "seq", None),
        ),
        out_specs=(
            P(("seq", "exp"), None),
            P("exp", None, None, "seq", None),
            P("exp", None, None, None, None),
            P("exp", "seq", None),
        ),
        check_vma=False,
    )
```

```python
import functools

import jax
import jax.numpy as jnp
from jax import lax
from jax.experimental import pallas as pl
from jax.experimental.pallas import tpu as pltpu
from jax.sharding import PartitionSpec as P

SELECTED = 64
NPHM = 4
VMEM_LIMIT = 63 * 1024 * 1024
F32 = jnp.float32
BF16 = jnp.bfloat16


def iota(shape, dim):
    return lax.broadcasted_iota(jnp.int32, shape, dim)


def dot(left, right):
    return jnp.dot(left, right, preferred_element_type=F32)


def dot_tn(left, right):
    return lax.dot_general(left, right, (((0,), (0,)), ((), ())), preferred_element_type=F32)


def dot_nt(left, right):
    return lax.dot_general(left, right, (((1,), (1,)), ((), ())), preferred_element_type=F32)


HBM = pl.BlockSpec(memory_space=pltpu.HBM)
VMEM = pl.BlockSpec(memory_space=pltpu.VMEM)
SMEM = pl.BlockSpec(memory_space=pltpu.SMEM)


def call(body, outs, ins, name, flops, scratch=()):
    moved = sum(x.size * x.dtype.itemsize for x, _ in list(ins) + list(outs))
    return pl.pallas_call(
        body,
        out_shape=[x for x, _ in outs],
        in_specs=[place for _, place in ins],
        out_specs=[place for _, place in outs],
        scratch_shapes=list(scratch),
        compiler_params=pltpu.CompilerParams(vmem_limit_bytes=VMEM_LIMIT),
        cost_estimate=pl.CostEstimate(flops=flops, bytes_accessed=moved, transcendentals=0),
        name=name,
    )(*[x for x, _ in ins])


def begin(source, target, sem):
    copy = pltpu.make_async_copy(source, target, sem)
    copy.start()
    return copy


def shaped(shape, dtype):
    return jax.ShapeDtypeStruct(shape, dtype)


def scratch_like(shape, dtype):
    return pltpu.VMEM(shape, dtype)


def chunks_of(part):
    chunk = min(part, 512)
    return [slice(c * chunk, (c + 1) * chunk) for c in range(part // chunk)]


def start_all(pairs, sems):
    return [begin(source, target, sems.at[n]) for n, (source, target) in enumerate(pairs)]


INFO = 16
DIGIT = 6


def spread_columns(me, source, chosen, half, direct, name):
    own_rows, width = source.shape
    part = width // half
    tall = own_rows + (INFO if chosen else 0)

    def body(me_ref, source_ref, *refs):
        chosen_refs, outs = refs[: len(chosen)], refs[len(chosen) : -4]
        held_ref, info_ref, in_sem, out_sem = refs[-4:]
        load = begin(source_ref, held_ref, in_sem)
        if chosen:
            digits = []
            for ref in chosen_refs:
                row = jnp.concatenate([ref[b : b + 1, :] for b in range(ref.shape[0])], axis=1)
                digits += [lax.shift_right_logical(row, DIGIT), row & ((1 << DIGIT) - 1)]
            info = jnp.concatenate(digits, axis=1).astype(F32)
            info_ref[...] = jnp.broadcast_to(info, info_ref.shape).astype(BF16)
        low = me_ref[0] & (half - 1)
        load.wait()
        copies = []
        for k in range(half):
            share = low ^ k if direct else k
            at = held_ref.at[:, pl.ds(pl.multiple_of(share * part, part), part)]
            out, first = (outs[k], 0) if direct else (outs[0], k * tall)
            copies.append(begin(at, out.at[pl.ds(first, own_rows)], out_sem.at[0, k]))
            if chosen:
                at = out.at[pl.ds(first + own_rows, INFO)]
                copies.append(begin(info_ref, at, out_sem.at[1, k]))
        wait_all(copies)

    if direct:
        outs = [(shaped((tall, part), BF16), HBM)] * half
    else:
        outs = [(shaped((half * tall, part), BF16), HBM)]
    scratch = [
        scratch_like((own_rows, width), BF16),
        scratch_like((INFO, part), BF16),
        pltpu.SemaphoreType.DMA,
        pltpu.SemaphoreType.DMA((2, half)),
    ]
    ins = [(me, SMEM), (source, HBM)] + [(x, VMEM) for x in chosen]
    return call(body, outs, ins, name, 0, scratch)


def cut_factors(factors, first):
    cuts = (slice(0, first), slice(first, factors.shape[0]))

    def body(factors_ref, *refs):
        outs, (held_ref, sems) = refs[:2], refs[2:]
        loads = [
            begin(factors_ref.at[at], held_ref.at[at], sems.at[0, n]) for n, at in enumerate(cuts)
        ]
        copies = []
        for n, at in enumerate(cuts):
            loads[n].wait()
            copies.append(begin(held_ref.at[at], outs[n], sems.at[1, n]))
        wait_all(copies)

    outs = [
        (shaped((at.stop - at.start,) + factors.shape[1:], BF16), HBM) for at in cuts
    ]
    scratch = [scratch_like(factors.shape, BF16), pltpu.SemaphoreType.DMA((2, 2))]
    return call(body, outs, [(factors, HBM)], "cut_factors", 0, scratch)


def mark_rows(target_ref, first, count, picks, block, block_at, chosen_ref):
    total = chosen_ref.shape[1]
    same = iota((picks, total), 0) + block_at * picks == iota((picks, total), 1)
    for e in range(count):
        wanted = chosen_ref[first + e : first + e + 1, :]
        column = jnp.sum(jnp.where(same, wanted, 0), axis=1, keepdims=True)
        target_ref[e * picks : (e + 1) * picks] = (column == iota((picks, block), 1)).astype(BF16)


def mark_all(me, half, own_rows, chosen):
    peers, total = chosen.shape
    picks, block = total * half // peers, half * own_rows
    batch = min(peers, 8)

    def body(me_ref, chosen_ref, out_ref, mark_ref, sems):
        block_at = lax.shift_right_logical(me_ref[0], half.bit_length() - 1)
        copies = []
        for n in range(peers // batch):
            if n > 1:
                copies[n - 2].wait()
            slot = mark_ref.at[n % 2]
            mark_rows(slot, n * batch, batch, picks, block, block_at, chosen_ref)
            at = out_ref.at[n * batch * picks : (n + 1) * batch * picks]
            copies.append(begin(slot, at, sems.at[n]))
        wait_all(copies[-2:])

    return call(
        body,
        [(shaped((peers * picks, block), BF16), HBM)],
        [(me, SMEM), (chosen, VMEM)],
        "mark_rows",
        1 << 20,
        [scratch_like((2, batch * picks, block), BF16), pltpu.SemaphoreType.DMA((peers // batch,))],
    )[0]


def pick_rows(me, half, own_rows, peers, total, shares, chosen, marks, after, name):
    picks, block = total * half // peers, half * own_rows
    part = shares[0].shape[1]
    tall = sum(x.shape[0] for x in shares) // half
    batch = min(peers, 8)
    told = [] if chosen is None else [(chosen, VMEM)]
    told = told if marks is None else [(marks, HBM)]

    def body(me_ref, *refs):
        told_refs, refs = refs[: len(told)], refs[len(told) + len(after) :]
        parts, refs = refs[: len(shares)], refs[len(shares) :]
        out_ref, refs = refs[0], refs[1:]
        if not told:
            chosen_ref, refs = refs[0], refs[1:]
        elif marks is None:
            chosen_ref = told_refs[0]
        rows_ref, mark_ref, sent_ref, info_ref, in_sem, mark_sem, out_sem = refs
        low = me_ref[0] & (half - 1)
        block_at = lax.shift_right_logical(me_ref[0], half.bit_length() - 1)
        infos, loads, marks_in = [], [], []
        if not told:
            for k in range(half):
                at = parts[k].at[own_rows : own_rows + INFO]
                infos.append(begin(at, info_ref.at[k], in_sem.at[1, k]))
        for k in range(half):
            place = low ^ k if len(parts) > 1 else k
            share, first = (parts[k], 0) if len(parts) > 1 else (parts[0], k * tall)
            target = rows_ref.at[pl.ds(pl.multiple_of(place * own_rows, own_rows), own_rows)]
            loads.append(begin(share.at[first : first + own_rows], target, in_sem.at[0, k]))
        if marks is not None:
            for n in range(peers // batch):
                at = slice(n * batch * picks, (n + 1) * batch * picks)
                marks_in.append(begin(told_refs[0].at[at], mark_ref.at[at], mark_sem.at[n]))
        for k, copy in enumerate(infos):
            copy.wait()
            info = info_ref[k].astype(F32)[0:1, :].astype(jnp.int32)
            for n in range(2):
                high = info[:, 2 * n * total : (2 * n + 1) * total]
                rest = info[:, (2 * n + 1) * total : (2 * n + 2) * total]
                expert = (low ^ k) + (block_at ^ n) * half
                chosen_ref[pl.ds(expert, 1), :] = high * (1 << DIGIT) + rest
        stores = []
        for n in range(peers // batch):
            at = slice(n * batch * picks, (n + 1) * batch * picks)
            if marks is None:
                mark_rows(mark_ref.at[at], n * batch, batch, picks, block, block_at, chosen_ref)
            else:
                marks_in[n].wait()
            if n == 0:
                wait_all(loads)
            sent_ref[at] = dot(mark_ref[at], rows_ref[...]).astype(BF16)
            stores.append(begin(sent_ref.at[at], out_ref.at[at], out_sem.at[n]))
        wait_all(stores)

    outs = [(shaped((peers * picks, part), BF16), HBM)]
    if not told:
        outs.append((shaped((peers, total), jnp.int32), VMEM))
    return call(
        body,
        outs,
        [(me, SMEM)] + told + [(x, HBM) for x in list(after) + list(shares)],
        name,
        2 * peers * picks * block * part,
        [
            scratch_like((block, part), BF16),
            scratch_like((peers * picks, block), BF16),
            scratch_like((peers * picks, part), BF16),
            scratch_like((half, INFO, part), BF16),
            pltpu.SemaphoreType.DMA((2, half)),
            pltpu.SemaphoreType.DMA((peers // batch,)),
            pltpu.SemaphoreType.DMA((peers // batch,)),
        ],
    )


def slot_body(cap, pieces, own_rows, block_len, chosen_ref, slot_ref):
    rows = slot_ref.shape[1]
    position = jnp.concatenate(
        [chosen_ref[b : b + 1, :] + b * block_len for b in range(chosen_ref.shape[0])], axis=1
    )
    owner = lax.shift_right_logical(position, own_rows.bit_length() - 1)
    peers = chosen_ref.shape[0] * block_len // own_rows
    peer = iota((peers, rows), 0)
    count = jnp.sum((peer == owner).astype(F32), axis=1, keepdims=True)
    earlier = jnp.sum(jnp.where(peer < owner, count, 0.0), axis=0, keepdims=True).astype(jnp.int32)
    slot_ref[...] = owner * (cap * pieces) + iota((1, rows), 1) - earlier


def place_rows(cap, pieces, own_rows, me, half, chosen):
    peers, total = chosen.shape
    picks = total * half // peers
    group = cap * pieces

    def body(me_ref, chosen_ref, out_ref, pick_ref):
        low = me_ref[0] & (half - 1)
        block_at = lax.shift_right_logical(me_ref[0], half.bit_length() - 1)
        lane = iota((peers, total), 1) - block_at * picks
        here = (lane >= 0) & (lane < picks)
        local = jnp.where(here, chosen_ref[...] - low * own_rows, own_rows)
        before = jnp.sum((local < 0).astype(F32), axis=1, keepdims=True).astype(jnp.int32)
        ranks = lane - before
        owned = jnp.where((local >= 0) & (local < own_rows), local + 1, 0)
        place = iota((group, total), 0)
        for e in range(peers):
            rank, mine = ranks[e : e + 1], owned[e : e + 1]
            column = jnp.zeros((group, 1), jnp.int32)
            for j in range(pieces):
                hit = jnp.where((place == rank + j * cap) & (rank >= 0) & (rank < cap), mine, 0)
                row = jnp.sum(hit, axis=1, keepdims=True)
                column = column + jnp.where(row > 0, row + j * own_rows, 0)
            pick_ref[e * group : (e + 1) * group] = (
                column == iota((group, pieces * own_rows), 1) + 1
            ).astype(F32)
        out_ref[...] = jnp.transpose(pick_ref[...]).astype(BF16)

    return call(
        body,
        [(shaped((pieces * own_rows, peers * group), BF16), VMEM)],
        [(me, SMEM), (chosen, VMEM)],
        "place_rows",
        1 << 20,
        [scratch_like((peers * group, pieces * own_rows), F32)],
    )[0]


def sum_rows(pieces, placed, returned):
    slots, part = returned.shape
    own_rows = placed.shape[0] // pieces
    columns = chunks_of(part)

    def body(placed_hbm, returned_ref, out_ref, place_ref, got_ref, sum_ref, in_sem, out_sem):
        first = begin(placed_hbm, place_ref, in_sem.at[len(columns)])
        loads = [
            begin(returned_ref.at[:, at], got_ref.at[:, at], in_sem.at[n])
            for n, at in enumerate(columns)
        ]
        first.wait()
        stores = []
        for n, at in enumerate(columns):
            loads[n].wait()
            summed = dot(place_ref[...], got_ref[:, at]).astype(BF16)
            for j in range(pieces):
                wide = slice(j * part + at.start, j * part + at.stop)
                sum_ref[:, wide] = summed[j * own_rows : (j + 1) * own_rows]
                stores.append(
                    begin(sum_ref.at[:, wide], out_ref.at[:, wide], out_sem.at[n, j])
                )
        wait_all(stores)

    return call(
        body,
        [(shaped((own_rows, part * pieces), BF16), HBM)],
        [(placed, HBM), (returned, HBM)],
        "sum_rows",
        2 * slots * pieces * own_rows * part,
        [
            scratch_like(placed.shape, BF16),
            scratch_like((slots, part), BF16),
            scratch_like((own_rows, part * pieces), BF16),
            pltpu.SemaphoreType.DMA((len(columns) + 1,)),
            pltpu.SemaphoreType.DMA((len(columns), pieces)),
        ],
    )[0]


def load_factor(order_ref, parts, m, target, sems):
    copies = []
    sides = [parts[0].at[m]]
    if len(parts) > 1:
        first = parts[1].shape[0]
        sides.append(parts[1].at[m] if m < first else parts[2].at[m - first])
    for n, side in enumerate(sides):
        count, rows, cols = side.shape
        place = order_ref[0] ^ n if len(parts) > 1 else 0
        start = pl.multiple_of(place * rows, rows)
        for i in range(count):
            at = target.at[pl.ds(start, rows), i * cols : (i + 1) * cols]
            copies.append(begin(side.at[i], at, sems.at[n, i]))
    return copies


def wait_all(copies):
    for copy in copies:
        copy.wait()


def place_matrix(cap, pieces, slots, slot):
    wide = jnp.concatenate([slot + j * cap for j in range(pieces)], axis=1)
    return (iota((slots, wide.shape[1]), 0) == wide).astype(BF16)


def load_rows(got_hbm, x_ref, sems):
    rows, depth = x_ref.shape[0] // NPHM, x_ref.shape[1]
    part = got_hbm.shape[1]
    shares = NPHM * depth // part
    picks = got_hbm.shape[0] * part // (NPHM * depth) // (rows // SELECTED)
    copies = []
    for n in range(got_hbm.shape[0] // picks):
        block, share = divmod(n, shares)
        a, start = share * part // depth, share * part % depth
        first = a * rows + block * picks
        at = x_ref.at[first : first + picks, start : start + part]
        copies.append(begin(got_hbm.at[n * picks : (n + 1) * picks], at, sems.at[n]))
    return copies


def store_parts(order_ref, source_ref, outs, sems):
    copies = []
    for n, out in enumerate(outs):
        size = out.shape[1]
        start = pl.multiple_of((order_ref[0] ^ n) * size if len(outs) > 1 else 0, size)
        copies.append(begin(source_ref.at[:, pl.ds(start, size)], out, sems.at[n]))
    return copies


STRIP = 64


def mix_in(mix_ref, m, y_ref, emit):
    rows, cols = y_ref.shape[0] // NPHM, y_ref.shape[1] // NPHM

    def strip(n, carry):
        start = pl.multiple_of(n * STRIP, STRIP)
        total = [jnp.zeros((STRIP, cols), F32)] * NPHM
        for a in range(NPHM):
            for i in range(NPHM):
                block = y_ref[pl.ds(a * rows + start, STRIP), i * cols : (i + 1) * cols]
                for b in range(NPHM):
                    total[b] = total[b] + mix_ref[m * 64 + i * 16 + a * 4 + b] * block
        emit(start, total)
        return carry

    lax.fori_loop(0, rows // STRIP, strip, 0)


def mix_out(mix_ref, m, d_ref, z_ref):
    rows, cols = d_ref.shape[0], d_ref.shape[1] // NPHM

    def strip(n, carry):
        start = pl.multiple_of(n * STRIP, STRIP)
        blocks = [
            d_ref[pl.ds(start, STRIP), b * cols : (b + 1) * cols].astype(F32) for b in range(NPHM)
        ]
        for a in range(NPHM):
            for i in range(NPHM):
                total = mix_ref[m * 64 + i * 16 + a * 4] * blocks[0]
                for b in range(1, NPHM):
                    total = total + mix_ref[m * 64 + i * 16 + a * 4 + b] * blocks[b]
                z_ref[pl.ds(a * rows + start, STRIP), i * cols : (i + 1) * cols] = total.astype(
                    z_ref.dtype
                )
        return carry

    lax.fori_loop(0, rows // STRIP, strip, 0)


def forward_body(
    sides, order_ref, mix_ref, got_hbm, *refs
):
    held = 2 if sides > 1 else 1
    parts, refs = refs[:held], refs[held:]
    x_outs, refs = refs[:sides], refs[sides:]
    yg_hbm, yu_hbm, act_hbm, slope_hbm, hid_hbm = refs[:5]
    side_ref, x_ref, yg_ref, yu_ref, pre_ref, act_ref, slope_ref, hid_ref = refs[5:13]
    got_sem, side_sem, out_sem = refs[13:]
    loads = load_rows(got_hbm, x_ref, got_sem)
    sides_in = [
        load_factor(order_ref, parts, m, side_ref.at[m], side_sem.at[m]) for m in range(2)
    ]
    wait_all(loads)
    stores = store_parts(order_ref, x_ref, x_outs, out_sem)
    wait_all(sides_in[0])
    yg_ref[...] = dot(x_ref[...], side_ref[0])
    stores.append(begin(yg_ref, yg_hbm, out_sem.at[2]))
    wait_all(sides_in[1])
    yu_ref[...] = dot(x_ref[...], side_ref[1])
    stores.append(begin(yu_ref, yu_hbm, out_sem.at[3]))
    cols = yg_ref.shape[1] // NPHM

    def keep(start, total):
        for b in range(NPHM):
            pre_ref[pl.ds(start, STRIP), b * cols : (b + 1) * cols] = total[b]

    def finish(start, total):
        for b in range(NPHM):
            at = (pl.ds(start, STRIP), slice(b * cols, (b + 1) * cols))
            gate = pre_ref[at]
            sig = jax.nn.sigmoid(gate)
            act = gate * sig
            act_ref[at] = act
            slope_ref[at] = total[b] * (sig + act * (1.0 - sig))
            hid_ref[at] = act * total[b]

    mix_in(mix_ref, 0, yg_ref, keep)
    mix_in(mix_ref, 1, yu_ref, finish)
    stores.append(begin(act_ref, act_hbm, out_sem.at[4]))
    stores.append(begin(slope_ref, slope_hbm, out_sem.at[5]))
    stores.append(begin(hid_ref, hid_hbm, out_sem.at[6]))
    wait_all(stores)


def backward_body(
    cap, pieces, sides, after, order_ref, mix_ref, slot_ref, score_ref, got_hbm, act_hbm, slope_hbm, hid_hbm,
    *refs,
):
    held = 3 if sides > 1 else 1
    parts, refs = refs[:held], refs[held + after :]
    back_hbm, x_outs, refs = refs[0], refs[1 : 1 + sides], refs[1 + sides :]
    y_hbm, d_hbm, inner_ref = refs[:3]
    (
        side_ref, x_ref, y_ref, d_ref, act_ref, slope_ref, hid_ref, zg_ref, zu_ref, grad_ref,
        back_ref, gate_ref, got_sem, side_sem, in_sem, out_sem,
    ) = refs[3:]
    loads = load_rows(got_hbm, x_ref, got_sem)
    down_in = load_factor(order_ref, parts, 2, side_ref.at[2], side_sem.at[2])
    flat_in = [
        begin(source, target, in_sem.at[n])
        for n, (source, target) in enumerate(
            ((act_hbm, act_ref), (slope_hbm, slope_ref), (hid_hbm, hid_ref))
        )
    ]
    sides_in = [
        load_factor(order_ref, parts, m, side_ref.at[m], side_sem.at[m]) for m in range(2)
    ]
    score = jnp.concatenate([score_ref[b : b + 1, :] for b in range(score_ref.shape[0])], axis=1)
    rows = score.shape[1]
    same = iota((rows, rows), 0) == iota((rows, rows), 1)
    score = jnp.sum(jnp.where(same, score.astype(F32), 0.0), axis=1, keepdims=True)
    gate_ref[...] = jnp.broadcast_to(jax.nn.sigmoid(score / 64.0), gate_ref.shape)
    wait_all(loads)
    stores = store_parts(order_ref, x_ref, x_outs, out_sem)
    wait_all(down_in)
    y_ref[...] = dot(x_ref[...], side_ref[2])
    stores.append(begin(y_ref, y_hbm, out_sem.at[2]))
    cols = y_ref.shape[1] // NPHM
    wait_all(flat_in)

    def finish(start, total):
        gate = gate_ref[pl.ds(start, STRIP), :]
        inner = jnp.zeros((STRIP, cols), F32)
        for b in range(NPHM):
            at = (pl.ds(start, STRIP), slice(b * cols, (b + 1) * cols))
            hidden = hid_ref[at]
            inner = inner + hidden * total[b]
            hidden_grad = gate * total[b]
            d_ref[(0,) + at] = (hidden_grad * slope_ref[at]).astype(BF16)
            d_ref[(1,) + at] = (hidden_grad * act_ref[at]).astype(BF16)
            d_ref[(2,) + at] = (hidden * gate).astype(BF16)
        inner_ref[pl.ds(start, STRIP), :] = inner

    mix_in(mix_ref, 2, y_ref, finish)
    stores.append(begin(d_ref, d_hbm, out_sem.at[3]))
    mix_out(mix_ref, 0, d_ref.at[0], zg_ref)
    mix_out(mix_ref, 1, d_ref.at[1], zu_ref)
    wait_all(sides_in[0])
    wait_all(sides_in[1])
    grad = dot_nt(zg_ref[...], side_ref[0]) + dot_nt(zu_ref[...], side_ref[1])
    grad_ref[...] = grad.astype(BF16)
    place = place_matrix(cap, pieces, back_ref.shape[0], slot_ref[...])
    part = back_ref.shape[1]
    rows, depth = x_ref.shape[0] // NPHM, x_ref.shape[1]
    for n, at in enumerate(chunks_of(part)):
        blocks = []
        for j in range(pieces):
            column = j * part + at.start
            a, start = column // depth, column % depth
            blocks.append(
                grad_ref[a * rows : (a + 1) * rows, start : start + at.stop - at.start]
            )
        back_ref[:, at] = dot(place, jnp.concatenate(blocks, axis=0)).astype(BF16)
        stores.append(begin(back_ref.at[:, at], back_hbm.at[:, at], out_sem.at[4 + n]))
    wait_all(stores)


def factor_body(count_groups, mix_ref, *refs):
    rows_in, refs = refs[: 3 * count_groups], refs[3 * count_groups :]
    out_hbm, x_ref, g_ref, d_ref, z_ref, sum_ref, in_sem, out_sem = refs
    loads = []
    for n in range(count_groups):
        for k, target in enumerate((x_ref, g_ref, d_ref)):
            loads.append(begin(rows_in[3 * n + k], target.at[n], in_sem.at[n, k]))
    stores = []
    cols = out_hbm.shape[3]
    wait_all(loads)
    for m in (2, 0, 1):
        for n in range(count_groups):
            mix_out(mix_ref, m, d_ref.at[n, m], z_ref.at[n])
        left = g_ref if m == 2 else x_ref
        sum_ref[m] = sum(dot_tn(left[n], z_ref[n]) for n in range(count_groups))
        for i in range(NPHM):
            at = sum_ref.at[m, :, i * cols : (i + 1) * cols]
            stores.append(begin(at, out_hbm.at[m, i], out_sem.at[m, i]))
    wait_all(stores)


def mix_grad_body(yg_hbm, yu_hbm, yd_hbm, d_hbm, out_ref, y_ref, d_ref, sems):
    loads = [begin(d_hbm, d_ref, sems.at[3])]
    for m, source in enumerate((yg_hbm, yu_hbm, yd_hbm)):
        loads.append(begin(source, y_ref.at[m], sems.at[m]))
    wait_all(loads)
    rows, cols = d_ref.shape[1], d_ref.shape[2] // NPHM
    for m in range(3):
        for a in range(NPHM):
            for i in range(NPHM):
                block = y_ref[m, a * rows : (a + 1) * rows, i * cols : (i + 1) * cols]
                for b in range(NPHM):
                    at = m * 64 + i * 16 + a * 4 + b
                    other = d_ref[m, :, b * cols : (b + 1) * cols].astype(F32)
                    out_ref[at : at + 1, :] = jnp.sum(block * other, axis=0, keepdims=True)


def shards(tokens, cotangent, factors, mix, selection, scores):
    peers = lax.axis_size("exp")
    groups = lax.axis_size("seq")
    own_rows, width = tokens.shape
    _, weights, count, depth_own, cols = factors.shape
    depth = depth_own * groups
    hidden = count * cols
    cap = 3 * own_rows // (2 * peers)
    pieces = 1
    while (cap * pieces) % 8:
        pieces *= 2
    slots = peers * cap * pieces
    part = width // pieces
    steps = len(chunks_of(part))
    block_len = peers * SELECTED
    rows = selection.shape[1] * selection.shape[2]
    stacked = count * rows
    swap = groups == 2
    pair = [(0, 1), (1, 0)]
    mixing = mix.reshape(-1)
    dma = pltpu.SemaphoreType.DMA

    def across(array):
        return lax.ppermute(array, "seq", pair)

    half = peers // selection.shape[1]
    direct = half == 8
    me = lax.axis_index("exp").astype(jnp.int32).reshape(1)
    group = lax.axis_index("seq").astype(jnp.int32).reshape(1)
    halves = [list(range(h, h + half)) for h in range(0, peers, half)]
    near = [k for k in range(1, half) if k >= 4] + [k for k in range(1, half) if k < 4]

    if swap:
        cuts = [across(x) for x in cut_factors(factors[0], 2)]
        factor_parts = [factors[0]] + cuts
        sides = 2
    else:
        cuts = []
        factor_parts = [lax.all_gather(factors, "seq", axis=3, tiled=True)[0]]
        sides = 1
    sides_in = [(x, HBM) for x in factor_parts]
    def to_peers(array):
        array = array.reshape(peers, -1, array.shape[1])
        array = lax.all_to_all(array, "exp", split_axis=0, concat_axis=0, tiled=True)
        return array.reshape(-1, array.shape[2])

    def collect(shares):
        if direct:
            moved = {
                k: lax.ppermute(shares[k], "exp", [(n, n ^ k) for n in range(peers)]) for k in near
            }
            return [shares[0]] + [moved[k] for k in range(1, half)]
        array = shares[0].reshape(half, -1, shares[0].shape[1])
        array = lax.all_to_all(
            array, "exp", split_axis=0, concat_axis=0, axis_index_groups=halves, tiled=True
        )
        return [array.reshape(shares[0].shape)]

    spread = functools.partial(spread_columns, me, half=half, direct=direct)
    pick = functools.partial(pick_rows, me, half, own_rows, peers, rows)
    if direct:
        mirror = lax.ppermute(selection, "exp", [(n, n ^ half) for n in range(peers)])
        told = [selection[0], mirror[0]]
        shares = collect(spread(tokens, told, name="spread_tokens"))
        picked, chosen = pick(shares, None, None, [], "pick_tokens")
        marks = mark_all(me, half, own_rows, chosen)
    else:
        told = jnp.broadcast_to(selection.reshape(1, rows), (peers, rows))
        chosen = lax.all_to_all(told, "exp", split_axis=0, concat_axis=0, tiled=True)
        shares = collect(spread(tokens, [], name="spread_tokens"))
        (picked,), marks = pick(shares, chosen, None, [], "pick_tokens"), None
    got_rows = to_peers(picked)
    shares = collect(spread(cotangent, [], name="spread_cotangent"))
    got_grads = to_peers(pick(shares, chosen, marks, cuts[:1], "pick_cotangent")[0])
    placed = place_rows(cap, pieces, own_rows, me, half, chosen)
    slot = call(
        functools.partial(slot_body, cap, pieces, own_rows, block_len),
        [(shaped((1, rows), jnp.int32), VMEM)],
        [(selection[0], VMEM)],
        "row_slots",
        1 << 16,
    )[0]

    gate = jax.nn.sigmoid(scores[0].reshape(-1).astype(F32) / 64.0)

    product = 2 * stacked * depth * hidden
    split = [(shaped((stacked, depth // sides), BF16), HBM)] * sides
    mixed = (shaped((stacked, hidden), F32), HBM)
    flat = (shaped((rows, hidden), F32), HBM)
    back_scratch = scratch_like((slots, part), BF16)
    pieces_in = got_rows.shape[0] // SELECTED
    stack_scratch = scratch_like((stacked, depth), BF16)
    mixed_scratch = scratch_like((stacked, hidden), F32)
    low_scratch = scratch_like((stacked, hidden), BF16)
    flat_scratch = scratch_like((rows, hidden), F32)
    outs = call(
        functools.partial(forward_body, sides),
        split + [mixed, mixed, flat, flat, flat],
        [(group, SMEM), (mixing, SMEM), (got_rows, HBM)] + sides_in[:2],
        "forward",
        2 * product,
        [scratch_like((2, depth, hidden), BF16), stack_scratch, mixed_scratch, mixed_scratch]
        + [flat_scratch] * 4
        + [dma((pieces_in,)), dma((2, sides, count)), dma((7,))],
    )
    x_parts, (y_gate, y_up, act, slope, hid) = outs[:sides], outs[sides:]
    x_rows = [x_parts[0]] + [across(x) for x in x_parts[1:]]
    after = x_rows[1:]
    outs = call(
        functools.partial(backward_body, cap, pieces, sides, len(after)),
        [(shaped((slots, part), BF16), HBM)]
        + split
        + [mixed, (shaped((weights, rows, hidden), BF16), HBM), (shaped((rows, cols), F32), VMEM)],
        [(group, SMEM), (mixing, SMEM), (slot, VMEM), (scores[0], VMEM), (got_grads, HBM)]
        + [(x, HBM) for x in (act, slope, hid)]
        + sides_in
        + [(x, HBM) for x in after],
        "backward",
        3 * product,
        [scratch_like((weights, depth, hidden), BF16), stack_scratch, mixed_scratch]
        + [scratch_like((weights, rows, hidden), BF16)]
        + [flat_scratch] * 3
        + [low_scratch] * 2
        + [stack_scratch, back_scratch, scratch_like((rows, cols), F32)]
        + [dma((pieces_in,)), dma((weights, sides, count)), dma((3,)), dma((4 + steps,))],
    )
    back, g_parts, (y_down, d_own, inner) = outs[0], outs[1 : 1 + sides], outs[1 + sides :]
    returned = to_peers(back)

    d_rows = [d_own] + [across(d_own) for _ in x_parts[1:]]
    g_rows = [g_parts[0]] + [across(x) for x in g_parts[1:]]
    depth_here = depth // sides
    factor_grad = call(
        functools.partial(factor_body, sides),
        [(shaped((weights, count, depth_here, cols), F32), HBM)],
        [(mixing, SMEM)]
        + [(x, HBM) for n in range(sides) for x in (x_rows[n], g_rows[n], d_rows[n])],
        "factor_grad",
        3 * product,
        [scratch_like((sides, stacked, depth_here), BF16)] * 2
        + [
            scratch_like((sides, weights, rows, hidden), BF16),
            scratch_like((sides, stacked, hidden), BF16),
            scratch_like((weights, depth_here, hidden), F32),
            dma((sides, 3)),
            dma((weights, count)),
        ],
    )[0]
    mix_rows = call(
        mix_grad_body,
        [(shaped((mixing.size, cols), F32), VMEM)],
        [(x, HBM) for x in (y_gate, y_up, y_down, d_own)],
        "mix_partials",
        weights * 64 * 2 * rows * cols,
        [
            scratch_like((weights, stacked, hidden), F32),
            scratch_like((weights, rows, hidden), BF16),
            dma((4,)),
        ],
    )[0]
    mix_part = jnp.sum(mix_rows, axis=1).reshape(mix.shape)
    if swap:
        mix_grad = mix_part + across(mix_part)
    else:
        factor_grad = lax.psum_scatter(
            factor_grad.astype(BF16), "seq", scatter_dimension=2, tiled=True
        ).astype(F32)
        mix_grad = lax.psum(mix_part, "seq")
    gate_grad = (jnp.sum(inner, axis=1) * gate * (1.0 - gate)).reshape(selection.shape)
    token_grad = sum_rows(pieces, placed, returned)
    return token_grad, factor_grad[None], mix_grad, gate_grad


def solution(mesh):
    return jax.shard_map(
        shards,
        mesh=mesh,
        in_specs=(
            P(("seq", "exp"), None),
            P(("seq", "exp"), None),
            P("exp", None, None, "seq", None),
            P("exp", None, None, None, None),
            P("exp", "seq", None),
            P("exp", "seq", None),
        ),
        out_specs=(
            P(("seq", "exp"), None),
            P("exp", None, None, "seq", None),
            P("exp", None, None, None, None),
            P("exp", "seq", None),
        ),
        check_vma=False,
    )
```

```python
import functools

import jax
import jax.numpy as jnp
from jax import lax
from jax.experimental import pallas as pl
from jax.experimental.pallas import tpu as pltpu
from jax.sharding import PartitionSpec as P

SELECTED = 64
NPHM = 4
VMEM_LIMIT = 63 * 1024 * 1024
F32 = jnp.float32
BF16 = jnp.bfloat16


def iota(shape, dim):
    return lax.broadcasted_iota(jnp.int32, shape, dim)


def dot(left, right):
    return jnp.dot(left, right, preferred_element_type=F32)


def dot_tn(left, right):
    return lax.dot_general(left, right, (((0,), (0,)), ((), ())), preferred_element_type=F32)


def dot_nt(left, right):
    return lax.dot_general(left, right, (((1,), (1,)), ((), ())), preferred_element_type=F32)


HBM = pl.BlockSpec(memory_space=pltpu.HBM)
VMEM = pl.BlockSpec(memory_space=pltpu.VMEM)
SMEM = pl.BlockSpec(memory_space=pltpu.SMEM)


def call(body, outs, ins, name, flops, scratch=()):
    moved = sum(x.size * x.dtype.itemsize for x, _ in list(ins) + list(outs))
    return pl.pallas_call(
        body,
        out_shape=[x for x, _ in outs],
        in_specs=[place for _, place in ins],
        out_specs=[place for _, place in outs],
        scratch_shapes=list(scratch),
        compiler_params=pltpu.CompilerParams(vmem_limit_bytes=VMEM_LIMIT),
        cost_estimate=pl.CostEstimate(flops=flops, bytes_accessed=moved, transcendentals=0),
        name=name,
    )(*[x for x, _ in ins])


def begin(source, target, sem):
    copy = pltpu.make_async_copy(source, target, sem)
    copy.start()
    return copy


def shaped(shape, dtype):
    return jax.ShapeDtypeStruct(shape, dtype)


def scratch_like(shape, dtype):
    return pltpu.VMEM(shape, dtype)


def chunks_of(part):
    chunk = min(part, 512)
    return [slice(c * chunk, (c + 1) * chunk) for c in range(part // chunk)]


def index_body(cap, pieces, own_rows, block_len, chosen_ref, told_ref, slot_ref):
    peers, rows = told_ref.shape[0] // 2, slot_ref.shape[1]
    blocks = [chosen_ref[b : b + 1, :] for b in range(chosen_ref.shape[0])]
    position = jnp.concatenate([x + b * block_len for b, x in enumerate(blocks)], axis=1)
    owner = lax.shift_right_logical(position, own_rows.bit_length() - 1)
    local = position & (own_rows - 1)
    peer = iota((peers, rows), 0)
    mine = (peer == owner).astype(F32)
    count = jnp.sum(mine, axis=1, keepdims=True)
    earlier = jnp.sum(jnp.where(peer < owner, count, 0.0), axis=0, keepdims=True).astype(jnp.int32)
    rank = iota((1, rows), 1) - earlier
    slot_ref[...] = owner * (cap * pieces) + rank
    lane = iota((rows, rows), 0)
    hit = jnp.zeros((rows, rows), F32)
    for j in range(pieces):
        hit = hit + (lane == rank + j * cap).astype(F32)
    twice = iota((2 * peers, rows), 0)
    marked = jnp.where(twice == 2 * owner, local + 1, 0).astype(F32)
    asked = dot_nt(marked.astype(BF16), hit.astype(BF16)).astype(jnp.int32)
    told_ref[...] = jnp.where((twice & 1) == 1, jnp.concatenate(blocks, axis=1), asked)


def pick_matrix(cap, pieces, own_rows, requested):
    told, lanes = requested.shape
    peers = told // 2
    group = cap * pieces
    slots = peers * group
    peer = 2 * iota((peers, group, told), 0).reshape(slots, told)
    spread = dot(
        (peer == iota((slots, told), 1)).astype(BF16), requested.astype(F32).astype(BF16)
    )
    place = iota((peers, group, lanes), 1).reshape(slots, lanes)
    row = jnp.sum(
        jnp.where(place == iota((slots, lanes), 1), spread, 0.0), axis=1, keepdims=True
    ).astype(jnp.int32)
    piece = iota((peers, group, 1), 1).reshape(slots, 1)
    shift = jnp.zeros((slots, 1), jnp.int32)
    for j in range(1, pieces):
        shift = shift + jnp.where(piece >= j * cap, own_rows, 0)
    target = jnp.where(row > 0, row - 1 + shift, -1)
    return (target == iota((slots, pieces * own_rows), 1)).astype(BF16)


def pick_slots(cap, pieces, requested, source, after, name):
    own_rows, width = source.shape
    part = width // pieces
    slots = requested.shape[0] // 2 * cap * pieces
    columns = chunks_of(part)

    def body(requested_hbm, source_ref, *refs):
        out_ref, requested_ref, rows_ref, sent_ref, in_sem, out_sem = refs[len(after) :]
        asked = begin(requested_hbm, requested_ref, in_sem.at[len(columns), 0])
        loads = []
        for n, at in enumerate(columns):
            for j in range(pieces):
                wide = slice(j * part + at.start, j * part + at.stop)
                target = rows_ref.at[j * own_rows : (j + 1) * own_rows, at]
                loads.append(begin(source_ref.at[:, wide], target, in_sem.at[n, j]))
        asked.wait()
        pick = pick_matrix(cap, pieces, own_rows, requested_ref[...])
        stores = []
        for n, at in enumerate(columns):
            for load in loads[n * pieces : (n + 1) * pieces]:
                load.wait()
            sent_ref[:, at] = dot(pick, rows_ref[:, at]).astype(BF16)
            stores.append(begin(sent_ref.at[:, at], out_ref.at[:, at], out_sem.at[n]))
        for store in stores:
            store.wait()

    return call(
        body,
        [(shaped((slots, part), BF16), HBM)],
        [(requested, HBM), (source, HBM)] + [(x, HBM) for x in after],
        name,
        2 * slots * pieces * own_rows * part,
        [
            scratch_like(requested.shape, jnp.int32),
            scratch_like((pieces * own_rows, part), BF16),
            scratch_like((slots, part), BF16),
            pltpu.SemaphoreType.DMA((len(columns) + 1, pieces)),
            pltpu.SemaphoreType.DMA((len(columns),)),
        ],
    )[0]


def spread_columns(me, sources, half, direct, name):
    own_rows, width = sources[0].shape
    count = len(sources)
    part = width // half
    tall = count * own_rows

    def body(me_ref, *refs):
        ins, outs = refs[:count], refs[count : -3]
        held_ref, in_sem, out_sem = refs[-3:]
        loads = [begin(ref, held_ref.at[n], in_sem.at[n]) for n, ref in enumerate(ins)]
        low = me_ref[0] & (half - 1)
        copies = []
        for n, load in enumerate(loads):
            load.wait()
            for k in range(half):
                share = low ^ k if direct else k
                at = held_ref.at[n, :, pl.ds(pl.multiple_of(share * part, part), part)]
                out, first = (outs[k], 0) if direct else (outs[0], k * tall)
                rows = pl.ds(first + n * own_rows, own_rows)
                copies.append(begin(at, out.at[rows], out_sem.at[n, k]))
        wait_all(copies)

    if direct:
        outs = [(shaped((tall, part), BF16), HBM)] * half
    else:
        outs = [(shaped((half * tall, part), BF16), HBM)]
    scratch = [
        scratch_like((count, own_rows, width), BF16),
        pltpu.SemaphoreType.DMA((count,)),
        pltpu.SemaphoreType.DMA((count, half)),
    ]
    return call(body, outs, [(me, SMEM)] + [(x, HBM) for x in sources], name, 0, scratch)


def cut_factors(factors, first):
    cuts = (slice(0, first), slice(first, factors.shape[0]))

    def body(factors_ref, *refs):
        outs, (held_ref, sems) = refs[:2], refs[2:]
        loads = [
            begin(factors_ref.at[at], held_ref.at[at], sems.at[0, n]) for n, at in enumerate(cuts)
        ]
        copies = []
        for n, at in enumerate(cuts):
            loads[n].wait()
            copies.append(begin(held_ref.at[at], outs[n], sems.at[1, n]))
        wait_all(copies)

    outs = [
        (shaped((at.stop - at.start,) + factors.shape[1:], BF16), HBM) for at in cuts
    ]
    scratch = [scratch_like(factors.shape, BF16), pltpu.SemaphoreType.DMA((2, 2))]
    return call(body, outs, [(factors, HBM)], "cut_factors", 0, scratch)


def pick_rows(me, half, own_rows, which, chosen, shares, after, name):
    peers, total = chosen.shape[0] // 2, chosen.shape[1]
    picks = total * half // peers
    part = shares[0].shape[1]
    block = half * own_rows
    tall = sum(x.shape[0] for x in shares) // half
    batch = min(peers, 8)

    def body(me_ref, chosen_ref, *refs):
        refs = refs[len(after) :]
        parts, (out_ref, rows_ref, pick_ref, sent_ref, in_sem, out_sem) = (
            refs[: len(shares)],
            refs[len(shares) :],
        )
        loads = []
        for k in range(half):
            place = (me_ref[0] & (half - 1)) ^ k if len(parts) > 1 else k
            share, first = (parts[k], 0) if len(parts) > 1 else (parts[0], k * tall)
            first += which * own_rows
            target = rows_ref.at[pl.ds(pl.multiple_of(place * own_rows, own_rows), own_rows)]
            loads.append(begin(share.at[first : first + own_rows], target, in_sem.at[k]))
        block_at = lax.shift_right_logical(me_ref[0], half.bit_length() - 1)
        same = iota((picks, total), 0) + block_at * picks == iota((picks, total), 1)
        stores = []
        for first in range(0, peers, batch):
            for e in range(batch):
                wanted = chosen_ref[2 * (first + e) + 1 : 2 * (first + e) + 2, :]
                column = jnp.sum(jnp.where(same, wanted, 0), axis=1, keepdims=True)
                pick_ref[first // batch % 2, e * picks : (e + 1) * picks] = (
                    column == iota((picks, block), 1)
                ).astype(BF16)
            if first == 0:
                wait_all(loads)
            at = slice(first * picks, (first + batch) * picks)
            sent_ref[at] = dot(pick_ref[first // batch % 2], rows_ref[...]).astype(BF16)
            stores.append(begin(sent_ref.at[at], out_ref.at[at], out_sem.at[first // batch]))
        wait_all(stores)

    return call(
        body,
        [(shaped((peers * picks, part), BF16), HBM)],
        [(me, SMEM), (chosen, VMEM)] + [(x, HBM) for x in list(after) + list(shares)],
        name,
        2 * peers * picks * block * part,
        [
            scratch_like((block, part), BF16),
            scratch_like((2, batch * picks, block), BF16),
            scratch_like((peers * picks, part), BF16),
            pltpu.SemaphoreType.DMA((half,)),
            pltpu.SemaphoreType.DMA((peers // batch,)),
        ],
    )[0]


def place_rows(cap, pieces, own_rows, me, half, chosen):
    peers, total = chosen.shape[0] // 2, chosen.shape[1]
    picks = total * half // peers
    group = cap * pieces

    def body(me_ref, chosen_ref, out_ref, pick_ref):
        low = me_ref[0] & (half - 1)
        block_at = lax.shift_right_logical(me_ref[0], half.bit_length() - 1)
        lane = iota((2 * peers, total), 1) - block_at * picks
        here = (lane >= 0) & (lane < picks)
        local = jnp.where(here, chosen_ref[...] - low * own_rows, own_rows)
        before = jnp.sum((local < 0).astype(F32), axis=1, keepdims=True).astype(jnp.int32)
        ranks = lane - before
        owned = jnp.where((local >= 0) & (local < own_rows), local + 1, 0)
        place = iota((group, total), 0)
        for e in range(peers):
            at = slice(2 * e + 1, 2 * e + 2)
            rank, mine = ranks[at], owned[at]
            column = jnp.zeros((group, 1), jnp.int32)
            for j in range(pieces):
                hit = jnp.where((place == rank + j * cap) & (rank >= 0) & (rank < cap), mine, 0)
                row = jnp.sum(hit, axis=1, keepdims=True)
                column = column + jnp.where(row > 0, row + j * own_rows, 0)
            pick_ref[e * group : (e + 1) * group] = (
                column == iota((group, pieces * own_rows), 1) + 1
            ).astype(F32)
        out_ref[...] = jnp.transpose(pick_ref[...]).astype(BF16)

    return call(
        body,
        [(shaped((pieces * own_rows, peers * group), BF16), VMEM)],
        [(me, SMEM), (chosen, VMEM)],
        "place_rows",
        1 << 20,
        [scratch_like((peers * group, pieces * own_rows), F32)],
    )[0]


def sum_rows(pieces, placed, returned):
    slots, part = returned.shape
    own_rows = placed.shape[0] // pieces
    columns = chunks_of(part)

    def body(placed_hbm, returned_ref, out_ref, place_ref, got_ref, sum_ref, in_sem, out_sem):
        first = begin(placed_hbm, place_ref, in_sem.at[len(columns)])
        loads = [
            begin(returned_ref.at[:, at], got_ref.at[:, at], in_sem.at[n])
            for n, at in enumerate(columns)
        ]
        first.wait()
        stores = []
        for n, at in enumerate(columns):
            loads[n].wait()
            summed = dot(place_ref[...], got_ref[:, at]).astype(BF16)
            for j in range(pieces):
                wide = slice(j * part + at.start, j * part + at.stop)
                sum_ref[:, wide] = summed[j * own_rows : (j + 1) * own_rows]
                stores.append(
                    begin(sum_ref.at[:, wide], out_ref.at[:, wide], out_sem.at[n, j])
                )
        wait_all(stores)

    return call(
        body,
        [(shaped((own_rows, part * pieces), BF16), HBM)],
        [(placed, HBM), (returned, HBM)],
        "sum_rows",
        2 * slots * pieces * own_rows * part,
        [
            scratch_like(placed.shape, BF16),
            scratch_like((slots, part), BF16),
            scratch_like((own_rows, part * pieces), BF16),
            pltpu.SemaphoreType.DMA((len(columns) + 1,)),
            pltpu.SemaphoreType.DMA((len(columns), pieces)),
        ],
    )[0]


def load_factor(order_ref, parts, m, target, sems):
    copies = []
    sides = [parts[0].at[m]]
    if len(parts) > 1:
        first = parts[1].shape[0]
        sides.append(parts[1].at[m] if m < first else parts[2].at[m - first])
    for n, side in enumerate(sides):
        count, rows, cols = side.shape
        place = order_ref[0] ^ n if len(parts) > 1 else 0
        start = pl.multiple_of(place * rows, rows)
        for i in range(count):
            at = target.at[pl.ds(start, rows), i * cols : (i + 1) * cols]
            copies.append(begin(side.at[i], at, sems.at[n, i]))
    return copies


def wait_all(copies):
    for copy in copies:
        copy.wait()


def place_matrix(cap, pieces, slots, slot):
    wide = jnp.concatenate([slot + j * cap for j in range(pieces)], axis=1)
    return (iota((slots, wide.shape[1]), 0) == wide).astype(BF16)


def load_rows(got_hbm, x_ref, sems):
    rows, depth = x_ref.shape[0] // NPHM, x_ref.shape[1]
    part = got_hbm.shape[1]
    shares = NPHM * depth // part
    picks = got_hbm.shape[0] * part // (NPHM * depth) // (rows // SELECTED)
    copies = []
    for n in range(got_hbm.shape[0] // picks):
        block, share = divmod(n, shares)
        a, start = share * part // depth, share * part % depth
        first = (block * NPHM + a) * picks
        at = x_ref.at[first : first + picks, start : start + part]
        copies.append(begin(got_hbm.at[n * picks : (n + 1) * picks], at, sems.at[n]))
    return copies


def load_slots(got_hbm, got_ref, sems):
    return [
        begin(got_hbm.at[:, at], got_ref.at[:, at], sems.at[n])
        for n, at in enumerate(chunks_of(got_ref.shape[1]))
    ]


def stack_rows(pieces, place, loads, got_ref, out_ref):
    part = got_ref.shape[1]
    rows, depth = out_ref.shape[0] // NPHM, out_ref.shape[1]
    for load, at in zip(loads, chunks_of(part)):
        load.wait()
        block = dot_tn(place, got_ref[:, at]).astype(BF16)
        for j in range(pieces):
            column = j * part + at.start
            a, start = column // depth, column % depth
            for n in range(rows // STRIP):
                first = (n * NPHM + a) * STRIP
                out_ref[first : first + STRIP, start : start + at.stop - at.start] = block[
                    j * rows + n * STRIP : j * rows + (n + 1) * STRIP
                ]


def store_parts(order_ref, source_ref, outs, sems):
    copies = []
    for n, out in enumerate(outs):
        size = out.shape[1]
        start = pl.multiple_of((order_ref[0] ^ n) * size if len(outs) > 1 else 0, size)
        copies.append(begin(source_ref.at[:, pl.ds(start, size)], out, sems.at[n]))
    return copies


STRIP = SELECTED


def rows_of(n, a):
    return slice((n * NPHM + a) * STRIP, (n * NPHM + a + 1) * STRIP)


def mix_in(mix_ref, m, y_ref, n):
    cols = y_ref.shape[1] // NPHM
    total = [jnp.zeros((STRIP, cols), F32)] * NPHM
    for a in range(NPHM):
        for i in range(NPHM):
            block = y_ref[rows_of(n, a), i * cols : (i + 1) * cols]
            for b in range(NPHM):
                total[b] = total[b] + mix_ref[m * 64 + i * 16 + a * 4 + b] * block
    return total


def mix_out(mix_ref, m, blocks, n, z_ref, offset=0):
    cols = blocks[0].shape[1]
    for a in range(NPHM):
        for i in range(NPHM):
            total = mix_ref[m * 64 + i * 16 + a * 4] * blocks[0]
            for b in range(1, NPHM):
                total = total + mix_ref[m * 64 + i * 16 + a * 4 + b] * blocks[b]
            z_ref[rows_of(n, a), offset + i * cols : offset + (i + 1) * cols] = total.astype(
                z_ref.dtype
            )


def blocks_of(d_ref, n):
    cols = d_ref.shape[1] // NPHM
    at = slice(n * STRIP, (n + 1) * STRIP)
    return [d_ref[at, b * cols : (b + 1) * cols].astype(F32) for b in range(NPHM)]


def forward_body(
    cap, pieces, sides, order_ref, mix_ref, slot_ref, got_hbm, *refs
):
    held = 2 if sides > 1 else 1
    parts, refs = refs[:held], refs[held:]
    x_outs, refs = refs[:sides], refs[sides:]
    yg_hbm, yu_hbm, act_hbm, slope_hbm, hid_hbm = refs[:5]
    got_ref, side_ref, x_ref, yg_ref, yu_ref, act_ref, slope_ref, hid_ref = refs[5:13]
    got_sem, side_sem, out_sem = refs[13:]
    loads = load_slots(got_hbm, got_ref, got_sem)
    sides_in = [
        load_factor(order_ref, parts, m, side_ref.at[m], side_sem.at[m]) for m in range(2)
    ]
    place = place_matrix(cap, pieces, got_ref.shape[0], slot_ref[...])
    stack_rows(pieces, place, loads, got_ref, x_ref)
    stores = store_parts(order_ref, x_ref, x_outs, out_sem)
    wait_all(sides_in[0])
    yg_ref[...] = dot(x_ref[...], side_ref[0])
    stores.append(begin(yg_ref, yg_hbm, out_sem.at[2]))
    wait_all(sides_in[1])
    yu_ref[...] = dot(x_ref[...], side_ref[1])
    stores.append(begin(yu_ref, yu_hbm, out_sem.at[3]))
    cols = yg_ref.shape[1] // NPHM
    for n in range(yg_ref.shape[0] // (NPHM * STRIP)):
        gates = mix_in(mix_ref, 0, yg_ref, n)
        ups = mix_in(mix_ref, 1, yu_ref, n)
        for b in range(NPHM):
            at = (slice(n * STRIP, (n + 1) * STRIP), slice(b * cols, (b + 1) * cols))
            sig = jax.nn.sigmoid(gates[b])
            act = gates[b] * sig
            act_ref[at] = act
            slope_ref[at] = ups[b] * (sig + act * (1.0 - sig))
            hid_ref[at] = act * ups[b]
    stores.append(begin(act_ref, act_hbm, out_sem.at[4]))
    stores.append(begin(slope_ref, slope_hbm, out_sem.at[5]))
    stores.append(begin(hid_ref, hid_hbm, out_sem.at[6]))
    wait_all(stores)


def backward_body(
    cap, pieces, sides, after, order_ref, mix_ref, slot_hbm, score_hbm, got_hbm, act_hbm, slope_hbm, hid_hbm,
    *refs,
):
    held = 3 if sides > 1 else 1
    parts, refs = refs[:held], refs[held + after :]
    back_hbm, x_outs, refs = refs[0], refs[1 : 1 + sides], refs[1 + sides :]
    y_hbm, d_hbm, inner_hbm = refs[:3]
    (
        down_ref, side_ref, x_ref, y_ref, d_ref, act_ref, slope_ref, hid_ref, z_ref, grad_ref,
        back_ref, inner_ref, slot_ref, score_ref, got_sem, side_sem, in_sem, out_sem,
    ) = refs[3:]
    loads = load_rows(got_hbm, x_ref, got_sem)
    down_in = load_factor(order_ref, parts, 2, down_ref, side_sem.at[2])
    small_in = [
        begin(source, target, in_sem.at[n])
        for n, (source, target) in enumerate(((score_hbm, score_ref), (slot_hbm, slot_ref)))
    ]
    flat_in = [
        begin(source, target, in_sem.at[2 + n])
        for n, (source, target) in enumerate(
            ((act_hbm, act_ref), (slope_hbm, slope_ref), (hid_hbm, hid_ref))
        )
    ]
    hidden = d_ref.shape[2]
    sides_in = []
    for m in range(2):
        target = side_ref.at[:, m * hidden : (m + 1) * hidden]
        sides_in += load_factor(order_ref, parts, m, target, side_sem.at[m])
    wait_all(small_in)
    score = jnp.concatenate([score_ref[b : b + 1, :] for b in range(score_ref.shape[0])], axis=1)
    rows = score.shape[1]
    same = iota((rows, rows), 0) == iota((rows, rows), 1)
    score = jnp.sum(jnp.where(same, score.astype(F32), 0.0), axis=1, keepdims=True)
    cols = hidden // NPHM
    gates = jnp.broadcast_to(jax.nn.sigmoid(score / 64.0), (rows, cols))
    place = place_matrix(cap, pieces, back_ref.shape[0], slot_ref[...])
    strips = rows // STRIP
    tall = NPHM * STRIP
    wait_all(loads)
    stores = store_parts(order_ref, x_ref, x_outs, out_sem)
    wait_all(down_in)
    for n in range(strips):
        y_ref[n * tall : (n + 1) * tall] = dot(x_ref[n * tall : (n + 1) * tall], down_ref[...])
    stores.append(begin(y_ref, y_hbm, out_sem.at[2]))
    wait_all(flat_in)
    wait_all(sides_in)
    for n in range(strips):
        down = mix_in(mix_ref, 2, y_ref, n)
        strip = slice(n * STRIP, (n + 1) * STRIP)
        gate = gates[strip]
        inner = jnp.zeros((STRIP, cols), F32)
        d_gate, d_up = [], []
        for b in range(NPHM):
            at = (strip, slice(b * cols, (b + 1) * cols))
            inner = inner + hid_ref[at] * down[b]
            hidden_grad = gate * down[b]
            d_gate.append(hidden_grad * slope_ref[at])
            d_up.append(hidden_grad * act_ref[at])
            d_ref[(0,) + at] = d_gate[b].astype(BF16)
            d_ref[(1,) + at] = d_up[b].astype(BF16)
            d_ref[(2,) + at] = (hid_ref[at] * gate).astype(BF16)
        inner_ref[strip] = inner
        mix_out(mix_ref, 0, d_gate, n, z_ref)
        mix_out(mix_ref, 1, d_up, n, z_ref, hidden)
        at = slice(n * tall, (n + 1) * tall)
        grad_ref[at] = dot_nt(z_ref[at], side_ref[...]).astype(BF16)
    stores.append(begin(d_ref, d_hbm, out_sem.at[3]))
    stores.append(begin(inner_ref, inner_hbm, out_sem.at[4]))
    part, depth = back_ref.shape[1], x_ref.shape[1]
    for k, at in enumerate(chunks_of(part)):
        blocks = []
        for j in range(pieces):
            column = j * part + at.start
            a, start = column // depth, column % depth
            wide = slice(start, start + at.stop - at.start)
            blocks += [grad_ref[rows_of(n, a), wide] for n in range(strips)]
        back_ref[:, at] = dot(place, jnp.concatenate(blocks, axis=0)).astype(BF16)
        stores.append(begin(back_ref.at[:, at], back_hbm.at[:, at], out_sem.at[5 + k]))
    wait_all(stores)


def factor_body(count_groups, mix_ref, *refs):
    rows_in, refs = refs[: 3 * count_groups], refs[3 * count_groups :]
    out_hbm, x_ref, g_ref, d_ref, z_ref, sum_ref, in_sem, out_sem = refs
    loads = []
    for n in range(count_groups):
        for k, target in enumerate((x_ref, g_ref, d_ref)):
            loads.append(begin(rows_in[3 * n + k], target.at[n], in_sem.at[n, k]))
    stores = []
    cols = out_hbm.shape[3]
    wait_all(loads)
    for m in (2, 0, 1):
        for n in range(count_groups):
            for strip in range(d_ref.shape[2] // STRIP):
                blocks = blocks_of(d_ref.at[n, m], strip)
                mix_out(mix_ref, m, blocks, strip, z_ref.at[n])
        left = g_ref if m == 2 else x_ref
        sum_ref[m] = sum(dot_tn(left[n], z_ref[n]) for n in range(count_groups))
        for i in range(NPHM):
            at = sum_ref.at[m, :, i * cols : (i + 1) * cols]
            stores.append(begin(at, out_hbm.at[m, i], out_sem.at[m, i]))
    wait_all(stores)


def mix_grad_body(yg_hbm, yu_hbm, yd_hbm, d_hbm, out_ref, y_ref, d_ref, sems):
    loads = [begin(d_hbm, d_ref, sems.at[3])]
    for m, source in enumerate((yg_hbm, yu_hbm, yd_hbm)):
        loads.append(begin(source, y_ref.at[m], sems.at[m]))
    wait_all(loads)
    rows, cols = d_ref.shape[1], d_ref.shape[2] // NPHM
    for m in range(3):
        for a in range(NPHM):
            for i in range(NPHM):
                at = slice(i * cols, (i + 1) * cols)
                strips = range(rows // STRIP)
                block = jnp.concatenate([y_ref[m, rows_of(n, a), at] for n in strips], axis=0)
                for b in range(NPHM):
                    at = m * 64 + i * 16 + a * 4 + b
                    other = d_ref[m, :, b * cols : (b + 1) * cols].astype(F32)
                    out_ref[at : at + 1, :] = jnp.sum(block * other, axis=0, keepdims=True)


def shards(tokens, cotangent, factors, mix, selection, scores):
    peers = lax.axis_size("exp")
    groups = lax.axis_size("seq")
    own_rows, width = tokens.shape
    _, weights, count, depth_own, cols = factors.shape
    depth = depth_own * groups
    hidden = count * cols
    cap = 3 * own_rows // (2 * peers)
    pieces = 1
    while (cap * pieces) % 8:
        pieces *= 2
    slots = peers * cap * pieces
    part = width // pieces
    steps = len(chunks_of(part))
    block_len = peers * SELECTED
    rows = selection.shape[1] * selection.shape[2]
    stacked = count * rows
    swap = groups == 2
    pair = [(0, 1), (1, 0)]
    mixing = mix.reshape(-1)
    dma = pltpu.SemaphoreType.DMA

    def across(array):
        return lax.ppermute(array, "seq", pair)

    half = peers // selection.shape[1]
    direct = half == 8
    me = lax.axis_index("exp").astype(jnp.int32).reshape(1)
    group = lax.axis_index("seq").astype(jnp.int32).reshape(1)
    halves = [list(range(h, h + half)) for h in range(0, peers, half)]
    near = [k for k in range(1, half) if k >= 4] + [k for k in range(1, half) if k < 4]

    if swap:
        cuts = [across(x) for x in cut_factors(factors[0], 2)]
        factor_parts = [factors[0]] + cuts
        sides = 2
    else:
        cuts = []
        factor_parts = [lax.all_gather(factors, "seq", axis=3, tiled=True)[0]]
        sides = 1
    sides_in = [(x, HBM) for x in factor_parts]
    told, slot = call(
        functools.partial(index_body, cap, pieces, own_rows, block_len),
        [(shaped((2 * peers, rows), jnp.int32), VMEM), (shaped((1, rows), jnp.int32), VMEM)],
        [(selection[0], VMEM)],
        "wanted_rows",
        1 << 20,
    )
    chosen = lax.all_to_all(told, "exp", split_axis=0, concat_axis=0, tiled=True)

    def to_peers(array):
        array = array.reshape(peers, -1, array.shape[1])
        array = lax.all_to_all(array, "exp", split_axis=0, concat_axis=0, tiled=True)
        return array.reshape(-1, array.shape[2])

    def collect(shares):
        if direct:
            moved = {
                k: lax.ppermute(shares[k], "exp", [(n, n ^ k) for n in range(peers)]) for k in near
            }
            return [shares[0]] + [moved[k] for k in range(1, half)]
        array = shares[0].reshape(half, -1, shares[0].shape[1])
        array = lax.all_to_all(
            array, "exp", split_axis=0, concat_axis=0, axis_index_groups=halves, tiled=True
        )
        return [array.reshape(shares[0].shape)]

    shares = collect(spread_columns(me, [cotangent], half, direct, "spread_cotangent"))
    early = shares[4:] if direct else []
    got_rows = to_peers(pick_slots(cap, pieces, chosen, tokens, early, "pick_tokens"))
    picked = pick_rows(me, half, own_rows, 0, chosen, shares, cuts[:1], "pick_cotangent")
    got_grads = to_peers(picked)
    placed = place_rows(cap, pieces, own_rows, me, half, chosen)
    gate = jax.nn.sigmoid(scores[0].reshape(-1).astype(F32) / 64.0)

    product = 2 * stacked * depth * hidden
    split = [(shaped((stacked, depth // sides), BF16), HBM)] * sides
    mixed = (shaped((stacked, hidden), F32), HBM)
    flat = (shaped((rows, hidden), F32), HBM)
    back_scratch = scratch_like((slots, part), BF16)
    pieces_in = got_grads.shape[0] // SELECTED
    stack_scratch = scratch_like((stacked, depth), BF16)
    mixed_scratch = scratch_like((stacked, hidden), F32)
    low_scratch = scratch_like((stacked, hidden), BF16)
    flat_scratch = scratch_like((rows, hidden), F32)
    outs = call(
        functools.partial(forward_body, cap, pieces, sides),
        split + [mixed, mixed, flat, flat, flat],
        [(group, SMEM), (mixing, SMEM), (slot, VMEM), (got_rows, HBM)] + sides_in[:2],
        "forward",
        2 * product,
        [back_scratch, scratch_like((2, depth, hidden), BF16), stack_scratch, mixed_scratch, mixed_scratch]
        + [flat_scratch] * 3
        + [dma((steps,)), dma((2, sides, count)), dma((7,))],
    )
    x_parts, (y_gate, y_up, act, slope, hid) = outs[:sides], outs[sides:]
    x_rows = [x_parts[0]] + [across(x) for x in x_parts[1:]]
    after = x_rows[1:]
    outs = call(
        functools.partial(backward_body, cap, pieces, sides, len(after)),
        [(shaped((slots, part), BF16), HBM)]
        + split
        + [mixed, (shaped((weights, rows, hidden), BF16), HBM), (shaped((rows, cols), F32), HBM)],
        [(group, SMEM), (mixing, SMEM), (slot, HBM), (scores[0], HBM), (got_grads, HBM)]
        + [(x, HBM) for x in (act, slope, hid)]
        + sides_in
        + [(x, HBM) for x in after],
        "backward",
        3 * product,
        [scratch_like((depth, hidden), BF16), scratch_like((depth, 2 * hidden), BF16)]
        + [stack_scratch, mixed_scratch, scratch_like((weights, rows, hidden), BF16)]
        + [flat_scratch] * 3
        + [scratch_like((stacked, 2 * hidden), BF16), stack_scratch, back_scratch]
        + [scratch_like((rows, cols), F32), scratch_like(slot.shape, jnp.int32)]
        + [scratch_like(scores.shape[1:], jnp.int32)]
        + [dma((pieces_in,)), dma((weights, sides, count)), dma((5,)), dma((5 + steps,))],
    )
    back, g_parts, (y_down, d_own, inner) = outs[0], outs[1 : 1 + sides], outs[1 + sides :]
    returned = to_peers(back)

    d_rows = [d_own] + [across(d_own) for _ in x_parts[1:]]
    g_rows = [g_parts[0]] + [across(x) for x in g_parts[1:]]
    depth_here = depth // sides
    factor_grad = call(
        functools.partial(factor_body, sides),
        [(shaped((weights, count, depth_here, cols), F32), HBM)],
        [(mixing, SMEM)]
        + [(x, HBM) for n in range(sides) for x in (x_rows[n], g_rows[n], d_rows[n])],
        "factor_grad",
        3 * product,
        [scratch_like((sides, stacked, depth_here), BF16)] * 2
        + [
            scratch_like((sides, weights, rows, hidden), BF16),
            scratch_like((sides, stacked, hidden), BF16),
            scratch_like((weights, depth_here, hidden), F32),
            dma((sides, 3)),
            dma((weights, count)),
        ],
    )[0]
    mix_rows = call(
        mix_grad_body,
        [(shaped((mixing.size, cols), F32), VMEM)],
        [(x, HBM) for x in (y_gate, y_up, y_down, d_own)],
        "mix_partials",
        weights * 64 * 2 * rows * cols,
        [
            scratch_like((weights, stacked, hidden), F32),
            scratch_like((weights, rows, hidden), BF16),
            dma((4,)),
        ],
    )[0]
    mix_part = jnp.sum(mix_rows, axis=1).reshape(mix.shape)
    if swap:
        mix_grad = mix_part + across(mix_part)
    else:
        factor_grad = lax.psum_scatter(
            factor_grad.astype(BF16), "seq", scatter_dimension=2, tiled=True
        ).astype(F32)
        mix_grad = lax.psum(mix_part, "seq")
    gate_grad = (jnp.sum(inner, axis=1) * gate * (1.0 - gate)).reshape(selection.shape)
    token_grad = sum_rows(pieces, placed, returned)
    return token_grad, factor_grad[None], mix_grad, gate_grad


def solution(mesh):
    return jax.shard_map(
        shards,
        mesh=mesh,
        in_specs=(
            P(("seq", "exp"), None),
            P(("seq", "exp"), None),
            P("exp", None, None, "seq", None),
            P("exp", None, None, None, None),
            P("exp", "seq", None),
            P("exp", "seq", None),
        ),
        out_specs=(
            P(("seq", "exp"), None),
            P("exp", None, None, "seq", None),
            P("exp", None, None, None, None),
            P("exp", "seq", None),
        ),
        check_vma=False,
    )
```

```python
import functools

import jax
import jax.numpy as jnp
from jax import lax
from jax.experimental import pallas as pl
from jax.experimental.pallas import tpu as pltpu
from jax.sharding import PartitionSpec as P

SELECTED = 64
NPHM = 4
VMEM_LIMIT = 63 * 1024 * 1024
F32 = jnp.float32
BF16 = jnp.bfloat16


def iota(shape, dim):
    return lax.broadcasted_iota(jnp.int32, shape, dim)


def dot(left, right):
    return jnp.dot(left, right, preferred_element_type=F32)


def dot_tn(left, right):
    return lax.dot_general(left, right, (((0,), (0,)), ((), ())), preferred_element_type=F32)


def dot_nt(left, right):
    return lax.dot_general(left, right, (((1,), (1,)), ((), ())), preferred_element_type=F32)


HBM = pl.BlockSpec(memory_space=pltpu.HBM)
VMEM = pl.BlockSpec(memory_space=pltpu.VMEM)
SMEM = pl.BlockSpec(memory_space=pltpu.SMEM)


def call(body, outs, ins, name, flops, scratch=()):
    moved = sum(x.size * x.dtype.itemsize for x, _ in list(ins) + list(outs))
    return pl.pallas_call(
        body,
        out_shape=[x for x, _ in outs],
        in_specs=[place for _, place in ins],
        out_specs=[place for _, place in outs],
        scratch_shapes=list(scratch),
        compiler_params=pltpu.CompilerParams(vmem_limit_bytes=VMEM_LIMIT),
        cost_estimate=pl.CostEstimate(flops=flops, bytes_accessed=moved, transcendentals=0),
        name=name,
    )(*[x for x, _ in ins])


def begin(source, target, sem):
    copy = pltpu.make_async_copy(source, target, sem)
    copy.start()
    return copy


def shaped(shape, dtype):
    return jax.ShapeDtypeStruct(shape, dtype)


def scratch_like(shape, dtype):
    return pltpu.VMEM(shape, dtype)


def chunks_of(part):
    chunk = min(part, 512)
    return [slice(c * chunk, (c + 1) * chunk) for c in range(part // chunk)]


def front_body(cap, pieces, own_rows, block_len, half, cross, me_ref, chosen_ref, *refs):
    if cross:
        source_ref, told_ref, slot_ref, cross_ref, held_ref, sems = refs
        width = cross_ref.shape[1]
        plane = lax.shift_right_logical(me_ref[0] & (half - 1), half.bit_length() - 2)
        at = pl.ds(pl.multiple_of((1 - plane) * width, width), width)
        load = begin(source_ref.at[:, at], held_ref, sems.at[0])
    else:
        told_ref, slot_ref = refs
    peers, rows = told_ref.shape[0] // 2, slot_ref.shape[1]
    blocks = [chosen_ref[b : b + 1, :] for b in range(chosen_ref.shape[0])]
    position = jnp.concatenate([x + b * block_len for b, x in enumerate(blocks)], axis=1)
    owner = lax.shift_right_logical(position, own_rows.bit_length() - 1)
    local = position & (own_rows - 1)
    peer = iota((peers, rows), 0)
    mine = (peer == owner).astype(F32)
    count = jnp.sum(mine, axis=1, keepdims=True)
    earlier = jnp.sum(jnp.where(peer < owner, count, 0.0), axis=0, keepdims=True).astype(jnp.int32)
    rank = iota((1, rows), 1) - earlier
    slot_ref[...] = owner * (cap * pieces) + rank
    lane = iota((rows, rows), 0)
    hit = jnp.zeros((rows, rows), F32)
    for j in range(pieces):
        hit = hit + (lane == rank + j * cap).astype(F32)
    twice = iota((2 * peers, rows), 0)
    marked = jnp.where(twice == 2 * owner, local + 1, 0).astype(F32)
    asked = dot_nt(marked.astype(BF16), hit.astype(BF16)).astype(jnp.int32)
    told_ref[...] = jnp.where((twice & 1) == 1, jnp.concatenate(blocks, axis=1), asked)
    if cross:
        load.wait()
        begin(held_ref, cross_ref, sems.at[1]).wait()


def plane_columns(me, source, crossed, half):
    own_rows, width = source.shape
    part, count = width // half, half // 2

    def body(me_ref, source_ref, crossed_ref, *refs):
        outs, (held_ref, in_sem, out_sem) = refs[:count], refs[count:]
        low = me_ref[0] & (half - 1)
        plane = lax.shift_right_logical(low, half.bit_length() - 2)
        wide = count * part
        at = pl.ds(pl.multiple_of(plane * wide, wide), wide)
        loads = [
            begin(source_ref.at[:, at], held_ref.at[0], in_sem.at[0]),
            begin(crossed_ref, held_ref.at[1], in_sem.at[1]),
        ]
        copies = []
        for n, load in enumerate(loads):
            load.wait()
            for k in range(count):
                share = (low & (count - 1)) ^ k
                at = held_ref.at[n, :, pl.ds(pl.multiple_of(share * part, part), part)]
                rows = pl.ds(n * own_rows, own_rows)
                copies.append(begin(at, outs[k].at[rows], out_sem.at[n, k]))
        wait_all(copies)

    return call(
        body,
        [(shaped((2 * own_rows, part), BF16), HBM)] * count,
        [(me, SMEM), (source, HBM), (crossed, HBM)],
        "plane_columns",
        0,
        [
            scratch_like((2, own_rows, count * part), BF16),
            pltpu.SemaphoreType.DMA((2,)),
            pltpu.SemaphoreType.DMA((2, count)),
        ],
    )


def pick_matrix(cap, pieces, own_rows, requested):
    told, lanes = requested.shape
    peers = told // 2
    group = cap * pieces
    slots = peers * group
    peer = 2 * iota((peers, group, told), 0).reshape(slots, told)
    spread = dot(
        (peer == iota((slots, told), 1)).astype(BF16), requested.astype(F32).astype(BF16)
    )
    place = iota((peers, group, lanes), 1).reshape(slots, lanes)
    row = jnp.sum(
        jnp.where(place == iota((slots, lanes), 1), spread, 0.0), axis=1, keepdims=True
    ).astype(jnp.int32)
    piece = iota((peers, group, 1), 1).reshape(slots, 1)
    shift = jnp.zeros((slots, 1), jnp.int32)
    for j in range(1, pieces):
        shift = shift + jnp.where(piece >= j * cap, own_rows, 0)
    target = jnp.where(row > 0, row - 1 + shift, -1)
    return (target == iota((slots, pieces * own_rows), 1)).astype(BF16)


def pick_slots(cap, pieces, requested, source, after, name):
    own_rows, width = source.shape
    part = width // pieces
    slots = requested.shape[0] // 2 * cap * pieces
    columns = chunks_of(part)

    def body(requested_hbm, source_ref, *refs):
        out_ref, requested_ref, rows_ref, sent_ref, in_sem, out_sem = refs[len(after) :]
        asked = begin(requested_hbm, requested_ref, in_sem.at[len(columns), 0])
        loads = []
        for n, at in enumerate(columns):
            for j in range(pieces):
                wide = slice(j * part + at.start, j * part + at.stop)
                target = rows_ref.at[j * own_rows : (j + 1) * own_rows, at]
                loads.append(begin(source_ref.at[:, wide], target, in_sem.at[n, j]))
        asked.wait()
        pick = pick_matrix(cap, pieces, own_rows, requested_ref[...])
        stores = []
        for n, at in enumerate(columns):
            for load in loads[n * pieces : (n + 1) * pieces]:
                load.wait()
            sent_ref[:, at] = dot(pick, rows_ref[:, at]).astype(BF16)
            stores.append(begin(sent_ref.at[:, at], out_ref.at[:, at], out_sem.at[n]))
        for store in stores:
            store.wait()

    return call(
        body,
        [(shaped((slots, part), BF16), HBM)],
        [(requested, HBM), (source, HBM)] + [(x, HBM) for x in after],
        name,
        2 * slots * pieces * own_rows * part,
        [
            scratch_like(requested.shape, jnp.int32),
            scratch_like((pieces * own_rows, part), BF16),
            scratch_like((slots, part), BF16),
            pltpu.SemaphoreType.DMA((len(columns) + 1, pieces)),
            pltpu.SemaphoreType.DMA((len(columns),)),
        ],
    )[0]


def spread_columns(source, half):
    own_rows, width = source.shape
    part = width // half

    def body(source_ref, out_ref, held_ref, in_sem, out_sem):
        begin(source_ref, held_ref, in_sem).wait()
        copies = []
        for k in range(half):
            at = held_ref.at[:, k * part : (k + 1) * part]
            out = out_ref.at[k * own_rows : (k + 1) * own_rows]
            copies.append(begin(at, out, out_sem.at[k]))
        wait_all(copies)

    scratch = [
        scratch_like((own_rows, width), BF16),
        pltpu.SemaphoreType.DMA,
        pltpu.SemaphoreType.DMA((half,)),
    ]
    outs = [(shaped((half * own_rows, part), BF16), HBM)]
    return call(body, outs, [(source, HBM)], "spread_columns", 0, scratch)[0]


def cut_factors(factors, first):
    cuts = (slice(0, first), slice(first, factors.shape[0]))

    def body(factors_ref, *refs):
        outs, (held_ref, sems) = refs[:2], refs[2:]
        loads = [
            begin(factors_ref.at[at], held_ref.at[at], sems.at[0, n]) for n, at in enumerate(cuts)
        ]
        copies = []
        for n, at in enumerate(cuts):
            loads[n].wait()
            copies.append(begin(held_ref.at[at], outs[n], sems.at[1, n]))
        wait_all(copies)

    outs = [
        (shaped((at.stop - at.start,) + factors.shape[1:], BF16), HBM) for at in cuts
    ]
    scratch = [scratch_like(factors.shape, BF16), pltpu.SemaphoreType.DMA((2, 2))]
    return call(body, outs, [(factors, HBM)], "cut_factors", 0, scratch)


def pick_rows(me, half, own_rows, chosen, shares, after, name):
    peers, total = chosen.shape[0] // 2, chosen.shape[1]
    picks = total * half // peers
    part = shares[0].shape[1]
    block = half * own_rows
    batch = min(peers, 8)

    def body(me_ref, chosen_ref, *refs):
        refs = refs[len(after) :]
        parts, (out_ref, rows_ref, pick_ref, sent_ref, in_sem, out_sem) = (
            refs[: len(shares)],
            refs[len(shares) :],
        )
        loads = []
        for k in range(half):
            place = (me_ref[0] & (half - 1)) ^ k if len(parts) > 1 else k
            n, first = (k % len(parts), k // len(parts)) if len(parts) > 1 else (0, k)
            at = parts[n].at[first * own_rows : (first + 1) * own_rows]
            target = rows_ref.at[pl.ds(pl.multiple_of(place * own_rows, own_rows), own_rows)]
            loads.append(begin(at, target, in_sem.at[k]))
        block_at = lax.shift_right_logical(me_ref[0], half.bit_length() - 1)
        same = iota((picks, total), 0) + block_at * picks == iota((picks, total), 1)
        stores = []
        for first in range(0, peers, batch):
            for e in range(batch):
                wanted = chosen_ref[2 * (first + e) + 1 : 2 * (first + e) + 2, :]
                column = jnp.sum(jnp.where(same, wanted, 0), axis=1, keepdims=True)
                pick_ref[first // batch % 2, e * picks : (e + 1) * picks] = (
                    column == iota((picks, block), 1)
                ).astype(BF16)
            if first == 0:
                wait_all(loads)
            at = slice(first * picks, (first + batch) * picks)
            sent_ref[at] = dot(pick_ref[first // batch % 2], rows_ref[...]).astype(BF16)
            stores.append(begin(sent_ref.at[at], out_ref.at[at], out_sem.at[first // batch]))
        wait_all(stores)

    return call(
        body,
        [(shaped((peers * picks, part), BF16), HBM)],
        [(me, SMEM), (chosen, VMEM)] + [(x, HBM) for x in list(after) + list(shares)],
        name,
        2 * peers * picks * block * part,
        [
            scratch_like((block, part), BF16),
            scratch_like((2, batch * picks, block), BF16),
            scratch_like((peers * picks, part), BF16),
            pltpu.SemaphoreType.DMA((half,)),
            pltpu.SemaphoreType.DMA((peers // batch,)),
        ],
    )[0]


def place_rows(cap, pieces, own_rows, me, half, chosen):
    peers, total = chosen.shape[0] // 2, chosen.shape[1]
    picks = total * half // peers
    group = cap * pieces

    def body(me_ref, chosen_ref, out_ref, pick_ref):
        low = me_ref[0] & (half - 1)
        block_at = lax.shift_right_logical(me_ref[0], half.bit_length() - 1)
        lane = iota((2 * peers, total), 1) - block_at * picks
        here = (lane >= 0) & (lane < picks)
        local = jnp.where(here, chosen_ref[...] - low * own_rows, own_rows)
        before = jnp.sum((local < 0).astype(F32), axis=1, keepdims=True).astype(jnp.int32)
        ranks = lane - before
        owned = jnp.where((local >= 0) & (local < own_rows), local + 1, 0)
        place = iota((group, total), 0)
        for e in range(peers):
            at = slice(2 * e + 1, 2 * e + 2)
            rank, mine = ranks[at], owned[at]
            column = jnp.zeros((group, 1), jnp.int32)
            for j in range(pieces):
                hit = jnp.where((place == rank + j * cap) & (rank >= 0) & (rank < cap), mine, 0)
                row = jnp.sum(hit, axis=1, keepdims=True)
                column = column + jnp.where(row > 0, row + j * own_rows, 0)
            pick_ref[e * group : (e + 1) * group] = (
                column == iota((group, pieces * own_rows), 1) + 1
            ).astype(F32)
        out_ref[...] = jnp.transpose(pick_ref[...]).astype(BF16)

    return call(
        body,
        [(shaped((pieces * own_rows, peers * group), BF16), VMEM)],
        [(me, SMEM), (chosen, VMEM)],
        "place_rows",
        1 << 20,
        [scratch_like((peers * group, pieces * own_rows), F32)],
    )[0]


def sum_rows(pieces, placed, returned):
    slots, part = returned.shape
    own_rows = placed.shape[0] // pieces
    columns = chunks_of(part)

    def body(placed_hbm, returned_ref, out_ref, place_ref, got_ref, sum_ref, in_sem, out_sem):
        first = begin(placed_hbm, place_ref, in_sem.at[len(columns)])
        loads = [
            begin(returned_ref.at[:, at], got_ref.at[:, at], in_sem.at[n])
            for n, at in enumerate(columns)
        ]
        first.wait()
        stores = []
        for n, at in enumerate(columns):
            loads[n].wait()
            summed = dot(place_ref[...], got_ref[:, at]).astype(BF16)
            for j in range(pieces):
                wide = slice(j * part + at.start, j * part + at.stop)
                sum_ref[:, wide] = summed[j * own_rows : (j + 1) * own_rows]
                stores.append(
                    begin(sum_ref.at[:, wide], out_ref.at[:, wide], out_sem.at[n, j])
                )
        wait_all(stores)

    return call(
        body,
        [(shaped((own_rows, part * pieces), BF16), HBM)],
        [(placed, HBM), (returned, HBM)],
        "sum_rows",
        2 * slots * pieces * own_rows * part,
        [
            scratch_like(placed.shape, BF16),
            scratch_like((slots, part), BF16),
            scratch_like((own_rows, part * pieces), BF16),
            pltpu.SemaphoreType.DMA((len(columns) + 1,)),
            pltpu.SemaphoreType.DMA((len(columns), pieces)),
        ],
    )[0]


def load_factor(order_ref, parts, m, target, sems):
    copies = []
    sides = [parts[0].at[m]]
    if len(parts) > 1:
        first = parts[1].shape[0]
        sides.append(parts[1].at[m] if m < first else parts[2].at[m - first])
    for n, side in enumerate(sides):
        count, rows, cols = side.shape
        place = order_ref[0] ^ n if len(parts) > 1 else 0
        start = pl.multiple_of(place * rows, rows)
        for i in range(count):
            at = target.at[pl.ds(start, rows), i * cols : (i + 1) * cols]
            copies.append(begin(side.at[i], at, sems.at[n, i]))
    return copies


def wait_all(copies):
    for copy in copies:
        copy.wait()


def place_matrix(cap, pieces, slots, slot):
    wide = jnp.concatenate([slot + j * cap for j in range(pieces)], axis=1)
    return (iota((slots, wide.shape[1]), 0) == wide).astype(BF16)


def load_rows(got_hbm, x_ref, sems):
    rows, depth = x_ref.shape[0] // NPHM, x_ref.shape[1]
    part = got_hbm.shape[1]
    shares = NPHM * depth // part
    picks = got_hbm.shape[0] * part // (NPHM * depth) // (rows // SELECTED)
    copies = []
    for n in range(got_hbm.shape[0] // picks):
        block, share = divmod(n, shares)
        a, start = share * part // depth, share * part % depth
        first = (block * NPHM + a) * picks
        at = x_ref.at[first : first + picks, start : start + part]
        copies.append(begin(got_hbm.at[n * picks : (n + 1) * picks], at, sems.at[n]))
    return copies


def load_slots(got_hbm, got_ref, sems):
    return [
        begin(got_hbm.at[:, at], got_ref.at[:, at], sems.at[n])
        for n, at in enumerate(chunks_of(got_ref.shape[1]))
    ]


def stack_rows(pieces, place, loads, got_ref, out_ref):
    part = got_ref.shape[1]
    rows, depth = out_ref.shape[0] // NPHM, out_ref.shape[1]
    for load, at in zip(loads, chunks_of(part)):
        load.wait()
        block = dot_tn(place, got_ref[:, at]).astype(BF16)
        for j in range(pieces):
            column = j * part + at.start
            a, start = column // depth, column % depth
            for n in range(rows // STRIP):
                first = (n * NPHM + a) * STRIP
                out_ref[first : first + STRIP, start : start + at.stop - at.start] = block[
                    j * rows + n * STRIP : j * rows + (n + 1) * STRIP
                ]


def store_parts(order_ref, source_ref, outs, sems):
    copies = []
    for n, out in enumerate(outs):
        size = out.shape[1]
        start = pl.multiple_of((order_ref[0] ^ n) * size if len(outs) > 1 else 0, size)
        copies.append(begin(source_ref.at[:, pl.ds(start, size)], out, sems.at[n]))
    return copies


STRIP = SELECTED


def rows_of(n, a):
    return slice((n * NPHM + a) * STRIP, (n * NPHM + a + 1) * STRIP)


def mix_in(mix_ref, m, y_ref, n):
    cols = y_ref.shape[1] // NPHM
    total = [jnp.zeros((STRIP, cols), F32)] * NPHM
    for a in range(NPHM):
        for i in range(NPHM):
            block = y_ref[rows_of(n, a), i * cols : (i + 1) * cols]
            for b in range(NPHM):
                total[b] = total[b] + mix_ref[m * 64 + i * 16 + a * 4 + b] * block
    return total


def mix_out(mix_ref, m, blocks, n, z_ref, offset=0):
    cols = blocks[0].shape[1]
    for a in range(NPHM):
        for i in range(NPHM):
            total = mix_ref[m * 64 + i * 16 + a * 4] * blocks[0]
            for b in range(1, NPHM):
                total = total + mix_ref[m * 64 + i * 16 + a * 4 + b] * blocks[b]
            z_ref[rows_of(n, a), offset + i * cols : offset + (i + 1) * cols] = total.astype(
                z_ref.dtype
            )


def blocks_of(d_ref, n):
    cols = d_ref.shape[1] // NPHM
    at = slice(n * STRIP, (n + 1) * STRIP)
    return [d_ref[at, b * cols : (b + 1) * cols].astype(F32) for b in range(NPHM)]


def forward_body(
    cap, pieces, sides, order_ref, mix_ref, slot_ref, got_hbm, *refs
):
    held = 2 if sides > 1 else 1
    parts, refs = refs[:held], refs[held:]
    x_outs, refs = refs[:sides], refs[sides:]
    yg_hbm, yu_hbm, act_hbm, slope_hbm, hid_hbm = refs[:5]
    got_ref, side_ref, x_ref, yg_ref, yu_ref, act_ref, slope_ref, hid_ref = refs[5:13]
    got_sem, side_sem, out_sem = refs[13:]
    loads = load_slots(got_hbm, got_ref, got_sem)
    sides_in = [
        load_factor(order_ref, parts, m, side_ref.at[m], side_sem.at[m]) for m in range(2)
    ]
    place = place_matrix(cap, pieces, got_ref.shape[0], slot_ref[...])
    stack_rows(pieces, place, loads, got_ref, x_ref)
    stores = store_parts(order_ref, x_ref, x_outs, out_sem)
    wait_all(sides_in[0])
    yg_ref[...] = dot(x_ref[...], side_ref[0])
    stores.append(begin(yg_ref, yg_hbm, out_sem.at[2]))
    wait_all(sides_in[1])
    yu_ref[...] = dot(x_ref[...], side_ref[1])
    stores.append(begin(yu_ref, yu_hbm, out_sem.at[3]))
    cols = yg_ref.shape[1] // NPHM
    for n in range(yg_ref.shape[0] // (NPHM * STRIP)):
        gates = mix_in(mix_ref, 0, yg_ref, n)
        ups = mix_in(mix_ref, 1, yu_ref, n)
        for b in range(NPHM):
            at = (slice(n * STRIP, (n + 1) * STRIP), slice(b * cols, (b + 1) * cols))
            sig = jax.nn.sigmoid(gates[b])
            act = gates[b] * sig
            act_ref[at] = act
            slope_ref[at] = ups[b] * (sig + act * (1.0 - sig))
            hid_ref[at] = act * ups[b]
    stores.append(begin(act_ref, act_hbm, out_sem.at[4]))
    stores.append(begin(slope_ref, slope_hbm, out_sem.at[5]))
    stores.append(begin(hid_ref, hid_hbm, out_sem.at[6]))
    wait_all(stores)


def backward_body(
    cap, pieces, sides, after, order_ref, mix_ref, slot_hbm, score_hbm, got_hbm, act_hbm, slope_hbm, hid_hbm,
    *refs,
):
    held = 3 if sides > 1 else 1
    parts, refs = refs[:held], refs[held + after :]
    back_hbm, x_outs, refs = refs[0], refs[1 : 1 + sides], refs[1 + sides :]
    y_hbm, d_hbm, inner_hbm = refs[:3]
    (
        down_ref, side_ref, x_ref, y_ref, d_ref, act_ref, slope_ref, hid_ref, z_ref, grad_ref,
        back_ref, inner_ref, slot_ref, score_ref, got_sem, side_sem, in_sem, out_sem,
    ) = refs[3:]
    loads = load_rows(got_hbm, x_ref, got_sem)
    down_in = load_factor(order_ref, parts, 2, down_ref, side_sem.at[2])
    small_in = [
        begin(source, target, in_sem.at[n])
        for n, (source, target) in enumerate(((score_hbm, score_ref), (slot_hbm, slot_ref)))
    ]
    flat_in = [
        begin(source, target, in_sem.at[2 + n])
        for n, (source, target) in enumerate(
            ((act_hbm, act_ref), (slope_hbm, slope_ref), (hid_hbm, hid_ref))
        )
    ]
    hidden = d_ref.shape[2]
    sides_in = []
    for m in range(2):
        target = side_ref.at[:, m * hidden : (m + 1) * hidden]
        sides_in += load_factor(order_ref, parts, m, target, side_sem.at[m])
    wait_all(small_in)
    score = jnp.concatenate([score_ref[b : b + 1, :] for b in range(score_ref.shape[0])], axis=1)
    rows = score.shape[1]
    same = iota((rows, rows), 0) == iota((rows, rows), 1)
    score = jnp.sum(jnp.where(same, score.astype(F32), 0.0), axis=1, keepdims=True)
    cols = hidden // NPHM
    gates = jnp.broadcast_to(jax.nn.sigmoid(score / 64.0), (rows, cols))
    place = place_matrix(cap, pieces, back_ref.shape[0], slot_ref[...])
    strips = rows // STRIP
    tall = NPHM * STRIP
    wait_all(loads)
    stores = store_parts(order_ref, x_ref, x_outs, out_sem)
    wait_all(down_in)
    for n in range(strips):
        y_ref[n * tall : (n + 1) * tall] = dot(x_ref[n * tall : (n + 1) * tall], down_ref[...])
    stores.append(begin(y_ref, y_hbm, out_sem.at[2]))
    wait_all(flat_in)
    wait_all(sides_in)
    for n in range(strips):
        down = mix_in(mix_ref, 2, y_ref, n)
        strip = slice(n * STRIP, (n + 1) * STRIP)
        gate = gates[strip]
        inner = jnp.zeros((STRIP, cols), F32)
        d_gate, d_up = [], []
        for b in range(NPHM):
            at = (strip, slice(b * cols, (b + 1) * cols))
            inner = inner + hid_ref[at] * down[b]
            hidden_grad = gate * down[b]
            d_gate.append(hidden_grad * slope_ref[at])
            d_up.append(hidden_grad * act_ref[at])
            d_ref[(0,) + at] = d_gate[b].astype(BF16)
            d_ref[(1,) + at] = d_up[b].astype(BF16)
            d_ref[(2,) + at] = (hid_ref[at] * gate).astype(BF16)
        inner_ref[strip] = inner
        mix_out(mix_ref, 0, d_gate, n, z_ref)
        mix_out(mix_ref, 1, d_up, n, z_ref, hidden)
        at = slice(n * tall, (n + 1) * tall)
        grad_ref[at] = dot_nt(z_ref[at], side_ref[...]).astype(BF16)
    stores.append(begin(d_ref, d_hbm, out_sem.at[3]))
    stores.append(begin(inner_ref, inner_hbm, out_sem.at[4]))
    part, depth = back_ref.shape[1], x_ref.shape[1]
    for k, at in enumerate(chunks_of(part)):
        blocks = []
        for j in range(pieces):
            column = j * part + at.start
            a, start = column // depth, column % depth
            wide = slice(start, start + at.stop - at.start)
            blocks += [grad_ref[rows_of(n, a), wide] for n in range(strips)]
        back_ref[:, at] = dot(place, jnp.concatenate(blocks, axis=0)).astype(BF16)
        stores.append(begin(back_ref.at[:, at], back_hbm.at[:, at], out_sem.at[5 + k]))
    wait_all(stores)


def factor_body(count_groups, mix_ref, *refs):
    rows_in, refs = refs[: 3 * count_groups], refs[3 * count_groups :]
    out_hbm, x_ref, g_ref, d_ref, z_ref, sum_ref, in_sem, out_sem = refs
    loads = []
    for n in range(count_groups):
        for k, target in enumerate((x_ref, g_ref, d_ref)):
            loads.append(begin(rows_in[3 * n + k], target.at[n], in_sem.at[n, k]))
    stores = []
    cols = out_hbm.shape[3]
    wait_all(loads)
    for m in (2, 0, 1):
        for n in range(count_groups):
            for strip in range(d_ref.shape[2] // STRIP):
                blocks = blocks_of(d_ref.at[n, m], strip)
                mix_out(mix_ref, m, blocks, strip, z_ref.at[n])
        left = g_ref if m == 2 else x_ref
        sum_ref[m] = sum(dot_tn(left[n], z_ref[n]) for n in range(count_groups))
        for i in range(NPHM):
            at = sum_ref.at[m, :, i * cols : (i + 1) * cols]
            stores.append(begin(at, out_hbm.at[m, i], out_sem.at[m, i]))
    wait_all(stores)


def mix_grad_body(yg_hbm, yu_hbm, yd_hbm, d_hbm, out_ref, y_ref, d_ref, sems):
    loads = [begin(d_hbm, d_ref, sems.at[3])]
    for m, source in enumerate((yg_hbm, yu_hbm, yd_hbm)):
        loads.append(begin(source, y_ref.at[m], sems.at[m]))
    wait_all(loads)
    rows, cols = d_ref.shape[1], d_ref.shape[2] // NPHM
    for m in range(3):
        for a in range(NPHM):
            for i in range(NPHM):
                at = slice(i * cols, (i + 1) * cols)
                strips = range(rows // STRIP)
                block = jnp.concatenate([y_ref[m, rows_of(n, a), at] for n in strips], axis=0)
                for b in range(NPHM):
                    at = m * 64 + i * 16 + a * 4 + b
                    other = d_ref[m, :, b * cols : (b + 1) * cols].astype(F32)
                    out_ref[at : at + 1, :] = jnp.sum(block * other, axis=0, keepdims=True)


def shards(tokens, cotangent, factors, mix, selection, scores):
    peers = lax.axis_size("exp")
    groups = lax.axis_size("seq")
    own_rows, width = tokens.shape
    _, weights, count, depth_own, cols = factors.shape
    depth = depth_own * groups
    hidden = count * cols
    cap = 3 * own_rows // (2 * peers)
    pieces = 1
    while (cap * pieces) % 8:
        pieces *= 2
    slots = peers * cap * pieces
    part = width // pieces
    steps = len(chunks_of(part))
    block_len = peers * SELECTED
    rows = selection.shape[1] * selection.shape[2]
    stacked = count * rows
    swap = groups == 2
    pair = [(0, 1), (1, 0)]
    mixing = mix.reshape(-1)
    dma = pltpu.SemaphoreType.DMA

    def across(array):
        return lax.ppermute(array, "seq", pair)

    half = peers // selection.shape[1]
    direct = half == 8
    me = lax.axis_index("exp").astype(jnp.int32).reshape(1)
    group = lax.axis_index("seq").astype(jnp.int32).reshape(1)
    halves = [list(range(h, h + half)) for h in range(0, peers, half)]
    if swap:
        cuts = [across(x) for x in cut_factors(factors[0], 2)]
        factor_parts = [factors[0]] + cuts
        sides = 2
    else:
        cuts = []
        factor_parts = [lax.all_gather(factors, "seq", axis=3, tiled=True)[0]]
        sides = 1
    sides_in = [(x, HBM) for x in factor_parts]
    cross = [(shaped((own_rows, width // 2), BF16), HBM)] if direct else []
    told, slot, *crossed = call(
        functools.partial(front_body, cap, pieces, own_rows, block_len, half, direct),
        [(shaped((2 * peers, rows), jnp.int32), VMEM), (shaped((1, rows), jnp.int32), VMEM)] + cross,
        [(me, SMEM), (selection[0], VMEM)] + ([(cotangent, HBM)] if direct else []),
        "wanted_rows",
        1 << 20,
        [scratch_like((own_rows, width // 2), BF16), dma((2,))] if direct else [],
    )
    if direct:
        crossed = [lax.ppermute(crossed[0], "exp", [(n, n ^ (half // 2)) for n in range(peers)])]
    chosen = lax.all_to_all(told, "exp", split_axis=0, concat_axis=0, tiled=True)

    def to_peers(array):
        array = array.reshape(peers, -1, array.shape[1])
        array = lax.all_to_all(array, "exp", split_axis=0, concat_axis=0, tiled=True)
        return array.reshape(-1, array.shape[2])

    got_rows = to_peers(pick_slots(cap, pieces, chosen, tokens, crossed, "pick_tokens"))
    if direct:
        shares = plane_columns(me, cotangent, crossed[0], half)
        shares = [shares[0]] + [
            lax.ppermute(shares[k], "exp", [(n, n ^ k) for n in range(peers)])
            for k in range(1, half // 2)
        ]
    else:
        array = spread_columns(cotangent, half).reshape(half, own_rows, -1)
        array = lax.all_to_all(
            array, "exp", split_axis=0, concat_axis=0, axis_index_groups=halves, tiled=True
        )
        shares = [array.reshape(half * own_rows, -1)]
    picked = pick_rows(me, half, own_rows, chosen, shares, cuts[:1], "pick_cotangent")
    got_grads = to_peers(picked)
    placed = place_rows(cap, pieces, own_rows, me, half, chosen)
    gate = jax.nn.sigmoid(scores[0].reshape(-1).astype(F32) / 64.0)

    product = 2 * stacked * depth * hidden
    split = [(shaped((stacked, depth // sides), BF16), HBM)] * sides
    mixed = (shaped((stacked, hidden), F32), HBM)
    flat = (shaped((rows, hidden), F32), HBM)
    back_scratch = scratch_like((slots, part), BF16)
    pieces_in = got_grads.shape[0] // SELECTED
    stack_scratch = scratch_like((stacked, depth), BF16)
    mixed_scratch = scratch_like((stacked, hidden), F32)
    low_scratch = scratch_like((stacked, hidden), BF16)
    flat_scratch = scratch_like((rows, hidden), F32)
    outs = call(
        functools.partial(forward_body, cap, pieces, sides),
        split + [mixed, mixed, flat, flat, flat],
        [(group, SMEM), (mixing, SMEM), (slot, VMEM), (got_rows, HBM)] + sides_in[:2],
        "forward",
        2 * product,
        [back_scratch, scratch_like((2, depth, hidden), BF16), stack_scratch, mixed_scratch, mixed_scratch]
        + [flat_scratch] * 3
        + [dma((steps,)), dma((2, sides, count)), dma((7,))],
    )
    x_parts, (y_gate, y_up, act, slope, hid) = outs[:sides], outs[sides:]
    x_rows = [x_parts[0]] + [across(x) for x in x_parts[1:]]
    after = x_rows[1:]
    outs = call(
        functools.partial(backward_body, cap, pieces, sides, len(after)),
        [(shaped((slots, part), BF16), HBM)]
        + split
        + [mixed, (shaped((weights, rows, hidden), BF16), HBM), (shaped((rows, cols), F32), HBM)],
        [(group, SMEM), (mixing, SMEM), (slot, HBM), (scores[0], HBM), (got_grads, HBM)]
        + [(x, HBM) for x in (act, slope, hid)]
        + sides_in
        + [(x, HBM) for x in after],
        "backward",
        3 * product,
        [scratch_like((depth, hidden), BF16), scratch_like((depth, 2 * hidden), BF16)]
        + [stack_scratch, mixed_scratch, scratch_like((weights, rows, hidden), BF16)]
        + [flat_scratch] * 3
        + [scratch_like((stacked, 2 * hidden), BF16), stack_scratch, back_scratch]
        + [scratch_like((rows, cols), F32), scratch_like(slot.shape, jnp.int32)]
        + [scratch_like(scores.shape[1:], jnp.int32)]
        + [dma((pieces_in,)), dma((weights, sides, count)), dma((5,)), dma((5 + steps,))],
    )
    back, g_parts, (y_down, d_own, inner) = outs[0], outs[1 : 1 + sides], outs[1 + sides :]
    returned = to_peers(back)

    d_rows = [d_own] + [across(d_own) for _ in x_parts[1:]]
    g_rows = [g_parts[0]] + [across(x) for x in g_parts[1:]]
    depth_here = depth // sides
    factor_grad = call(
        functools.partial(factor_body, sides),
        [(shaped((weights, count, depth_here, cols), F32), HBM)],
        [(mixing, SMEM)]
        + [(x, HBM) for n in range(sides) for x in (x_rows[n], g_rows[n], d_rows[n])],
        "factor_grad",
        3 * product,
        [scratch_like((sides, stacked, depth_here), BF16)] * 2
        + [
            scratch_like((sides, weights, rows, hidden), BF16),
            scratch_like((sides, stacked, hidden), BF16),
            scratch_like((weights, depth_here, hidden), F32),
            dma((sides, 3)),
            dma((weights, count)),
        ],
    )[0]
    mix_rows = call(
        mix_grad_body,
        [(shaped((mixing.size, cols), F32), VMEM)],
        [(x, HBM) for x in (y_gate, y_up, y_down, d_own)],
        "mix_partials",
        weights * 64 * 2 * rows * cols,
        [
            scratch_like((weights, stacked, hidden), F32),
            scratch_like((weights, rows, hidden), BF16),
            dma((4,)),
        ],
    )[0]
    mix_part = jnp.sum(mix_rows, axis=1).reshape(mix.shape)
    if swap:
        mix_grad = mix_part + across(mix_part)
    else:
        factor_grad = lax.psum_scatter(
            factor_grad.astype(BF16), "seq", scatter_dimension=2, tiled=True
        ).astype(F32)
        mix_grad = lax.psum(mix_part, "seq")
    gate_grad = (jnp.sum(inner, axis=1) * gate * (1.0 - gate)).reshape(selection.shape)
    token_grad = sum_rows(pieces, placed, returned)
    return token_grad, factor_grad[None], mix_grad, gate_grad


def solution(mesh):
    return jax.shard_map(
        shards,
        mesh=mesh,
        in_specs=(
            P(("seq", "exp"), None),
            P(("seq", "exp"), None),
            P("exp", None, None, "seq", None),
            P("exp", None, None, None, None),
            P("exp", "seq", None),
            P("exp", "seq", None),
        ),
        out_specs=(
            P(("seq", "exp"), None),
            P("exp", None, None, "seq", None),
            P("exp", None, None, None, None),
            P("exp", "seq", None),
        ),
        check_vma=False,
    )
```

```python
import functools

import jax
import jax.numpy as jnp
from jax import lax
from jax.experimental import pallas as pl
from jax.experimental.pallas import tpu as pltpu
from jax.sharding import PartitionSpec as P

SELECTED = 64
NPHM = 4
VMEM_LIMIT = 63 * 1024 * 1024
F32 = jnp.float32
BF16 = jnp.bfloat16


def iota(shape, dim):
    return lax.broadcasted_iota(jnp.int32, shape, dim)


def dot(left, right):
    return jnp.dot(left, right, preferred_element_type=F32)


def dot_tn(left, right):
    return lax.dot_general(left, right, (((0,), (0,)), ((), ())), preferred_element_type=F32)


def dot_nt(left, right):
    return lax.dot_general(left, right, (((1,), (1,)), ((), ())), preferred_element_type=F32)


HBM = pl.BlockSpec(memory_space=pltpu.HBM)
VMEM = pl.BlockSpec(memory_space=pltpu.VMEM)
SMEM = pl.BlockSpec(memory_space=pltpu.SMEM)


def call(body, outs, ins, name, flops, scratch=()):
    moved = sum(x.size * x.dtype.itemsize for x, _ in list(ins) + list(outs))
    return pl.pallas_call(
        body,
        out_shape=[x for x, _ in outs],
        in_specs=[place for _, place in ins],
        out_specs=[place for _, place in outs],
        scratch_shapes=list(scratch),
        compiler_params=pltpu.CompilerParams(vmem_limit_bytes=VMEM_LIMIT),
        cost_estimate=pl.CostEstimate(flops=flops, bytes_accessed=moved, transcendentals=0),
        name=name,
    )(*[x for x, _ in ins])


def begin(source, target, sem):
    copy = pltpu.make_async_copy(source, target, sem)
    copy.start()
    return copy


def shaped(shape, dtype):
    return jax.ShapeDtypeStruct(shape, dtype)


def scratch_like(shape, dtype):
    return pltpu.VMEM(shape, dtype)


def chunks_of(part):
    chunk = min(part, 512)
    return [slice(c * chunk, (c + 1) * chunk) for c in range(part // chunk)]


def front_body(cap, pieces, own_rows, block_len, half, cross, me_ref, chosen_ref, *refs):
    if cross:
        source_ref, told_ref, slot_ref, cross_ref, rest_ref, held_ref, sems = refs
        width = held_ref.shape[1]
        plane = lax.shift_right_logical(me_ref[0] & (half - 1), half.bit_length() - 2)
        at = pl.ds(pl.multiple_of((1 - plane) * width, width), width)
        load = begin(source_ref.at[:, at], held_ref, sems.at[0])
    else:
        told_ref, slot_ref = refs
    peers, rows = told_ref.shape[0] // 2, slot_ref.shape[1]
    blocks = [chosen_ref[b : b + 1, :] for b in range(chosen_ref.shape[0])]
    position = jnp.concatenate([x + b * block_len for b, x in enumerate(blocks)], axis=1)
    owner = lax.shift_right_logical(position, own_rows.bit_length() - 1)
    local = position & (own_rows - 1)
    peer = iota((peers, rows), 0)
    mine = (peer == owner).astype(F32)
    count = jnp.sum(mine, axis=1, keepdims=True)
    earlier = jnp.sum(jnp.where(peer < owner, count, 0.0), axis=0, keepdims=True).astype(jnp.int32)
    rank = iota((1, rows), 1) - earlier
    slot_ref[...] = owner * (cap * pieces) + rank
    lane = iota((rows, rows), 0)
    hit = jnp.zeros((rows, rows), F32)
    for j in range(pieces):
        hit = hit + (lane == rank + j * cap).astype(F32)
    twice = iota((2 * peers, rows), 0)
    marked = jnp.where(twice == 2 * owner, local + 1, 0).astype(F32)
    asked = dot_nt(marked.astype(BF16), hit.astype(BF16)).astype(jnp.int32)
    told_ref[...] = jnp.where((twice & 1) == 1, jnp.concatenate(blocks, axis=1), asked)
    if cross:
        load.wait()
        first = begin(held_ref.at[:, : width // 2], cross_ref, sems.at[1])
        begin(held_ref.at[:, width // 2 :], rest_ref, sems.at[2]).wait()
        first.wait()


def plane_columns(me, source, crossed, rest, half):
    own_rows, width = source.shape
    part, count = width // half, half // 2

    def body(me_ref, source_ref, crossed_ref, rest_ref, *refs):
        outs, (held_ref, in_sem, out_sem) = refs[:count], refs[count:]
        low = me_ref[0] & (half - 1)
        plane = lax.shift_right_logical(low, half.bit_length() - 2)
        wide = count * part
        at = pl.ds(pl.multiple_of(plane * wide, wide), wide)
        loads = [
            begin(source_ref.at[:, at], held_ref.at[0], in_sem.at[0]),
            begin(crossed_ref, held_ref.at[1, :, : wide // 2], in_sem.at[1]),
            begin(rest_ref, held_ref.at[1, :, wide // 2 :], in_sem.at[2]),
        ]
        copies = []
        for n in range(2):
            wait_all(loads[n : 1 + 2 * n])
            for k in range(count):
                share = (low & (count - 1)) ^ k
                at = held_ref.at[n, :, pl.ds(pl.multiple_of(share * part, part), part)]
                rows = pl.ds(n * own_rows, own_rows)
                copies.append(begin(at, outs[k].at[rows], out_sem.at[n, k]))
        wait_all(copies)

    return call(
        body,
        [(shaped((2 * own_rows, part), BF16), HBM)] * count,
        [(me, SMEM), (source, HBM), (crossed, HBM), (rest, HBM)],
        "plane_columns",
        0,
        [
            scratch_like((2, own_rows, count * part), BF16),
            pltpu.SemaphoreType.DMA((3,)),
            pltpu.SemaphoreType.DMA((2, count)),
        ],
    )


def pick_matrix(cap, pieces, own_rows, requested):
    told, lanes = requested.shape
    peers = told // 2
    group = cap * pieces
    slots = peers * group
    peer = 2 * iota((peers, group, told), 0).reshape(slots, told)
    spread = dot(
        (peer == iota((slots, told), 1)).astype(BF16), requested.astype(F32).astype(BF16)
    )
    place = iota((peers, group, lanes), 1).reshape(slots, lanes)
    row = jnp.sum(
        jnp.where(place == iota((slots, lanes), 1), spread, 0.0), axis=1, keepdims=True
    ).astype(jnp.int32)
    piece = iota((peers, group, 1), 1).reshape(slots, 1)
    shift = jnp.zeros((slots, 1), jnp.int32)
    for j in range(1, pieces):
        shift = shift + jnp.where(piece >= j * cap, own_rows, 0)
    target = jnp.where(row > 0, row - 1 + shift, -1)
    return (target == iota((slots, pieces * own_rows), 1)).astype(BF16)


def pick_slots(cap, pieces, requested, source, after, name):
    own_rows, width = source.shape
    part = width // pieces
    slots = requested.shape[0] // 2 * cap * pieces
    columns = chunks_of(part)

    def body(requested_hbm, source_ref, *refs):
        out_ref, requested_ref, rows_ref, sent_ref, in_sem, out_sem = refs[len(after) :]
        asked = begin(requested_hbm, requested_ref, in_sem.at[len(columns), 0])
        loads = []
        for n, at in enumerate(columns):
            for j in range(pieces):
                wide = slice(j * part + at.start, j * part + at.stop)
                target = rows_ref.at[j * own_rows : (j + 1) * own_rows, at]
                loads.append(begin(source_ref.at[:, wide], target, in_sem.at[n, j]))
        asked.wait()
        pick = pick_matrix(cap, pieces, own_rows, requested_ref[...])
        stores = []
        for n, at in enumerate(columns):
            for load in loads[n * pieces : (n + 1) * pieces]:
                load.wait()
            sent_ref[:, at] = dot(pick, rows_ref[:, at]).astype(BF16)
            stores.append(begin(sent_ref.at[:, at], out_ref.at[:, at], out_sem.at[n]))
        for store in stores:
            store.wait()

    return call(
        body,
        [(shaped((slots, part), BF16), HBM)],
        [(requested, HBM), (source, HBM)] + [(x, HBM) for x in after],
        name,
        2 * slots * pieces * own_rows * part,
        [
            scratch_like(requested.shape, jnp.int32),
            scratch_like((pieces * own_rows, part), BF16),
            scratch_like((slots, part), BF16),
            pltpu.SemaphoreType.DMA((len(columns) + 1, pieces)),
            pltpu.SemaphoreType.DMA((len(columns),)),
        ],
    )[0]


def spread_columns(source, half):
    own_rows, width = source.shape
    part = width // half

    def body(source_ref, out_ref, held_ref, in_sem, out_sem):
        begin(source_ref, held_ref, in_sem).wait()
        copies = []
        for k in range(half):
            at = held_ref.at[:, k * part : (k + 1) * part]
            out = out_ref.at[k * own_rows : (k + 1) * own_rows]
            copies.append(begin(at, out, out_sem.at[k]))
        wait_all(copies)

    scratch = [
        scratch_like((own_rows, width), BF16),
        pltpu.SemaphoreType.DMA,
        pltpu.SemaphoreType.DMA((half,)),
    ]
    outs = [(shaped((half * own_rows, part), BF16), HBM)]
    return call(body, outs, [(source, HBM)], "spread_columns", 0, scratch)[0]


def cut_factors(factors, first):
    cuts = (slice(0, first), slice(first, factors.shape[0]))

    def body(factors_ref, *refs):
        outs, (held_ref, sems) = refs[:2], refs[2:]
        loads = [
            begin(factors_ref.at[at], held_ref.at[at], sems.at[0, n]) for n, at in enumerate(cuts)
        ]
        copies = []
        for n, at in enumerate(cuts):
            loads[n].wait()
            copies.append(begin(held_ref.at[at], outs[n], sems.at[1, n]))
        wait_all(copies)

    outs = [
        (shaped((at.stop - at.start,) + factors.shape[1:], BF16), HBM) for at in cuts
    ]
    scratch = [scratch_like(factors.shape, BF16), pltpu.SemaphoreType.DMA((2, 2))]
    return call(body, outs, [(factors, HBM)], "cut_factors", 0, scratch)


def pick_rows(me, half, own_rows, chosen, shares, after, name):
    peers, total = chosen.shape[0] // 2, chosen.shape[1]
    picks = total * half // peers
    part = shares[0].shape[1]
    block = half * own_rows
    batch = min(peers, 8)

    def body(me_ref, chosen_ref, *refs):
        refs = refs[len(after) :]
        parts, (out_ref, rows_ref, pick_ref, sent_ref, in_sem, out_sem) = (
            refs[: len(shares)],
            refs[len(shares) :],
        )
        loads = []
        for k in range(half):
            place = (me_ref[0] & (half - 1)) ^ k if len(parts) > 1 else k
            n, first = (k % len(parts), k // len(parts)) if len(parts) > 1 else (0, k)
            at = parts[n].at[first * own_rows : (first + 1) * own_rows]
            target = rows_ref.at[pl.ds(pl.multiple_of(place * own_rows, own_rows), own_rows)]
            loads.append(begin(at, target, in_sem.at[k]))
        block_at = lax.shift_right_logical(me_ref[0], half.bit_length() - 1)
        same = iota((picks, total), 0) + block_at * picks == iota((picks, total), 1)
        stores = []
        for first in range(0, peers, batch):
            for e in range(batch):
                wanted = chosen_ref[2 * (first + e) + 1 : 2 * (first + e) + 2, :]
                column = jnp.sum(jnp.where(same, wanted, 0), axis=1, keepdims=True)
                pick_ref[first // batch % 2, e * picks : (e + 1) * picks] = (
                    column == iota((picks, block), 1)
                ).astype(BF16)
            if first == 0:
                wait_all(loads)
            at = slice(first * picks, (first + batch) * picks)
            sent_ref[at] = dot(pick_ref[first // batch % 2], rows_ref[...]).astype(BF16)
            stores.append(begin(sent_ref.at[at], out_ref.at[at], out_sem.at[first // batch]))
        wait_all(stores)

    return call(
        body,
        [(shaped((peers * picks, part), BF16), HBM)],
        [(me, SMEM), (chosen, VMEM)] + [(x, HBM) for x in list(after) + list(shares)],
        name,
        2 * peers * picks * block * part,
        [
            scratch_like((block, part), BF16),
            scratch_like((2, batch * picks, block), BF16),
            scratch_like((peers * picks, part), BF16),
            pltpu.SemaphoreType.DMA((half,)),
            pltpu.SemaphoreType.DMA((peers // batch,)),
        ],
    )[0]


def place_rows(cap, pieces, own_rows, me, half, chosen):
    peers, total = chosen.shape[0] // 2, chosen.shape[1]
    picks = total * half // peers
    group = cap * pieces

    def body(me_ref, chosen_ref, out_ref, pick_ref):
        low = me_ref[0] & (half - 1)
        block_at = lax.shift_right_logical(me_ref[0], half.bit_length() - 1)
        lane = iota((2 * peers, total), 1) - block_at * picks
        here = (lane >= 0) & (lane < picks)
        local = jnp.where(here, chosen_ref[...] - low * own_rows, own_rows)
        before = jnp.sum((local < 0).astype(F32), axis=1, keepdims=True).astype(jnp.int32)
        ranks = lane - before
        owned = jnp.where((local >= 0) & (local < own_rows), local + 1, 0)
        place = iota((group, total), 0)
        for e in range(peers):
            at = slice(2 * e + 1, 2 * e + 2)
            rank, mine = ranks[at], owned[at]
            column = jnp.zeros((group, 1), jnp.int32)
            for j in range(pieces):
                hit = jnp.where((place == rank + j * cap) & (rank >= 0) & (rank < cap), mine, 0)
                row = jnp.sum(hit, axis=1, keepdims=True)
                column = column + jnp.where(row > 0, row + j * own_rows, 0)
            pick_ref[e * group : (e + 1) * group] = (
                column == iota((group, pieces * own_rows), 1) + 1
            ).astype(F32)
        out_ref[...] = jnp.transpose(pick_ref[...]).astype(BF16)

    return call(
        body,
        [(shaped((pieces * own_rows, peers * group), BF16), VMEM)],
        [(me, SMEM), (chosen, VMEM)],
        "place_rows",
        1 << 20,
        [scratch_like((peers * group, pieces * own_rows), F32)],
    )[0]


def sum_rows(pieces, placed, returned):
    slots, part = returned.shape
    own_rows = placed.shape[0] // pieces
    columns = chunks_of(part)

    def body(placed_hbm, returned_ref, out_ref, place_ref, got_ref, sum_ref, in_sem, out_sem):
        first = begin(placed_hbm, place_ref, in_sem.at[len(columns)])
        loads = [
            begin(returned_ref.at[:, at], got_ref.at[:, at], in_sem.at[n])
            for n, at in enumerate(columns)
        ]
        first.wait()
        stores = []
        for n, at in enumerate(columns):
            loads[n].wait()
            summed = dot(place_ref[...], got_ref[:, at]).astype(BF16)
            for j in range(pieces):
                wide = slice(j * part + at.start, j * part + at.stop)
                sum_ref[:, wide] = summed[j * own_rows : (j + 1) * own_rows]
                stores.append(
                    begin(sum_ref.at[:, wide], out_ref.at[:, wide], out_sem.at[n, j])
                )
        wait_all(stores)

    return call(
        body,
        [(shaped((own_rows, part * pieces), BF16), HBM)],
        [(placed, HBM), (returned, HBM)],
        "sum_rows",
        2 * slots * pieces * own_rows * part,
        [
            scratch_like(placed.shape, BF16),
            scratch_like((slots, part), BF16),
            scratch_like((own_rows, part * pieces), BF16),
            pltpu.SemaphoreType.DMA((len(columns) + 1,)),
            pltpu.SemaphoreType.DMA((len(columns), pieces)),
        ],
    )[0]


def load_factor(order_ref, parts, m, target, sems):
    copies = []
    sides = [parts[0].at[m]]
    if len(parts) > 1:
        first = parts[1].shape[0]
        sides.append(parts[1].at[m] if m < first else parts[2].at[m - first])
    for n, side in enumerate(sides):
        count, rows, cols = side.shape
        place = order_ref[0] ^ n if len(parts) > 1 else 0
        start = pl.multiple_of(place * rows, rows)
        for i in range(count):
            at = target.at[pl.ds(start, rows), i * cols : (i + 1) * cols]
            copies.append(begin(side.at[i], at, sems.at[n, i]))
    return copies


def wait_all(copies):
    for copy in copies:
        copy.wait()


def place_matrix(cap, pieces, slots, slot):
    wide = jnp.concatenate([slot + j * cap for j in range(pieces)], axis=1)
    return (iota((slots, wide.shape[1]), 0) == wide).astype(BF16)


def load_rows(got_hbm, x_ref, sems):
    rows, depth = x_ref.shape[0] // NPHM, x_ref.shape[1]
    part = got_hbm.shape[1]
    shares = NPHM * depth // part
    picks = got_hbm.shape[0] * part // (NPHM * depth) // (rows // SELECTED)
    copies = []
    for n in range(got_hbm.shape[0] // picks):
        block, share = divmod(n, shares)
        a, start = share * part // depth, share * part % depth
        first = (block * NPHM + a) * picks
        at = x_ref.at[first : first + picks, start : start + part]
        copies.append(begin(got_hbm.at[n * picks : (n + 1) * picks], at, sems.at[n]))
    return copies


def load_slots(got_hbm, got_ref, sems):
    return [
        begin(got_hbm.at[:, at], got_ref.at[:, at], sems.at[n])
        for n, at in enumerate(chunks_of(got_ref.shape[1]))
    ]


def stack_rows(pieces, place, loads, got_ref, out_ref):
    part = got_ref.shape[1]
    rows, depth = out_ref.shape[0] // NPHM, out_ref.shape[1]
    for load, at in zip(loads, chunks_of(part)):
        load.wait()
        block = dot_tn(place, got_ref[:, at]).astype(BF16)
        for j in range(pieces):
            column = j * part + at.start
            a, start = column // depth, column % depth
            for n in range(rows // STRIP):
                first = (n * NPHM + a) * STRIP
                out_ref[first : first + STRIP, start : start + at.stop - at.start] = block[
                    j * rows + n * STRIP : j * rows + (n + 1) * STRIP
                ]


def store_parts(order_ref, source_ref, outs, sems):
    copies = []
    for n, out in enumerate(outs):
        size = out.shape[1]
        start = pl.multiple_of((order_ref[0] ^ n) * size if len(outs) > 1 else 0, size)
        copies.append(begin(source_ref.at[:, pl.ds(start, size)], out, sems.at[n]))
    return copies


STRIP = SELECTED


def rows_of(n, a):
    return slice((n * NPHM + a) * STRIP, (n * NPHM + a + 1) * STRIP)


def mix_in(mix_ref, m, y_ref, n):
    cols = y_ref.shape[1] // NPHM
    total = [jnp.zeros((STRIP, cols), F32)] * NPHM
    for a in range(NPHM):
        for i in range(NPHM):
            block = y_ref[rows_of(n, a), i * cols : (i + 1) * cols]
            for b in range(NPHM):
                total[b] = total[b] + mix_ref[m * 64 + i * 16 + a * 4 + b] * block
    return total


def mix_out(mix_ref, m, blocks, n, z_ref, offset=0):
    cols = blocks[0].shape[1]
    for a in range(NPHM):
        for i in range(NPHM):
            total = mix_ref[m * 64 + i * 16 + a * 4] * blocks[0]
            for b in range(1, NPHM):
                total = total + mix_ref[m * 64 + i * 16 + a * 4 + b] * blocks[b]
            z_ref[rows_of(n, a), offset + i * cols : offset + (i + 1) * cols] = total.astype(
                z_ref.dtype
            )


def blocks_of(d_ref, n):
    cols = d_ref.shape[1] // NPHM
    at = slice(n * STRIP, (n + 1) * STRIP)
    return [d_ref[at, b * cols : (b + 1) * cols].astype(F32) for b in range(NPHM)]


def forward_body(
    cap, pieces, sides, order_ref, mix_ref, slot_ref, got_hbm, *refs
):
    held = 2 if sides > 1 else 1
    parts, refs = refs[:held], refs[held:]
    x_outs, refs = refs[:sides], refs[sides:]
    yg_hbm, yu_hbm, act_hbm, slope_hbm, hid_hbm = refs[:5]
    got_ref, side_ref, x_ref, yg_ref, yu_ref, act_ref, slope_ref, hid_ref = refs[5:13]
    got_sem, side_sem, out_sem = refs[13:]
    loads = load_slots(got_hbm, got_ref, got_sem)
    sides_in = [
        load_factor(order_ref, parts, m, side_ref.at[m], side_sem.at[m]) for m in range(2)
    ]
    place = place_matrix(cap, pieces, got_ref.shape[0], slot_ref[...])
    stack_rows(pieces, place, loads, got_ref, x_ref)
    stores = store_parts(order_ref, x_ref, x_outs, out_sem)
    wait_all(sides_in[0])
    yg_ref[...] = dot(x_ref[...], side_ref[0])
    stores.append(begin(yg_ref, yg_hbm, out_sem.at[2]))
    wait_all(sides_in[1])
    yu_ref[...] = dot(x_ref[...], side_ref[1])
    stores.append(begin(yu_ref, yu_hbm, out_sem.at[3]))
    cols = yg_ref.shape[1] // NPHM
    for n in range(yg_ref.shape[0] // (NPHM * STRIP)):
        gates = mix_in(mix_ref, 0, yg_ref, n)
        ups = mix_in(mix_ref, 1, yu_ref, n)
        for b in range(NPHM):
            at = (slice(n * STRIP, (n + 1) * STRIP), slice(b * cols, (b + 1) * cols))
            sig = jax.nn.sigmoid(gates[b])
            act = gates[b] * sig
            act_ref[at] = act
            slope_ref[at] = ups[b] * (sig + act * (1.0 - sig))
            hid_ref[at] = act * ups[b]
    stores.append(begin(act_ref, act_hbm, out_sem.at[4]))
    stores.append(begin(slope_ref, slope_hbm, out_sem.at[5]))
    stores.append(begin(hid_ref, hid_hbm, out_sem.at[6]))
    wait_all(stores)


def backward_body(
    cap, pieces, sides, after, order_ref, mix_ref, slot_hbm, score_hbm, got_hbm, act_hbm, slope_hbm, hid_hbm,
    *refs,
):
    held = 3 if sides > 1 else 1
    parts, refs = refs[:held], refs[held + after :]
    back_hbm, x_outs, refs = refs[0], refs[1 : 1 + sides], refs[1 + sides :]
    y_hbm, d_hbm, inner_hbm = refs[:3]
    (
        down_ref, side_ref, x_ref, y_ref, d_ref, act_ref, slope_ref, hid_ref, z_ref, grad_ref,
        back_ref, inner_ref, slot_ref, score_ref, got_sem, side_sem, in_sem, out_sem,
    ) = refs[3:]
    loads = load_rows(got_hbm, x_ref, got_sem)
    down_in = load_factor(order_ref, parts, 2, down_ref, side_sem.at[2])
    small_in = [
        begin(source, target, in_sem.at[n])
        for n, (source, target) in enumerate(((score_hbm, score_ref), (slot_hbm, slot_ref)))
    ]
    flat_in = [
        begin(source, target, in_sem.at[2 + n])
        for n, (source, target) in enumerate(
            ((act_hbm, act_ref), (slope_hbm, slope_ref), (hid_hbm, hid_ref))
        )
    ]
    hidden = d_ref.shape[2]
    sides_in = []
    for m in range(2):
        target = side_ref.at[:, m * hidden : (m + 1) * hidden]
        sides_in += load_factor(order_ref, parts, m, target, side_sem.at[m])
    wait_all(small_in)
    score = jnp.concatenate([score_ref[b : b + 1, :] for b in range(score_ref.shape[0])], axis=1)
    rows = score.shape[1]
    same = iota((rows, rows), 0) == iota((rows, rows), 1)
    score = jnp.sum(jnp.where(same, score.astype(F32), 0.0), axis=1, keepdims=True)
    cols = hidden // NPHM
    gates = jnp.broadcast_to(jax.nn.sigmoid(score / 64.0), (rows, cols))
    place = place_matrix(cap, pieces, back_ref.shape[0], slot_ref[...])
    strips = rows // STRIP
    tall = NPHM * STRIP
    wait_all(loads)
    stores = store_parts(order_ref, x_ref, x_outs, out_sem)
    wait_all(down_in)
    for n in range(strips):
        y_ref[n * tall : (n + 1) * tall] = dot(x_ref[n * tall : (n + 1) * tall], down_ref[...])
    stores.append(begin(y_ref, y_hbm, out_sem.at[2]))
    wait_all(flat_in)
    wait_all(sides_in)
    for n in range(strips):
        down = mix_in(mix_ref, 2, y_ref, n)
        strip = slice(n * STRIP, (n + 1) * STRIP)
        gate = gates[strip]
        inner = jnp.zeros((STRIP, cols), F32)
        d_gate, d_up = [], []
        for b in range(NPHM):
            at = (strip, slice(b * cols, (b + 1) * cols))
            inner = inner + hid_ref[at] * down[b]
            hidden_grad = gate * down[b]
            d_gate.append(hidden_grad * slope_ref[at])
            d_up.append(hidden_grad * act_ref[at])
            d_ref[(0,) + at] = d_gate[b].astype(BF16)
            d_ref[(1,) + at] = d_up[b].astype(BF16)
            d_ref[(2,) + at] = (hid_ref[at] * gate).astype(BF16)
        inner_ref[strip] = inner
        mix_out(mix_ref, 0, d_gate, n, z_ref)
        mix_out(mix_ref, 1, d_up, n, z_ref, hidden)
        at = slice(n * tall, (n + 1) * tall)
        grad_ref[at] = dot_nt(z_ref[at], side_ref[...]).astype(BF16)
    stores.append(begin(d_ref, d_hbm, out_sem.at[3]))
    stores.append(begin(inner_ref, inner_hbm, out_sem.at[4]))
    part, depth = back_ref.shape[1], x_ref.shape[1]
    for k, at in enumerate(chunks_of(part)):
        blocks = []
        for j in range(pieces):
            column = j * part + at.start
            a, start = column // depth, column % depth
            wide = slice(start, start + at.stop - at.start)
            blocks += [grad_ref[rows_of(n, a), wide] for n in range(strips)]
        back_ref[:, at] = dot(place, jnp.concatenate(blocks, axis=0)).astype(BF16)
        stores.append(begin(back_ref.at[:, at], back_hbm.at[:, at], out_sem.at[5 + k]))
    wait_all(stores)


def factor_body(count_groups, mix_ref, *refs):
    rows_in, refs = refs[: 3 * count_groups], refs[3 * count_groups :]
    out_hbm, x_ref, g_ref, d_ref, z_ref, sum_ref, in_sem, out_sem = refs
    loads = []
    for n in range(count_groups):
        for k, target in enumerate((x_ref, g_ref, d_ref)):
            loads.append(begin(rows_in[3 * n + k], target.at[n], in_sem.at[n, k]))
    stores = []
    cols = out_hbm.shape[3]
    wait_all(loads)
    for m in (2, 0, 1):
        for n in range(count_groups):
            for strip in range(d_ref.shape[2] // STRIP):
                blocks = blocks_of(d_ref.at[n, m], strip)
                mix_out(mix_ref, m, blocks, strip, z_ref.at[n])
        left = g_ref if m == 2 else x_ref
        sum_ref[m] = sum(dot_tn(left[n], z_ref[n]) for n in range(count_groups))
        for i in range(NPHM):
            at = sum_ref.at[m, :, i * cols : (i + 1) * cols]
            stores.append(begin(at, out_hbm.at[m, i], out_sem.at[m, i]))
    wait_all(stores)


def mix_grad_body(yg_hbm, yu_hbm, yd_hbm, d_hbm, out_ref, y_ref, d_ref, sems):
    loads = [begin(d_hbm, d_ref, sems.at[3])]
    for m, source in enumerate((yg_hbm, yu_hbm, yd_hbm)):
        loads.append(begin(source, y_ref.at[m], sems.at[m]))
    wait_all(loads)
    rows, cols = d_ref.shape[1], d_ref.shape[2] // NPHM
    for m in range(3):
        for a in range(NPHM):
            for i in range(NPHM):
                at = slice(i * cols, (i + 1) * cols)
                strips = range(rows // STRIP)
                block = jnp.concatenate([y_ref[m, rows_of(n, a), at] for n in strips], axis=0)
                for b in range(NPHM):
                    at = m * 64 + i * 16 + a * 4 + b
                    other = d_ref[m, :, b * cols : (b + 1) * cols].astype(F32)
                    out_ref[at : at + 1, :] = jnp.sum(block * other, axis=0, keepdims=True)


def shards(tokens, cotangent, factors, mix, selection, scores):
    peers = lax.axis_size("exp")
    groups = lax.axis_size("seq")
    own_rows, width = tokens.shape
    _, weights, count, depth_own, cols = factors.shape
    depth = depth_own * groups
    hidden = count * cols
    cap = 3 * own_rows // (2 * peers)
    pieces = 1
    while (cap * pieces) % 8:
        pieces *= 2
    slots = peers * cap * pieces
    part = width // pieces
    steps = len(chunks_of(part))
    block_len = peers * SELECTED
    rows = selection.shape[1] * selection.shape[2]
    stacked = count * rows
    swap = groups == 2
    pair = [(0, 1), (1, 0)]
    mixing = mix.reshape(-1)
    dma = pltpu.SemaphoreType.DMA

    def across(array):
        return lax.ppermute(array, "seq", pair)

    half = peers // selection.shape[1]
    direct = half == 8
    me = lax.axis_index("exp").astype(jnp.int32).reshape(1)
    group = lax.axis_index("seq").astype(jnp.int32).reshape(1)
    halves = [list(range(h, h + half)) for h in range(0, peers, half)]
    if swap:
        cuts = [across(x) for x in cut_factors(factors[0], 2)]
        factor_parts = [factors[0]] + cuts
        sides = 2
    else:
        cuts = []
        factor_parts = [lax.all_gather(factors, "seq", axis=3, tiled=True)[0]]
        sides = 1
    sides_in = [(x, HBM) for x in factor_parts]
    cross = [(shaped((own_rows, width // 4), BF16), HBM)] * 2 if direct else []
    told, slot, *crossed = call(
        functools.partial(front_body, cap, pieces, own_rows, block_len, half, direct),
        [(shaped((2 * peers, rows), jnp.int32), VMEM), (shaped((1, rows), jnp.int32), VMEM)] + cross,
        [(me, SMEM), (selection[0], VMEM)] + ([(cotangent, HBM)] if direct else []),
        "wanted_rows",
        1 << 20,
        [scratch_like((own_rows, width // 2), BF16), dma((3,))] if direct else [],
    )
    if direct:
        crossed = [
            lax.ppermute(x, "exp", [(n, n ^ (half // 2)) for n in range(peers)]) for x in crossed
        ]
    chosen = lax.all_to_all(told, "exp", split_axis=0, concat_axis=0, tiled=True)

    def to_peers(array):
        array = array.reshape(peers, -1, array.shape[1])
        array = lax.all_to_all(array, "exp", split_axis=0, concat_axis=0, tiled=True)
        return array.reshape(-1, array.shape[2])

    got_rows = to_peers(pick_slots(cap, pieces, chosen, tokens, crossed[:1], "pick_tokens"))
    if direct:
        shares = plane_columns(me, cotangent, *crossed, half)
        shares = [shares[0]] + [
            lax.ppermute(shares[k], "exp", [(n, n ^ k) for n in range(peers)])
            for k in range(1, half // 2)
        ]
    else:
        array = spread_columns(cotangent, half).reshape(half, own_rows, -1)
        array = lax.all_to_all(
            array, "exp", split_axis=0, concat_axis=0, axis_index_groups=halves, tiled=True
        )
        shares = [array.reshape(half * own_rows, -1)]
    picked = pick_rows(me, half, own_rows, chosen, shares, cuts[:1], "pick_cotangent")
    got_grads = to_peers(picked)
    placed = place_rows(cap, pieces, own_rows, me, half, chosen)
    gate = jax.nn.sigmoid(scores[0].reshape(-1).astype(F32) / 64.0)

    product = 2 * stacked * depth * hidden
    split = [(shaped((stacked, depth // sides), BF16), HBM)] * sides
    mixed = (shaped((stacked, hidden), F32), HBM)
    flat = (shaped((rows, hidden), F32), HBM)
    back_scratch = scratch_like((slots, part), BF16)
    pieces_in = got_grads.shape[0] // SELECTED
    stack_scratch = scratch_like((stacked, depth), BF16)
    mixed_scratch = scratch_like((stacked, hidden), F32)
    low_scratch = scratch_like((stacked, hidden), BF16)
    flat_scratch = scratch_like((rows, hidden), F32)
    outs = call(
        functools.partial(forward_body, cap, pieces, sides),
        split + [mixed, mixed, flat, flat, flat],
        [(group, SMEM), (mixing, SMEM), (slot, VMEM), (got_rows, HBM)] + sides_in[:2],
        "forward",
        2 * product,
        [back_scratch, scratch_like((2, depth, hidden), BF16), stack_scratch, mixed_scratch, mixed_scratch]
        + [flat_scratch] * 3
        + [dma((steps,)), dma((2, sides, count)), dma((7,))],
    )
    x_parts, (y_gate, y_up, act, slope, hid) = outs[:sides], outs[sides:]
    x_rows = [x_parts[0]] + [across(x) for x in x_parts[1:]]
    after = x_rows[1:]
    outs = call(
        functools.partial(backward_body, cap, pieces, sides, len(after)),
        [(shaped((slots, part), BF16), HBM)]
        + split
        + [mixed, (shaped((weights, rows, hidden), BF16), HBM), (shaped((rows, cols), F32), HBM)],
        [(group, SMEM), (mixing, SMEM), (slot, HBM), (scores[0], HBM), (got_grads, HBM)]
        + [(x, HBM) for x in (act, slope, hid)]
        + sides_in
        + [(x, HBM) for x in after],
        "backward",
        3 * product,
        [scratch_like((depth, hidden), BF16), scratch_like((depth, 2 * hidden), BF16)]
        + [stack_scratch, mixed_scratch, scratch_like((weights, rows, hidden), BF16)]
        + [flat_scratch] * 3
        + [scratch_like((stacked, 2 * hidden), BF16), stack_scratch, back_scratch]
        + [scratch_like((rows, cols), F32), scratch_like(slot.shape, jnp.int32)]
        + [scratch_like(scores.shape[1:], jnp.int32)]
        + [dma((pieces_in,)), dma((weights, sides, count)), dma((5,)), dma((5 + steps,))],
    )
    back, g_parts, (y_down, d_own, inner) = outs[0], outs[1 : 1 + sides], outs[1 + sides :]
    returned = to_peers(back)

    d_rows = [d_own] + [across(d_own) for _ in x_parts[1:]]
    g_rows = [g_parts[0]] + [across(x) for x in g_parts[1:]]
    depth_here = depth // sides
    factor_grad = call(
        functools.partial(factor_body, sides),
        [(shaped((weights, count, depth_here, cols), F32), HBM)],
        [(mixing, SMEM)]
        + [(x, HBM) for n in range(sides) for x in (x_rows[n], g_rows[n], d_rows[n])],
        "factor_grad",
        3 * product,
        [scratch_like((sides, stacked, depth_here), BF16)] * 2
        + [
            scratch_like((sides, weights, rows, hidden), BF16),
            scratch_like((sides, stacked, hidden), BF16),
            scratch_like((weights, depth_here, hidden), F32),
            dma((sides, 3)),
            dma((weights, count)),
        ],
    )[0]
    mix_rows = call(
        mix_grad_body,
        [(shaped((mixing.size, cols), F32), VMEM)],
        [(x, HBM) for x in (y_gate, y_up, y_down, d_own)],
        "mix_partials",
        weights * 64 * 2 * rows * cols,
        [
            scratch_like((weights, stacked, hidden), F32),
            scratch_like((weights, rows, hidden), BF16),
            dma((4,)),
        ],
    )[0]
    mix_part = jnp.sum(mix_rows, axis=1).reshape(mix.shape)
    if swap:
        mix_grad = mix_part + across(mix_part)
    else:
        factor_grad = lax.psum_scatter(
            factor_grad.astype(BF16), "seq", scatter_dimension=2, tiled=True
        ).astype(F32)
        mix_grad = lax.psum(mix_part, "seq")
    gate_grad = (jnp.sum(inner, axis=1) * gate * (1.0 - gate)).reshape(selection.shape)
    token_grad = sum_rows(pieces, placed, returned)
    return token_grad, factor_grad[None], mix_grad, gate_grad


def solution(mesh):
    return jax.shard_map(
        shards,
        mesh=mesh,
        in_specs=(
            P(("seq", "exp"), None),
            P(("seq", "exp"), None),
            P("exp", None, None, "seq", None),
            P("exp", None, None, None, None),
            P("exp", "seq", None),
            P("exp", "seq", None),
        ),
        out_specs=(
            P(("seq", "exp"), None),
            P("exp", None, None, "seq", None),
            P("exp", None, None, None, None),
            P("exp", "seq", None),
        ),
        check_vma=False,
    )
```

```python
import functools

import jax
import jax.numpy as jnp
from jax import lax
from jax.experimental import pallas as pl
from jax.experimental.pallas import tpu as pltpu
from jax.sharding import PartitionSpec as P

SELECTED = 64
NPHM = 4
VMEM_LIMIT = 63 * 1024 * 1024
F32 = jnp.float32
BF16 = jnp.bfloat16


def iota(shape, dim):
    return lax.broadcasted_iota(jnp.int32, shape, dim)


def dot(left, right):
    return jnp.dot(left, right, preferred_element_type=F32)


def dot_tn(left, right):
    return lax.dot_general(left, right, (((0,), (0,)), ((), ())), preferred_element_type=F32)


def dot_nt(left, right):
    return lax.dot_general(left, right, (((1,), (1,)), ((), ())), preferred_element_type=F32)


HBM = pl.BlockSpec(memory_space=pltpu.HBM)
VMEM = pl.BlockSpec(memory_space=pltpu.VMEM)
SMEM = pl.BlockSpec(memory_space=pltpu.SMEM)


def call(body, outs, ins, name, flops, scratch=()):
    moved = sum(x.size * x.dtype.itemsize for x, _ in list(ins) + list(outs))
    return pl.pallas_call(
        body,
        out_shape=[x for x, _ in outs],
        in_specs=[place for _, place in ins],
        out_specs=[place for _, place in outs],
        scratch_shapes=list(scratch),
        compiler_params=pltpu.CompilerParams(vmem_limit_bytes=VMEM_LIMIT),
        cost_estimate=pl.CostEstimate(flops=flops, bytes_accessed=moved, transcendentals=0),
        name=name,
    )(*[x for x, _ in ins])


def begin(source, target, sem):
    copy = pltpu.make_async_copy(source, target, sem)
    copy.start()
    return copy


def shaped(shape, dtype):
    return jax.ShapeDtypeStruct(shape, dtype)


def scratch_like(shape, dtype):
    return pltpu.VMEM(shape, dtype)


def chunks_of(part):
    chunk = min(part, 512)
    return [slice(c * chunk, (c + 1) * chunk) for c in range(part // chunk)]


def front_body(cap, pieces, back_pieces, own_rows, block_len, half, cross, me_ref, chosen_ref, *refs):
    if cross:
        source_ref, told_ref, slot_ref, cross_ref, held_ref, sems = refs
        width = cross_ref.shape[1]
        plane = lax.shift_right_logical(me_ref[0] & (half - 1), half.bit_length() - 2)
        at = pl.ds(pl.multiple_of((1 - plane) * width, width), width)
        load = begin(source_ref.at[:, at], held_ref, sems.at[0])
    else:
        told_ref, slot_ref = refs
    peers, rows = told_ref.shape[0] // 2, slot_ref.shape[1]
    blocks = [chosen_ref[b : b + 1, :] for b in range(chosen_ref.shape[0])]
    position = jnp.concatenate([x + b * block_len for b, x in enumerate(blocks)], axis=1)
    owner = lax.shift_right_logical(position, own_rows.bit_length() - 1)
    local = position & (own_rows - 1)
    peer = iota((peers, rows), 0)
    mine = (peer == owner).astype(F32)
    count = jnp.sum(mine, axis=1, keepdims=True)
    earlier = jnp.sum(jnp.where(peer < owner, count, 0.0), axis=0, keepdims=True).astype(jnp.int32)
    rank = iota((1, rows), 1) - earlier
    slot_ref[0:1, :] = owner * (cap * pieces) + rank
    slot_ref[1:2, :] = (owner ^ me_ref[0] if cross else owner) * (cap * back_pieces) + rank
    lane = iota((rows, rows), 0)
    hit = jnp.zeros((rows, rows), F32)
    for j in range(pieces):
        hit = hit + (lane == rank + j * cap).astype(F32)
    twice = iota((2 * peers, rows), 0)
    marked = jnp.where(twice == 2 * owner, local + 1, 0).astype(F32)
    asked = dot_nt(marked.astype(BF16), hit.astype(BF16)).astype(jnp.int32)
    told_ref[...] = jnp.where((twice & 1) == 1, jnp.concatenate(blocks, axis=1), asked)
    if cross:
        load.wait()
        begin(held_ref, cross_ref, sems.at[1]).wait()


def plane_columns(me, source, crossed, half):
    own_rows, width = source.shape
    part, count = width // half, half // 2

    def body(me_ref, source_ref, crossed_ref, *refs):
        outs, (held_ref, in_sem, out_sem) = refs[:count], refs[count:]
        low = me_ref[0] & (half - 1)
        plane = lax.shift_right_logical(low, half.bit_length() - 2)
        wide = count * part
        at = pl.ds(pl.multiple_of(plane * wide, wide), wide)
        loads = [
            begin(source_ref.at[:, at], held_ref.at[0], in_sem.at[0]),
            begin(crossed_ref, held_ref.at[1], in_sem.at[1]),
        ]
        copies = []
        for n, load in enumerate(loads):
            load.wait()
            for k in range(count):
                share = (low & (count - 1)) ^ k
                at = held_ref.at[n, :, pl.ds(pl.multiple_of(share * part, part), part)]
                rows = pl.ds(n * own_rows, own_rows)
                copies.append(begin(at, outs[k].at[rows], out_sem.at[n, k]))
        wait_all(copies)

    return call(
        body,
        [(shaped((2 * own_rows, part), BF16), HBM)] * count,
        [(me, SMEM), (source, HBM), (crossed, HBM)],
        "plane_columns",
        0,
        [
            scratch_like((2, own_rows, count * part), BF16),
            pltpu.SemaphoreType.DMA((2,)),
            pltpu.SemaphoreType.DMA((2, count)),
        ],
    )


def pick_matrix(cap, pieces, own_rows, requested):
    told, lanes = requested.shape
    peers = told // 2
    group = cap * pieces
    slots = peers * group
    peer = 2 * iota((peers, group, told), 0).reshape(slots, told)
    spread = dot(
        (peer == iota((slots, told), 1)).astype(BF16), requested.astype(F32).astype(BF16)
    )
    place = iota((peers, group, lanes), 1).reshape(slots, lanes)
    row = jnp.sum(
        jnp.where(place == iota((slots, lanes), 1), spread, 0.0), axis=1, keepdims=True
    ).astype(jnp.int32)
    piece = iota((peers, group, 1), 1).reshape(slots, 1)
    shift = jnp.zeros((slots, 1), jnp.int32)
    for j in range(1, pieces):
        shift = shift + jnp.where(piece >= j * cap, own_rows, 0)
    target = jnp.where(row > 0, row - 1 + shift, -1)
    return (target == iota((slots, pieces * own_rows), 1)).astype(BF16)


def pick_slots(cap, pieces, requested, source, after, name):
    own_rows, width = source.shape
    part = width // pieces
    slots = requested.shape[0] // 2 * cap * pieces
    columns = chunks_of(part)

    def body(requested_hbm, source_ref, *refs):
        out_ref, requested_ref, rows_ref, sent_ref, in_sem, out_sem = refs[len(after) :]
        asked = begin(requested_hbm, requested_ref, in_sem.at[len(columns), 0])
        loads = []
        for n, at in enumerate(columns):
            for j in range(pieces):
                wide = slice(j * part + at.start, j * part + at.stop)
                target = rows_ref.at[j * own_rows : (j + 1) * own_rows, at]
                loads.append(begin(source_ref.at[:, wide], target, in_sem.at[n, j]))
        asked.wait()
        pick = pick_matrix(cap, pieces, own_rows, requested_ref[...])
        stores = []
        for n, at in enumerate(columns):
            for load in loads[n * pieces : (n + 1) * pieces]:
                load.wait()
            sent_ref[:, at] = dot(pick, rows_ref[:, at]).astype(BF16)
            stores.append(begin(sent_ref.at[:, at], out_ref.at[:, at], out_sem.at[n]))
        for store in stores:
            store.wait()

    return call(
        body,
        [(shaped((slots, part), BF16), HBM)],
        [(requested, HBM), (source, HBM)] + [(x, HBM) for x in after],
        name,
        2 * slots * pieces * own_rows * part,
        [
            scratch_like(requested.shape, jnp.int32),
            scratch_like((pieces * own_rows, part), BF16),
            scratch_like((slots, part), BF16),
            pltpu.SemaphoreType.DMA((len(columns) + 1, pieces)),
            pltpu.SemaphoreType.DMA((len(columns),)),
        ],
    )[0]


def spread_columns(source, half):
    own_rows, width = source.shape
    part = width // half

    def body(source_ref, out_ref, held_ref, in_sem, out_sem):
        begin(source_ref, held_ref, in_sem).wait()
        copies = []
        for k in range(half):
            at = held_ref.at[:, k * part : (k + 1) * part]
            out = out_ref.at[k * own_rows : (k + 1) * own_rows]
            copies.append(begin(at, out, out_sem.at[k]))
        wait_all(copies)

    scratch = [
        scratch_like((own_rows, width), BF16),
        pltpu.SemaphoreType.DMA,
        pltpu.SemaphoreType.DMA((half,)),
    ]
    outs = [(shaped((half * own_rows, part), BF16), HBM)]
    return call(body, outs, [(source, HBM)], "spread_columns", 0, scratch)[0]


def cut_factors(factors, first):
    cuts = (slice(0, first), slice(first, factors.shape[0]))

    def body(factors_ref, *refs):
        outs, (held_ref, sems) = refs[:2], refs[2:]
        loads = [
            begin(factors_ref.at[at], held_ref.at[at], sems.at[0, n]) for n, at in enumerate(cuts)
        ]
        copies = []
        for n, at in enumerate(cuts):
            loads[n].wait()
            copies.append(begin(held_ref.at[at], outs[n], sems.at[1, n]))
        wait_all(copies)

    outs = [
        (shaped((at.stop - at.start,) + factors.shape[1:], BF16), HBM) for at in cuts
    ]
    scratch = [scratch_like(factors.shape, BF16), pltpu.SemaphoreType.DMA((2, 2))]
    return call(body, outs, [(factors, HBM)], "cut_factors", 0, scratch)


def pick_rows(me, half, own_rows, chosen, shares, after, name):
    peers, total = chosen.shape[0] // 2, chosen.shape[1]
    picks = total * half // peers
    part = shares[0].shape[1]
    block = half * own_rows
    batch = min(peers, 8)

    def body(me_ref, chosen_ref, *refs):
        refs = refs[len(after) :]
        parts, (out_ref, rows_ref, pick_ref, sent_ref, in_sem, out_sem) = (
            refs[: len(shares)],
            refs[len(shares) :],
        )
        loads = []
        for k in range(half):
            place = (me_ref[0] & (half - 1)) ^ k if len(parts) > 1 else k
            n, first = (k % len(parts), k // len(parts)) if len(parts) > 1 else (0, k)
            at = parts[n].at[first * own_rows : (first + 1) * own_rows]
            target = rows_ref.at[pl.ds(pl.multiple_of(place * own_rows, own_rows), own_rows)]
            loads.append(begin(at, target, in_sem.at[k]))
        block_at = lax.shift_right_logical(me_ref[0], half.bit_length() - 1)
        same = iota((picks, total), 0) + block_at * picks == iota((picks, total), 1)
        stores = []
        for first in range(0, peers, batch):
            for e in range(batch):
                wanted = chosen_ref[2 * (first + e) + 1 : 2 * (first + e) + 2, :]
                column = jnp.sum(jnp.where(same, wanted, 0), axis=1, keepdims=True)
                pick_ref[first // batch % 2, e * picks : (e + 1) * picks] = (
                    column == iota((picks, block), 1)
                ).astype(BF16)
            if first == 0:
                wait_all(loads)
            at = slice(first * picks, (first + batch) * picks)
            sent_ref[at] = dot(pick_ref[first // batch % 2], rows_ref[...]).astype(BF16)
            stores.append(begin(sent_ref.at[at], out_ref.at[at], out_sem.at[first // batch]))
        wait_all(stores)

    return call(
        body,
        [(shaped((peers * picks, part), BF16), HBM)],
        [(me, SMEM), (chosen, VMEM)] + [(x, HBM) for x in list(after) + list(shares)],
        name,
        2 * peers * picks * block * part,
        [
            scratch_like((block, part), BF16),
            scratch_like((2, batch * picks, block), BF16),
            scratch_like((peers * picks, part), BF16),
            pltpu.SemaphoreType.DMA((half,)),
            pltpu.SemaphoreType.DMA((peers // batch,)),
        ],
    )[0]


def place_rows(cap, pieces, own_rows, me, half, relative, chosen):
    peers, total = chosen.shape[0] // 2, chosen.shape[1]
    picks = total * half // peers
    group = cap * pieces

    def body(me_ref, chosen_ref, out_ref, pick_ref):
        low = me_ref[0] & (half - 1)
        block_at = lax.shift_right_logical(me_ref[0], half.bit_length() - 1)
        lane = iota((2 * peers, total), 1) - block_at * picks
        here = (lane >= 0) & (lane < picks)
        local = jnp.where(here, chosen_ref[...] - low * own_rows, own_rows)
        before = jnp.sum((local < 0).astype(F32), axis=1, keepdims=True).astype(jnp.int32)
        ranks = lane - before
        owned = jnp.where((local >= 0) & (local < own_rows), local + 1, 0)
        place = iota((group, total), 0)
        for e in range(peers):
            at = slice(2 * e + 1, 2 * e + 2)
            rank, mine = ranks[at], owned[at]
            column = jnp.zeros((group, 1), jnp.int32)
            for j in range(pieces):
                hit = jnp.where((place == rank + j * cap) & (rank >= 0) & (rank < cap), mine, 0)
                row = jnp.sum(hit, axis=1, keepdims=True)
                column = column + jnp.where(row > 0, row + j * own_rows, 0)
            place_at = (me_ref[0] ^ e if relative else e) * group
            pick_ref[pl.ds(pl.multiple_of(place_at, 8), group), :] = (
                column == iota((group, pieces * own_rows), 1) + 1
            ).astype(F32)
        out_ref[...] = jnp.transpose(pick_ref[...]).astype(BF16)

    return call(
        body,
        [(shaped((pieces * own_rows, peers * group), BF16), VMEM)],
        [(me, SMEM), (chosen, VMEM)],
        "place_rows",
        1 << 20,
        [scratch_like((peers * group, pieces * own_rows), F32)],
    )[0]


def sum_rows(pieces, placed, returned):
    count, (size, part) = len(returned), returned[0].shape
    own_rows = placed.shape[0] // pieces
    columns = chunks_of(part)

    def body(placed_hbm, *refs):
        slabs, (out_ref, place_ref, got_ref, sum_ref, in_sem, out_sem) = refs[:count], refs[count:]
        loads = [begin(placed_hbm, place_ref, in_sem.at[count])]
        for n, slab in enumerate(slabs):
            target = got_ref.at[n * size : (n + 1) * size]
            loads.append(begin(slab, target, in_sem.at[n]))
        wait_all(loads)
        stores = []
        for n, at in enumerate(columns):
            summed = dot(place_ref[...], got_ref[:, at]).astype(BF16)
            for j in range(pieces):
                wide = slice(j * part + at.start, j * part + at.stop)
                sum_ref[:, wide] = summed[j * own_rows : (j + 1) * own_rows]
                stores.append(
                    begin(sum_ref.at[:, wide], out_ref.at[:, wide], out_sem.at[n, j])
                )
        wait_all(stores)

    return call(
        body,
        [(shaped((own_rows, part * pieces), BF16), HBM)],
        [(placed, HBM)] + [(x, HBM) for x in returned],
        "sum_rows",
        2 * count * size * pieces * own_rows * part,
        [
            scratch_like(placed.shape, BF16),
            scratch_like((count * size, part), BF16),
            scratch_like((own_rows, part * pieces), BF16),
            pltpu.SemaphoreType.DMA((count + 1,)),
            pltpu.SemaphoreType.DMA((len(columns), pieces)),
        ],
    )[0]


def load_factor(order_ref, parts, m, target, sems):
    copies = []
    sides = [parts[0].at[m]]
    if len(parts) > 1:
        first = parts[1].shape[0]
        sides.append(parts[1].at[m] if m < first else parts[2].at[m - first])
    for n, side in enumerate(sides):
        count, rows, cols = side.shape
        place = order_ref[0] ^ n if len(parts) > 1 else 0
        start = pl.multiple_of(place * rows, rows)
        for i in range(count):
            at = target.at[pl.ds(start, rows), i * cols : (i + 1) * cols]
            copies.append(begin(side.at[i], at, sems.at[n, i]))
    return copies


def wait_all(copies):
    for copy in copies:
        copy.wait()


def place_matrix(cap, pieces, slots, slot):
    wide = jnp.concatenate([slot + j * cap for j in range(pieces)], axis=1)
    return (iota((slots, wide.shape[1]), 0) == wide).astype(BF16)


def load_rows(got_hbm, x_ref, sems):
    rows, depth = x_ref.shape[0] // NPHM, x_ref.shape[1]
    part = got_hbm.shape[1]
    shares = NPHM * depth // part
    picks = got_hbm.shape[0] * part // (NPHM * depth) // (rows // SELECTED)
    copies = []
    for n in range(got_hbm.shape[0] // picks):
        block, share = divmod(n, shares)
        a, start = share * part // depth, share * part % depth
        first = (block * NPHM + a) * picks
        at = x_ref.at[first : first + picks, start : start + part]
        copies.append(begin(got_hbm.at[n * picks : (n + 1) * picks], at, sems.at[n]))
    return copies


def load_slots(got_hbm, got_ref, sems):
    return [
        begin(got_hbm.at[:, at], got_ref.at[:, at], sems.at[n])
        for n, at in enumerate(chunks_of(got_ref.shape[1]))
    ]


def stack_rows(pieces, place, loads, got_ref, out_ref):
    part = got_ref.shape[1]
    rows, depth = out_ref.shape[0] // NPHM, out_ref.shape[1]
    for load, at in zip(loads, chunks_of(part)):
        load.wait()
        block = dot_tn(place, got_ref[:, at]).astype(BF16)
        for j in range(pieces):
            column = j * part + at.start
            a, start = column // depth, column % depth
            for n in range(rows // STRIP):
                first = (n * NPHM + a) * STRIP
                out_ref[first : first + STRIP, start : start + at.stop - at.start] = block[
                    j * rows + n * STRIP : j * rows + (n + 1) * STRIP
                ]


def store_parts(order_ref, source_ref, outs, sems):
    copies = []
    for n, out in enumerate(outs):
        size = out.shape[1]
        start = pl.multiple_of((order_ref[0] ^ n) * size if len(outs) > 1 else 0, size)
        copies.append(begin(source_ref.at[:, pl.ds(start, size)], out, sems.at[n]))
    return copies


STRIP = SELECTED


def rows_of(n, a):
    return slice((n * NPHM + a) * STRIP, (n * NPHM + a + 1) * STRIP)


def mix_in(mix_ref, m, y_ref, n):
    cols = y_ref.shape[1] // NPHM
    total = [jnp.zeros((STRIP, cols), F32)] * NPHM
    for a in range(NPHM):
        for i in range(NPHM):
            block = y_ref[rows_of(n, a), i * cols : (i + 1) * cols]
            for b in range(NPHM):
                total[b] = total[b] + mix_ref[m * 64 + i * 16 + a * 4 + b] * block
    return total


def mix_out(mix_ref, m, blocks, n, z_ref, offset=0):
    cols = blocks[0].shape[1]
    for a in range(NPHM):
        for i in range(NPHM):
            total = mix_ref[m * 64 + i * 16 + a * 4] * blocks[0]
            for b in range(1, NPHM):
                total = total + mix_ref[m * 64 + i * 16 + a * 4 + b] * blocks[b]
            z_ref[rows_of(n, a), offset + i * cols : offset + (i + 1) * cols] = total.astype(
                z_ref.dtype
            )


def blocks_of(d_ref, n):
    cols = d_ref.shape[1] // NPHM
    at = slice(n * STRIP, (n + 1) * STRIP)
    return [d_ref[at, b * cols : (b + 1) * cols].astype(F32) for b in range(NPHM)]


def forward_body(
    cap, pieces, sides, order_ref, mix_ref, slot_ref, got_hbm, *refs
):
    held = 2 if sides > 1 else 1
    parts, refs = refs[:held], refs[held:]
    x_outs, refs = refs[:sides], refs[sides:]
    yg_hbm, yu_hbm, act_hbm, slope_hbm, hid_hbm = refs[:5]
    got_ref, side_ref, x_ref, yg_ref, yu_ref, act_ref, slope_ref, hid_ref = refs[5:13]
    got_sem, side_sem, out_sem = refs[13:]
    loads = load_slots(got_hbm, got_ref, got_sem)
    sides_in = [
        load_factor(order_ref, parts, m, side_ref.at[m], side_sem.at[m]) for m in range(2)
    ]
    place = place_matrix(cap, pieces, got_ref.shape[0], slot_ref[0:1, :])
    stack_rows(pieces, place, loads, got_ref, x_ref)
    stores = store_parts(order_ref, x_ref, x_outs, out_sem)
    wait_all(sides_in[0])
    yg_ref[...] = dot(x_ref[...], side_ref[0])
    stores.append(begin(yg_ref, yg_hbm, out_sem.at[2]))
    wait_all(sides_in[1])
    yu_ref[...] = dot(x_ref[...], side_ref[1])
    stores.append(begin(yu_ref, yu_hbm, out_sem.at[3]))
    cols = yg_ref.shape[1] // NPHM
    for n in range(yg_ref.shape[0] // (NPHM * STRIP)):
        gates = mix_in(mix_ref, 0, yg_ref, n)
        ups = mix_in(mix_ref, 1, yu_ref, n)
        for b in range(NPHM):
            at = (slice(n * STRIP, (n + 1) * STRIP), slice(b * cols, (b + 1) * cols))
            sig = jax.nn.sigmoid(gates[b])
            act = gates[b] * sig
            act_ref[at] = act
            slope_ref[at] = ups[b] * (sig + act * (1.0 - sig))
            hid_ref[at] = act * ups[b]
    stores.append(begin(act_ref, act_hbm, out_sem.at[4]))
    stores.append(begin(slope_ref, slope_hbm, out_sem.at[5]))
    stores.append(begin(hid_ref, hid_hbm, out_sem.at[6]))
    wait_all(stores)


def backward_body(
    cap, pieces, slabs, sides, after, order_ref, mix_ref, slot_hbm, score_hbm, got_hbm, act_hbm, slope_hbm, hid_hbm,
    *refs,
):
    held = 3 if sides > 1 else 1
    parts, refs = refs[:held], refs[held + after :]
    backs, x_outs, refs = refs[:slabs], refs[slabs : slabs + sides], refs[slabs + sides :]
    y_hbm, d_hbm, inner_hbm = refs[:3]
    (
        down_ref, side_ref, x_ref, y_ref, d_ref, act_ref, slope_ref, hid_ref, z_ref, grad_ref,
        back_ref, inner_ref, slot_ref, score_ref, got_sem, side_sem, in_sem, out_sem, back_sem,
    ) = refs[3:]
    loads = load_rows(got_hbm, x_ref, got_sem)
    down_in = load_factor(order_ref, parts, 2, down_ref, side_sem.at[2])
    small_in = [
        begin(source, target, in_sem.at[n])
        for n, (source, target) in enumerate(((score_hbm, score_ref), (slot_hbm, slot_ref)))
    ]
    flat_in = [
        begin(source, target, in_sem.at[2 + n])
        for n, (source, target) in enumerate(
            ((act_hbm, act_ref), (slope_hbm, slope_ref), (hid_hbm, hid_ref))
        )
    ]
    hidden = d_ref.shape[2]
    sides_in = []
    for m in range(2):
        target = side_ref.at[:, m * hidden : (m + 1) * hidden]
        sides_in += load_factor(order_ref, parts, m, target, side_sem.at[m])
    wait_all(small_in)
    score = jnp.concatenate([score_ref[b : b + 1, :] for b in range(score_ref.shape[0])], axis=1)
    rows = score.shape[1]
    same = iota((rows, rows), 0) == iota((rows, rows), 1)
    score = jnp.sum(jnp.where(same, score.astype(F32), 0.0), axis=1, keepdims=True)
    cols = hidden // NPHM
    gates = jnp.broadcast_to(jax.nn.sigmoid(score / 64.0), (rows, cols))
    place = place_matrix(cap, pieces, back_ref.shape[0], slot_ref[1:2, :])
    strips = rows // STRIP
    tall = NPHM * STRIP
    wait_all(loads)
    stores = store_parts(order_ref, x_ref, x_outs, out_sem)
    wait_all(down_in)
    for n in range(strips):
        y_ref[n * tall : (n + 1) * tall] = dot(x_ref[n * tall : (n + 1) * tall], down_ref[...])
    stores.append(begin(y_ref, y_hbm, out_sem.at[2]))
    wait_all(flat_in)
    wait_all(sides_in)
    for n in range(strips):
        down = mix_in(mix_ref, 2, y_ref, n)
        strip = slice(n * STRIP, (n + 1) * STRIP)
        gate = gates[strip]
        inner = jnp.zeros((STRIP, cols), F32)
        d_gate, d_up = [], []
        for b in range(NPHM):
            at = (strip, slice(b * cols, (b + 1) * cols))
            inner = inner + hid_ref[at] * down[b]
            hidden_grad = gate * down[b]
            d_gate.append(hidden_grad * slope_ref[at])
            d_up.append(hidden_grad * act_ref[at])
            d_ref[(0,) + at] = d_gate[b].astype(BF16)
            d_ref[(1,) + at] = d_up[b].astype(BF16)
            d_ref[(2,) + at] = (hid_ref[at] * gate).astype(BF16)
        inner_ref[strip] = inner
        mix_out(mix_ref, 0, d_gate, n, z_ref)
        mix_out(mix_ref, 1, d_up, n, z_ref, hidden)
        at = slice(n * tall, (n + 1) * tall)
        grad_ref[at] = dot_nt(z_ref[at], side_ref[...]).astype(BF16)
    stores.append(begin(d_ref, d_hbm, out_sem.at[3]))
    stores.append(begin(inner_ref, inner_hbm, out_sem.at[4]))
    part, depth = back_ref.shape[1], x_ref.shape[1]
    for k, at in enumerate(chunks_of(part)):
        blocks = []
        for j in range(pieces):
            column = j * part + at.start
            a, start = column // depth, column % depth
            wide = slice(start, start + at.stop - at.start)
            blocks += [grad_ref[rows_of(n, a), wide] for n in range(strips)]
        back_ref[:, at] = dot(place, jnp.concatenate(blocks, axis=0)).astype(BF16)
        for n, out in enumerate(backs):
            size = out.shape[0]
            source = back_ref.at[n * size : (n + 1) * size, at]
            stores.append(begin(source, out.at[:, at], back_sem.at[n, k]))
    wait_all(stores)


def factor_body(count_groups, after, mix_ref, *refs):
    rows_in, refs = refs[: 3 * count_groups], refs[3 * count_groups + after :]
    out_hbm, x_ref, g_ref, d_ref, z_ref, sum_ref, in_sem, out_sem = refs
    loads = []
    for n in range(count_groups):
        for k, target in enumerate((x_ref, g_ref, d_ref)):
            loads.append(begin(rows_in[3 * n + k], target.at[n], in_sem.at[n, k]))
    stores = []
    cols = out_hbm.shape[3]
    wait_all(loads)
    for m in (2, 0, 1):
        for n in range(count_groups):
            for strip in range(d_ref.shape[2] // STRIP):
                blocks = blocks_of(d_ref.at[n, m], strip)
                mix_out(mix_ref, m, blocks, strip, z_ref.at[n])
        left = g_ref if m == 2 else x_ref
        sum_ref[m] = sum(dot_tn(left[n], z_ref[n]) for n in range(count_groups))
        for i in range(NPHM):
            at = sum_ref.at[m, :, i * cols : (i + 1) * cols]
            stores.append(begin(at, out_hbm.at[m, i], out_sem.at[m, i]))
    wait_all(stores)


def mix_grad_body(yg_hbm, yu_hbm, yd_hbm, d_hbm, *refs):
    out_ref, y_ref, d_ref, sems = refs[-4:]
    loads = [begin(d_hbm, d_ref, sems.at[3])]
    for m, source in enumerate((yg_hbm, yu_hbm, yd_hbm)):
        loads.append(begin(source, y_ref.at[m], sems.at[m]))
    wait_all(loads)
    rows, cols = d_ref.shape[1], d_ref.shape[2] // NPHM
    for m in range(3):
        for a in range(NPHM):
            for i in range(NPHM):
                at = slice(i * cols, (i + 1) * cols)
                strips = range(rows // STRIP)
                block = jnp.concatenate([y_ref[m, rows_of(n, a), at] for n in strips], axis=0)
                for b in range(NPHM):
                    at = m * 64 + i * 16 + a * 4 + b
                    other = d_ref[m, :, b * cols : (b + 1) * cols].astype(F32)
                    out_ref[at : at + 1, :] = jnp.sum(block * other, axis=0, keepdims=True)


def shards(tokens, cotangent, factors, mix, selection, scores):
    peers = lax.axis_size("exp")
    groups = lax.axis_size("seq")
    own_rows, width = tokens.shape
    _, weights, count, depth_own, cols = factors.shape
    depth = depth_own * groups
    hidden = count * cols
    cap = 3 * own_rows // (2 * peers)
    pieces = 1
    while (cap * pieces) % 8:
        pieces *= 2
    slots = peers * cap * pieces
    part = width // pieces
    steps = len(chunks_of(part))
    back_pieces = 2 * pieces if selection.shape[1] * 8 == peers else pieces
    back_part = width // back_pieces
    back_slots = peers * cap * back_pieces
    back_steps = len(chunks_of(back_part))
    block_len = peers * SELECTED
    rows = selection.shape[1] * selection.shape[2]
    stacked = count * rows
    swap = groups == 2
    pair = [(0, 1), (1, 0)]
    mixing = mix.reshape(-1)
    dma = pltpu.SemaphoreType.DMA

    def across(array):
        return lax.ppermute(array, "seq", pair)

    half = peers // selection.shape[1]
    direct = half == 8
    me = lax.axis_index("exp").astype(jnp.int32).reshape(1)
    group = lax.axis_index("seq").astype(jnp.int32).reshape(1)
    halves = [list(range(h, h + half)) for h in range(0, peers, half)]
    if swap:
        cuts = [across(x) for x in cut_factors(factors[0], 2)]
        factor_parts = [factors[0]] + cuts
        sides = 2
    else:
        cuts = []
        factor_parts = [lax.all_gather(factors, "seq", axis=3, tiled=True)[0]]
        sides = 1
    sides_in = [(x, HBM) for x in factor_parts]
    cross = [(shaped((own_rows, width // 2), BF16), HBM)] if direct else []
    told, slot, *crossed = call(
        functools.partial(front_body, cap, pieces, back_pieces, own_rows, block_len, half, direct),
        [(shaped((2 * peers, rows), jnp.int32), VMEM), (shaped((2, rows), jnp.int32), VMEM)] + cross,
        [(me, SMEM), (selection[0], VMEM)] + ([(cotangent, HBM)] if direct else []),
        "wanted_rows",
        1 << 20,
        [scratch_like((own_rows, width // 2), BF16), dma((2,))] if direct else [],
    )
    if direct:
        crossed = [lax.ppermute(crossed[0], "exp", [(n, n ^ (half // 2)) for n in range(peers)])]
    chosen = lax.all_to_all(told, "exp", split_axis=0, concat_axis=0, tiled=True)

    def to_peers(array):
        array = array.reshape(peers, -1, array.shape[1])
        array = lax.all_to_all(array, "exp", split_axis=0, concat_axis=0, tiled=True)
        return array.reshape(-1, array.shape[2])

    got_rows = to_peers(pick_slots(cap, pieces, chosen, tokens, crossed, "pick_tokens"))
    if direct:
        shares = plane_columns(me, cotangent, crossed[0], half)
        shares = [shares[0]] + [
            lax.ppermute(shares[k], "exp", [(n, n ^ k) for n in range(peers)])
            for k in range(1, half // 2)
        ]
    else:
        array = spread_columns(cotangent, half).reshape(half, own_rows, -1)
        array = lax.all_to_all(
            array, "exp", split_axis=0, concat_axis=0, axis_index_groups=halves, tiled=True
        )
        shares = [array.reshape(half * own_rows, -1)]
    picked = pick_rows(me, half, own_rows, chosen, shares, cuts[:1], "pick_cotangent")
    got_grads = to_peers(picked)
    placed = place_rows(cap, back_pieces, own_rows, me, half, direct, chosen)
    gate = jax.nn.sigmoid(scores[0].reshape(-1).astype(F32) / 64.0)

    product = 2 * stacked * depth * hidden
    split = [(shaped((stacked, depth // sides), BF16), HBM)] * sides
    mixed = (shaped((stacked, hidden), F32), HBM)
    flat = (shaped((rows, hidden), F32), HBM)
    back_scratch = scratch_like((slots, part), BF16)
    pieces_in = got_grads.shape[0] // SELECTED
    stack_scratch = scratch_like((stacked, depth), BF16)
    mixed_scratch = scratch_like((stacked, hidden), F32)
    low_scratch = scratch_like((stacked, hidden), BF16)
    flat_scratch = scratch_like((rows, hidden), F32)
    outs = call(
        functools.partial(forward_body, cap, pieces, sides),
        split + [mixed, mixed, flat, flat, flat],
        [(group, SMEM), (mixing, SMEM), (slot, VMEM), (got_rows, HBM)] + sides_in[:2],
        "forward",
        2 * product,
        [back_scratch, scratch_like((2, depth, hidden), BF16), stack_scratch, mixed_scratch, mixed_scratch]
        + [flat_scratch] * 3
        + [dma((steps,)), dma((2, sides, count)), dma((7,))],
    )
    x_parts, (y_gate, y_up, act, slope, hid) = outs[:sides], outs[sides:]
    x_rows = [x_parts[0]] + [across(x) for x in x_parts[1:]]
    after = x_rows[1:]
    slabs = peers if direct else 1
    outs = call(
        functools.partial(backward_body, cap, back_pieces, slabs, sides, len(after)),
        [(shaped((back_slots // slabs, back_part), BF16), HBM)] * slabs
        + split
        + [mixed, (shaped((weights, rows, hidden), BF16), HBM), (shaped((rows, cols), F32), HBM)],
        [(group, SMEM), (mixing, SMEM), (slot, HBM), (scores[0], HBM), (got_grads, HBM)]
        + [(x, HBM) for x in (act, slope, hid)]
        + sides_in
        + [(x, HBM) for x in after],
        "backward",
        3 * product,
        [scratch_like((depth, hidden), BF16), scratch_like((depth, 2 * hidden), BF16)]
        + [stack_scratch, mixed_scratch, scratch_like((weights, rows, hidden), BF16)]
        + [flat_scratch] * 3
        + [scratch_like((stacked, 2 * hidden), BF16), stack_scratch]
        + [scratch_like((back_slots, back_part), BF16)]
        + [scratch_like((rows, cols), F32), scratch_like(slot.shape, jnp.int32)]
        + [scratch_like(scores.shape[1:], jnp.int32)]
        + [dma((pieces_in,)), dma((weights, sides, count)), dma((5,)), dma((5,))]
        + [dma((slabs, back_steps))],
    )
    backs, outs = outs[:slabs], outs[slabs:]
    g_parts, (y_down, d_own, inner) = outs[:sides], outs[sides:]
    if direct:
        order = [k for n in range(half) for k in (half + n, n)][:1]
        order += [k for n in range(1, half) for k in (n, half + n)]
        moved = {0: backs[0]}
        for k in order:
            moved[k] = lax.ppermute(backs[k], "exp", [(n, n ^ k) for n in range(peers)])
        returned = [moved[k] for k in range(peers)]
        soon, late = [moved[k] for k in order[:3]], [moved[k] for k in order[:11]]
    else:
        returned, soon, late = [to_peers(backs[0])], [], []

    d_rows = [d_own] + [across(d_own) for _ in x_parts[1:]]
    g_rows = [g_parts[0]] + [across(x) for x in g_parts[1:]]
    depth_here = depth // sides
    factor_grad = call(
        functools.partial(factor_body, sides, len(late)),
        [(shaped((weights, count, depth_here, cols), F32), HBM)],
        [(mixing, SMEM)]
        + [(x, HBM) for n in range(sides) for x in (x_rows[n], g_rows[n], d_rows[n])]
        + [(x, HBM) for x in late],
        "factor_grad",
        3 * product,
        [scratch_like((sides, stacked, depth_here), BF16)] * 2
        + [
            scratch_like((sides, weights, rows, hidden), BF16),
            scratch_like((sides, stacked, hidden), BF16),
            scratch_like((weights, depth_here, hidden), F32),
            dma((sides, 3)),
            dma((weights, count)),
        ],
    )[0]
    mix_rows = call(
        mix_grad_body,
        [(shaped((mixing.size, cols), F32), VMEM)],
        [(x, HBM) for x in [y_gate, y_up, y_down, d_own] + soon],
        "mix_partials",
        weights * 64 * 2 * rows * cols,
        [
            scratch_like((weights, stacked, hidden), F32),
            scratch_like((weights, rows, hidden), BF16),
            dma((4,)),
        ],
    )[0]
    mix_part = jnp.sum(mix_rows, axis=1).reshape(mix.shape)
    if swap:
        mix_grad = mix_part + across(mix_part)
    else:
        factor_grad = lax.psum_scatter(
            factor_grad.astype(BF16), "seq", scatter_dimension=2, tiled=True
        ).astype(F32)
        mix_grad = lax.psum(mix_part, "seq")
    gate_grad = (jnp.sum(inner, axis=1) * gate * (1.0 - gate)).reshape(selection.shape)
    token_grad = sum_rows(back_pieces, placed, returned)
    return token_grad, factor_grad[None], mix_grad, gate_grad


def solution(mesh):
    return jax.shard_map(
        shards,
        mesh=mesh,
        in_specs=(
            P(("seq", "exp"), None),
            P(("seq", "exp"), None),
            P("exp", None, None, "seq", None),
            P("exp", None, None, None, None),
            P("exp", "seq", None),
            P("exp", "seq", None),
        ),
        out_specs=(
            P(("seq", "exp"), None),
            P("exp", None, None, "seq", None),
            P("exp", None, None, None, None),
            P("exp", "seq", None),
        ),
        check_vma=False,
    )
```

```python
import functools

import jax
import jax.numpy as jnp
from jax import lax
from jax.experimental import pallas as pl
from jax.experimental.pallas import tpu as pltpu
from jax.sharding import PartitionSpec as P

SELECTED = 64
NPHM = 4
VMEM_LIMIT = 63 * 1024 * 1024
F32 = jnp.float32
BF16 = jnp.bfloat16


def iota(shape, dim):
    return lax.broadcasted_iota(jnp.int32, shape, dim)


def dot(left, right):
    return jnp.dot(left, right, preferred_element_type=F32)


def dot_tn(left, right):
    return lax.dot_general(left, right, (((0,), (0,)), ((), ())), preferred_element_type=F32)


def dot_nt(left, right):
    return lax.dot_general(left, right, (((1,), (1,)), ((), ())), preferred_element_type=F32)


HBM = pl.BlockSpec(memory_space=pltpu.HBM)
VMEM = pl.BlockSpec(memory_space=pltpu.VMEM)
SMEM = pl.BlockSpec(memory_space=pltpu.SMEM)


def call(body, outs, ins, name, flops, scratch=()):
    moved = sum(x.size * x.dtype.itemsize for x, _ in list(ins) + list(outs))
    return pl.pallas_call(
        body,
        out_shape=[x for x, _ in outs],
        in_specs=[place for _, place in ins],
        out_specs=[place for _, place in outs],
        scratch_shapes=list(scratch),
        compiler_params=pltpu.CompilerParams(vmem_limit_bytes=VMEM_LIMIT),
        cost_estimate=pl.CostEstimate(flops=flops, bytes_accessed=moved, transcendentals=0),
        name=name,
    )(*[x for x, _ in ins])


def begin(source, target, sem):
    copy = pltpu.make_async_copy(source, target, sem)
    copy.start()
    return copy


def shaped(shape, dtype):
    return jax.ShapeDtypeStruct(shape, dtype)


def scratch_like(shape, dtype):
    return pltpu.VMEM(shape, dtype)


def chunks_of(part):
    chunk = min(part, 512)
    return [slice(c * chunk, (c + 1) * chunk) for c in range(part // chunk)]


def front_body(cap, pieces, own_rows, block_len, half, cross, me_ref, chosen_ref, *refs):
    if cross:
        source_ref, told_ref, slot_ref, cross_ref, held_ref, sems = refs
        width = cross_ref.shape[1]
        plane = lax.shift_right_logical(me_ref[0] & (half - 1), half.bit_length() - 2)
        at = pl.ds(pl.multiple_of((1 - plane) * width, width), width)
        load = begin(source_ref.at[:, at], held_ref, sems.at[0])
    else:
        told_ref, slot_ref = refs
    peers, rows = told_ref.shape[0] // 2, slot_ref.shape[1]
    blocks = [chosen_ref[b : b + 1, :] for b in range(chosen_ref.shape[0])]
    position = jnp.concatenate([x + b * block_len for b, x in enumerate(blocks)], axis=1)
    owner = lax.shift_right_logical(position, own_rows.bit_length() - 1)
    local = position & (own_rows - 1)
    peer = iota((peers, rows), 0)
    mine = (peer == owner).astype(F32)
    count = jnp.sum(mine, axis=1, keepdims=True)
    earlier = jnp.sum(jnp.where(peer < owner, count, 0.0), axis=0, keepdims=True).astype(jnp.int32)
    rank = iota((1, rows), 1) - earlier
    slot_ref[...] = owner * (cap * pieces) + rank
    lane = iota((rows, rows), 0)
    hit = jnp.zeros((rows, rows), F32)
    for j in range(pieces):
        hit = hit + (lane == rank + j * cap).astype(F32)
    twice = iota((2 * peers, rows), 0)
    marked = jnp.where(twice == 2 * owner, local + 1, 0).astype(F32)
    asked = dot_nt(marked.astype(BF16), hit.astype(BF16)).astype(jnp.int32)
    told_ref[...] = jnp.where((twice & 1) == 1, jnp.concatenate(blocks, axis=1), asked)
    if cross:
        load.wait()
        begin(held_ref, cross_ref, sems.at[1]).wait()


def plane_columns(me, source, crossed, half, after):
    own_rows, width = source.shape
    part, count = width // half, half // 2

    def body(me_ref, source_ref, crossed_ref, *refs):
        refs = refs[len(after) :]
        outs, (held_ref, in_sem, out_sem) = refs[:count], refs[count:]
        low = me_ref[0] & (half - 1)
        plane = lax.shift_right_logical(low, half.bit_length() - 2)
        wide = count * part
        at = pl.ds(pl.multiple_of(plane * wide, wide), wide)
        loads = [
            begin(source_ref.at[:, at], held_ref.at[0], in_sem.at[0]),
            begin(crossed_ref, held_ref.at[1], in_sem.at[1]),
        ]
        copies = []
        for n, load in enumerate(loads):
            load.wait()
            for k in range(count):
                share = (low & (count - 1)) ^ k
                at = held_ref.at[n, :, pl.ds(pl.multiple_of(share * part, part), part)]
                rows = pl.ds(n * own_rows, own_rows)
                copies.append(begin(at, outs[k].at[rows], out_sem.at[n, k]))
        wait_all(copies)

    return call(
        body,
        [(shaped((2 * own_rows, part), BF16), HBM)] * count,
        [(me, SMEM), (source, HBM), (crossed, HBM)] + [(x, HBM) for x in after],
        "plane_columns",
        0,
        [
            scratch_like((2, own_rows, count * part), BF16),
            pltpu.SemaphoreType.DMA((2,)),
            pltpu.SemaphoreType.DMA((2, count)),
        ],
    )


def pick_matrix(cap, pieces, own_rows, requested):
    told, lanes = requested.shape
    peers = told // 2
    group = cap * pieces
    slots = peers * group
    peer = 2 * iota((peers, group, told), 0).reshape(slots, told)
    spread = dot(
        (peer == iota((slots, told), 1)).astype(BF16), requested.astype(F32).astype(BF16)
    )
    place = iota((peers, group, lanes), 1).reshape(slots, lanes)
    row = jnp.sum(
        jnp.where(place == iota((slots, lanes), 1), spread, 0.0), axis=1, keepdims=True
    ).astype(jnp.int32)
    piece = iota((peers, group, 1), 1).reshape(slots, 1)
    shift = jnp.zeros((slots, 1), jnp.int32)
    for j in range(1, pieces):
        shift = shift + jnp.where(piece >= j * cap, own_rows, 0)
    target = jnp.where(row > 0, row - 1 + shift, -1)
    return (target == iota((slots, pieces * own_rows), 1)).astype(BF16)


def pick_slots(cap, pieces, requested, source, after, name):
    own_rows, width = source.shape
    part = width // pieces
    slots = requested.shape[0] // 2 * cap * pieces
    columns = chunks_of(part)

    def body(requested_hbm, source_ref, *refs):
        out_ref, requested_ref, rows_ref, sent_ref, in_sem, out_sem = refs[len(after) :]
        asked = begin(requested_hbm, requested_ref, in_sem.at[len(columns), 0])
        loads = []
        for n, at in enumerate(columns):
            for j in range(pieces):
                wide = slice(j * part + at.start, j * part + at.stop)
                target = rows_ref.at[j * own_rows : (j + 1) * own_rows, at]
                loads.append(begin(source_ref.at[:, wide], target, in_sem.at[n, j]))
        asked.wait()
        pick = pick_matrix(cap, pieces, own_rows, requested_ref[...])
        stores = []
        for n, at in enumerate(columns):
            for load in loads[n * pieces : (n + 1) * pieces]:
                load.wait()
            sent_ref[:, at] = dot(pick, rows_ref[:, at]).astype(BF16)
            stores.append(begin(sent_ref.at[:, at], out_ref.at[:, at], out_sem.at[n]))
        for store in stores:
            store.wait()

    return call(
        body,
        [(shaped((slots, part), BF16), HBM)],
        [(requested, HBM), (source, HBM)] + [(x, HBM) for x in after],
        name,
        2 * slots * pieces * own_rows * part,
        [
            scratch_like(requested.shape, jnp.int32),
            scratch_like((pieces * own_rows, part), BF16),
            scratch_like((slots, part), BF16),
            pltpu.SemaphoreType.DMA((len(columns) + 1, pieces)),
            pltpu.SemaphoreType.DMA((len(columns),)),
        ],
    )[0]


def spread_columns(source, half):
    own_rows, width = source.shape
    part = width // half

    def body(source_ref, out_ref, held_ref, in_sem, out_sem):
        begin(source_ref, held_ref, in_sem).wait()
        copies = []
        for k in range(half):
            at = held_ref.at[:, k * part : (k + 1) * part]
            out = out_ref.at[k * own_rows : (k + 1) * own_rows]
            copies.append(begin(at, out, out_sem.at[k]))
        wait_all(copies)

    scratch = [
        scratch_like((own_rows, width), BF16),
        pltpu.SemaphoreType.DMA,
        pltpu.SemaphoreType.DMA((half,)),
    ]
    outs = [(shaped((half * own_rows, part), BF16), HBM)]
    return call(body, outs, [(source, HBM)], "spread_columns", 0, scratch)[0]


def pick_rows(me, half, own_rows, chosen, shares, after, name):
    peers, total = chosen.shape[0] // 2, chosen.shape[1]
    picks = total * half // peers
    part = shares[0].shape[1]
    block = half * own_rows
    batch = min(peers, 8)

    def body(me_ref, chosen_ref, *refs):
        refs = refs[len(after) :]
        parts, (out_ref, rows_ref, pick_ref, sent_ref, in_sem, out_sem) = (
            refs[: len(shares)],
            refs[len(shares) :],
        )
        loads = []
        for k in range(half):
            place = (me_ref[0] & (half - 1)) ^ k if len(parts) > 1 else k
            n, first = (k % len(parts), k // len(parts)) if len(parts) > 1 else (0, k)
            at = parts[n].at[first * own_rows : (first + 1) * own_rows]
            target = rows_ref.at[pl.ds(pl.multiple_of(place * own_rows, own_rows), own_rows)]
            loads.append(begin(at, target, in_sem.at[k]))
        block_at = lax.shift_right_logical(me_ref[0], half.bit_length() - 1)
        same = iota((picks, total), 0) + block_at * picks == iota((picks, total), 1)
        stores = []
        for first in range(0, peers, batch):
            for e in range(batch):
                wanted = chosen_ref[2 * (first + e) + 1 : 2 * (first + e) + 2, :]
                column = jnp.sum(jnp.where(same, wanted, 0), axis=1, keepdims=True)
                pick_ref[first // batch % 2, e * picks : (e + 1) * picks] = (
                    column == iota((picks, block), 1)
                ).astype(BF16)
            if first == 0:
                wait_all(loads)
            at = slice(first * picks, (first + batch) * picks)
            sent_ref[at] = dot(pick_ref[first // batch % 2], rows_ref[...]).astype(BF16)
            stores.append(begin(sent_ref.at[at], out_ref.at[at], out_sem.at[first // batch]))
        wait_all(stores)

    return call(
        body,
        [(shaped((peers * picks, part), BF16), HBM)],
        [(me, SMEM), (chosen, VMEM)] + [(x, HBM) for x in list(after) + list(shares)],
        name,
        2 * peers * picks * block * part,
        [
            scratch_like((block, part), BF16),
            scratch_like((2, batch * picks, block), BF16),
            scratch_like((peers * picks, part), BF16),
            pltpu.SemaphoreType.DMA((half,)),
            pltpu.SemaphoreType.DMA((peers // batch,)),
        ],
    )[0]


def place_rows(cap, pieces, own_rows, me, half, chosen):
    peers, total = chosen.shape[0] // 2, chosen.shape[1]
    picks = total * half // peers
    group = cap * pieces

    def body(me_ref, chosen_ref, out_ref, pick_ref):
        low = me_ref[0] & (half - 1)
        block_at = lax.shift_right_logical(me_ref[0], half.bit_length() - 1)
        lane = iota((2 * peers, total), 1) - block_at * picks
        here = (lane >= 0) & (lane < picks)
        local = jnp.where(here, chosen_ref[...] - low * own_rows, own_rows)
        before = jnp.sum((local < 0).astype(F32), axis=1, keepdims=True).astype(jnp.int32)
        ranks = lane - before
        owned = jnp.where((local >= 0) & (local < own_rows), local + 1, 0)
        place = iota((group, total), 0)
        for e in range(peers):
            at = slice(2 * e + 1, 2 * e + 2)
            rank, mine = ranks[at], owned[at]
            column = jnp.zeros((group, 1), jnp.int32)
            for j in range(pieces):
                hit = jnp.where((place == rank + j * cap) & (rank >= 0) & (rank < cap), mine, 0)
                row = jnp.sum(hit, axis=1, keepdims=True)
                column = column + jnp.where(row > 0, row + j * own_rows, 0)
            pick_ref[e * group : (e + 1) * group] = (
                column == iota((group, pieces * own_rows), 1) + 1
            ).astype(F32)
        out_ref[...] = jnp.transpose(pick_ref[...]).astype(BF16)

    return call(
        body,
        [(shaped((pieces * own_rows, peers * group), BF16), VMEM)],
        [(me, SMEM), (chosen, VMEM)],
        "place_rows",
        1 << 20,
        [scratch_like((peers * group, pieces * own_rows), F32)],
    )[0]


def sum_rows(pieces, placed, returned):
    slots, part = returned.shape
    own_rows = placed.shape[0] // pieces
    columns = chunks_of(part)

    def body(placed_hbm, returned_ref, out_ref, place_ref, got_ref, sum_ref, in_sem, out_sem):
        first = begin(placed_hbm, place_ref, in_sem.at[len(columns)])
        loads = [
            begin(returned_ref.at[:, at], got_ref.at[:, at], in_sem.at[n])
            for n, at in enumerate(columns)
        ]
        first.wait()
        stores = []
        for n, at in enumerate(columns):
            loads[n].wait()
            summed = dot(place_ref[...], got_ref[:, at]).astype(BF16)
            for j in range(pieces):
                wide = slice(j * part + at.start, j * part + at.stop)
                sum_ref[:, wide] = summed[j * own_rows : (j + 1) * own_rows]
                stores.append(
                    begin(sum_ref.at[:, wide], out_ref.at[:, wide], out_sem.at[n, j])
                )
        wait_all(stores)

    return call(
        body,
        [(shaped((own_rows, part * pieces), BF16), HBM)],
        [(placed, HBM), (returned, HBM)],
        "sum_rows",
        2 * slots * pieces * own_rows * part,
        [
            scratch_like(placed.shape, BF16),
            scratch_like((slots, part), BF16),
            scratch_like((own_rows, part * pieces), BF16),
            pltpu.SemaphoreType.DMA((len(columns) + 1,)),
            pltpu.SemaphoreType.DMA((len(columns), pieces)),
        ],
    )[0]


def load_factor(order_ref, parts, m, target, sems):
    copies = []
    sides = [part.at[m] for part in parts]
    for n, side in enumerate(sides):
        count, rows, cols = side.shape
        place = order_ref[0] ^ n if len(parts) > 1 else 0
        start = pl.multiple_of(place * rows, rows)
        for i in range(count):
            at = target.at[pl.ds(start, rows), i * cols : (i + 1) * cols]
            copies.append(begin(side.at[i], at, sems.at[n, i]))
    return copies


def wait_all(copies):
    for copy in copies:
        copy.wait()


def place_matrix(cap, pieces, slots, slot):
    wide = jnp.concatenate([slot + j * cap for j in range(pieces)], axis=1)
    return (iota((slots, wide.shape[1]), 0) == wide).astype(BF16)


def load_rows(got_hbm, x_ref, sems):
    rows, depth = x_ref.shape[0] // NPHM, x_ref.shape[1]
    part = got_hbm.shape[1]
    shares = NPHM * depth // part
    picks = got_hbm.shape[0] * part // (NPHM * depth) // (rows // SELECTED)
    copies = []
    for n in range(got_hbm.shape[0] // picks):
        block, share = divmod(n, shares)
        a, start = share * part // depth, share * part % depth
        first = (block * NPHM + a) * picks
        at = x_ref.at[first : first + picks, start : start + part]
        copies.append(begin(got_hbm.at[n * picks : (n + 1) * picks], at, sems.at[n]))
    return copies


def load_slots(got_hbm, got_ref, sems):
    return [
        begin(got_hbm.at[:, at], got_ref.at[:, at], sems.at[n])
        for n, at in enumerate(chunks_of(got_ref.shape[1]))
    ]


def stack_rows(pieces, place, loads, got_ref, out_ref):
    part = got_ref.shape[1]
    rows, depth = out_ref.shape[0] // NPHM, out_ref.shape[1]
    for load, at in zip(loads, chunks_of(part)):
        load.wait()
        block = dot_tn(place, got_ref[:, at]).astype(BF16)
        for j in range(pieces):
            column = j * part + at.start
            a, start = column // depth, column % depth
            for n in range(rows // STRIP):
                first = (n * NPHM + a) * STRIP
                out_ref[first : first + STRIP, start : start + at.stop - at.start] = block[
                    j * rows + n * STRIP : j * rows + (n + 1) * STRIP
                ]


def store_parts(order_ref, source_ref, outs, sems):
    copies = []
    for n, out in enumerate(outs):
        size = out.shape[1]
        start = pl.multiple_of((order_ref[0] ^ n) * size if len(outs) > 1 else 0, size)
        copies.append(begin(source_ref.at[:, pl.ds(start, size)], out, sems.at[n]))
    return copies


STRIP = SELECTED


def rows_of(n, a):
    return slice((n * NPHM + a) * STRIP, (n * NPHM + a + 1) * STRIP)


def mix_in(mix_ref, m, y_ref, n):
    cols = y_ref.shape[1] // NPHM
    total = [jnp.zeros((STRIP, cols), F32)] * NPHM
    for a in range(NPHM):
        for i in range(NPHM):
            block = y_ref[rows_of(n, a), i * cols : (i + 1) * cols]
            for b in range(NPHM):
                total[b] = total[b] + mix_ref[m * 64 + i * 16 + a * 4 + b] * block
    return total


def mix_out(mix_ref, m, blocks, n, z_ref, offset=0):
    cols = blocks[0].shape[1]
    for a in range(NPHM):
        for i in range(NPHM):
            total = mix_ref[m * 64 + i * 16 + a * 4] * blocks[0]
            for b in range(1, NPHM):
                total = total + mix_ref[m * 64 + i * 16 + a * 4 + b] * blocks[b]
            z_ref[rows_of(n, a), offset + i * cols : offset + (i + 1) * cols] = total.astype(
                z_ref.dtype
            )


def blocks_of(d_ref, n):
    cols = d_ref.shape[1] // NPHM
    at = slice(n * STRIP, (n + 1) * STRIP)
    return [d_ref[at, b * cols : (b + 1) * cols].astype(F32) for b in range(NPHM)]


def forward_body(
    cap, pieces, sides, order_ref, mix_ref, slot_ref, got_hbm, *refs
):
    parts, refs = refs[:sides], refs[sides:]
    x_outs, refs = refs[:sides], refs[sides:]
    yg_hbm, yu_hbm, act_hbm, slope_hbm, hid_hbm = refs[:5]
    got_ref, side_ref, x_ref, yg_ref, yu_ref, act_ref, slope_ref, hid_ref = refs[5:13]
    got_sem, side_sem, out_sem = refs[13:]
    loads = load_slots(got_hbm, got_ref, got_sem)
    sides_in = [
        load_factor(order_ref, parts, m, side_ref.at[m], side_sem.at[m]) for m in range(2)
    ]
    place = place_matrix(cap, pieces, got_ref.shape[0], slot_ref[...])
    stack_rows(pieces, place, loads, got_ref, x_ref)
    stores = store_parts(order_ref, x_ref, x_outs, out_sem)
    wait_all(sides_in[0])
    yg_ref[...] = dot(x_ref[...], side_ref[0])
    stores.append(begin(yg_ref, yg_hbm, out_sem.at[2]))
    wait_all(sides_in[1])
    yu_ref[...] = dot(x_ref[...], side_ref[1])
    stores.append(begin(yu_ref, yu_hbm, out_sem.at[3]))
    cols = yg_ref.shape[1] // NPHM
    for n in range(yg_ref.shape[0] // (NPHM * STRIP)):
        gates = mix_in(mix_ref, 0, yg_ref, n)
        ups = mix_in(mix_ref, 1, yu_ref, n)
        for b in range(NPHM):
            at = (slice(n * STRIP, (n + 1) * STRIP), slice(b * cols, (b + 1) * cols))
            sig = jax.nn.sigmoid(gates[b])
            act = gates[b] * sig
            act_ref[at] = act
            slope_ref[at] = ups[b] * (sig + act * (1.0 - sig))
            hid_ref[at] = act * ups[b]
    stores.append(begin(act_ref, act_hbm, out_sem.at[4]))
    stores.append(begin(slope_ref, slope_hbm, out_sem.at[5]))
    stores.append(begin(hid_ref, hid_hbm, out_sem.at[6]))
    wait_all(stores)


def backward_body(
    cap, pieces, sides, after, order_ref, mix_ref, slot_hbm, score_hbm, got_hbm, act_hbm, slope_hbm, hid_hbm,
    *refs,
):
    parts, refs = refs[:sides], refs[sides + after :]
    back_hbm, x_outs, refs = refs[0], refs[1 : 1 + sides], refs[1 + sides :]
    y_hbm, d_hbm, inner_hbm = refs[:3]
    (
        down_ref, side_ref, x_ref, y_ref, d_ref, act_ref, slope_ref, hid_ref, z_ref, grad_ref,
        back_ref, inner_ref, slot_ref, score_ref, got_sem, side_sem, in_sem, out_sem,
    ) = refs[3:]
    loads = load_rows(got_hbm, x_ref, got_sem)
    down_in = load_factor(order_ref, parts, 2, down_ref, side_sem.at[2])
    small_in = [
        begin(source, target, in_sem.at[n])
        for n, (source, target) in enumerate(((score_hbm, score_ref), (slot_hbm, slot_ref)))
    ]
    flat_in = [
        begin(source, target, in_sem.at[2 + n])
        for n, (source, target) in enumerate(
            ((act_hbm, act_ref), (slope_hbm, slope_ref), (hid_hbm, hid_ref))
        )
    ]
    hidden = d_ref.shape[2]
    sides_in = []
    for m in range(2):
        target = side_ref.at[:, m * hidden : (m + 1) * hidden]
        sides_in += load_factor(order_ref, parts, m, target, side_sem.at[m])
    wait_all(small_in)
    score = jnp.concatenate([score_ref[b : b + 1, :] for b in range(score_ref.shape[0])], axis=1)
    rows = score.shape[1]
    same = iota((rows, rows), 0) == iota((rows, rows), 1)
    score = jnp.sum(jnp.where(same, score.astype(F32), 0.0), axis=1, keepdims=True)
    cols = hidden // NPHM
    gates = jnp.broadcast_to(jax.nn.sigmoid(score / 64.0), (rows, cols))
    place = place_matrix(cap, pieces, back_ref.shape[0], slot_ref[...])
    strips = rows // STRIP
    tall = NPHM * STRIP
    wait_all(loads)
    stores = store_parts(order_ref, x_ref, x_outs, out_sem)
    wait_all(down_in)
    for n in range(strips):
        y_ref[n * tall : (n + 1) * tall] = dot(x_ref[n * tall : (n + 1) * tall], down_ref[...])
    stores.append(begin(y_ref, y_hbm, out_sem.at[2]))
    wait_all(flat_in)
    wait_all(sides_in)
    for n in range(strips):
        down = mix_in(mix_ref, 2, y_ref, n)
        strip = slice(n * STRIP, (n + 1) * STRIP)
        gate = gates[strip]
        inner = jnp.zeros((STRIP, cols), F32)
        d_gate, d_up = [], []
        for b in range(NPHM):
            at = (strip, slice(b * cols, (b + 1) * cols))
            inner = inner + hid_ref[at] * down[b]
            hidden_grad = gate * down[b]
            d_gate.append(hidden_grad * slope_ref[at])
            d_up.append(hidden_grad * act_ref[at])
            d_ref[(0,) + at] = d_gate[b].astype(BF16)
            d_ref[(1,) + at] = d_up[b].astype(BF16)
            d_ref[(2,) + at] = (hid_ref[at] * gate).astype(BF16)
        inner_ref[strip] = inner
        mix_out(mix_ref, 0, d_gate, n, z_ref)
        mix_out(mix_ref, 1, d_up, n, z_ref, hidden)
        at = slice(n * tall, (n + 1) * tall)
        grad_ref[at] = dot_nt(z_ref[at], side_ref[...]).astype(BF16)
    stores.append(begin(d_ref, d_hbm, out_sem.at[3]))
    stores.append(begin(inner_ref, inner_hbm, out_sem.at[4]))
    part, depth = back_ref.shape[1], x_ref.shape[1]
    for k, at in enumerate(chunks_of(part)):
        blocks = []
        for j in range(pieces):
            column = j * part + at.start
            a, start = column // depth, column % depth
            wide = slice(start, start + at.stop - at.start)
            blocks += [grad_ref[rows_of(n, a), wide] for n in range(strips)]
        back_ref[:, at] = dot(place, jnp.concatenate(blocks, axis=0)).astype(BF16)
        stores.append(begin(back_ref.at[:, at], back_hbm.at[:, at], out_sem.at[5 + k]))
    wait_all(stores)


def factor_body(count_groups, mix_ref, *refs):
    rows_in, refs = refs[: 3 * count_groups], refs[3 * count_groups :]
    out_hbm, x_ref, g_ref, d_ref, z_ref, sum_ref, in_sem, out_sem = refs
    loads = []
    for n in range(count_groups):
        for k, target in enumerate((x_ref, g_ref, d_ref)):
            loads.append(begin(rows_in[3 * n + k], target.at[n], in_sem.at[n, k]))
    stores = []
    cols = out_hbm.shape[3]
    wait_all(loads)
    for m in (2, 0, 1):
        for n in range(count_groups):
            for strip in range(d_ref.shape[2] // STRIP):
                blocks = blocks_of(d_ref.at[n, m], strip)
                mix_out(mix_ref, m, blocks, strip, z_ref.at[n])
        left = g_ref if m == 2 else x_ref
        sum_ref[m] = sum(dot_tn(left[n], z_ref[n]) for n in range(count_groups))
        for i in range(NPHM):
            at = sum_ref.at[m, :, i * cols : (i + 1) * cols]
            stores.append(begin(at, out_hbm.at[m, i], out_sem.at[m, i]))
    wait_all(stores)


def mix_grad_body(yg_hbm, yu_hbm, yd_hbm, d_hbm, out_ref, y_ref, d_ref, sems):
    loads = [begin(d_hbm, d_ref, sems.at[3])]
    for m, source in enumerate((yg_hbm, yu_hbm, yd_hbm)):
        loads.append(begin(source, y_ref.at[m], sems.at[m]))
    wait_all(loads)
    rows, cols = d_ref.shape[1], d_ref.shape[2] // NPHM
    for m in range(3):
        for a in range(NPHM):
            for i in range(NPHM):
                at = slice(i * cols, (i + 1) * cols)
                strips = range(rows // STRIP)
                block = jnp.concatenate([y_ref[m, rows_of(n, a), at] for n in strips], axis=0)
                for b in range(NPHM):
                    at = m * 64 + i * 16 + a * 4 + b
                    other = d_ref[m, :, b * cols : (b + 1) * cols].astype(F32)
                    out_ref[at : at + 1, :] = jnp.sum(block * other, axis=0, keepdims=True)


def shards(tokens, cotangent, factors, mix, selection, scores):
    peers = lax.axis_size("exp")
    groups = lax.axis_size("seq")
    own_rows, width = tokens.shape
    _, weights, count, depth_own, cols = factors.shape
    depth = depth_own * groups
    hidden = count * cols
    cap = 3 * own_rows // (2 * peers)
    pieces = 1
    while (cap * pieces) % 8:
        pieces *= 2
    slots = peers * cap * pieces
    part = width // pieces
    steps = len(chunks_of(part))
    block_len = peers * SELECTED
    rows = selection.shape[1] * selection.shape[2]
    stacked = count * rows
    swap = groups == 2
    pair = [(0, 1), (1, 0)]
    mixing = mix.reshape(-1)
    dma = pltpu.SemaphoreType.DMA

    def across(array):
        return lax.ppermute(array, "seq", pair)

    half = peers // selection.shape[1]
    direct = half == 8
    me = lax.axis_index("exp").astype(jnp.int32).reshape(1)
    group = lax.axis_index("seq").astype(jnp.int32).reshape(1)
    halves = [list(range(h, h + half)) for h in range(0, peers, half)]
    if swap:
        factor_parts = [factors[0], across(factors)[0]]
        sides = 2
    else:
        factor_parts = [lax.all_gather(factors, "seq", axis=3, tiled=True)[0]]
        sides = 1
    sides_in = [(x, HBM) for x in factor_parts]
    cross = [(shaped((own_rows, width // 2), BF16), HBM)] if direct else []
    told, slot, *crossed = call(
        functools.partial(front_body, cap, pieces, own_rows, block_len, half, direct),
        [(shaped((2 * peers, rows), jnp.int32), VMEM), (shaped((1, rows), jnp.int32), VMEM)] + cross,
        [(me, SMEM), (selection[0], VMEM)] + ([(cotangent, HBM)] if direct else []),
        "wanted_rows",
        1 << 20,
        [scratch_like((own_rows, width // 2), BF16), dma((2,))] if direct else [],
    )
    if direct:
        crossed = [lax.ppermute(crossed[0], "exp", [(n, n ^ (half // 2)) for n in range(peers)])]
    chosen = lax.all_to_all(told, "exp", split_axis=0, concat_axis=0, tiled=True)

    def to_peers(array):
        array = array.reshape(peers, -1, array.shape[1])
        array = lax.all_to_all(array, "exp", split_axis=0, concat_axis=0, tiled=True)
        return array.reshape(-1, array.shape[2])

    got_rows = to_peers(pick_slots(cap, pieces, chosen, tokens, crossed, "pick_tokens"))
    if direct:
        shares = plane_columns(me, cotangent, crossed[0], half, factor_parts[1:])
        shares = [shares[0]] + [
            lax.ppermute(shares[k], "exp", [(n, n ^ k) for n in range(peers)])
            for k in range(1, half // 2)
        ]
    else:
        array = spread_columns(cotangent, half).reshape(half, own_rows, -1)
        array = lax.all_to_all(
            array, "exp", split_axis=0, concat_axis=0, axis_index_groups=halves, tiled=True
        )
        shares = [array.reshape(half * own_rows, -1)]
    picked = pick_rows(me, half, own_rows, chosen, shares, [], "pick_cotangent")
    got_grads = to_peers(picked)
    placed = place_rows(cap, pieces, own_rows, me, half, chosen)
    gate = jax.nn.sigmoid(scores[0].reshape(-1).astype(F32) / 64.0)

    product = 2 * stacked * depth * hidden
    split = [(shaped((stacked, depth // sides), BF16), HBM)] * sides
    mixed = (shaped((stacked, hidden), F32), HBM)
    flat = (shaped((rows, hidden), F32), HBM)
    back_scratch = scratch_like((slots, part), BF16)
    pieces_in = got_grads.shape[0] // SELECTED
    stack_scratch = scratch_like((stacked, depth), BF16)
    mixed_scratch = scratch_like((stacked, hidden), F32)
    low_scratch = scratch_like((stacked, hidden), BF16)
    flat_scratch = scratch_like((rows, hidden), F32)
    outs = call(
        functools.partial(forward_body, cap, pieces, sides),
        split + [mixed, mixed, flat, flat, flat],
        [(group, SMEM), (mixing, SMEM), (slot, VMEM), (got_rows, HBM)] + sides_in,
        "forward",
        2 * product,
        [back_scratch, scratch_like((2, depth, hidden), BF16), stack_scratch, mixed_scratch, mixed_scratch]
        + [flat_scratch] * 3
        + [dma((steps,)), dma((2, sides, count)), dma((7,))],
    )
    x_parts, (y_gate, y_up, act, slope, hid) = outs[:sides], outs[sides:]
    x_rows = [x_parts[0]] + [across(x) for x in x_parts[1:]]
    after = x_rows[1:]
    outs = call(
        functools.partial(backward_body, cap, pieces, sides, len(after)),
        [(shaped((slots, part), BF16), HBM)]
        + split
        + [mixed, (shaped((weights, rows, hidden), BF16), HBM), (shaped((rows, cols), F32), HBM)],
        [(group, SMEM), (mixing, SMEM), (slot, HBM), (scores[0], HBM), (got_grads, HBM)]
        + [(x, HBM) for x in (act, slope, hid)]
        + sides_in
        + [(x, HBM) for x in after],
        "backward",
        3 * product,
        [scratch_like((depth, hidden), BF16), scratch_like((depth, 2 * hidden), BF16)]
        + [stack_scratch, mixed_scratch, scratch_like((weights, rows, hidden), BF16)]
        + [flat_scratch] * 3
        + [scratch_like((stacked, 2 * hidden), BF16), stack_scratch, back_scratch]
        + [scratch_like((rows, cols), F32), scratch_like(slot.shape, jnp.int32)]
        + [scratch_like(scores.shape[1:], jnp.int32)]
        + [dma((pieces_in,)), dma((weights, sides, count)), dma((5,)), dma((5 + steps,))],
    )
    back, g_parts, (y_down, d_own, inner) = outs[0], outs[1 : 1 + sides], outs[1 + sides :]
    returned = to_peers(back)

    d_rows = [d_own] + [across(d_own) for _ in x_parts[1:]]
    g_rows = [g_parts[0]] + [across(x) for x in g_parts[1:]]
    depth_here = depth // sides
    factor_grad = call(
        functools.partial(factor_body, sides),
        [(shaped((weights, count, depth_here, cols), F32), HBM)],
        [(mixing, SMEM)]
        + [(x, HBM) for n in range(sides) for x in (x_rows[n], g_rows[n], d_rows[n])],
        "factor_grad",
        3 * product,
        [scratch_like((sides, stacked, depth_here), BF16)] * 2
        + [
            scratch_like((sides, weights, rows, hidden), BF16),
            scratch_like((sides, stacked, hidden), BF16),
            scratch_like((weights, depth_here, hidden), F32),
            dma((sides, 3)),
            dma((weights, count)),
        ],
    )[0]
    mix_rows = call(
        mix_grad_body,
        [(shaped((mixing.size, cols), F32), VMEM)],
        [(x, HBM) for x in (y_gate, y_up, y_down, d_own)],
        "mix_partials",
        weights * 64 * 2 * rows * cols,
        [
            scratch_like((weights, stacked, hidden), F32),
            scratch_like((weights, rows, hidden), BF16),
            dma((4,)),
        ],
    )[0]
    mix_part = jnp.sum(mix_rows, axis=1).reshape(mix.shape)
    if swap:
        mix_grad = mix_part + across(mix_part)
    else:
        factor_grad = lax.psum_scatter(
            factor_grad.astype(BF16), "seq", scatter_dimension=2, tiled=True
        ).astype(F32)
        mix_grad = lax.psum(mix_part, "seq")
    gate_grad = (jnp.sum(inner, axis=1) * gate * (1.0 - gate)).reshape(selection.shape)
    token_grad = sum_rows(pieces, placed, returned)
    return token_grad, factor_grad[None], mix_grad, gate_grad


def solution(mesh):
    return jax.shard_map(
        shards,
        mesh=mesh,
        in_specs=(
            P(("seq", "exp"), None),
            P(("seq", "exp"), None),
            P("exp", None, None, "seq", None),
            P("exp", None, None, None, None),
            P("exp", "seq", None),
            P("exp", "seq", None),
        ),
        out_specs=(
            P(("seq", "exp"), None),
            P("exp", None, None, "seq", None),
            P("exp", None, None, None, None),
            P("exp", "seq", None),
        ),
        check_vma=False,
    )
```

```python
import functools

import jax
import jax.numpy as jnp
from jax import lax
from jax.experimental import pallas as pl
from jax.experimental.pallas import tpu as pltpu
from jax.sharding import PartitionSpec as P

SELECTED = 64
NPHM = 4
VMEM_LIMIT = 63 * 1024 * 1024
F32 = jnp.float32
BF16 = jnp.bfloat16


def iota(shape, dim):
    return lax.broadcasted_iota(jnp.int32, shape, dim)


def dot(left, right):
    return jnp.dot(left, right, preferred_element_type=F32)


def dot_tn(left, right):
    return lax.dot_general(left, right, (((0,), (0,)), ((), ())), preferred_element_type=F32)


def dot_nt(left, right):
    return lax.dot_general(left, right, (((1,), (1,)), ((), ())), preferred_element_type=F32)


HBM = pl.BlockSpec(memory_space=pltpu.HBM)
VMEM = pl.BlockSpec(memory_space=pltpu.VMEM)
SMEM = pl.BlockSpec(memory_space=pltpu.SMEM)


def call(body, outs, ins, name, flops, scratch=()):
    moved = sum(x.size * x.dtype.itemsize for x, _ in list(ins) + list(outs))
    return pl.pallas_call(
        body,
        out_shape=[x for x, _ in outs],
        in_specs=[place for _, place in ins],
        out_specs=[place for _, place in outs],
        scratch_shapes=list(scratch),
        compiler_params=pltpu.CompilerParams(vmem_limit_bytes=VMEM_LIMIT),
        cost_estimate=pl.CostEstimate(flops=flops, bytes_accessed=moved, transcendentals=0),
        name=name,
    )(*[x for x, _ in ins])


def begin(source, target, sem):
    copy = pltpu.make_async_copy(source, target, sem)
    copy.start()
    return copy


def shaped(shape, dtype):
    return jax.ShapeDtypeStruct(shape, dtype)


def scratch_like(shape, dtype):
    return pltpu.VMEM(shape, dtype)


def chunks_of(part):
    chunk = min(part, 512)
    return [slice(c * chunk, (c + 1) * chunk) for c in range(part // chunk)]


def front_body(cap, pieces, own_rows, block_len, half, cross, me_ref, chosen_hbm, *refs):
    chosen_ref, told_ref, slot_ref, small_sem = refs[-4:]
    small = begin(chosen_hbm, chosen_ref, small_sem.at[0])
    if cross:
        source_ref, told_hbm, slot_hbm, cross_ref, held_ref, sems = refs[:-4]
        width = cross_ref.shape[1]
        plane = lax.shift_right_logical(me_ref[0] & (half - 1), half.bit_length() - 2)
        at = pl.ds(pl.multiple_of((1 - plane) * width, width), width)
        load = begin(source_ref.at[:, at], held_ref, sems.at[0])
    else:
        told_hbm, slot_hbm = refs[:-4]
    small.wait()
    peers, rows = told_ref.shape[0] // 2, slot_ref.shape[1]
    blocks = [chosen_ref[b : b + 1, :] for b in range(chosen_ref.shape[0])]
    position = jnp.concatenate([x + b * block_len for b, x in enumerate(blocks)], axis=1)
    owner = lax.shift_right_logical(position, own_rows.bit_length() - 1)
    local = position & (own_rows - 1)
    peer = iota((peers, rows), 0)
    mine = (peer == owner).astype(F32)
    count = jnp.sum(mine, axis=1, keepdims=True)
    earlier = jnp.sum(jnp.where(peer < owner, count, 0.0), axis=0, keepdims=True).astype(jnp.int32)
    rank = iota((1, rows), 1) - earlier
    slot_ref[...] = owner * (cap * pieces) + rank
    lane = iota((rows, rows), 0)
    hit = jnp.zeros((rows, rows), F32)
    for j in range(pieces):
        hit = hit + (lane == rank + j * cap).astype(F32)
    twice = iota((2 * peers, rows), 0)
    marked = jnp.where(twice == 2 * owner, local + 1, 0).astype(F32)
    asked = dot_nt(marked.astype(BF16), hit.astype(BF16)).astype(jnp.int32)
    told_ref[...] = jnp.where((twice & 1) == 1, jnp.concatenate(blocks, axis=1), asked)
    stores = [
        begin(told_ref, told_hbm, small_sem.at[1]),
        begin(slot_ref, slot_hbm, small_sem.at[2]),
    ]
    if cross:
        load.wait()
        stores.append(begin(held_ref, cross_ref, sems.at[1]))
    for store in stores:
        store.wait()


def plane_columns(me, source, crossed, half):
    own_rows, width = source.shape
    part, count = width // half, half // 2

    def body(me_ref, source_ref, crossed_ref, *refs):
        outs, (held_ref, in_sem, out_sem) = refs[:count], refs[count:]
        low = me_ref[0] & (half - 1)
        plane = lax.shift_right_logical(low, half.bit_length() - 2)
        wide = count * part
        at = pl.ds(pl.multiple_of(plane * wide, wide), wide)
        loads = [
            begin(source_ref.at[:, at], held_ref.at[0], in_sem.at[0]),
            begin(crossed_ref, held_ref.at[1], in_sem.at[1]),
        ]
        copies = []
        for n, load in enumerate(loads):
            load.wait()
            for k in range(count):
                share = (low & (count - 1)) ^ k
                at = held_ref.at[n, :, pl.ds(pl.multiple_of(share * part, part), part)]
                rows = pl.ds(n * own_rows, own_rows)
                copies.append(begin(at, outs[k].at[rows], out_sem.at[n, k]))
        wait_all(copies)

    return call(
        body,
        [(shaped((2 * own_rows, part), BF16), HBM)] * count,
        [(me, SMEM), (source, HBM), (crossed, HBM)],
        "plane_columns",
        0,
        [
            scratch_like((2, own_rows, count * part), BF16),
            pltpu.SemaphoreType.DMA((2,)),
            pltpu.SemaphoreType.DMA((2, count)),
        ],
    )


def pick_matrix(cap, pieces, own_rows, requested):
    told, lanes = requested.shape
    peers = told // 2
    group = cap * pieces
    slots = peers * group
    peer = 2 * iota((peers, group, told), 0).reshape(slots, told)
    spread = dot(
        (peer == iota((slots, told), 1)).astype(BF16), requested.astype(F32).astype(BF16)
    )
    place = iota((peers, group, lanes), 1).reshape(slots, lanes)
    row = jnp.sum(
        jnp.where(place == iota((slots, lanes), 1), spread, 0.0), axis=1, keepdims=True
    ).astype(jnp.int32)
    piece = iota((peers, group, 1), 1).reshape(slots, 1)
    shift = jnp.zeros((slots, 1), jnp.int32)
    for j in range(1, pieces):
        shift = shift + jnp.where(piece >= j * cap, own_rows, 0)
    target = jnp.where(row > 0, row - 1 + shift, -1)
    return (target == iota((slots, pieces * own_rows), 1)).astype(BF16)


def pick_slots(cap, pieces, requested, source, after, name):
    own_rows, width = source.shape
    part = width // pieces
    slots = requested.shape[0] // 2 * cap * pieces
    columns = chunks_of(part)

    def body(requested_hbm, source_ref, *refs):
        out_ref, requested_ref, rows_ref, sent_ref, in_sem, out_sem = refs[len(after) :]
        asked = begin(requested_hbm, requested_ref, in_sem.at[len(columns), 0])
        loads = []
        for n, at in enumerate(columns):
            for j in range(pieces):
                wide = slice(j * part + at.start, j * part + at.stop)
                target = rows_ref.at[j * own_rows : (j + 1) * own_rows, at]
                loads.append(begin(source_ref.at[:, wide], target, in_sem.at[n, j]))
        asked.wait()
        pick = pick_matrix(cap, pieces, own_rows, requested_ref[...])
        stores = []
        for n, at in enumerate(columns):
            for load in loads[n * pieces : (n + 1) * pieces]:
                load.wait()
            sent_ref[:, at] = dot(pick, rows_ref[:, at]).astype(BF16)
            stores.append(begin(sent_ref.at[:, at], out_ref.at[:, at], out_sem.at[n]))
        for store in stores:
            store.wait()

    return call(
        body,
        [(shaped((slots, part), BF16), HBM)],
        [(requested, HBM), (source, HBM)] + [(x, HBM) for x in after],
        name,
        2 * slots * pieces * own_rows * part,
        [
            scratch_like(requested.shape, jnp.int32),
            scratch_like((pieces * own_rows, part), BF16),
            scratch_like((slots, part), BF16),
            pltpu.SemaphoreType.DMA((len(columns) + 1, pieces)),
            pltpu.SemaphoreType.DMA((len(columns),)),
        ],
    )[0]


def spread_columns(source, half):
    own_rows, width = source.shape
    part = width // half

    def body(source_ref, out_ref, held_ref, in_sem, out_sem):
        begin(source_ref, held_ref, in_sem).wait()
        copies = []
        for k in range(half):
            at = held_ref.at[:, k * part : (k + 1) * part]
            out = out_ref.at[k * own_rows : (k + 1) * own_rows]
            copies.append(begin(at, out, out_sem.at[k]))
        wait_all(copies)

    scratch = [
        scratch_like((own_rows, width), BF16),
        pltpu.SemaphoreType.DMA,
        pltpu.SemaphoreType.DMA((half,)),
    ]
    outs = [(shaped((half * own_rows, part), BF16), HBM)]
    return call(body, outs, [(source, HBM)], "spread_columns", 0, scratch)[0]


def cut_factors(factors, first):
    cuts = (slice(0, first), slice(first, factors.shape[0]))

    def body(factors_ref, *refs):
        outs, (held_ref, sems) = refs[:2], refs[2:]
        loads = [
            begin(factors_ref.at[at], held_ref.at[at], sems.at[0, n]) for n, at in enumerate(cuts)
        ]
        copies = []
        for n, at in enumerate(cuts):
            loads[n].wait()
            copies.append(begin(held_ref.at[at], outs[n], sems.at[1, n]))
        wait_all(copies)

    outs = [
        (shaped((at.stop - at.start,) + factors.shape[1:], BF16), HBM) for at in cuts
    ]
    scratch = [scratch_like(factors.shape, BF16), pltpu.SemaphoreType.DMA((2, 2))]
    return call(body, outs, [(factors, HBM)], "cut_factors", 0, scratch)


def pick_rows(me, half, own_rows, chosen, shares, after, name):
    peers, total = chosen.shape[0] // 2, chosen.shape[1]
    picks = total * half // peers
    part = shares[0].shape[1]
    block = half * own_rows
    batch = min(peers, 8)

    def body(me_ref, chosen_ref, *refs):
        refs = refs[len(after) :]
        parts, (out_ref, rows_ref, pick_ref, sent_ref, in_sem, out_sem) = (
            refs[: len(shares)],
            refs[len(shares) :],
        )
        loads = []
        for k in range(half):
            place = (me_ref[0] & (half - 1)) ^ k if len(parts) > 1 else k
            n, first = (k % len(parts), k // len(parts)) if len(parts) > 1 else (0, k)
            at = parts[n].at[first * own_rows : (first + 1) * own_rows]
            target = rows_ref.at[pl.ds(pl.multiple_of(place * own_rows, own_rows), own_rows)]
            loads.append(begin(at, target, in_sem.at[k]))
        block_at = lax.shift_right_logical(me_ref[0], half.bit_length() - 1)
        same = iota((picks, total), 0) + block_at * picks == iota((picks, total), 1)
        stores = []
        for first in range(0, peers, batch):
            for e in range(batch):
                wanted = chosen_ref[2 * (first + e) + 1 : 2 * (first + e) + 2, :]
                column = jnp.sum(jnp.where(same, wanted, 0), axis=1, keepdims=True)
                pick_ref[first // batch % 2, e * picks : (e + 1) * picks] = (
                    column == iota((picks, block), 1)
                ).astype(BF16)
            if first == 0:
                wait_all(loads)
            at = slice(first * picks, (first + batch) * picks)
            sent_ref[at] = dot(pick_ref[first // batch % 2], rows_ref[...]).astype(BF16)
            stores.append(begin(sent_ref.at[at], out_ref.at[at], out_sem.at[first // batch]))
        wait_all(stores)

    return call(
        body,
        [(shaped((peers * picks, part), BF16), HBM)],
        [(me, SMEM), (chosen, VMEM)] + [(x, HBM) for x in list(after) + list(shares)],
        name,
        2 * peers * picks * block * part,
        [
            scratch_like((block, part), BF16),
            scratch_like((2, batch * picks, block), BF16),
            scratch_like((peers * picks, part), BF16),
            pltpu.SemaphoreType.DMA((half,)),
            pltpu.SemaphoreType.DMA((peers // batch,)),
        ],
    )[0]


def place_rows(cap, pieces, own_rows, me, half, chosen):
    peers, total = chosen.shape[0] // 2, chosen.shape[1]
    picks = total * half // peers
    group = cap * pieces

    def body(me_ref, chosen_ref, out_ref, pick_ref):
        low = me_ref[0] & (half - 1)
        block_at = lax.shift_right_logical(me_ref[0], half.bit_length() - 1)
        lane = iota((2 * peers, total), 1) - block_at * picks
        here = (lane >= 0) & (lane < picks)
        local = jnp.where(here, chosen_ref[...] - low * own_rows, own_rows)
        before = jnp.sum((local < 0).astype(F32), axis=1, keepdims=True).astype(jnp.int32)
        ranks = lane - before
        owned = jnp.where((local >= 0) & (local < own_rows), local + 1, 0)
        place = iota((group, total), 0)
        for e in range(peers):
            at = slice(2 * e + 1, 2 * e + 2)
            rank, mine = ranks[at], owned[at]
            column = jnp.zeros((group, 1), jnp.int32)
            for j in range(pieces):
                hit = jnp.where((place == rank + j * cap) & (rank >= 0) & (rank < cap), mine, 0)
                row = jnp.sum(hit, axis=1, keepdims=True)
                column = column + jnp.where(row > 0, row + j * own_rows, 0)
            pick_ref[e * group : (e + 1) * group] = (
                column == iota((group, pieces * own_rows), 1) + 1
            ).astype(F32)
        out_ref[...] = jnp.transpose(pick_ref[...]).astype(BF16)

    return call(
        body,
        [(shaped((pieces * own_rows, peers * group), BF16), VMEM)],
        [(me, SMEM), (chosen, VMEM)],
        "place_rows",
        1 << 20,
        [scratch_like((peers * group, pieces * own_rows), F32)],
    )[0]


def sum_rows(pieces, placed, returned):
    slots, part = returned.shape
    own_rows = placed.shape[0] // pieces
    columns = chunks_of(part)

    def body(placed_hbm, returned_ref, out_ref, place_ref, got_ref, sum_ref, in_sem, out_sem):
        first = begin(placed_hbm, place_ref, in_sem.at[len(columns)])
        loads = [
            begin(returned_ref.at[:, at], got_ref.at[:, at], in_sem.at[n])
            for n, at in enumerate(columns)
        ]
        first.wait()
        stores = []
        for n, at in enumerate(columns):
            loads[n].wait()
            summed = dot(place_ref[...], got_ref[:, at]).astype(BF16)
            for j in range(pieces):
                wide = slice(j * part + at.start, j * part + at.stop)
                sum_ref[:, wide] = summed[j * own_rows : (j + 1) * own_rows]
                stores.append(
                    begin(sum_ref.at[:, wide], out_ref.at[:, wide], out_sem.at[n, j])
                )
        wait_all(stores)

    return call(
        body,
        [(shaped((own_rows, part * pieces), BF16), HBM)],
        [(placed, HBM), (returned, HBM)],
        "sum_rows",
        2 * slots * pieces * own_rows * part,
        [
            scratch_like(placed.shape, BF16),
            scratch_like((slots, part), BF16),
            scratch_like((own_rows, part * pieces), BF16),
            pltpu.SemaphoreType.DMA((len(columns) + 1,)),
            pltpu.SemaphoreType.DMA((len(columns), pieces)),
        ],
    )[0]


def load_factor(order_ref, parts, m, target, sems):
    copies = []
    _, count, rows, cols = parts[0].shape
    first = parts[1].shape[0] if len(parts) > 1 else 0
    for n in range(2 if len(parts) > 1 else 1):
        place = order_ref[0] ^ n if len(parts) > 1 else 0
        start = pl.multiple_of(place * rows, rows)
        for i in range(count):
            side = parts[0].at[m, i]
            if n == 1:
                flat = m * count + i
                side = parts[1].at[flat] if flat < first else parts[2].at[flat - first]
            at = target.at[pl.ds(start, rows), i * cols : (i + 1) * cols]
            copies.append(begin(side, at, sems.at[n, i]))
    return copies


def wait_all(copies):
    for copy in copies:
        copy.wait()


def place_matrix(cap, pieces, slots, slot):
    wide = jnp.concatenate([slot + j * cap for j in range(pieces)], axis=1)
    return (iota((slots, wide.shape[1]), 0) == wide).astype(BF16)


def load_rows(got_hbm, x_ref, sems):
    rows, depth = x_ref.shape[0] // NPHM, x_ref.shape[1]
    part = got_hbm.shape[1]
    shares = NPHM * depth // part
    picks = got_hbm.shape[0] * part // (NPHM * depth) // (rows // SELECTED)
    copies = []
    for n in range(got_hbm.shape[0] // picks):
        block, share = divmod(n, shares)
        a, start = share * part // depth, share * part % depth
        first = (block * NPHM + a) * picks
        at = x_ref.at[first : first + picks, start : start + part]
        copies.append(begin(got_hbm.at[n * picks : (n + 1) * picks], at, sems.at[n]))
    return copies


def load_slots(got_hbm, got_ref, sems):
    return [
        begin(got_hbm.at[:, at], got_ref.at[:, at], sems.at[n])
        for n, at in enumerate(chunks_of(got_ref.shape[1]))
    ]


def stack_rows(pieces, place, loads, got_ref, out_ref):
    part = got_ref.shape[1]
    rows, depth = out_ref.shape[0] // NPHM, out_ref.shape[1]
    for load, at in zip(loads, chunks_of(part)):
        load.wait()
        block = dot_tn(place, got_ref[:, at]).astype(BF16)
        for j in range(pieces):
            column = j * part + at.start
            a, start = column // depth, column % depth
            for n in range(rows // STRIP):
                first = (n * NPHM + a) * STRIP
                out_ref[first : first + STRIP, start : start + at.stop - at.start] = block[
                    j * rows + n * STRIP : j * rows + (n + 1) * STRIP
                ]


def store_parts(order_ref, source_ref, outs, sems):
    copies = []
    for n, out in enumerate(outs):
        size = out.shape[1]
        start = pl.multiple_of((order_ref[0] ^ n) * size if len(outs) > 1 else 0, size)
        copies.append(begin(source_ref.at[:, pl.ds(start, size)], out, sems.at[n]))
    return copies


STRIP = SELECTED


def rows_of(n, a):
    return slice((n * NPHM + a) * STRIP, (n * NPHM + a + 1) * STRIP)


def mix_in(mix_ref, m, y_ref, n):
    cols = y_ref.shape[1] // NPHM
    total = [jnp.zeros((STRIP, cols), F32)] * NPHM
    for a in range(NPHM):
        for i in range(NPHM):
            block = y_ref[rows_of(n, a), i * cols : (i + 1) * cols]
            for b in range(NPHM):
                total[b] = total[b] + mix_ref[m * 64 + i * 16 + a * 4 + b] * block
    return total


def mix_out(mix_ref, m, blocks, n, z_ref, offset=0):
    cols = blocks[0].shape[1]
    for a in range(NPHM):
        for i in range(NPHM):
            total = mix_ref[m * 64 + i * 16 + a * 4] * blocks[0]
            for b in range(1, NPHM):
                total = total + mix_ref[m * 64 + i * 16 + a * 4 + b] * blocks[b]
            z_ref[rows_of(n, a), offset + i * cols : offset + (i + 1) * cols] = total.astype(
                z_ref.dtype
            )


def blocks_of(d_ref, n):
    cols = d_ref.shape[1] // NPHM
    at = slice(n * STRIP, (n + 1) * STRIP)
    return [d_ref[at, b * cols : (b + 1) * cols].astype(F32) for b in range(NPHM)]


def forward_body(
    cap, pieces, sides, order_ref, mix_ref, slot_ref, got_hbm, *refs
):
    held = 2 if sides > 1 else 1
    parts, refs = refs[:held], refs[held:]
    x_outs, refs = refs[:sides], refs[sides:]
    yg_hbm, yu_hbm, act_hbm, slope_hbm, hid_hbm = refs[:5]
    got_ref, side_ref, x_ref, yg_ref, yu_ref, act_ref, slope_ref, hid_ref = refs[5:13]
    got_sem, side_sem, out_sem = refs[13:]
    loads = load_slots(got_hbm, got_ref, got_sem)
    sides_in = [
        load_factor(order_ref, parts, m, side_ref.at[m], side_sem.at[m]) for m in range(2)
    ]
    place = place_matrix(cap, pieces, got_ref.shape[0], slot_ref[...])
    stack_rows(pieces, place, loads, got_ref, x_ref)
    stores = store_parts(order_ref, x_ref, x_outs, out_sem)
    wait_all(sides_in[0])
    yg_ref[...] = dot(x_ref[...], side_ref[0])
    stores.append(begin(yg_ref, yg_hbm, out_sem.at[2]))
    wait_all(sides_in[1])
    yu_ref[...] = dot(x_ref[...], side_ref[1])
    stores.append(begin(yu_ref, yu_hbm, out_sem.at[3]))
    cols = yg_ref.shape[1] // NPHM
    for n in range(yg_ref.shape[0] // (NPHM * STRIP)):
        gates = mix_in(mix_ref, 0, yg_ref, n)
        ups = mix_in(mix_ref, 1, yu_ref, n)
        for b in range(NPHM):
            at = (slice(n * STRIP, (n + 1) * STRIP), slice(b * cols, (b + 1) * cols))
            sig = jax.nn.sigmoid(gates[b])
            act = gates[b] * sig
            act_ref[at] = act
            slope_ref[at] = ups[b] * (sig + act * (1.0 - sig))
            hid_ref[at] = act * ups[b]
    stores.append(begin(act_ref, act_hbm, out_sem.at[4]))
    stores.append(begin(slope_ref, slope_hbm, out_sem.at[5]))
    stores.append(begin(hid_ref, hid_hbm, out_sem.at[6]))
    wait_all(stores)


def backward_body(
    cap, pieces, sides, after, order_ref, mix_ref, slot_hbm, score_hbm, got_hbm, act_hbm, slope_hbm, hid_hbm,
    *refs,
):
    held = 3 if sides > 1 else 1
    parts, refs = refs[:held], refs[held + after :]
    back_hbm, x_outs, refs = refs[0], refs[1 : 1 + sides], refs[1 + sides :]
    y_hbm, d_hbm, inner_hbm = refs[:3]
    (
        down_ref, side_ref, x_ref, y_ref, d_ref, act_ref, slope_ref, hid_ref, z_ref, grad_ref,
        back_ref, inner_ref, slot_ref, score_ref, got_sem, side_sem, in_sem, out_sem,
    ) = refs[3:]
    loads = load_rows(got_hbm, x_ref, got_sem)
    down_in = load_factor(order_ref, parts, 2, down_ref, side_sem.at[2])
    small_in = [
        begin(source, target, in_sem.at[n])
        for n, (source, target) in enumerate(((score_hbm, score_ref), (slot_hbm, slot_ref)))
    ]
    flat_in = [
        begin(source, target, in_sem.at[2 + n])
        for n, (source, target) in enumerate(
            ((act_hbm, act_ref), (slope_hbm, slope_ref), (hid_hbm, hid_ref))
        )
    ]
    hidden = d_ref.shape[2]
    sides_in = []
    for m in range(2):
        target = side_ref.at[:, m * hidden : (m + 1) * hidden]
        sides_in += load_factor(order_ref, parts, m, target, side_sem.at[m])
    wait_all(small_in)
    score = jnp.concatenate([score_ref[b : b + 1, :] for b in range(score_ref.shape[0])], axis=1)
    rows = score.shape[1]
    same = iota((rows, rows), 0) == iota((rows, rows), 1)
    score = jnp.sum(jnp.where(same, score.astype(F32), 0.0), axis=1, keepdims=True)
    cols = hidden // NPHM
    gates = jnp.broadcast_to(jax.nn.sigmoid(score / 64.0), (rows, cols))
    place = place_matrix(cap, pieces, back_ref.shape[0], slot_ref[...])
    strips = rows // STRIP
    tall = NPHM * STRIP
    wait_all(loads)
    stores = store_parts(order_ref, x_ref, x_outs, out_sem)
    wait_all(down_in)
    for n in range(strips):
        y_ref[n * tall : (n + 1) * tall] = dot(x_ref[n * tall : (n + 1) * tall], down_ref[...])
    stores.append(begin(y_ref, y_hbm, out_sem.at[2]))
    wait_all(flat_in)
    wait_all(sides_in)
    for n in range(strips):
        down = mix_in(mix_ref, 2, y_ref, n)
        strip = slice(n * STRIP, (n + 1) * STRIP)
        gate = gates[strip]
        inner = jnp.zeros((STRIP, cols), F32)
        d_gate, d_up = [], []
        for b in range(NPHM):
            at = (strip, slice(b * cols, (b + 1) * cols))
            inner = inner + hid_ref[at] * down[b]
            hidden_grad = gate * down[b]
            d_gate.append(hidden_grad * slope_ref[at])
            d_up.append(hidden_grad * act_ref[at])
            d_ref[(0,) + at] = d_gate[b].astype(BF16)
            d_ref[(1,) + at] = d_up[b].astype(BF16)
            d_ref[(2,) + at] = (hid_ref[at] * gate).astype(BF16)
        inner_ref[strip] = inner
        mix_out(mix_ref, 0, d_gate, n, z_ref)
        mix_out(mix_ref, 1, d_up, n, z_ref, hidden)
        at = slice(n * tall, (n + 1) * tall)
        grad_ref[at] = dot_nt(z_ref[at], side_ref[...]).astype(BF16)
    stores.append(begin(d_ref, d_hbm, out_sem.at[3]))
    stores.append(begin(inner_ref, inner_hbm, out_sem.at[4]))
    part, depth = back_ref.shape[1], x_ref.shape[1]
    for k, at in enumerate(chunks_of(part)):
        blocks = []
        for j in range(pieces):
            column = j * part + at.start
            a, start = column // depth, column % depth
            wide = slice(start, start + at.stop - at.start)
            blocks += [grad_ref[rows_of(n, a), wide] for n in range(strips)]
        back_ref[:, at] = dot(place, jnp.concatenate(blocks, axis=0)).astype(BF16)
        stores.append(begin(back_ref.at[:, at], back_hbm.at[:, at], out_sem.at[5 + k]))
    wait_all(stores)


def factor_body(count_groups, mix_ref, *refs):
    rows_in, refs = refs[: 3 * count_groups], refs[3 * count_groups :]
    out_hbm, x_ref, g_ref, d_ref, z_ref, sum_ref, in_sem, out_sem = refs
    loads = []
    for n in range(count_groups):
        for k, target in enumerate((x_ref, g_ref, d_ref)):
            loads.append(begin(rows_in[3 * n + k], target.at[n], in_sem.at[n, k]))
    stores = []
    cols = out_hbm.shape[3]
    wait_all(loads)
    for m in (2, 0, 1):
        for n in range(count_groups):
            for strip in range(d_ref.shape[2] // STRIP):
                blocks = blocks_of(d_ref.at[n, m], strip)
                mix_out(mix_ref, m, blocks, strip, z_ref.at[n])
        left = g_ref if m == 2 else x_ref
        sum_ref[m] = sum(dot_tn(left[n], z_ref[n]) for n in range(count_groups))
        for i in range(NPHM):
            at = sum_ref.at[m, :, i * cols : (i + 1) * cols]
            stores.append(begin(at, out_hbm.at[m, i], out_sem.at[m, i]))
    wait_all(stores)


def mix_grad_body(yg_hbm, yu_hbm, yd_hbm, d_hbm, out_ref, y_ref, d_ref, sems):
    loads = [begin(d_hbm, d_ref, sems.at[3])]
    for m, source in enumerate((yg_hbm, yu_hbm, yd_hbm)):
        loads.append(begin(source, y_ref.at[m], sems.at[m]))
    wait_all(loads)
    rows, cols = d_ref.shape[1], d_ref.shape[2] // NPHM
    for m in range(3):
        for a in range(NPHM):
            for i in range(NPHM):
                at = slice(i * cols, (i + 1) * cols)
                strips = range(rows // STRIP)
                block = jnp.concatenate([y_ref[m, rows_of(n, a), at] for n in strips], axis=0)
                for b in range(NPHM):
                    at = m * 64 + i * 16 + a * 4 + b
                    other = d_ref[m, :, b * cols : (b + 1) * cols].astype(F32)
                    out_ref[at : at + 1, :] = jnp.sum(block * other, axis=0, keepdims=True)


def shards(tokens, cotangent, factors, mix, selection, scores):
    peers = lax.axis_size("exp")
    groups = lax.axis_size("seq")
    own_rows, width = tokens.shape
    _, weights, count, depth_own, cols = factors.shape
    depth = depth_own * groups
    hidden = count * cols
    cap = 3 * own_rows // (2 * peers)
    pieces = 1
    while (cap * pieces) % 8:
        pieces *= 2
    slots = peers * cap * pieces
    part = width // pieces
    steps = len(chunks_of(part))
    block_len = peers * SELECTED
    rows = selection.shape[1] * selection.shape[2]
    stacked = count * rows
    swap = groups == 2
    pair = [(0, 1), (1, 0)]
    mixing = mix.reshape(-1)
    dma = pltpu.SemaphoreType.DMA

    def across(array):
        return lax.ppermute(array, "seq", pair)

    half = peers // selection.shape[1]
    direct = half == 8
    me = lax.axis_index("exp").astype(jnp.int32).reshape(1)
    group = lax.axis_index("seq").astype(jnp.int32).reshape(1)
    halves = [list(range(h, h + half)) for h in range(0, peers, half)]
    if swap:
        flat_factors = factors[0].reshape(weights * count, depth_own, cols)
        cuts = [across(x) for x in cut_factors(flat_factors, 10)]
        factor_parts = [factors[0]] + cuts
        sides = 2
    else:
        cuts = []
        factor_parts = [lax.all_gather(factors, "seq", axis=3, tiled=True)[0]]
        sides = 1
    sides_in = [(x, HBM) for x in factor_parts]
    cross = [(shaped((own_rows, width // 2), BF16), HBM)] if direct else []
    told, slot, *crossed = call(
        functools.partial(front_body, cap, pieces, own_rows, block_len, half, direct),
        [(shaped((2 * peers, rows), jnp.int32), HBM), (shaped((1, rows), jnp.int32), HBM)] + cross,
        [(me, SMEM), (selection[0], HBM)] + ([(cotangent, HBM)] if direct else []),
        "wanted_rows",
        1 << 20,
        ([scratch_like((own_rows, width // 2), BF16), dma((2,))] if direct else [])
        + [scratch_like(selection.shape[1:], jnp.int32)]
        + [scratch_like((2 * peers, rows), jnp.int32), scratch_like((1, rows), jnp.int32)]
        + [dma((3,))],
    )
    if direct:
        crossed = [lax.ppermute(crossed[0], "exp", [(n, n ^ (half // 2)) for n in range(peers)])]
    chosen = lax.all_to_all(told, "exp", split_axis=0, concat_axis=0, tiled=True)

    def to_peers(array):
        array = array.reshape(peers, -1, array.shape[1])
        array = lax.all_to_all(array, "exp", split_axis=0, concat_axis=0, tiled=True)
        return array.reshape(-1, array.shape[2])

    got_rows = to_peers(pick_slots(cap, pieces, chosen, tokens, crossed, "pick_tokens"))
    if direct:
        shares = plane_columns(me, cotangent, crossed[0], half)
        shares = [shares[0]] + [
            lax.ppermute(shares[k], "exp", [(n, n ^ k) for n in range(peers)])
            for k in range(1, half // 2)
        ]
    else:
        array = spread_columns(cotangent, half).reshape(half, own_rows, -1)
        array = lax.all_to_all(
            array, "exp", split_axis=0, concat_axis=0, axis_index_groups=halves, tiled=True
        )
        shares = [array.reshape(half * own_rows, -1)]
    picked = pick_rows(me, half, own_rows, chosen, shares, cuts[:1], "pick_cotangent")
    got_grads = to_peers(picked)
    placed = place_rows(cap, pieces, own_rows, me, half, chosen)
    gate = jax.nn.sigmoid(scores[0].reshape(-1).astype(F32) / 64.0)

    product = 2 * stacked * depth * hidden
    split = [(shaped((stacked, depth // sides), BF16), HBM)] * sides
    mixed = (shaped((stacked, hidden), F32), HBM)
    flat = (shaped((rows, hidden), F32), HBM)
    back_scratch = scratch_like((slots, part), BF16)
    pieces_in = got_grads.shape[0] // SELECTED
    stack_scratch = scratch_like((stacked, depth), BF16)
    mixed_scratch = scratch_like((stacked, hidden), F32)
    low_scratch = scratch_like((stacked, hidden), BF16)
    flat_scratch = scratch_like((rows, hidden), F32)
    outs = call(
        functools.partial(forward_body, cap, pieces, sides),
        split + [mixed, mixed, flat, flat, flat],
        [(group, SMEM), (mixing, SMEM), (slot, VMEM), (got_rows, HBM)] + sides_in[:2],
        "forward",
        2 * product,
        [back_scratch, scratch_like((2, depth, hidden), BF16), stack_scratch, mixed_scratch, mixed_scratch]
        + [flat_scratch] * 3
        + [dma((steps,)), dma((2, sides, count)), dma((7,))],
    )
    x_parts, (y_gate, y_up, act, slope, hid) = outs[:sides], outs[sides:]
    x_rows = [x_parts[0]] + [across(x) for x in x_parts[1:]]
    after = x_rows[1:]
    outs = call(
        functools.partial(backward_body, cap, pieces, sides, len(after)),
        [(shaped((slots, part), BF16), HBM)]
        + split
        + [mixed, (shaped((weights, rows, hidden), BF16), HBM), (shaped((rows, cols), F32), HBM)],
        [(group, SMEM), (mixing, SMEM), (slot, HBM), (scores[0], HBM), (got_grads, HBM)]
        + [(x, HBM) for x in (act, slope, hid)]
        + sides_in
        + [(x, HBM) for x in after],
        "backward",
        3 * product,
        [scratch_like((depth, hidden), BF16), scratch_like((depth, 2 * hidden), BF16)]
        + [stack_scratch, mixed_scratch, scratch_like((weights, rows, hidden), BF16)]
        + [flat_scratch] * 3
        + [scratch_like((stacked, 2 * hidden), BF16), stack_scratch, back_scratch]
        + [scratch_like((rows, cols), F32), scratch_like(slot.shape, jnp.int32)]
        + [scratch_like(scores.shape[1:], jnp.int32)]
        + [dma((pieces_in,)), dma((weights, sides, count)), dma((5,)), dma((5 + steps,))],
    )
    back, g_parts, (y_down, d_own, inner) = outs[0], outs[1 : 1 + sides], outs[1 + sides :]
    returned = to_peers(back)

    d_rows = [d_own] + [across(d_own) for _ in x_parts[1:]]
    g_rows = [g_parts[0]] + [across(x) for x in g_parts[1:]]
    depth_here = depth // sides
    factor_grad = call(
        functools.partial(factor_body, sides),
        [(shaped((weights, count, depth_here, cols), F32), HBM)],
        [(mixing, SMEM)]
        + [(x, HBM) for n in range(sides) for x in (x_rows[n], g_rows[n], d_rows[n])],
        "factor_grad",
        3 * product,
        [scratch_like((sides, stacked, depth_here), BF16)] * 2
        + [
            scratch_like((sides, weights, rows, hidden), BF16),
            scratch_like((sides, stacked, hidden), BF16),
            scratch_like((weights, depth_here, hidden), F32),
            dma((sides, 3)),
            dma((weights, count)),
        ],
    )[0]
    mix_rows = call(
        mix_grad_body,
        [(shaped((mixing.size, cols), F32), VMEM)],
        [(x, HBM) for x in (y_gate, y_up, y_down, d_own)],
        "mix_partials",
        weights * 64 * 2 * rows * cols,
        [
            scratch_like((weights, stacked, hidden), F32),
            scratch_like((weights, rows, hidden), BF16),
            dma((4,)),
        ],
    )[0]
    mix_part = jnp.sum(mix_rows, axis=1).reshape(mix.shape)
    if swap:
        mix_grad = mix_part + across(mix_part)
    else:
        factor_grad = lax.psum_scatter(
            factor_grad.astype(BF16), "seq", scatter_dimension=2, tiled=True
        ).astype(F32)
        mix_grad = lax.psum(mix_part, "seq")
    gate_grad = (jnp.sum(inner, axis=1) * gate * (1.0 - gate)).reshape(selection.shape)
    token_grad = sum_rows(pieces, placed, returned)
    return token_grad, factor_grad[None], mix_grad, gate_grad


def solution(mesh):
    return jax.shard_map(
        shards,
        mesh=mesh,
        in_specs=(
            P(("seq", "exp"), None),
            P(("seq", "exp"), None),
            P("exp", None, None, "seq", None),
            P("exp", None, None, None, None),
            P("exp", "seq", None),
            P("exp", "seq", None),
        ),
        out_specs=(
            P(("seq", "exp"), None),
            P("exp", None, None, "seq", None),
            P("exp", None, None, None, None),
            P("exp", "seq", None),
        ),
        check_vma=False,
    )
```

```python
import functools

import jax
import jax.numpy as jnp
from jax import lax
from jax.experimental import pallas as pl
from jax.experimental.pallas import tpu as pltpu
from jax.sharding import PartitionSpec as P

SELECTED = 64
NPHM = 4
VMEM_LIMIT = 63 * 1024 * 1024
F32 = jnp.float32
BF16 = jnp.bfloat16


def iota(shape, dim):
    return lax.broadcasted_iota(jnp.int32, shape, dim)


def dot(left, right):
    return jnp.dot(left, right, preferred_element_type=F32)


def dot_tn(left, right):
    return lax.dot_general(left, right, (((0,), (0,)), ((), ())), preferred_element_type=F32)


def dot_nt(left, right):
    return lax.dot_general(left, right, (((1,), (1,)), ((), ())), preferred_element_type=F32)


HBM = pl.BlockSpec(memory_space=pltpu.HBM)
VMEM = pl.BlockSpec(memory_space=pltpu.VMEM)
SMEM = pl.BlockSpec(memory_space=pltpu.SMEM)


def call(body, outs, ins, name, flops, scratch=()):
    moved = sum(x.size * x.dtype.itemsize for x, _ in list(ins) + list(outs))
    return pl.pallas_call(
        body,
        out_shape=[x for x, _ in outs],
        in_specs=[place for _, place in ins],
        out_specs=[place for _, place in outs],
        scratch_shapes=list(scratch),
        compiler_params=pltpu.CompilerParams(vmem_limit_bytes=VMEM_LIMIT),
        cost_estimate=pl.CostEstimate(flops=flops, bytes_accessed=moved, transcendentals=0),
        name=name,
    )(*[x for x, _ in ins])


def begin(source, target, sem):
    copy = pltpu.make_async_copy(source, target, sem)
    copy.start()
    return copy


def shaped(shape, dtype):
    return jax.ShapeDtypeStruct(shape, dtype)


def scratch_like(shape, dtype):
    return pltpu.VMEM(shape, dtype)


def chunks_of(part):
    chunk = min(part, 512)
    return [slice(c * chunk, (c + 1) * chunk) for c in range(part // chunk)]


def front_body(cap, pieces, own_rows, block_len, half, cross, me_ref, chosen_hbm, *refs):
    chosen_ref, told_ref, slot_ref, small_sem = refs[-4:]
    small = begin(chosen_hbm, chosen_ref, small_sem.at[0])
    if cross:
        source_ref, told_hbm, slot_hbm, cross_ref, held_ref, sems = refs[:-4]
        width = cross_ref.shape[1]
        plane = lax.shift_right_logical(me_ref[0] & (half - 1), half.bit_length() - 2)
        at = pl.ds(pl.multiple_of((1 - plane) * width, width), width)
        load = begin(source_ref.at[:, at], held_ref, sems.at[0])
    else:
        told_hbm, slot_hbm = refs[:-4]
    small.wait()
    peers, rows = told_ref.shape[0] // 2, slot_ref.shape[1]
    blocks = [chosen_ref[b : b + 1, :] for b in range(chosen_ref.shape[0])]
    position = jnp.concatenate([x + b * block_len for b, x in enumerate(blocks)], axis=1)
    owner = lax.shift_right_logical(position, own_rows.bit_length() - 1)
    local = position & (own_rows - 1)
    peer = iota((peers, rows), 0)
    mine = (peer == owner).astype(F32)
    count = jnp.sum(mine, axis=1, keepdims=True)
    earlier = jnp.sum(jnp.where(peer < owner, count, 0.0), axis=0, keepdims=True).astype(jnp.int32)
    rank = iota((1, rows), 1) - earlier
    slot_ref[...] = owner * (cap * pieces) + rank
    lane = iota((rows, rows), 0)
    hit = jnp.zeros((rows, rows), F32)
    for j in range(pieces):
        hit = hit + (lane == rank + j * cap).astype(F32)
    twice = iota((2 * peers, rows), 0)
    marked = jnp.where(twice == 2 * owner, local + 1, 0).astype(F32)
    asked = dot_nt(marked.astype(BF16), hit.astype(BF16)).astype(jnp.int32)
    told_ref[...] = jnp.where((twice & 1) == 1, jnp.concatenate(blocks, axis=1), asked)
    stores = [
        begin(told_ref, told_hbm, small_sem.at[1]),
        begin(slot_ref, slot_hbm, small_sem.at[2]),
    ]
    if cross:
        load.wait()
        stores.append(begin(held_ref, cross_ref, sems.at[1]))
    for store in stores:
        store.wait()


def plane_columns(me, source, crossed, half):
    own_rows, width = source.shape
    part, count = width // half, half // 2

    def body(me_ref, source_ref, crossed_ref, *refs):
        outs, (held_ref, in_sem, out_sem) = refs[:count], refs[count:]
        low = me_ref[0] & (half - 1)
        plane = lax.shift_right_logical(low, half.bit_length() - 2)
        wide = count * part
        at = pl.ds(pl.multiple_of(plane * wide, wide), wide)
        loads = [
            begin(source_ref.at[:, at], held_ref.at[0], in_sem.at[0]),
            begin(crossed_ref, held_ref.at[1], in_sem.at[1]),
        ]
        copies = []
        for n, load in enumerate(loads):
            load.wait()
            for k in range(count):
                share = (low & (count - 1)) ^ k
                at = held_ref.at[n, :, pl.ds(pl.multiple_of(share * part, part), part)]
                rows = pl.ds(n * own_rows, own_rows)
                copies.append(begin(at, outs[k].at[rows], out_sem.at[n, k]))
        wait_all(copies)

    return call(
        body,
        [(shaped((2 * own_rows, part), BF16), HBM)] * count,
        [(me, SMEM), (source, HBM), (crossed, HBM)],
        "plane_columns",
        0,
        [
            scratch_like((2, own_rows, count * part), BF16),
            pltpu.SemaphoreType.DMA((2,)),
            pltpu.SemaphoreType.DMA((2, count)),
        ],
    )


def pick_matrix(cap, pieces, own_rows, requested):
    told, lanes = requested.shape
    peers = told // 2
    group = cap * pieces
    slots = peers * group
    peer = 2 * iota((peers, group, told), 0).reshape(slots, told)
    spread = dot(
        (peer == iota((slots, told), 1)).astype(BF16), requested.astype(F32).astype(BF16)
    )
    place = iota((peers, group, lanes), 1).reshape(slots, lanes)
    row = jnp.sum(
        jnp.where(place == iota((slots, lanes), 1), spread, 0.0), axis=1, keepdims=True
    ).astype(jnp.int32)
    piece = iota((peers, group, 1), 1).reshape(slots, 1)
    shift = jnp.zeros((slots, 1), jnp.int32)
    for j in range(1, pieces):
        shift = shift + jnp.where(piece >= j * cap, own_rows, 0)
    target = jnp.where(row > 0, row - 1 + shift, -1)
    return (target == iota((slots, pieces * own_rows), 1)).astype(BF16)


def pick_slots(cap, pieces, requested, source, after, name):
    own_rows, width = source.shape
    part = width // pieces
    slots = requested.shape[0] // 2 * cap * pieces
    columns = chunks_of(part)

    def body(requested_hbm, source_ref, *refs):
        out_ref, requested_ref, rows_ref, sent_ref, in_sem, out_sem = refs[len(after) :]
        asked = begin(requested_hbm, requested_ref, in_sem.at[len(columns), 0])
        loads = []
        for n, at in enumerate(columns):
            for j in range(pieces):
                wide = slice(j * part + at.start, j * part + at.stop)
                target = rows_ref.at[j * own_rows : (j + 1) * own_rows, at]
                loads.append(begin(source_ref.at[:, wide], target, in_sem.at[n, j]))
        asked.wait()
        pick = pick_matrix(cap, pieces, own_rows, requested_ref[...])
        stores = []
        for n, at in enumerate(columns):
            for load in loads[n * pieces : (n + 1) * pieces]:
                load.wait()
            sent_ref[:, at] = dot(pick, rows_ref[:, at]).astype(BF16)
            stores.append(begin(sent_ref.at[:, at], out_ref.at[:, at], out_sem.at[n]))
        for store in stores:
            store.wait()

    return call(
        body,
        [(shaped((slots, part), BF16), HBM)],
        [(requested, HBM), (source, HBM)] + [(x, HBM) for x in after],
        name,
        2 * slots * pieces * own_rows * part,
        [
            scratch_like(requested.shape, jnp.int32),
            scratch_like((pieces * own_rows, part), BF16),
            scratch_like((slots, part), BF16),
            pltpu.SemaphoreType.DMA((len(columns) + 1, pieces)),
            pltpu.SemaphoreType.DMA((len(columns),)),
        ],
    )[0]


def spread_columns(source, half):
    own_rows, width = source.shape
    part = width // half

    def body(source_ref, out_ref, held_ref, in_sem, out_sem):
        begin(source_ref, held_ref, in_sem).wait()
        copies = []
        for k in range(half):
            at = held_ref.at[:, k * part : (k + 1) * part]
            out = out_ref.at[k * own_rows : (k + 1) * own_rows]
            copies.append(begin(at, out, out_sem.at[k]))
        wait_all(copies)

    scratch = [
        scratch_like((own_rows, width), BF16),
        pltpu.SemaphoreType.DMA,
        pltpu.SemaphoreType.DMA((half,)),
    ]
    outs = [(shaped((half * own_rows, part), BF16), HBM)]
    return call(body, outs, [(source, HBM)], "spread_columns", 0, scratch)[0]


def cut_factors(factors, first):
    cuts = (slice(0, first), slice(first, factors.shape[0]))

    def body(factors_ref, *refs):
        outs, (held_ref, sems) = refs[:2], refs[2:]
        loads = [
            begin(factors_ref.at[at], held_ref.at[at], sems.at[0, n]) for n, at in enumerate(cuts)
        ]
        copies = []
        for n, at in enumerate(cuts):
            loads[n].wait()
            copies.append(begin(held_ref.at[at], outs[n], sems.at[1, n]))
        wait_all(copies)

    outs = [
        (shaped((at.stop - at.start,) + factors.shape[1:], BF16), HBM) for at in cuts
    ]
    scratch = [scratch_like(factors.shape, BF16), pltpu.SemaphoreType.DMA((2, 2))]
    return call(body, outs, [(factors, HBM)], "cut_factors", 0, scratch)


def pick_rows(me, half, own_rows, chosen, shares, after, name):
    peers, total = chosen.shape[0] // 2, chosen.shape[1]
    picks = total * half // peers
    part = shares[0].shape[1]
    block = half * own_rows
    batch = min(peers, 8)

    def body(me_ref, chosen_ref, *refs):
        refs = refs[len(after) :]
        parts, (out_ref, rows_ref, pick_ref, sent_ref, in_sem, out_sem) = (
            refs[: len(shares)],
            refs[len(shares) :],
        )
        loads = []
        for k in range(half):
            place = (me_ref[0] & (half - 1)) ^ k if len(parts) > 1 else k
            n, first = (k % len(parts), k // len(parts)) if len(parts) > 1 else (0, k)
            at = parts[n].at[first * own_rows : (first + 1) * own_rows]
            target = rows_ref.at[pl.ds(pl.multiple_of(place * own_rows, own_rows), own_rows)]
            loads.append(begin(at, target, in_sem.at[k]))
        block_at = lax.shift_right_logical(me_ref[0], half.bit_length() - 1)
        same = iota((picks, total), 0) + block_at * picks == iota((picks, total), 1)
        stores = []
        for first in range(0, peers, batch):
            for e in range(batch):
                wanted = chosen_ref[2 * (first + e) + 1 : 2 * (first + e) + 2, :]
                column = jnp.sum(jnp.where(same, wanted, 0), axis=1, keepdims=True)
                pick_ref[first // batch % 2, e * picks : (e + 1) * picks] = (
                    column == iota((picks, block), 1)
                ).astype(BF16)
            if first == 0:
                wait_all(loads)
            at = slice(first * picks, (first + batch) * picks)
            sent_ref[at] = dot(pick_ref[first // batch % 2], rows_ref[...]).astype(BF16)
            stores.append(begin(sent_ref.at[at], out_ref.at[at], out_sem.at[first // batch]))
        wait_all(stores)

    return call(
        body,
        [(shaped((peers * picks, part), BF16), HBM)],
        [(me, SMEM), (chosen, VMEM)] + [(x, HBM) for x in list(after) + list(shares)],
        name,
        2 * peers * picks * block * part,
        [
            scratch_like((block, part), BF16),
            scratch_like((2, batch * picks, block), BF16),
            scratch_like((peers * picks, part), BF16),
            pltpu.SemaphoreType.DMA((half,)),
            pltpu.SemaphoreType.DMA((peers // batch,)),
        ],
    )[0]


def place_rows(cap, pieces, own_rows, me, half, chosen):
    peers, total = chosen.shape[0] // 2, chosen.shape[1]
    picks = total * half // peers
    group = cap * pieces

    def body(me_ref, chosen_ref, out_ref, pick_ref):
        low = me_ref[0] & (half - 1)
        block_at = lax.shift_right_logical(me_ref[0], half.bit_length() - 1)
        lane = iota((2 * peers, total), 1) - block_at * picks
        here = (lane >= 0) & (lane < picks)
        local = jnp.where(here, chosen_ref[...] - low * own_rows, own_rows)
        before = jnp.sum((local < 0).astype(F32), axis=1, keepdims=True).astype(jnp.int32)
        ranks = lane - before
        owned = jnp.where((local >= 0) & (local < own_rows), local + 1, 0)
        place = iota((group, total), 0)
        for e in range(peers):
            at = slice(2 * e + 1, 2 * e + 2)
            rank, mine = ranks[at], owned[at]
            column = jnp.zeros((group, 1), jnp.int32)
            for j in range(pieces):
                hit = jnp.where((place == rank + j * cap) & (rank >= 0) & (rank < cap), mine, 0)
                row = jnp.sum(hit, axis=1, keepdims=True)
                column = column + jnp.where(row > 0, row + j * own_rows, 0)
            pick_ref[e * group : (e + 1) * group] = (
                column == iota((group, pieces * own_rows), 1) + 1
            ).astype(F32)
        out_ref[...] = jnp.transpose(pick_ref[...]).astype(BF16)

    return call(
        body,
        [(shaped((pieces * own_rows, peers * group), BF16), VMEM)],
        [(me, SMEM), (chosen, VMEM)],
        "place_rows",
        1 << 20,
        [scratch_like((peers * group, pieces * own_rows), F32)],
    )[0]


def sum_rows(pieces, placed, returned):
    slots, part = returned.shape
    own_rows = placed.shape[0] // pieces
    columns = chunks_of(part)

    def body(placed_hbm, returned_ref, out_ref, place_ref, got_ref, sum_ref, in_sem, out_sem):
        first = begin(placed_hbm, place_ref, in_sem.at[len(columns)])
        loads = [
            begin(returned_ref.at[:, at], got_ref.at[:, at], in_sem.at[n])
            for n, at in enumerate(columns)
        ]
        first.wait()
        stores = []
        for n, at in enumerate(columns):
            loads[n].wait()
            summed = dot(place_ref[...], got_ref[:, at]).astype(BF16)
            for j in range(pieces):
                wide = slice(j * part + at.start, j * part + at.stop)
                sum_ref[:, wide] = summed[j * own_rows : (j + 1) * own_rows]
                stores.append(
                    begin(sum_ref.at[:, wide], out_ref.at[:, wide], out_sem.at[n, j])
                )
        wait_all(stores)

    return call(
        body,
        [(shaped((own_rows, part * pieces), BF16), HBM)],
        [(placed, HBM), (returned, HBM)],
        "sum_rows",
        2 * slots * pieces * own_rows * part,
        [
            scratch_like(placed.shape, BF16),
            scratch_like((slots, part), BF16),
            scratch_like((own_rows, part * pieces), BF16),
            pltpu.SemaphoreType.DMA((len(columns) + 1,)),
            pltpu.SemaphoreType.DMA((len(columns), pieces)),
        ],
    )[0]


def load_factor(order_ref, parts, m, target, sems):
    copies = []
    _, count, rows, cols = parts[0].shape
    first = parts[1].shape[0] if len(parts) > 1 else 0
    for n in range(2 if len(parts) > 1 else 1):
        place = order_ref[0] ^ n if len(parts) > 1 else 0
        start = pl.multiple_of(place * rows, rows)
        for i in range(count):
            side = parts[0].at[m, i]
            if n == 1:
                flat = m * count + i
                side = parts[1].at[flat] if flat < first else parts[2].at[flat - first]
            at = target.at[pl.ds(start, rows), i * cols : (i + 1) * cols]
            copies.append(begin(side, at, sems.at[n, i]))
    return copies


def wait_all(copies):
    for copy in copies:
        copy.wait()


def place_matrix(cap, pieces, slots, slot):
    wide = jnp.concatenate([slot + j * cap for j in range(pieces)], axis=1)
    return (iota((slots, wide.shape[1]), 0) == wide).astype(BF16)


def load_rows(got_hbm, x_ref, sems):
    rows, depth = x_ref.shape[0] // NPHM, x_ref.shape[1]
    part = got_hbm.shape[1]
    shares = NPHM * depth // part
    picks = got_hbm.shape[0] * part // (NPHM * depth) // (rows // SELECTED)
    copies = []
    for n in range(got_hbm.shape[0] // picks):
        block, share = divmod(n, shares)
        a, start = share * part // depth, share * part % depth
        first = (block * NPHM + a) * picks
        at = x_ref.at[first : first + picks, start : start + part]
        copies.append(begin(got_hbm.at[n * picks : (n + 1) * picks], at, sems.at[n]))
    return copies


def load_slots(got_hbm, got_ref, sems):
    return [
        begin(got_hbm.at[:, at], got_ref.at[:, at], sems.at[n])
        for n, at in enumerate(chunks_of(got_ref.shape[1]))
    ]


def stack_rows(pieces, place, loads, got_ref, out_ref):
    part = got_ref.shape[1]
    rows, depth = out_ref.shape[0] // NPHM, out_ref.shape[1]
    for load, at in zip(loads, chunks_of(part)):
        load.wait()
        block = dot_tn(place, got_ref[:, at]).astype(BF16)
        for j in range(pieces):
            column = j * part + at.start
            a, start = column // depth, column % depth
            for n in range(rows // STRIP):
                first = (n * NPHM + a) * STRIP
                out_ref[first : first + STRIP, start : start + at.stop - at.start] = block[
                    j * rows + n * STRIP : j * rows + (n + 1) * STRIP
                ]


def store_parts(order_ref, source_ref, outs, sems):
    copies = []
    for n, out in enumerate(outs):
        size = out.shape[1]
        start = pl.multiple_of((order_ref[0] ^ n) * size if len(outs) > 1 else 0, size)
        copies.append(begin(source_ref.at[:, pl.ds(start, size)], out, sems.at[n]))
    return copies


STRIP = SELECTED


def rows_of(n, a):
    return slice((n * NPHM + a) * STRIP, (n * NPHM + a + 1) * STRIP)


def mix_in(mix_ref, m, y_ref, n):
    cols = y_ref.shape[1] // NPHM
    total = [jnp.zeros((STRIP, cols), F32)] * NPHM
    for a in range(NPHM):
        for i in range(NPHM):
            block = y_ref[rows_of(n, a), i * cols : (i + 1) * cols]
            for b in range(NPHM):
                total[b] = total[b] + mix_ref[m * 64 + i * 16 + a * 4 + b] * block
    return total


def mix_out(mix_ref, m, blocks, n, z_ref, offset=0):
    cols = blocks[0].shape[1]
    for a in range(NPHM):
        for i in range(NPHM):
            total = mix_ref[m * 64 + i * 16 + a * 4] * blocks[0]
            for b in range(1, NPHM):
                total = total + mix_ref[m * 64 + i * 16 + a * 4 + b] * blocks[b]
            z_ref[rows_of(n, a), offset + i * cols : offset + (i + 1) * cols] = total.astype(
                z_ref.dtype
            )


def blocks_of(d_ref, n):
    cols = d_ref.shape[1] // NPHM
    at = slice(n * STRIP, (n + 1) * STRIP)
    return [d_ref[at, b * cols : (b + 1) * cols].astype(F32) for b in range(NPHM)]


def forward_body(
    cap, pieces, sides, order_ref, mix_ref, slot_ref, got_hbm, *refs
):
    held = 2 if sides > 1 else 1
    parts, refs = refs[:held], refs[held:]
    x_outs, refs = refs[:sides], refs[sides:]
    yg_hbm, yu_hbm, act_hbm, slope_hbm, hid_hbm = refs[:5]
    got_ref, side_ref, x_ref, yg_ref, yu_ref, act_ref, slope_ref, hid_ref = refs[5:13]
    got_sem, side_sem, out_sem = refs[13:]
    loads = load_slots(got_hbm, got_ref, got_sem)
    sides_in = [
        load_factor(order_ref, parts, m, side_ref.at[m], side_sem.at[m]) for m in range(2)
    ]
    place = place_matrix(cap, pieces, got_ref.shape[0], slot_ref[...])
    stack_rows(pieces, place, loads, got_ref, x_ref)
    stores = store_parts(order_ref, x_ref, x_outs, out_sem)
    wait_all(sides_in[0])
    yg_ref[...] = dot(x_ref[...], side_ref[0])
    stores.append(begin(yg_ref, yg_hbm, out_sem.at[2]))
    wait_all(sides_in[1])
    yu_ref[...] = dot(x_ref[...], side_ref[1])
    stores.append(begin(yu_ref, yu_hbm, out_sem.at[3]))
    cols = yg_ref.shape[1] // NPHM
    for n in range(yg_ref.shape[0] // (NPHM * STRIP)):
        gates = mix_in(mix_ref, 0, yg_ref, n)
        ups = mix_in(mix_ref, 1, yu_ref, n)
        for b in range(NPHM):
            at = (slice(n * STRIP, (n + 1) * STRIP), slice(b * cols, (b + 1) * cols))
            sig = jax.nn.sigmoid(gates[b])
            act = gates[b] * sig
            act_ref[at] = act
            slope_ref[at] = ups[b] * (sig + act * (1.0 - sig))
            hid_ref[at] = act * ups[b]
    stores.append(begin(act_ref, act_hbm, out_sem.at[4]))
    stores.append(begin(slope_ref, slope_hbm, out_sem.at[5]))
    stores.append(begin(hid_ref, hid_hbm, out_sem.at[6]))
    wait_all(stores)


def backward_body(
    cap, pieces, sides, after, order_ref, mix_ref, slot_hbm, score_hbm, got_hbm, act_hbm, slope_hbm, hid_hbm,
    *refs,
):
    held = 3 if sides > 1 else 1
    parts, refs = refs[:held], refs[held + after :]
    back_hbm, x_outs, refs = refs[0], refs[1 : 1 + sides], refs[1 + sides :]
    y_hbm, d_hbm, inner_hbm = refs[:3]
    (
        down_ref, side_ref, x_ref, y_ref, d_ref, act_ref, slope_ref, hid_ref, z_ref, grad_ref,
        back_ref, inner_ref, slot_ref, score_ref, got_sem, side_sem, in_sem, out_sem,
    ) = refs[3:]
    loads = load_rows(got_hbm, x_ref, got_sem)
    down_in = load_factor(order_ref, parts, 2, down_ref, side_sem.at[2])
    small_in = [
        begin(source, target, in_sem.at[n])
        for n, (source, target) in enumerate(((score_hbm, score_ref), (slot_hbm, slot_ref)))
    ]
    flat_in = [
        begin(source, target, in_sem.at[2 + n])
        for n, (source, target) in enumerate(
            ((act_hbm, act_ref), (slope_hbm, slope_ref), (hid_hbm, hid_ref))
        )
    ]
    hidden = d_ref.shape[2]
    sides_in = []
    for m in range(2):
        target = side_ref.at[:, m * hidden : (m + 1) * hidden]
        sides_in += load_factor(order_ref, parts, m, target, side_sem.at[m])
    wait_all(small_in)
    score = jnp.concatenate([score_ref[b : b + 1, :] for b in range(score_ref.shape[0])], axis=1)
    rows = score.shape[1]
    same = iota((rows, rows), 0) == iota((rows, rows), 1)
    score = jnp.sum(jnp.where(same, score.astype(F32), 0.0), axis=1, keepdims=True)
    cols = hidden // NPHM
    gates = jnp.broadcast_to(jax.nn.sigmoid(score / 64.0), (rows, cols))
    place = place_matrix(cap, pieces, back_ref.shape[0], slot_ref[...])
    strips = rows // STRIP
    tall = NPHM * STRIP
    wait_all(loads)
    stores = store_parts(order_ref, x_ref, x_outs, out_sem)
    wait_all(down_in)
    for n in range(strips):
        y_ref[n * tall : (n + 1) * tall] = dot(x_ref[n * tall : (n + 1) * tall], down_ref[...])
    stores.append(begin(y_ref, y_hbm, out_sem.at[2]))
    wait_all(flat_in)
    wait_all(sides_in)
    for n in range(strips):
        down = mix_in(mix_ref, 2, y_ref, n)
        strip = slice(n * STRIP, (n + 1) * STRIP)
        gate = gates[strip]
        inner = jnp.zeros((STRIP, cols), F32)
        d_gate, d_up = [], []
        for b in range(NPHM):
            at = (strip, slice(b * cols, (b + 1) * cols))
            inner = inner + hid_ref[at] * down[b]
            hidden_grad = gate * down[b]
            d_gate.append(hidden_grad * slope_ref[at])
            d_up.append(hidden_grad * act_ref[at])
            d_ref[(0,) + at] = d_gate[b].astype(BF16)
            d_ref[(1,) + at] = d_up[b].astype(BF16)
            d_ref[(2,) + at] = (hid_ref[at] * gate).astype(BF16)
        inner_ref[strip] = inner
        mix_out(mix_ref, 0, d_gate, n, z_ref)
        mix_out(mix_ref, 1, d_up, n, z_ref, hidden)
        at = slice(n * tall, (n + 1) * tall)
        grad_ref[at] = dot_nt(z_ref[at], side_ref[...]).astype(BF16)
    stores.append(begin(d_ref, d_hbm, out_sem.at[3]))
    stores.append(begin(inner_ref, inner_hbm, out_sem.at[4]))
    part, depth = back_ref.shape[1], x_ref.shape[1]
    for k, at in enumerate(chunks_of(part)):
        blocks = []
        for j in range(pieces):
            column = j * part + at.start
            a, start = column // depth, column % depth
            wide = slice(start, start + at.stop - at.start)
            blocks += [grad_ref[rows_of(n, a), wide] for n in range(strips)]
        back_ref[:, at] = dot(place, jnp.concatenate(blocks, axis=0)).astype(BF16)
        stores.append(begin(back_ref.at[:, at], back_hbm.at[:, at], out_sem.at[5 + k]))
    wait_all(stores)


def factor_body(count_groups, mix_ref, *refs):
    rows_in, refs = refs[: 3 * count_groups], refs[3 * count_groups :]
    out_hbm, x_ref, g_ref, d_ref, z_ref, sum_ref, in_sem, out_sem = refs
    loads = []
    for n in range(count_groups):
        for k, target in enumerate((x_ref, g_ref, d_ref)):
            loads.append(begin(rows_in[3 * n + k], target.at[n], in_sem.at[n, k]))
    stores = []
    cols = out_hbm.shape[3]
    wait_all(loads)
    for m in (2, 0, 1):
        for n in range(count_groups):
            for strip in range(d_ref.shape[2] // STRIP):
                blocks = blocks_of(d_ref.at[n, m], strip)
                mix_out(mix_ref, m, blocks, strip, z_ref.at[n])
        left = g_ref if m == 2 else x_ref
        sum_ref[m] = sum(dot_tn(left[n], z_ref[n]) for n in range(count_groups))
        for i in range(NPHM):
            at = sum_ref.at[m, :, i * cols : (i + 1) * cols]
            stores.append(begin(at, out_hbm.at[m, i], out_sem.at[m, i]))
    wait_all(stores)


def mix_grad_body(yg_hbm, yu_hbm, yd_hbm, d_hbm, out_ref, y_ref, d_ref, sems):
    loads = [begin(d_hbm, d_ref, sems.at[3])]
    for m, source in enumerate((yg_hbm, yu_hbm, yd_hbm)):
        loads.append(begin(source, y_ref.at[m], sems.at[m]))
    wait_all(loads)
    rows, cols = d_ref.shape[1], d_ref.shape[2] // NPHM
    for m in range(3):
        for a in range(NPHM):
            for i in range(NPHM):
                at = slice(i * cols, (i + 1) * cols)
                strips = range(rows // STRIP)
                block = jnp.concatenate([y_ref[m, rows_of(n, a), at] for n in strips], axis=0)
                for b in range(NPHM):
                    at = m * 64 + i * 16 + a * 4 + b
                    other = d_ref[m, :, b * cols : (b + 1) * cols].astype(F32)
                    out_ref[at : at + 1, :] = jnp.sum(block * other, axis=0, keepdims=True)


def shards(tokens, cotangent, factors, mix, selection, scores):
    peers = lax.axis_size("exp")
    groups = lax.axis_size("seq")
    own_rows, width = tokens.shape
    _, weights, count, depth_own, cols = factors.shape
    depth = depth_own * groups
    hidden = count * cols
    cap = 3 * own_rows // (2 * peers)
    pieces = 1
    while (cap * pieces) % 8:
        pieces *= 2
    slots = peers * cap * pieces
    part = width // pieces
    steps = len(chunks_of(part))
    block_len = peers * SELECTED
    rows = selection.shape[1] * selection.shape[2]
    stacked = count * rows
    swap = groups == 2
    pair = [(0, 1), (1, 0)]
    mixing = mix.reshape(-1)
    dma = pltpu.SemaphoreType.DMA

    def across(array):
        return lax.ppermute(array, "seq", pair)

    half = peers // selection.shape[1]
    direct = half == 8
    me = lax.axis_index("exp").astype(jnp.int32).reshape(1)
    group = lax.axis_index("seq").astype(jnp.int32).reshape(1)
    halves = [list(range(h, h + half)) for h in range(0, peers, half)]
    if swap:
        flat_factors = factors[0].reshape(weights * count, depth_own, cols)
        cuts = [across(x) for x in cut_factors(flat_factors, 2 * count)]
        factor_parts = [factors[0]] + cuts
        sides = 2
    else:
        cuts = []
        factor_parts = [lax.all_gather(factors, "seq", axis=3, tiled=True)[0]]
        sides = 1
    sides_in = [(x, HBM) for x in factor_parts]
    cross = [(shaped((own_rows, width // 2), BF16), HBM)] if direct else []
    told, slot, *crossed = call(
        functools.partial(front_body, cap, pieces, own_rows, block_len, half, direct),
        [(shaped((2 * peers, rows), jnp.int32), HBM), (shaped((1, rows), jnp.int32), HBM)] + cross,
        [(me, SMEM), (selection[0], HBM)] + ([(cotangent, HBM)] if direct else []),
        "wanted_rows",
        1 << 20,
        ([scratch_like((own_rows, width // 2), BF16), dma((2,))] if direct else [])
        + [scratch_like(selection.shape[1:], jnp.int32)]
        + [scratch_like((2 * peers, rows), jnp.int32), scratch_like((1, rows), jnp.int32)]
        + [dma((3,))],
    )
    if direct:
        crossed = [lax.ppermute(crossed[0], "exp", [(n, n ^ (half // 2)) for n in range(peers)])]
    chosen = lax.all_to_all(told, "exp", split_axis=0, concat_axis=0, tiled=True)

    def to_peers(array):
        array = array.reshape(peers, -1, array.shape[1])
        array = lax.all_to_all(array, "exp", split_axis=0, concat_axis=0, tiled=True)
        return array.reshape(-1, array.shape[2])

    got_rows = to_peers(pick_slots(cap, pieces, chosen, tokens, crossed, "pick_tokens"))
    if direct:
        shares = plane_columns(me, cotangent, crossed[0], half)
        shares = [shares[0]] + [
            lax.ppermute(shares[k], "exp", [(n, n ^ k) for n in range(peers)])
            for k in range(1, half // 2)
        ]
    else:
        array = spread_columns(cotangent, half).reshape(half, own_rows, -1)
        array = lax.all_to_all(
            array, "exp", split_axis=0, concat_axis=0, axis_index_groups=halves, tiled=True
        )
        shares = [array.reshape(half * own_rows, -1)]
    picked = pick_rows(me, half, own_rows, chosen, shares, cuts[:1], "pick_cotangent")
    got_grads = to_peers(picked)
    placed = place_rows(cap, pieces, own_rows, me, half, chosen)
    gate = jax.nn.sigmoid(scores[0].reshape(-1).astype(F32) / 64.0)

    product = 2 * stacked * depth * hidden
    split = [(shaped((stacked, depth // sides), BF16), HBM)] * sides
    mixed = (shaped((stacked, hidden), F32), HBM)
    flat = (shaped((rows, hidden), F32), HBM)
    back_scratch = scratch_like((slots, part), BF16)
    pieces_in = got_grads.shape[0] // SELECTED
    stack_scratch = scratch_like((stacked, depth), BF16)
    mixed_scratch = scratch_like((stacked, hidden), F32)
    low_scratch = scratch_like((stacked, hidden), BF16)
    flat_scratch = scratch_like((rows, hidden), F32)
    outs = call(
        functools.partial(forward_body, cap, pieces, sides),
        split + [mixed, mixed, flat, flat, flat],
        [(group, SMEM), (mixing, SMEM), (slot, VMEM), (got_rows, HBM)] + sides_in[:2],
        "forward",
        2 * product,
        [back_scratch, scratch_like((2, depth, hidden), BF16), stack_scratch, mixed_scratch, mixed_scratch]
        + [flat_scratch] * 3
        + [dma((steps,)), dma((2, sides, count)), dma((7,))],
    )
    x_parts, (y_gate, y_up, act, slope, hid) = outs[:sides], outs[sides:]
    x_rows = [x_parts[0]] + [across(x) for x in x_parts[1:]]
    after = x_rows[1:]
    outs = call(
        functools.partial(backward_body, cap, pieces, sides, len(after)),
        [(shaped((slots, part), BF16), HBM)]
        + split
        + [mixed, (shaped((weights, rows, hidden), BF16), HBM), (shaped((rows, cols), F32), HBM)],
        [(group, SMEM), (mixing, SMEM), (slot, HBM), (scores[0], HBM), (got_grads, HBM)]
        + [(x, HBM) for x in (act, slope, hid)]
        + sides_in
        + [(x, HBM) for x in after],
        "backward",
        3 * product,
        [scratch_like((depth, hidden), BF16), scratch_like((depth, 2 * hidden), BF16)]
        + [stack_scratch, mixed_scratch, scratch_like((weights, rows, hidden), BF16)]
        + [flat_scratch] * 3
        + [scratch_like((stacked, 2 * hidden), BF16), stack_scratch, back_scratch]
        + [scratch_like((rows, cols), F32), scratch_like(slot.shape, jnp.int32)]
        + [scratch_like(scores.shape[1:], jnp.int32)]
        + [dma((pieces_in,)), dma((weights, sides, count)), dma((5,)), dma((5 + steps,))],
    )
    back, g_parts, (y_down, d_own, inner) = outs[0], outs[1 : 1 + sides], outs[1 + sides :]
    returned = to_peers(back)

    d_rows = [d_own] + [across(d_own) for _ in x_parts[1:]]
    g_rows = [g_parts[0]] + [across(x) for x in g_parts[1:]]
    depth_here = depth // sides
    factor_grad = call(
        functools.partial(factor_body, sides),
        [(shaped((weights, count, depth_here, cols), F32), HBM)],
        [(mixing, SMEM)]
        + [(x, HBM) for n in range(sides) for x in (x_rows[n], g_rows[n], d_rows[n])],
        "factor_grad",
        3 * product,
        [scratch_like((sides, stacked, depth_here), BF16)] * 2
        + [
            scratch_like((sides, weights, rows, hidden), BF16),
            scratch_like((sides, stacked, hidden), BF16),
            scratch_like((weights, depth_here, hidden), F32),
            dma((sides, 3)),
            dma((weights, count)),
        ],
    )[0]
    mix_rows = call(
        mix_grad_body,
        [(shaped((mixing.size, cols), F32), VMEM)],
        [(x, HBM) for x in (y_gate, y_up, y_down, d_own)],
        "mix_partials",
        weights * 64 * 2 * rows * cols,
        [
            scratch_like((weights, stacked, hidden), F32),
            scratch_like((weights, rows, hidden), BF16),
            dma((4,)),
        ],
    )[0]
    mix_part = jnp.sum(mix_rows, axis=1).reshape(mix.shape)
    if swap:
        mix_grad = mix_part + across(mix_part)
    else:
        factor_grad = lax.psum_scatter(
            factor_grad.astype(BF16), "seq", scatter_dimension=2, tiled=True
        ).astype(F32)
        mix_grad = lax.psum(mix_part, "seq")
    gate_grad = (jnp.sum(inner, axis=1) * gate * (1.0 - gate)).reshape(selection.shape)
    token_grad = sum_rows(pieces, placed, returned)
    return token_grad, factor_grad[None], mix_grad, gate_grad


def solution(mesh):
    return jax.shard_map(
        shards,
        mesh=mesh,
        in_specs=(
            P(("seq", "exp"), None),
            P(("seq", "exp"), None),
            P("exp", None, None, "seq", None),
            P("exp", None, None, None, None),
            P("exp", "seq", None),
            P("exp", "seq", None),
        ),
        out_specs=(
            P(("seq", "exp"), None),
            P("exp", None, None, "seq", None),
            P("exp", None, None, None, None),
            P("exp", "seq", None),
        ),
        check_vma=False,
    )
```

```python
import functools

import jax
import jax.numpy as jnp
from jax import lax
from jax.experimental import pallas as pl
from jax.experimental.pallas import tpu as pltpu
from jax.sharding import PartitionSpec as P

SELECTED = 64
NPHM = 4
VMEM_LIMIT = 63 * 1024 * 1024
F32 = jnp.float32
BF16 = jnp.bfloat16


def iota(shape, dim):
    return lax.broadcasted_iota(jnp.int32, shape, dim)


def dot(left, right):
    return jnp.dot(left, right, preferred_element_type=F32)


def dot_tn(left, right):
    return lax.dot_general(left, right, (((0,), (0,)), ((), ())), preferred_element_type=F32)


def dot_nt(left, right):
    return lax.dot_general(left, right, (((1,), (1,)), ((), ())), preferred_element_type=F32)


HBM = pl.BlockSpec(memory_space=pltpu.HBM)
VMEM = pl.BlockSpec(memory_space=pltpu.VMEM)
SMEM = pl.BlockSpec(memory_space=pltpu.SMEM)


def call(body, outs, ins, name, flops, scratch=()):
    moved = sum(x.size * x.dtype.itemsize for x, _ in list(ins) + list(outs))
    return pl.pallas_call(
        body,
        out_shape=[x for x, _ in outs],
        in_specs=[place for _, place in ins],
        out_specs=[place for _, place in outs],
        scratch_shapes=list(scratch),
        compiler_params=pltpu.CompilerParams(vmem_limit_bytes=VMEM_LIMIT),
        cost_estimate=pl.CostEstimate(flops=flops, bytes_accessed=moved, transcendentals=0),
        name=name,
    )(*[x for x, _ in ins])


def begin(source, target, sem):
    copy = pltpu.make_async_copy(source, target, sem)
    copy.start()
    return copy


def shaped(shape, dtype):
    return jax.ShapeDtypeStruct(shape, dtype)


def scratch_like(shape, dtype):
    return pltpu.VMEM(shape, dtype)


def chunks_of(part):
    chunk = min(part, 512)
    return [slice(c * chunk, (c + 1) * chunk) for c in range(part // chunk)]


def front_body(cap, pieces, own_rows, block_len, half, cross, me_ref, chosen_hbm, *refs):
    chosen_ref, told_ref, slot_ref, small_sem = refs[-4:]
    small = begin(chosen_hbm, chosen_ref, small_sem.at[0])
    if cross:
        source_ref, told_hbm, slot_hbm, cross_ref, held_ref, sems = refs[:-4]
        width = cross_ref.shape[1]
        plane = lax.shift_right_logical(me_ref[0] & (half - 1), half.bit_length() - 2)
        at = pl.ds(pl.multiple_of((1 - plane) * width, width), width)
        load = begin(source_ref.at[:, at], held_ref, sems.at[0])
    else:
        told_hbm, slot_hbm = refs[:-4]
    small.wait()
    peers, rows = told_ref.shape[0] // 2, slot_ref.shape[1]
    blocks = [chosen_ref[b : b + 1, :] for b in range(chosen_ref.shape[0])]
    position = jnp.concatenate([x + b * block_len for b, x in enumerate(blocks)], axis=1)
    owner = lax.shift_right_logical(position, own_rows.bit_length() - 1)
    local = position & (own_rows - 1)
    peer = iota((peers, rows), 0)
    mine = (peer == owner).astype(F32)
    count = jnp.sum(mine, axis=1, keepdims=True)
    earlier = jnp.sum(jnp.where(peer < owner, count, 0.0), axis=0, keepdims=True).astype(jnp.int32)
    rank = iota((1, rows), 1) - earlier
    slot_ref[...] = owner * (cap * pieces) + rank
    lane = iota((rows, rows), 0)
    hit = jnp.zeros((rows, rows), F32)
    for j in range(pieces):
        hit = hit + (lane == rank + j * cap).astype(F32)
    twice = iota((2 * peers, rows), 0)
    marked = jnp.where(twice == 2 * owner, local + 1, 0).astype(F32)
    asked = dot_nt(marked.astype(BF16), hit.astype(BF16)).astype(jnp.int32)
    told_ref[...] = jnp.where((twice & 1) == 1, jnp.concatenate(blocks, axis=1), asked)
    stores = [
        begin(told_ref, told_hbm, small_sem.at[1]),
        begin(slot_ref, slot_hbm, small_sem.at[2]),
    ]
    if cross:
        load.wait()
        stores.append(begin(held_ref, cross_ref, sems.at[1]))
    for store in stores:
        store.wait()


def plane_columns(me, source, crossed, half):
    own_rows, width = source.shape
    part, count = width // half, half // 2

    def body(me_ref, source_ref, crossed_ref, *refs):
        outs, (held_ref, in_sem, out_sem) = refs[:count], refs[count:]
        low = me_ref[0] & (half - 1)
        plane = lax.shift_right_logical(low, half.bit_length() - 2)
        wide = count * part
        at = pl.ds(pl.multiple_of(plane * wide, wide), wide)
        loads = [
            begin(source_ref.at[:, at], held_ref.at[0], in_sem.at[0]),
            begin(crossed_ref, held_ref.at[1], in_sem.at[1]),
        ]
        copies = []
        for n, load in enumerate(loads):
            load.wait()
            for k in range(count):
                share = (low & (count - 1)) ^ k
                at = held_ref.at[n, :, pl.ds(pl.multiple_of(share * part, part), part)]
                rows = pl.ds(n * own_rows, own_rows)
                copies.append(begin(at, outs[k].at[rows], out_sem.at[n, k]))
        wait_all(copies)

    return call(
        body,
        [(shaped((2 * own_rows, part), BF16), HBM)] * count,
        [(me, SMEM), (source, HBM), (crossed, HBM)],
        "plane_columns",
        0,
        [
            scratch_like((2, own_rows, count * part), BF16),
            pltpu.SemaphoreType.DMA((2,)),
            pltpu.SemaphoreType.DMA((2, count)),
        ],
    )


def pick_matrix(cap, pieces, own_rows, requested):
    told, lanes = requested.shape
    peers = told // 2
    group = cap * pieces
    slots = peers * group
    peer = 2 * iota((peers, group, told), 0).reshape(slots, told)
    spread = dot(
        (peer == iota((slots, told), 1)).astype(BF16), requested.astype(F32).astype(BF16)
    )
    place = iota((peers, group, lanes), 1).reshape(slots, lanes)
    row = jnp.sum(
        jnp.where(place == iota((slots, lanes), 1), spread, 0.0), axis=1, keepdims=True
    ).astype(jnp.int32)
    piece = iota((peers, group, 1), 1).reshape(slots, 1)
    shift = jnp.zeros((slots, 1), jnp.int32)
    for j in range(1, pieces):
        shift = shift + jnp.where(piece >= j * cap, own_rows, 0)
    target = jnp.where(row > 0, row - 1 + shift, -1)
    return (target == iota((slots, pieces * own_rows), 1)).astype(BF16)


def pick_slots(cap, pieces, requested, source, after, name):
    own_rows, width = source.shape
    part = width // pieces
    slots = requested.shape[0] // 2 * cap * pieces
    columns = chunks_of(part)

    def body(requested_hbm, source_ref, *refs):
        out_ref, requested_ref, rows_ref, sent_ref, in_sem, out_sem = refs[len(after) :]
        asked = begin(requested_hbm, requested_ref, in_sem.at[len(columns), 0])
        loads = []
        for n, at in enumerate(columns):
            for j in range(pieces):
                wide = slice(j * part + at.start, j * part + at.stop)
                target = rows_ref.at[j * own_rows : (j + 1) * own_rows, at]
                loads.append(begin(source_ref.at[:, wide], target, in_sem.at[n, j]))
        asked.wait()
        pick = pick_matrix(cap, pieces, own_rows, requested_ref[...])
        stores = []
        for n, at in enumerate(columns):
            for load in loads[n * pieces : (n + 1) * pieces]:
                load.wait()
            sent_ref[:, at] = dot(pick, rows_ref[:, at]).astype(BF16)
            stores.append(begin(sent_ref.at[:, at], out_ref.at[:, at], out_sem.at[n]))
        for store in stores:
            store.wait()

    return call(
        body,
        [(shaped((slots, part), BF16), HBM)],
        [(requested, HBM), (source, HBM)] + [(x, HBM) for x in after],
        name,
        2 * slots * pieces * own_rows * part,
        [
            scratch_like(requested.shape, jnp.int32),
            scratch_like((pieces * own_rows, part), BF16),
            scratch_like((slots, part), BF16),
            pltpu.SemaphoreType.DMA((len(columns) + 1, pieces)),
            pltpu.SemaphoreType.DMA((len(columns),)),
        ],
    )[0]


def spread_columns(source, half):
    own_rows, width = source.shape
    part = width // half

    def body(source_ref, out_ref, held_ref, in_sem, out_sem):
        begin(source_ref, held_ref, in_sem).wait()
        copies = []
        for k in range(half):
            at = held_ref.at[:, k * part : (k + 1) * part]
            out = out_ref.at[k * own_rows : (k + 1) * own_rows]
            copies.append(begin(at, out, out_sem.at[k]))
        wait_all(copies)

    scratch = [
        scratch_like((own_rows, width), BF16),
        pltpu.SemaphoreType.DMA,
        pltpu.SemaphoreType.DMA((half,)),
    ]
    outs = [(shaped((half * own_rows, part), BF16), HBM)]
    return call(body, outs, [(source, HBM)], "spread_columns", 0, scratch)[0]


def cut_factors(factors, first):
    cuts = (slice(0, first), slice(first, factors.shape[0]))

    def body(factors_ref, *refs):
        outs, (held_ref, sems) = refs[:2], refs[2:]
        loads = [
            begin(factors_ref.at[at], held_ref.at[at], sems.at[0, n]) for n, at in enumerate(cuts)
        ]
        copies = []
        for n, at in enumerate(cuts):
            loads[n].wait()
            copies.append(begin(held_ref.at[at], outs[n], sems.at[1, n]))
        wait_all(copies)

    outs = [
        (shaped((at.stop - at.start,) + factors.shape[1:], BF16), HBM) for at in cuts
    ]
    scratch = [scratch_like(factors.shape, BF16), pltpu.SemaphoreType.DMA((2, 2))]
    return call(body, outs, [(factors, HBM)], "cut_factors", 0, scratch)


def pick_rows(me, half, own_rows, chosen, shares, after, name):
    peers, total = chosen.shape[0] // 2, chosen.shape[1]
    picks = total * half // peers
    part = shares[0].shape[1]
    block = half * own_rows
    batch = min(peers, 8)

    def body(me_ref, chosen_ref, *refs):
        refs = refs[len(after) :]
        parts, (out_ref, rows_ref, pick_ref, sent_ref, in_sem, out_sem) = (
            refs[: len(shares)],
            refs[len(shares) :],
        )
        loads = []
        for k in range(half):
            place = (me_ref[0] & (half - 1)) ^ k if len(parts) > 1 else k
            n, first = (k % len(parts), k // len(parts)) if len(parts) > 1 else (0, k)
            at = parts[n].at[first * own_rows : (first + 1) * own_rows]
            target = rows_ref.at[pl.ds(pl.multiple_of(place * own_rows, own_rows), own_rows)]
            loads.append(begin(at, target, in_sem.at[k]))
        block_at = lax.shift_right_logical(me_ref[0], half.bit_length() - 1)
        same = iota((picks, total), 0) + block_at * picks == iota((picks, total), 1)
        stores = []
        for first in range(0, peers, batch):
            for e in range(batch):
                wanted = chosen_ref[2 * (first + e) + 1 : 2 * (first + e) + 2, :]
                column = jnp.sum(jnp.where(same, wanted, 0), axis=1, keepdims=True)
                pick_ref[first // batch % 2, e * picks : (e + 1) * picks] = (
                    column == iota((picks, block), 1)
                ).astype(BF16)
            if first == 0:
                wait_all(loads)
            at = slice(first * picks, (first + batch) * picks)
            sent_ref[at] = dot(pick_ref[first // batch % 2], rows_ref[...]).astype(BF16)
            stores.append(begin(sent_ref.at[at], out_ref.at[at], out_sem.at[first // batch]))
        wait_all(stores)

    return call(
        body,
        [(shaped((peers * picks, part), BF16), HBM)],
        [(me, SMEM), (chosen, VMEM)] + [(x, HBM) for x in list(after) + list(shares)],
        name,
        2 * peers * picks * block * part,
        [
            scratch_like((block, part), BF16),
            scratch_like((2, batch * picks, block), BF16),
            scratch_like((peers * picks, part), BF16),
            pltpu.SemaphoreType.DMA((half,)),
            pltpu.SemaphoreType.DMA((peers // batch,)),
        ],
    )[0]


def place_rows(cap, pieces, own_rows, me, half, chosen):
    peers, total = chosen.shape[0] // 2, chosen.shape[1]
    picks = total * half // peers
    group = cap * pieces

    def body(me_ref, chosen_ref, out_ref, pick_ref):
        low = me_ref[0] & (half - 1)
        block_at = lax.shift_right_logical(me_ref[0], half.bit_length() - 1)
        lane = iota((2 * peers, total), 1) - block_at * picks
        here = (lane >= 0) & (lane < picks)
        local = jnp.where(here, chosen_ref[...] - low * own_rows, own_rows)
        before = jnp.sum((local < 0).astype(F32), axis=1, keepdims=True).astype(jnp.int32)
        ranks = lane - before
        owned = jnp.where((local >= 0) & (local < own_rows), local + 1, 0)
        place = iota((group, total), 0)
        for e in range(peers):
            at = slice(2 * e + 1, 2 * e + 2)
            rank, mine = ranks[at], owned[at]
            column = jnp.zeros((group, 1), jnp.int32)
            for j in range(pieces):
                hit = jnp.where((place == rank + j * cap) & (rank >= 0) & (rank < cap), mine, 0)
                row = jnp.sum(hit, axis=1, keepdims=True)
                column = column + jnp.where(row > 0, row + j * own_rows, 0)
            pick_ref[e * group : (e + 1) * group] = (
                column == iota((group, pieces * own_rows), 1) + 1
            ).astype(F32)
        out_ref[...] = jnp.transpose(pick_ref[...]).astype(BF16)

    return call(
        body,
        [(shaped((pieces * own_rows, peers * group), BF16), VMEM)],
        [(me, SMEM), (chosen, VMEM)],
        "place_rows",
        1 << 20,
        [scratch_like((peers * group, pieces * own_rows), F32)],
    )[0]


def sum_rows(pieces, placed, returned):
    slots, part = returned.shape
    own_rows = placed.shape[0] // pieces
    columns = chunks_of(part)

    def body(placed_hbm, returned_ref, out_ref, place_ref, got_ref, sum_ref, in_sem, out_sem):
        first = begin(placed_hbm, place_ref, in_sem.at[len(columns)])
        loads = [
            begin(returned_ref.at[:, at], got_ref.at[:, at], in_sem.at[n])
            for n, at in enumerate(columns)
        ]
        first.wait()
        stores = []
        for n, at in enumerate(columns):
            loads[n].wait()
            summed = dot(place_ref[...], got_ref[:, at]).astype(BF16)
            for j in range(pieces):
                wide = slice(j * part + at.start, j * part + at.stop)
                sum_ref[:, wide] = summed[j * own_rows : (j + 1) * own_rows]
                stores.append(
                    begin(sum_ref.at[:, wide], out_ref.at[:, wide], out_sem.at[n, j])
                )
        wait_all(stores)

    return call(
        body,
        [(shaped((own_rows, part * pieces), BF16), HBM)],
        [(placed, HBM), (returned, HBM)],
        "sum_rows",
        2 * slots * pieces * own_rows * part,
        [
            scratch_like(placed.shape, BF16),
            scratch_like((slots, part), BF16),
            scratch_like((own_rows, part * pieces), BF16),
            pltpu.SemaphoreType.DMA((len(columns) + 1,)),
            pltpu.SemaphoreType.DMA((len(columns), pieces)),
        ],
    )[0]


def load_factor(order_ref, parts, m, target, sems):
    copies = []
    _, count, rows, cols = parts[0].shape
    first = parts[1].shape[0] if len(parts) > 1 else 0
    for n in range(2 if len(parts) > 1 else 1):
        place = order_ref[0] ^ n if len(parts) > 1 else 0
        start = pl.multiple_of(place * rows, rows)
        for i in range(count):
            side = parts[0].at[m, i]
            if n == 1:
                flat = m * count + i
                side = parts[1].at[flat] if flat < first else parts[2].at[flat - first]
            at = target.at[pl.ds(start, rows), i * cols : (i + 1) * cols]
            copies.append(begin(side, at, sems.at[n, i]))
    return copies


def wait_all(copies):
    for copy in copies:
        copy.wait()


def place_matrix(cap, pieces, slots, slot):
    wide = jnp.concatenate([slot + j * cap for j in range(pieces)], axis=1)
    return (iota((slots, wide.shape[1]), 0) == wide).astype(BF16)


def load_rows(got_hbm, x_ref, sems):
    rows, depth = x_ref.shape[0] // NPHM, x_ref.shape[1]
    part = got_hbm.shape[1]
    shares = NPHM * depth // part
    picks = got_hbm.shape[0] * part // (NPHM * depth) // (rows // SELECTED)
    copies = []
    for n in range(got_hbm.shape[0] // picks):
        block, share = divmod(n, shares)
        a, start = share * part // depth, share * part % depth
        first = (block * NPHM + a) * picks
        at = x_ref.at[first : first + picks, start : start + part]
        copies.append(begin(got_hbm.at[n * picks : (n + 1) * picks], at, sems.at[n]))
    return copies


def load_slots(got_hbm, got_ref, sems):
    return [
        begin(got_hbm.at[:, at], got_ref.at[:, at], sems.at[n])
        for n, at in enumerate(chunks_of(got_ref.shape[1]))
    ]


def stack_rows(pieces, place, loads, got_ref, out_ref):
    part = got_ref.shape[1]
    rows, depth = out_ref.shape[0] // NPHM, out_ref.shape[1]
    for load, at in zip(loads, chunks_of(part)):
        load.wait()
        block = dot_tn(place, got_ref[:, at]).astype(BF16)
        for j in range(pieces):
            column = j * part + at.start
            a, start = column // depth, column % depth
            for n in range(rows // STRIP):
                first = (n * NPHM + a) * STRIP
                out_ref[first : first + STRIP, start : start + at.stop - at.start] = block[
                    j * rows + n * STRIP : j * rows + (n + 1) * STRIP
                ]


def store_parts(order_ref, source_ref, outs, sems):
    copies = []
    for n, out in enumerate(outs):
        size = out.shape[1]
        start = pl.multiple_of((order_ref[0] ^ n) * size if len(outs) > 1 else 0, size)
        copies.append(begin(source_ref.at[:, pl.ds(start, size)], out, sems.at[n]))
    return copies


STRIP = SELECTED


def rows_of(n, a):
    return slice((n * NPHM + a) * STRIP, (n * NPHM + a + 1) * STRIP)


def mix_in(mix_ref, m, y_ref, n):
    cols = y_ref.shape[1] // NPHM
    total = [jnp.zeros((STRIP, cols), F32)] * NPHM
    for a in range(NPHM):
        for i in range(NPHM):
            block = y_ref[rows_of(n, a), i * cols : (i + 1) * cols]
            for b in range(NPHM):
                total[b] = total[b] + mix_ref[m * 64 + i * 16 + a * 4 + b] * block
    return total


def mix_out(mix_ref, m, blocks, n, z_ref, offset=0):
    cols = blocks[0].shape[1]
    for a in range(NPHM):
        for i in range(NPHM):
            total = mix_ref[m * 64 + i * 16 + a * 4] * blocks[0]
            for b in range(1, NPHM):
                total = total + mix_ref[m * 64 + i * 16 + a * 4 + b] * blocks[b]
            z_ref[rows_of(n, a), offset + i * cols : offset + (i + 1) * cols] = total.astype(
                z_ref.dtype
            )


def blocks_of(d_ref, n):
    cols = d_ref.shape[1] // NPHM
    at = slice(n * STRIP, (n + 1) * STRIP)
    return [d_ref[at, b * cols : (b + 1) * cols].astype(F32) for b in range(NPHM)]


def order_body(cap, pieces, order_ref, slot_hbm, got_hbm, *refs):
    x_outs, (got_ref, x_ref, slot_ref, got_sem, out_sem) = refs[:-5], refs[-5:]
    small = begin(slot_hbm, slot_ref, got_sem.at[got_sem.shape[0] - 1])
    loads = load_slots(got_hbm, got_ref, got_sem)
    small.wait()
    place = place_matrix(cap, pieces, got_ref.shape[0], slot_ref[...])
    stack_rows(pieces, place, loads, got_ref, x_ref)
    wait_all(store_parts(order_ref, x_ref, x_outs, out_sem))


def forward_body(sides, order_ref, mix_ref, *refs):
    x_parts, refs = refs[:sides], refs[sides:]
    held = 2 if sides > 1 else 1
    parts, refs = refs[:held], refs[held:]
    yg_hbm, yu_hbm, act_hbm, slope_hbm, hid_hbm = refs[:5]
    side_ref, x_ref, yg_ref, yu_ref, act_ref, slope_ref, hid_ref = refs[5:12]
    x_sem, side_sem, out_sem = refs[12:]
    loads = []
    for n, part in enumerate(x_parts):
        size = part.shape[1]
        start = pl.multiple_of((order_ref[0] ^ n) * size if sides > 1 else 0, size)
        loads.append(begin(part, x_ref.at[:, pl.ds(start, size)], x_sem.at[n]))
    sides_in = [
        load_factor(order_ref, parts, m, side_ref.at[m], side_sem.at[m]) for m in range(2)
    ]
    wait_all(loads)
    stores = []
    wait_all(sides_in[0])
    yg_ref[...] = dot(x_ref[...], side_ref[0])
    stores.append(begin(yg_ref, yg_hbm, out_sem.at[2]))
    wait_all(sides_in[1])
    yu_ref[...] = dot(x_ref[...], side_ref[1])
    stores.append(begin(yu_ref, yu_hbm, out_sem.at[3]))
    cols = yg_ref.shape[1] // NPHM
    for n in range(yg_ref.shape[0] // (NPHM * STRIP)):
        gates = mix_in(mix_ref, 0, yg_ref, n)
        ups = mix_in(mix_ref, 1, yu_ref, n)
        for b in range(NPHM):
            at = (slice(n * STRIP, (n + 1) * STRIP), slice(b * cols, (b + 1) * cols))
            sig = jax.nn.sigmoid(gates[b])
            act = gates[b] * sig
            act_ref[at] = act
            slope_ref[at] = ups[b] * (sig + act * (1.0 - sig))
            hid_ref[at] = act * ups[b]
    stores.append(begin(act_ref, act_hbm, out_sem.at[4]))
    stores.append(begin(slope_ref, slope_hbm, out_sem.at[5]))
    stores.append(begin(hid_ref, hid_hbm, out_sem.at[6]))
    wait_all(stores)


def backward_body(
    cap, pieces, sides, after, order_ref, mix_ref, slot_hbm, score_hbm, got_hbm, act_hbm, slope_hbm, hid_hbm,
    *refs,
):
    held = 3 if sides > 1 else 1
    parts, refs = refs[:held], refs[held + after :]
    back_hbm, x_outs, refs = refs[0], refs[1 : 1 + sides], refs[1 + sides :]
    y_hbm, d_hbm, inner_hbm = refs[:3]
    (
        down_ref, side_ref, x_ref, y_ref, d_ref, act_ref, slope_ref, hid_ref, z_ref, grad_ref,
        back_ref, inner_ref, slot_ref, score_ref, got_sem, side_sem, in_sem, out_sem,
    ) = refs[3:]
    loads = load_rows(got_hbm, x_ref, got_sem)
    down_in = load_factor(order_ref, parts, 2, down_ref, side_sem.at[2])
    small_in = [
        begin(source, target, in_sem.at[n])
        for n, (source, target) in enumerate(((score_hbm, score_ref), (slot_hbm, slot_ref)))
    ]
    flat_in = [
        begin(source, target, in_sem.at[2 + n])
        for n, (source, target) in enumerate(
            ((act_hbm, act_ref), (slope_hbm, slope_ref), (hid_hbm, hid_ref))
        )
    ]
    hidden = d_ref.shape[2]
    sides_in = []
    for m in range(2):
        target = side_ref.at[:, m * hidden : (m + 1) * hidden]
        sides_in += load_factor(order_ref, parts, m, target, side_sem.at[m])
    wait_all(small_in)
    score = jnp.concatenate([score_ref[b : b + 1, :] for b in range(score_ref.shape[0])], axis=1)
    rows = score.shape[1]
    same = iota((rows, rows), 0) == iota((rows, rows), 1)
    score = jnp.sum(jnp.where(same, score.astype(F32), 0.0), axis=1, keepdims=True)
    cols = hidden // NPHM
    gates = jnp.broadcast_to(jax.nn.sigmoid(score / 64.0), (rows, cols))
    place = place_matrix(cap, pieces, back_ref.shape[0], slot_ref[...])
    strips = rows // STRIP
    tall = NPHM * STRIP
    wait_all(loads)
    stores = store_parts(order_ref, x_ref, x_outs, out_sem)
    wait_all(down_in)
    for n in range(strips):
        y_ref[n * tall : (n + 1) * tall] = dot(x_ref[n * tall : (n + 1) * tall], down_ref[...])
    stores.append(begin(y_ref, y_hbm, out_sem.at[2]))
    wait_all(flat_in)
    wait_all(sides_in)
    for n in range(strips):
        down = mix_in(mix_ref, 2, y_ref, n)
        strip = slice(n * STRIP, (n + 1) * STRIP)
        gate = gates[strip]
        inner = jnp.zeros((STRIP, cols), F32)
        d_gate, d_up = [], []
        for b in range(NPHM):
            at = (strip, slice(b * cols, (b + 1) * cols))
            inner = inner + hid_ref[at] * down[b]
            hidden_grad = gate * down[b]
            d_gate.append(hidden_grad * slope_ref[at])
            d_up.append(hidden_grad * act_ref[at])
            d_ref[(0,) + at] = d_gate[b].astype(BF16)
            d_ref[(1,) + at] = d_up[b].astype(BF16)
            d_ref[(2,) + at] = (hid_ref[at] * gate).astype(BF16)
        inner_ref[strip] = inner
        mix_out(mix_ref, 0, d_gate, n, z_ref)
        mix_out(mix_ref, 1, d_up, n, z_ref, hidden)
        at = slice(n * tall, (n + 1) * tall)
        grad_ref[at] = dot_nt(z_ref[at], side_ref[...]).astype(BF16)
    stores.append(begin(d_ref, d_hbm, out_sem.at[3]))
    stores.append(begin(inner_ref, inner_hbm, out_sem.at[4]))
    part, depth = back_ref.shape[1], x_ref.shape[1]
    for k, at in enumerate(chunks_of(part)):
        blocks = []
        for j in range(pieces):
            column = j * part + at.start
            a, start = column // depth, column % depth
            wide = slice(start, start + at.stop - at.start)
            blocks += [grad_ref[rows_of(n, a), wide] for n in range(strips)]
        back_ref[:, at] = dot(place, jnp.concatenate(blocks, axis=0)).astype(BF16)
        stores.append(begin(back_ref.at[:, at], back_hbm.at[:, at], out_sem.at[5 + k]))
    wait_all(stores)


def factor_body(count_groups, mix_ref, *refs):
    rows_in, refs = refs[: 3 * count_groups], refs[3 * count_groups :]
    out_hbm, x_ref, g_ref, d_ref, z_ref, sum_ref, in_sem, out_sem = refs
    loads = []
    for n in range(count_groups):
        for k, target in enumerate((x_ref, g_ref, d_ref)):
            loads.append(begin(rows_in[3 * n + k], target.at[n], in_sem.at[n, k]))
    stores = []
    cols = out_hbm.shape[3]
    wait_all(loads)
    for m in (2, 0, 1):
        for n in range(count_groups):
            for strip in range(d_ref.shape[2] // STRIP):
                blocks = blocks_of(d_ref.at[n, m], strip)
                mix_out(mix_ref, m, blocks, strip, z_ref.at[n])
        left = g_ref if m == 2 else x_ref
        sum_ref[m] = sum(dot_tn(left[n], z_ref[n]) for n in range(count_groups))
        for i in range(NPHM):
            at = sum_ref.at[m, :, i * cols : (i + 1) * cols]
            stores.append(begin(at, out_hbm.at[m, i], out_sem.at[m, i]))
    wait_all(stores)


def mix_grad_body(yg_hbm, yu_hbm, yd_hbm, d_hbm, out_ref, y_ref, d_ref, sems):
    loads = [begin(d_hbm, d_ref, sems.at[3])]
    for m, source in enumerate((yg_hbm, yu_hbm, yd_hbm)):
        loads.append(begin(source, y_ref.at[m], sems.at[m]))
    wait_all(loads)
    rows, cols = d_ref.shape[1], d_ref.shape[2] // NPHM
    for m in range(3):
        for a in range(NPHM):
            for i in range(NPHM):
                at = slice(i * cols, (i + 1) * cols)
                strips = range(rows // STRIP)
                block = jnp.concatenate([y_ref[m, rows_of(n, a), at] for n in strips], axis=0)
                for b in range(NPHM):
                    at = m * 64 + i * 16 + a * 4 + b
                    other = d_ref[m, :, b * cols : (b + 1) * cols].astype(F32)
                    out_ref[at : at + 1, :] = jnp.sum(block * other, axis=0, keepdims=True)


def shards(tokens, cotangent, factors, mix, selection, scores):
    peers = lax.axis_size("exp")
    groups = lax.axis_size("seq")
    own_rows, width = tokens.shape
    _, weights, count, depth_own, cols = factors.shape
    depth = depth_own * groups
    hidden = count * cols
    cap = 3 * own_rows // (2 * peers)
    pieces = 1
    while (cap * pieces) % 8:
        pieces *= 2
    slots = peers * cap * pieces
    part = width // pieces
    steps = len(chunks_of(part))
    block_len = peers * SELECTED
    rows = selection.shape[1] * selection.shape[2]
    stacked = count * rows
    swap = groups == 2
    pair = [(0, 1), (1, 0)]
    mixing = mix.reshape(-1)
    dma = pltpu.SemaphoreType.DMA

    def across(array):
        return lax.ppermute(array, "seq", pair)

    half = peers // selection.shape[1]
    direct = half == 8
    me = lax.axis_index("exp").astype(jnp.int32).reshape(1)
    group = lax.axis_index("seq").astype(jnp.int32).reshape(1)
    halves = [list(range(h, h + half)) for h in range(0, peers, half)]
    if swap:
        flat_factors = factors[0].reshape(weights * count, depth_own, cols)
        cuts = [across(x) for x in cut_factors(flat_factors, 2 * count)]
        factor_parts = [factors[0]] + cuts
        sides = 2
    else:
        cuts = []
        factor_parts = [lax.all_gather(factors, "seq", axis=3, tiled=True)[0]]
        sides = 1
    sides_in = [(x, HBM) for x in factor_parts]
    cross = [(shaped((own_rows, width // 2), BF16), HBM)] if direct else []
    told, slot, *crossed = call(
        functools.partial(front_body, cap, pieces, own_rows, block_len, half, direct),
        [(shaped((2 * peers, rows), jnp.int32), HBM), (shaped((1, rows), jnp.int32), HBM)] + cross,
        [(me, SMEM), (selection[0], HBM)] + ([(cotangent, HBM)] if direct else []),
        "wanted_rows",
        1 << 20,
        ([scratch_like((own_rows, width // 2), BF16), dma((2,))] if direct else [])
        + [scratch_like(selection.shape[1:], jnp.int32)]
        + [scratch_like((2 * peers, rows), jnp.int32), scratch_like((1, rows), jnp.int32)]
        + [dma((3,))],
    )
    if direct:
        crossed = [lax.ppermute(crossed[0], "exp", [(n, n ^ (half // 2)) for n in range(peers)])]
    chosen = lax.all_to_all(told, "exp", split_axis=0, concat_axis=0, tiled=True)

    def to_peers(array):
        array = array.reshape(peers, -1, array.shape[1])
        array = lax.all_to_all(array, "exp", split_axis=0, concat_axis=0, tiled=True)
        return array.reshape(-1, array.shape[2])

    got_rows = to_peers(pick_slots(cap, pieces, chosen, tokens, crossed, "pick_tokens"))
    if direct:
        shares = plane_columns(me, cotangent, crossed[0], half)
        shares = [shares[0]] + [
            lax.ppermute(shares[k], "exp", [(n, n ^ k) for n in range(peers)])
            for k in range(1, half // 2)
        ]
    else:
        array = spread_columns(cotangent, half).reshape(half, own_rows, -1)
        array = lax.all_to_all(
            array, "exp", split_axis=0, concat_axis=0, axis_index_groups=halves, tiled=True
        )
        shares = [array.reshape(half * own_rows, -1)]
    picked = pick_rows(me, half, own_rows, chosen, shares, cuts[:1], "pick_cotangent")
    got_grads = to_peers(picked)
    placed = place_rows(cap, pieces, own_rows, me, half, chosen)
    gate = jax.nn.sigmoid(scores[0].reshape(-1).astype(F32) / 64.0)

    product = 2 * stacked * depth * hidden
    split = [(shaped((stacked, depth // sides), BF16), HBM)] * sides
    mixed = (shaped((stacked, hidden), F32), HBM)
    flat = (shaped((rows, hidden), F32), HBM)
    back_scratch = scratch_like((slots, part), BF16)
    pieces_in = got_grads.shape[0] // SELECTED
    stack_scratch = scratch_like((stacked, depth), BF16)
    mixed_scratch = scratch_like((stacked, hidden), F32)
    low_scratch = scratch_like((stacked, hidden), BF16)
    flat_scratch = scratch_like((rows, hidden), F32)
    x_parts = call(
        functools.partial(order_body, cap, pieces),
        split,
        [(group, SMEM), (slot, HBM), (got_rows, HBM)],
        "order_rows",
        product // 4,
        [back_scratch, stack_scratch, scratch_like(slot.shape, jnp.int32)]
        + [dma((steps + 1,)), dma((2,))],
    )
    y_gate, y_up, act, slope, hid = call(
        functools.partial(forward_body, sides),
        [mixed, mixed, flat, flat, flat],
        [(group, SMEM), (mixing, SMEM)] + [(x, HBM) for x in x_parts] + sides_in[:2],
        "forward",
        2 * product,
        [scratch_like((2, depth, hidden), BF16), stack_scratch, mixed_scratch, mixed_scratch]
        + [flat_scratch] * 3
        + [dma((2,)), dma((2, sides, count)), dma((7,))],
    )
    x_rows = [x_parts[0]] + [across(x) for x in x_parts[1:]]
    after = x_rows[1:]
    outs = call(
        functools.partial(backward_body, cap, pieces, sides, len(after)),
        [(shaped((slots, part), BF16), HBM)]
        + split
        + [mixed, (shaped((weights, rows, hidden), BF16), HBM), (shaped((rows, cols), F32), HBM)],
        [(group, SMEM), (mixing, SMEM), (slot, HBM), (scores[0], HBM), (got_grads, HBM)]
        + [(x, HBM) for x in (act, slope, hid)]
        + sides_in
        + [(x, HBM) for x in after],
        "backward",
        3 * product,
        [scratch_like((depth, hidden), BF16), scratch_like((depth, 2 * hidden), BF16)]
        + [stack_scratch, mixed_scratch, scratch_like((weights, rows, hidden), BF16)]
        + [flat_scratch] * 3
        + [scratch_like((stacked, 2 * hidden), BF16), stack_scratch, back_scratch]
        + [scratch_like((rows, cols), F32), scratch_like(slot.shape, jnp.int32)]
        + [scratch_like(scores.shape[1:], jnp.int32)]
        + [dma((pieces_in,)), dma((weights, sides, count)), dma((5,)), dma((5 + steps,))],
    )
    back, g_parts, (y_down, d_own, inner) = outs[0], outs[1 : 1 + sides], outs[1 + sides :]
    returned = to_peers(back)

    d_rows = [d_own] + [across(d_own) for _ in x_parts[1:]]
    g_rows = [g_parts[0]] + [across(x) for x in g_parts[1:]]
    depth_here = depth // sides
    factor_grad = call(
        functools.partial(factor_body, sides),
        [(shaped((weights, count, depth_here, cols), F32), HBM)],
        [(mixing, SMEM)]
        + [(x, HBM) for n in range(sides) for x in (x_rows[n], g_rows[n], d_rows[n])],
        "factor_grad",
        3 * product,
        [scratch_like((sides, stacked, depth_here), BF16)] * 2
        + [
            scratch_like((sides, weights, rows, hidden), BF16),
            scratch_like((sides, stacked, hidden), BF16),
            scratch_like((weights, depth_here, hidden), F32),
            dma((sides, 3)),
            dma((weights, count)),
        ],
    )[0]
    mix_rows = call(
        mix_grad_body,
        [(shaped((mixing.size, cols), F32), VMEM)],
        [(x, HBM) for x in (y_gate, y_up, y_down, d_own)],
        "mix_partials",
        weights * 64 * 2 * rows * cols,
        [
            scratch_like((weights, stacked, hidden), F32),
            scratch_like((weights, rows, hidden), BF16),
            dma((4,)),
        ],
    )[0]
    mix_part = jnp.sum(mix_rows, axis=1).reshape(mix.shape)
    if swap:
        mix_grad = mix_part + across(mix_part)
    else:
        factor_grad = lax.psum_scatter(
            factor_grad.astype(BF16), "seq", scatter_dimension=2, tiled=True
        ).astype(F32)
        mix_grad = lax.psum(mix_part, "seq")
    gate_grad = (jnp.sum(inner, axis=1) * gate * (1.0 - gate)).reshape(selection.shape)
    token_grad = sum_rows(pieces, placed, returned)
    return token_grad, factor_grad[None], mix_grad, gate_grad


def solution(mesh):
    return jax.shard_map(
        shards,
        mesh=mesh,
        in_specs=(
            P(("seq", "exp"), None),
            P(("seq", "exp"), None),
            P("exp", None, None, "seq", None),
            P("exp", None, None, None, None),
            P("exp", "seq", None),
            P("exp", "seq", None),
        ),
        out_specs=(
            P(("seq", "exp"), None),
            P("exp", None, None, "seq", None),
            P("exp", None, None, None, None),
            P("exp", "seq", None),
        ),
        check_vma=False,
    )
```

```python
import functools

import jax
import jax.numpy as jnp
from jax import lax
from jax.experimental import pallas as pl
from jax.experimental.pallas import tpu as pltpu
from jax.sharding import PartitionSpec as P

SELECTED = 64
NPHM = 4
VMEM_LIMIT = 63 * 1024 * 1024
F32 = jnp.float32
BF16 = jnp.bfloat16


def iota(shape, dim):
    return lax.broadcasted_iota(jnp.int32, shape, dim)


def dot(left, right):
    return jnp.dot(left, right, preferred_element_type=F32)


def dot_tn(left, right):
    return lax.dot_general(left, right, (((0,), (0,)), ((), ())), preferred_element_type=F32)


def dot_nt(left, right):
    return lax.dot_general(left, right, (((1,), (1,)), ((), ())), preferred_element_type=F32)


HBM = pl.BlockSpec(memory_space=pltpu.HBM)
VMEM = pl.BlockSpec(memory_space=pltpu.VMEM)
SMEM = pl.BlockSpec(memory_space=pltpu.SMEM)


def call(body, outs, ins, name, flops, scratch=()):
    moved = sum(x.size * x.dtype.itemsize for x, _ in list(ins) + list(outs))
    return pl.pallas_call(
        body,
        out_shape=[x for x, _ in outs],
        in_specs=[place for _, place in ins],
        out_specs=[place for _, place in outs],
        scratch_shapes=list(scratch),
        compiler_params=pltpu.CompilerParams(vmem_limit_bytes=VMEM_LIMIT),
        cost_estimate=pl.CostEstimate(flops=flops, bytes_accessed=moved, transcendentals=0),
        name=name,
    )(*[x for x, _ in ins])


def begin(source, target, sem):
    copy = pltpu.make_async_copy(source, target, sem)
    copy.start()
    return copy


def shaped(shape, dtype):
    return jax.ShapeDtypeStruct(shape, dtype)


def scratch_like(shape, dtype):
    return pltpu.VMEM(shape, dtype)


def chunks_of(part):
    chunk = min(part, 512)
    return [slice(c * chunk, (c + 1) * chunk) for c in range(part // chunk)]


def front_body(cap, pieces, own_rows, block_len, half, cross, me_ref, chosen_hbm, *refs):
    chosen_ref, told_ref, slot_ref, small_sem = refs[-4:]
    small = begin(chosen_hbm, chosen_ref, small_sem.at[0])
    if cross:
        source_ref, told_hbm, slot_hbm, cross_ref, held_ref, sems = refs[:-4]
        width = cross_ref.shape[1]
        plane = lax.shift_right_logical(me_ref[0] & (half - 1), half.bit_length() - 2)
        at = pl.ds(pl.multiple_of((1 - plane) * width, width), width)
        load = begin(source_ref.at[:, at], held_ref, sems.at[0])
    else:
        told_hbm, slot_hbm = refs[:-4]
    small.wait()
    peers, rows = told_ref.shape[0] // 2, slot_ref.shape[1]
    blocks = [chosen_ref[b : b + 1, :] for b in range(chosen_ref.shape[0])]
    position = jnp.concatenate([x + b * block_len for b, x in enumerate(blocks)], axis=1)
    owner = lax.shift_right_logical(position, own_rows.bit_length() - 1)
    local = position & (own_rows - 1)
    peer = iota((peers, rows), 0)
    mine = (peer == owner).astype(F32)
    count = jnp.sum(mine, axis=1, keepdims=True)
    earlier = jnp.sum(jnp.where(peer < owner, count, 0.0), axis=0, keepdims=True).astype(jnp.int32)
    rank = iota((1, rows), 1) - earlier
    slot_ref[...] = owner * (cap * pieces) + rank
    lane = iota((rows, rows), 0)
    hit = jnp.zeros((rows, rows), F32)
    for j in range(pieces):
        hit = hit + (lane == rank + j * cap).astype(F32)
    twice = iota((2 * peers, rows), 0)
    marked = jnp.where(twice == 2 * owner, local + 1, 0).astype(F32)
    asked = dot_nt(marked.astype(BF16), hit.astype(BF16)).astype(jnp.int32)
    told_ref[...] = jnp.where((twice & 1) == 1, jnp.concatenate(blocks, axis=1), asked)
    stores = [
        begin(told_ref, told_hbm, small_sem.at[1]),
        begin(slot_ref, slot_hbm, small_sem.at[2]),
    ]
    if cross:
        load.wait()
        stores.append(begin(held_ref, cross_ref, sems.at[1]))
    for store in stores:
        store.wait()


def plane_columns(me, source, crossed, half):
    own_rows, width = source.shape
    part, count = width // half, half // 2

    def body(me_ref, source_ref, crossed_ref, *refs):
        outs, (held_ref, in_sem, out_sem) = refs[:count], refs[count:]
        low = me_ref[0] & (half - 1)
        plane = lax.shift_right_logical(low, half.bit_length() - 2)
        wide = count * part
        at = pl.ds(pl.multiple_of(plane * wide, wide), wide)
        loads = [
            begin(source_ref.at[:, at], held_ref.at[0], in_sem.at[0]),
            begin(crossed_ref, held_ref.at[1], in_sem.at[1]),
        ]
        copies = []
        for n, load in enumerate(loads):
            load.wait()
            for k in range(count):
                share = (low & (count - 1)) ^ k
                at = held_ref.at[n, :, pl.ds(pl.multiple_of(share * part, part), part)]
                rows = pl.ds(n * own_rows, own_rows)
                copies.append(begin(at, outs[k].at[rows], out_sem.at[n, k]))
        wait_all(copies)

    return call(
        body,
        [(shaped((2 * own_rows, part), BF16), HBM)] * count,
        [(me, SMEM), (source, HBM), (crossed, HBM)],
        "plane_columns",
        0,
        [
            scratch_like((2, own_rows, count * part), BF16),
            pltpu.SemaphoreType.DMA((2,)),
            pltpu.SemaphoreType.DMA((2, count)),
        ],
    )


def pick_matrix(cap, pieces, own_rows, requested):
    told, lanes = requested.shape
    peers = told // 2
    group = cap * pieces
    slots = peers * group
    peer = 2 * iota((peers, group, told), 0).reshape(slots, told)
    spread = dot(
        (peer == iota((slots, told), 1)).astype(BF16), requested.astype(F32).astype(BF16)
    )
    place = iota((peers, group, lanes), 1).reshape(slots, lanes)
    row = jnp.sum(
        jnp.where(place == iota((slots, lanes), 1), spread, 0.0), axis=1, keepdims=True
    ).astype(jnp.int32)
    piece = iota((peers, group, 1), 1).reshape(slots, 1)
    shift = jnp.zeros((slots, 1), jnp.int32)
    for j in range(1, pieces):
        shift = shift + jnp.where(piece >= j * cap, own_rows, 0)
    target = jnp.where(row > 0, row - 1 + shift, -1)
    return (target == iota((slots, pieces * own_rows), 1)).astype(BF16)


def pick_slots(cap, pieces, requested, source, after, name):
    own_rows, width = source.shape
    part = width // pieces
    slots = requested.shape[0] // 2 * cap * pieces
    columns = chunks_of(part)

    def body(requested_hbm, source_ref, *refs):
        out_ref, requested_ref, rows_ref, sent_ref, in_sem, out_sem = refs[len(after) :]
        asked = begin(requested_hbm, requested_ref, in_sem.at[len(columns), 0])
        loads = []
        for n, at in enumerate(columns):
            for j in range(pieces):
                wide = slice(j * part + at.start, j * part + at.stop)
                target = rows_ref.at[j * own_rows : (j + 1) * own_rows, at]
                loads.append(begin(source_ref.at[:, wide], target, in_sem.at[n, j]))
        asked.wait()
        pick = pick_matrix(cap, pieces, own_rows, requested_ref[...])
        stores = []
        for n, at in enumerate(columns):
            for load in loads[n * pieces : (n + 1) * pieces]:
                load.wait()
            sent_ref[:, at] = dot(pick, rows_ref[:, at]).astype(BF16)
            stores.append(begin(sent_ref.at[:, at], out_ref.at[:, at], out_sem.at[n]))
        for store in stores:
            store.wait()

    return call(
        body,
        [(shaped((slots, part), BF16), HBM)],
        [(requested, HBM), (source, HBM)] + [(x, HBM) for x in after],
        name,
        2 * slots * pieces * own_rows * part,
        [
            scratch_like(requested.shape, jnp.int32),
            scratch_like((pieces * own_rows, part), BF16),
            scratch_like((slots, part), BF16),
            pltpu.SemaphoreType.DMA((len(columns) + 1, pieces)),
            pltpu.SemaphoreType.DMA((len(columns),)),
        ],
    )[0]


def spread_columns(source, half):
    own_rows, width = source.shape
    part = width // half

    def body(source_ref, out_ref, held_ref, in_sem, out_sem):
        begin(source_ref, held_ref, in_sem).wait()
        copies = []
        for k in range(half):
            at = held_ref.at[:, k * part : (k + 1) * part]
            out = out_ref.at[k * own_rows : (k + 1) * own_rows]
            copies.append(begin(at, out, out_sem.at[k]))
        wait_all(copies)

    scratch = [
        scratch_like((own_rows, width), BF16),
        pltpu.SemaphoreType.DMA,
        pltpu.SemaphoreType.DMA((half,)),
    ]
    outs = [(shaped((half * own_rows, part), BF16), HBM)]
    return call(body, outs, [(source, HBM)], "spread_columns", 0, scratch)[0]


def cut_factors(factors, first):
    cuts = (slice(0, first), slice(first, factors.shape[0]))

    def body(factors_ref, *refs):
        outs, (held_ref, sems) = refs[:2], refs[2:]
        loads = [
            begin(factors_ref.at[at], held_ref.at[at], sems.at[0, n]) for n, at in enumerate(cuts)
        ]
        copies = []
        for n, at in enumerate(cuts):
            loads[n].wait()
            copies.append(begin(held_ref.at[at], outs[n], sems.at[1, n]))
        wait_all(copies)

    outs = [
        (shaped((at.stop - at.start,) + factors.shape[1:], BF16), HBM) for at in cuts
    ]
    scratch = [scratch_like(factors.shape, BF16), pltpu.SemaphoreType.DMA((2, 2))]
    return call(body, outs, [(factors, HBM)], "cut_factors", 0, scratch)


def pick_rows(me, half, own_rows, chosen, shares, after, name):
    peers, total = chosen.shape[0] // 2, chosen.shape[1]
    picks = total * half // peers
    part = shares[0].shape[1]
    block = half * own_rows
    batch = min(peers, 8)

    def body(me_ref, chosen_ref, *refs):
        refs = refs[len(after) :]
        parts, (out_ref, rows_ref, pick_ref, sent_ref, in_sem, out_sem) = (
            refs[: len(shares)],
            refs[len(shares) :],
        )
        loads = []
        for k in range(half):
            place = (me_ref[0] & (half - 1)) ^ k if len(parts) > 1 else k
            n, first = (k % len(parts), k // len(parts)) if len(parts) > 1 else (0, k)
            at = parts[n].at[first * own_rows : (first + 1) * own_rows]
            target = rows_ref.at[pl.ds(pl.multiple_of(place * own_rows, own_rows), own_rows)]
            loads.append(begin(at, target, in_sem.at[k]))
        block_at = lax.shift_right_logical(me_ref[0], half.bit_length() - 1)
        same = iota((picks, total), 0) + block_at * picks == iota((picks, total), 1)
        stores = []
        for first in range(0, peers, batch):
            for e in range(batch):
                wanted = chosen_ref[2 * (first + e) + 1 : 2 * (first + e) + 2, :]
                column = jnp.sum(jnp.where(same, wanted, 0), axis=1, keepdims=True)
                pick_ref[first // batch % 2, e * picks : (e + 1) * picks] = (
                    column == iota((picks, block), 1)
                ).astype(BF16)
            if first == 0:
                wait_all(loads)
            at = slice(first * picks, (first + batch) * picks)
            sent_ref[at] = dot(pick_ref[first // batch % 2], rows_ref[...]).astype(BF16)
            stores.append(begin(sent_ref.at[at], out_ref.at[at], out_sem.at[first // batch]))
        wait_all(stores)

    return call(
        body,
        [(shaped((peers * picks, part), BF16), HBM)],
        [(me, SMEM), (chosen, VMEM)] + [(x, HBM) for x in list(after) + list(shares)],
        name,
        2 * peers * picks * block * part,
        [
            scratch_like((block, part), BF16),
            scratch_like((2, batch * picks, block), BF16),
            scratch_like((peers * picks, part), BF16),
            pltpu.SemaphoreType.DMA((half,)),
            pltpu.SemaphoreType.DMA((peers // batch,)),
        ],
    )[0]


def place_rows(cap, pieces, own_rows, me, half, chosen):
    peers, total = chosen.shape[0] // 2, chosen.shape[1]
    picks = total * half // peers
    group = cap * pieces

    def body(me_ref, chosen_ref, out_ref, pick_ref):
        low = me_ref[0] & (half - 1)
        block_at = lax.shift_right_logical(me_ref[0], half.bit_length() - 1)
        lane = iota((2 * peers, total), 1) - block_at * picks
        here = (lane >= 0) & (lane < picks)
        local = jnp.where(here, chosen_ref[...] - low * own_rows, own_rows)
        before = jnp.sum((local < 0).astype(F32), axis=1, keepdims=True).astype(jnp.int32)
        ranks = lane - before
        owned = jnp.where((local >= 0) & (local < own_rows), local + 1, 0)
        place = iota((group, total), 0)
        for e in range(peers):
            at = slice(2 * e + 1, 2 * e + 2)
            rank, mine = ranks[at], owned[at]
            column = jnp.zeros((group, 1), jnp.int32)
            for j in range(pieces):
                hit = jnp.where((place == rank + j * cap) & (rank >= 0) & (rank < cap), mine, 0)
                row = jnp.sum(hit, axis=1, keepdims=True)
                column = column + jnp.where(row > 0, row + j * own_rows, 0)
            pick_ref[e * group : (e + 1) * group] = (
                column == iota((group, pieces * own_rows), 1) + 1
            ).astype(F32)
        out_ref[...] = jnp.transpose(pick_ref[...]).astype(BF16)

    return call(
        body,
        [(shaped((pieces * own_rows, peers * group), BF16), VMEM)],
        [(me, SMEM), (chosen, VMEM)],
        "place_rows",
        1 << 20,
        [scratch_like((peers * group, pieces * own_rows), F32)],
    )[0]


def sum_rows(pieces, placed, returned):
    slots, part = returned.shape
    own_rows = placed.shape[0] // pieces
    columns = chunks_of(part)

    def body(placed_hbm, returned_ref, out_ref, place_ref, got_ref, sum_ref, in_sem, out_sem):
        first = begin(placed_hbm, place_ref, in_sem.at[len(columns)])
        loads = [
            begin(returned_ref.at[:, at], got_ref.at[:, at], in_sem.at[n])
            for n, at in enumerate(columns)
        ]
        first.wait()
        stores = []
        for n, at in enumerate(columns):
            loads[n].wait()
            summed = dot(place_ref[...], got_ref[:, at]).astype(BF16)
            for j in range(pieces):
                wide = slice(j * part + at.start, j * part + at.stop)
                sum_ref[:, wide] = summed[j * own_rows : (j + 1) * own_rows]
                stores.append(
                    begin(sum_ref.at[:, wide], out_ref.at[:, wide], out_sem.at[n, j])
                )
        wait_all(stores)

    return call(
        body,
        [(shaped((own_rows, part * pieces), BF16), HBM)],
        [(placed, HBM), (returned, HBM)],
        "sum_rows",
        2 * slots * pieces * own_rows * part,
        [
            scratch_like(placed.shape, BF16),
            scratch_like((slots, part), BF16),
            scratch_like((own_rows, part * pieces), BF16),
            pltpu.SemaphoreType.DMA((len(columns) + 1,)),
            pltpu.SemaphoreType.DMA((len(columns), pieces)),
        ],
    )[0]


def load_factor(order_ref, parts, m, target, sems):
    copies = []
    _, count, rows, cols = parts[0].shape
    first = parts[1].shape[0] if len(parts) > 1 else 0
    for n in range(2 if len(parts) > 1 else 1):
        place = order_ref[0] ^ n if len(parts) > 1 else 0
        start = pl.multiple_of(place * rows, rows)
        for i in range(count):
            side = parts[0].at[m, i]
            if n == 1:
                flat = m * count + i
                side = parts[1].at[flat] if flat < first else parts[2].at[flat - first]
            at = target.at[pl.ds(start, rows), i * cols : (i + 1) * cols]
            copies.append(begin(side, at, sems.at[n, i]))
    return copies


def wait_all(copies):
    for copy in copies:
        copy.wait()


def place_matrix(cap, pieces, slots, slot):
    wide = jnp.concatenate([slot + j * cap for j in range(pieces)], axis=1)
    return (iota((slots, wide.shape[1]), 0) == wide).astype(BF16)


def load_rows(got_hbm, x_ref, sems):
    rows, depth = x_ref.shape[0] // NPHM, x_ref.shape[1]
    part = got_hbm.shape[1]
    shares = NPHM * depth // part
    picks = got_hbm.shape[0] * part // (NPHM * depth) // (rows // SELECTED)
    copies = []
    for n in range(got_hbm.shape[0] // picks):
        block, share = divmod(n, shares)
        a, start = share * part // depth, share * part % depth
        first = (block * NPHM + a) * picks
        at = x_ref.at[first : first + picks, start : start + part]
        copies.append(begin(got_hbm.at[n * picks : (n + 1) * picks], at, sems.at[n]))
    return copies


def load_slots(got_hbm, got_ref, sems):
    return [
        begin(got_hbm.at[:, at], got_ref.at[:, at], sems.at[n])
        for n, at in enumerate(chunks_of(got_ref.shape[1]))
    ]


def stack_rows(pieces, place, loads, got_ref, out_ref):
    part = got_ref.shape[1]
    rows, depth = out_ref.shape[0] // NPHM, out_ref.shape[1]
    for load, at in zip(loads, chunks_of(part)):
        load.wait()
        block = dot_tn(place, got_ref[:, at]).astype(BF16)
        for j in range(pieces):
            column = j * part + at.start
            a, start = column // depth, column % depth
            for n in range(rows // STRIP):
                first = (n * NPHM + a) * STRIP
                out_ref[first : first + STRIP, start : start + at.stop - at.start] = block[
                    j * rows + n * STRIP : j * rows + (n + 1) * STRIP
                ]


def store_parts(order_ref, source_ref, outs, sems):
    copies = []
    for n, out in enumerate(outs):
        size = out.shape[1]
        start = pl.multiple_of((order_ref[0] ^ n) * size if len(outs) > 1 else 0, size)
        copies.append(begin(source_ref.at[:, pl.ds(start, size)], out, sems.at[n]))
    return copies


STRIP = SELECTED


def rows_of(n, a):
    return slice((n * NPHM + a) * STRIP, (n * NPHM + a + 1) * STRIP)


def mix_in(mix_ref, m, y_ref, n):
    cols = y_ref.shape[1] // NPHM
    total = [jnp.zeros((STRIP, cols), F32)] * NPHM
    for a in range(NPHM):
        for i in range(NPHM):
            block = y_ref[rows_of(n, a), i * cols : (i + 1) * cols]
            for b in range(NPHM):
                total[b] = total[b] + mix_ref[m * 64 + i * 16 + a * 4 + b] * block
    return total


def mix_out(mix_ref, m, blocks, n, z_ref, offset=0):
    cols = blocks[0].shape[1]
    for a in range(NPHM):
        for i in range(NPHM):
            total = mix_ref[m * 64 + i * 16 + a * 4] * blocks[0]
            for b in range(1, NPHM):
                total = total + mix_ref[m * 64 + i * 16 + a * 4 + b] * blocks[b]
            z_ref[rows_of(n, a), offset + i * cols : offset + (i + 1) * cols] = total.astype(
                z_ref.dtype
            )


def blocks_of(d_ref, n):
    cols = d_ref.shape[1] // NPHM
    at = slice(n * STRIP, (n + 1) * STRIP)
    return [d_ref[at, b * cols : (b + 1) * cols].astype(F32) for b in range(NPHM)]


def order_body(cap, pieces, order_ref, slot_hbm, got_hbm, *refs):
    x_outs, (got_ref, x_ref, slot_ref, got_sem, out_sem) = refs[:-5], refs[-5:]
    small = begin(slot_hbm, slot_ref, got_sem.at[got_sem.shape[0] - 1])
    loads = load_slots(got_hbm, got_ref, got_sem)
    small.wait()
    place = place_matrix(cap, pieces, got_ref.shape[0], slot_ref[...])
    stack_rows(pieces, place, loads, got_ref, x_ref)
    wait_all(store_parts(order_ref, x_ref, x_outs, out_sem))


def forward_body(sides, order_ref, mix_ref, *refs):
    x_parts, refs = refs[:sides], refs[sides:]
    held = 2 if sides > 1 else 1
    parts, refs = refs[:held], refs[held:]
    yg_hbm, yu_hbm, act_hbm, slope_hbm, hid_hbm = refs[:5]
    side_ref, x_ref, yg_ref, yu_ref, act_ref, slope_ref, hid_ref = refs[5:12]
    x_sem, side_sem, out_sem = refs[12:]
    loads = []
    for n, part in enumerate(x_parts):
        size = part.shape[1]
        start = pl.multiple_of((order_ref[0] ^ n) * size if sides > 1 else 0, size)
        loads.append(begin(part, x_ref.at[:, pl.ds(start, size)], x_sem.at[n]))
    sides_in = [
        load_factor(order_ref, parts, m, side_ref.at[m], side_sem.at[m]) for m in range(2)
    ]
    wait_all(loads)
    stores = []
    wait_all(sides_in[0])
    yg_ref[...] = dot(x_ref[...], side_ref[0])
    stores.append(begin(yg_ref, yg_hbm, out_sem.at[2]))
    wait_all(sides_in[1])
    yu_ref[...] = dot(x_ref[...], side_ref[1])
    stores.append(begin(yu_ref, yu_hbm, out_sem.at[3]))
    cols = yg_ref.shape[1] // NPHM
    for n in range(yg_ref.shape[0] // (NPHM * STRIP)):
        gates = mix_in(mix_ref, 0, yg_ref, n)
        ups = mix_in(mix_ref, 1, yu_ref, n)
        for b in range(NPHM):
            at = (slice(n * STRIP, (n + 1) * STRIP), slice(b * cols, (b + 1) * cols))
            sig = jax.nn.sigmoid(gates[b])
            act = gates[b] * sig
            act_ref[at] = act
            slope_ref[at] = ups[b] * (sig + act * (1.0 - sig))
            hid_ref[at] = act * ups[b]
    stores.append(begin(act_ref, act_hbm, out_sem.at[4]))
    stores.append(begin(slope_ref, slope_hbm, out_sem.at[5]))
    stores.append(begin(hid_ref, hid_hbm, out_sem.at[6]))
    wait_all(stores)


def backward_body(
    cap, pieces, sides, after, order_ref, mix_ref, slot_hbm, score_hbm, got_hbm, act_hbm, slope_hbm, hid_hbm,
    *refs,
):
    held = 3 if sides > 1 else 1
    parts, refs = refs[:held], refs[held + after :]
    back_hbm, x_outs, refs = refs[0], refs[1 : 1 + sides], refs[1 + sides :]
    y_hbm, d_hbm, inner_hbm = refs[:3]
    (
        down_ref, side_ref, x_ref, y_ref, d_ref, act_ref, slope_ref, hid_ref, z_ref, grad_ref,
        back_ref, inner_ref, slot_ref, score_ref, got_sem, side_sem, in_sem, out_sem,
    ) = refs[3:]
    loads = load_rows(got_hbm, x_ref, got_sem)
    down_in = load_factor(order_ref, parts, 2, down_ref, side_sem.at[2])
    small_in = [
        begin(source, target, in_sem.at[n])
        for n, (source, target) in enumerate(((score_hbm, score_ref), (slot_hbm, slot_ref)))
    ]
    flat_in = [
        begin(source, target, in_sem.at[2 + n])
        for n, (source, target) in enumerate(
            ((act_hbm, act_ref), (slope_hbm, slope_ref), (hid_hbm, hid_ref))
        )
    ]
    hidden = d_ref.shape[2]
    sides_in = []
    for m in range(2):
        target = side_ref.at[:, m * hidden : (m + 1) * hidden]
        sides_in += load_factor(order_ref, parts, m, target, side_sem.at[m])
    wait_all(small_in)
    score = jnp.concatenate([score_ref[b : b + 1, :] for b in range(score_ref.shape[0])], axis=1)
    rows = score.shape[1]
    same = iota((rows, rows), 0) == iota((rows, rows), 1)
    score = jnp.sum(jnp.where(same, score.astype(F32), 0.0), axis=1, keepdims=True)
    cols = hidden // NPHM
    gates = jnp.broadcast_to(jax.nn.sigmoid(score / 64.0), (rows, cols))
    place = place_matrix(cap, pieces, back_ref.shape[0], slot_ref[...])
    strips = rows // STRIP
    tall = NPHM * STRIP
    wait_all(loads)
    stores = store_parts(order_ref, x_ref, x_outs, out_sem)
    wait_all(down_in)
    for n in range(strips):
        y_ref[n * tall : (n + 1) * tall] = dot(x_ref[n * tall : (n + 1) * tall], down_ref[...])
    stores.append(begin(y_ref, y_hbm, out_sem.at[2]))
    wait_all(flat_in)
    wait_all(sides_in)
    for n in range(strips):
        down = mix_in(mix_ref, 2, y_ref, n)
        strip = slice(n * STRIP, (n + 1) * STRIP)
        gate = gates[strip]
        inner = jnp.zeros((STRIP, cols), F32)
        d_gate, d_up = [], []
        for b in range(NPHM):
            at = (strip, slice(b * cols, (b + 1) * cols))
            inner = inner + hid_ref[at] * down[b]
            hidden_grad = gate * down[b]
            d_gate.append(hidden_grad * slope_ref[at])
            d_up.append(hidden_grad * act_ref[at])
            d_ref[(0,) + at] = d_gate[b].astype(BF16)
            d_ref[(1,) + at] = d_up[b].astype(BF16)
            d_ref[(2,) + at] = (hid_ref[at] * gate).astype(BF16)
        inner_ref[strip] = inner
        mix_out(mix_ref, 0, d_gate, n, z_ref)
        mix_out(mix_ref, 1, d_up, n, z_ref, hidden)
        at = slice(n * tall, (n + 1) * tall)
        grad_ref[at] = dot_nt(z_ref[at], side_ref[...]).astype(BF16)
    stores.append(begin(d_ref, d_hbm, out_sem.at[3]))
    stores.append(begin(inner_ref, inner_hbm, out_sem.at[4]))
    part, depth = back_ref.shape[1], x_ref.shape[1]
    for k, at in enumerate(chunks_of(part)):
        blocks = []
        for j in range(pieces):
            column = j * part + at.start
            a, start = column // depth, column % depth
            wide = slice(start, start + at.stop - at.start)
            blocks += [grad_ref[rows_of(n, a), wide] for n in range(strips)]
        back_ref[:, at] = dot(place, jnp.concatenate(blocks, axis=0)).astype(BF16)
        stores.append(begin(back_ref.at[:, at], back_hbm.at[:, at], out_sem.at[5 + k]))
    wait_all(stores)


def factor_body(count_groups, mix_ref, *refs):
    rows_in, refs = refs[: 3 * count_groups], refs[3 * count_groups :]
    out_hbm, x_ref, g_ref, d_ref, z_ref, sum_ref, in_sem, out_sem = refs
    loads = []
    for n in range(count_groups):
        for k, target in enumerate((x_ref, g_ref, d_ref)):
            loads.append(begin(rows_in[3 * n + k], target.at[n], in_sem.at[n, k]))
    stores = []
    cols = out_hbm.shape[3]
    wait_all(loads)
    for m in (2, 0, 1):
        for n in range(count_groups):
            for strip in range(d_ref.shape[2] // STRIP):
                blocks = blocks_of(d_ref.at[n, m], strip)
                mix_out(mix_ref, m, blocks, strip, z_ref.at[n])
        left = g_ref if m == 2 else x_ref
        sum_ref[m] = sum(dot_tn(left[n], z_ref[n]) for n in range(count_groups))
        for i in range(NPHM):
            at = sum_ref.at[m, :, i * cols : (i + 1) * cols]
            stores.append(begin(at, out_hbm.at[m, i], out_sem.at[m, i]))
    wait_all(stores)


def mix_grad_body(yg_hbm, yu_hbm, yd_hbm, d_hbm, out_ref, y_ref, d_ref, sems):
    loads = [begin(d_hbm, d_ref, sems.at[3])]
    for m, source in enumerate((yg_hbm, yu_hbm, yd_hbm)):
        loads.append(begin(source, y_ref.at[m], sems.at[m]))
    wait_all(loads)
    rows, cols = d_ref.shape[1], d_ref.shape[2] // NPHM
    for m in range(3):
        for a in range(NPHM):
            for i in range(NPHM):
                at = slice(i * cols, (i + 1) * cols)
                strips = range(rows // STRIP)
                block = jnp.concatenate([y_ref[m, rows_of(n, a), at] for n in strips], axis=0)
                for b in range(NPHM):
                    at = m * 64 + i * 16 + a * 4 + b
                    other = d_ref[m, :, b * cols : (b + 1) * cols].astype(F32)
                    out_ref[at : at + 1, :] = jnp.sum(block * other, axis=0, keepdims=True)


def shards(tokens, cotangent, factors, mix, selection, scores):
    peers = lax.axis_size("exp")
    groups = lax.axis_size("seq")
    own_rows, width = tokens.shape
    _, weights, count, depth_own, cols = factors.shape
    depth = depth_own * groups
    hidden = count * cols
    cap = 3 * own_rows // (2 * peers)
    pieces = 1
    while (cap * pieces) % 8:
        pieces *= 2
    slots = peers * cap * pieces
    part = width // pieces
    steps = len(chunks_of(part))
    block_len = peers * SELECTED
    rows = selection.shape[1] * selection.shape[2]
    stacked = count * rows
    swap = groups == 2
    pair = [(0, 1), (1, 0)]
    mixing = mix.reshape(-1)
    dma = pltpu.SemaphoreType.DMA

    def across(array):
        return lax.ppermute(array, "seq", pair)

    half = peers // selection.shape[1]
    direct = half == 8
    me = lax.axis_index("exp").astype(jnp.int32).reshape(1)
    group = lax.axis_index("seq").astype(jnp.int32).reshape(1)
    halves = [list(range(h, h + half)) for h in range(0, peers, half)]
    if swap:
        flat_factors = factors[0].reshape(weights * count, depth_own, cols)
        cuts = [across(x) for x in cut_factors(flat_factors, 2 * count + 1)]
        factor_parts = [factors[0]] + cuts
        sides = 2
    else:
        cuts = []
        factor_parts = [lax.all_gather(factors, "seq", axis=3, tiled=True)[0]]
        sides = 1
    sides_in = [(x, HBM) for x in factor_parts]
    cross = [(shaped((own_rows, width // 2), BF16), HBM)] if direct else []
    told, slot, *crossed = call(
        functools.partial(front_body, cap, pieces, own_rows, block_len, half, direct),
        [(shaped((2 * peers, rows), jnp.int32), HBM), (shaped((1, rows), jnp.int32), HBM)] + cross,
        [(me, SMEM), (selection[0], HBM)] + ([(cotangent, HBM)] if direct else []),
        "wanted_rows",
        1 << 20,
        ([scratch_like((own_rows, width // 2), BF16), dma((2,))] if direct else [])
        + [scratch_like(selection.shape[1:], jnp.int32)]
        + [scratch_like((2 * peers, rows), jnp.int32), scratch_like((1, rows), jnp.int32)]
        + [dma((3,))],
    )
    if direct:
        crossed = [lax.ppermute(crossed[0], "exp", [(n, n ^ (half // 2)) for n in range(peers)])]
    chosen = lax.all_to_all(told, "exp", split_axis=0, concat_axis=0, tiled=True)

    def to_peers(array):
        array = array.reshape(peers, -1, array.shape[1])
        array = lax.all_to_all(array, "exp", split_axis=0, concat_axis=0, tiled=True)
        return array.reshape(-1, array.shape[2])

    got_rows = to_peers(pick_slots(cap, pieces, chosen, tokens, crossed, "pick_tokens"))
    if direct:
        shares = plane_columns(me, cotangent, crossed[0], half)
        shares = [shares[0]] + [
            lax.ppermute(shares[k], "exp", [(n, n ^ k) for n in range(peers)])
            for k in range(1, half // 2)
        ]
    else:
        array = spread_columns(cotangent, half).reshape(half, own_rows, -1)
        array = lax.all_to_all(
            array, "exp", split_axis=0, concat_axis=0, axis_index_groups=halves, tiled=True
        )
        shares = [array.reshape(half * own_rows, -1)]
    picked = pick_rows(me, half, own_rows, chosen, shares, cuts[:1], "pick_cotangent")
    got_grads = to_peers(picked)
    placed = place_rows(cap, pieces, own_rows, me, half, chosen)
    gate = jax.nn.sigmoid(scores[0].reshape(-1).astype(F32) / 64.0)

    product = 2 * stacked * depth * hidden
    split = [(shaped((stacked, depth // sides), BF16), HBM)] * sides
    mixed = (shaped((stacked, hidden), F32), HBM)
    flat = (shaped((rows, hidden), F32), HBM)
    back_scratch = scratch_like((slots, part), BF16)
    pieces_in = got_grads.shape[0] // SELECTED
    stack_scratch = scratch_like((stacked, depth), BF16)
    mixed_scratch = scratch_like((stacked, hidden), F32)
    low_scratch = scratch_like((stacked, hidden), BF16)
    flat_scratch = scratch_like((rows, hidden), F32)
    x_parts = call(
        functools.partial(order_body, cap, pieces),
        split,
        [(group, SMEM), (slot, HBM), (got_rows, HBM)],
        "order_rows",
        product // 4,
        [back_scratch, stack_scratch, scratch_like(slot.shape, jnp.int32)]
        + [dma((steps + 1,)), dma((2,))],
    )
    y_gate, y_up, act, slope, hid = call(
        functools.partial(forward_body, sides),
        [mixed, mixed, flat, flat, flat],
        [(group, SMEM), (mixing, SMEM)] + [(x, HBM) for x in x_parts] + sides_in[:2],
        "forward",
        2 * product,
        [scratch_like((2, depth, hidden), BF16), stack_scratch, mixed_scratch, mixed_scratch]
        + [flat_scratch] * 3
        + [dma((2,)), dma((2, sides, count)), dma((7,))],
    )
    x_rows = [x_parts[0]] + [across(x) for x in x_parts[1:]]
    after = x_rows[1:]
    outs = call(
        functools.partial(backward_body, cap, pieces, sides, len(after)),
        [(shaped((slots, part), BF16), HBM)]
        + split
        + [mixed, (shaped((weights, rows, hidden), BF16), HBM), (shaped((rows, cols), F32), HBM)],
        [(group, SMEM), (mixing, SMEM), (slot, HBM), (scores[0], HBM), (got_grads, HBM)]
        + [(x, HBM) for x in (act, slope, hid)]
        + sides_in
        + [(x, HBM) for x in after],
        "backward",
        3 * product,
        [scratch_like((depth, hidden), BF16), scratch_like((depth, 2 * hidden), BF16)]
        + [stack_scratch, mixed_scratch, scratch_like((weights, rows, hidden), BF16)]
        + [flat_scratch] * 3
        + [scratch_like((stacked, 2 * hidden), BF16), stack_scratch, back_scratch]
        + [scratch_like((rows, cols), F32), scratch_like(slot.shape, jnp.int32)]
        + [scratch_like(scores.shape[1:], jnp.int32)]
        + [dma((pieces_in,)), dma((weights, sides, count)), dma((5,)), dma((5 + steps,))],
    )
    back, g_parts, (y_down, d_own, inner) = outs[0], outs[1 : 1 + sides], outs[1 + sides :]
    returned = to_peers(back)

    d_rows = [d_own] + [across(d_own) for _ in x_parts[1:]]
    g_rows = [g_parts[0]] + [across(x) for x in g_parts[1:]]
    depth_here = depth // sides
    factor_grad = call(
        functools.partial(factor_body, sides),
        [(shaped((weights, count, depth_here, cols), F32), HBM)],
        [(mixing, SMEM)]
        + [(x, HBM) for n in range(sides) for x in (x_rows[n], g_rows[n], d_rows[n])],
        "factor_grad",
        3 * product,
        [scratch_like((sides, stacked, depth_here), BF16)] * 2
        + [
            scratch_like((sides, weights, rows, hidden), BF16),
            scratch_like((sides, stacked, hidden), BF16),
            scratch_like((weights, depth_here, hidden), F32),
            dma((sides, 3)),
            dma((weights, count)),
        ],
    )[0]
    mix_rows = call(
        mix_grad_body,
        [(shaped((mixing.size, cols), F32), VMEM)],
        [(x, HBM) for x in (y_gate, y_up, y_down, d_own)],
        "mix_partials",
        weights * 64 * 2 * rows * cols,
        [
            scratch_like((weights, stacked, hidden), F32),
            scratch_like((weights, rows, hidden), BF16),
            dma((4,)),
        ],
    )[0]
    mix_part = jnp.sum(mix_rows, axis=1).reshape(mix.shape)
    if swap:
        mix_grad = mix_part + across(mix_part)
    else:
        factor_grad = lax.psum_scatter(
            factor_grad.astype(BF16), "seq", scatter_dimension=2, tiled=True
        ).astype(F32)
        mix_grad = lax.psum(mix_part, "seq")
    gate_grad = (jnp.sum(inner, axis=1) * gate * (1.0 - gate)).reshape(selection.shape)
    token_grad = sum_rows(pieces, placed, returned)
    return token_grad, factor_grad[None], mix_grad, gate_grad


def solution(mesh):
    return jax.shard_map(
        shards,
        mesh=mesh,
        in_specs=(
            P(("seq", "exp"), None),
            P(("seq", "exp"), None),
            P("exp", None, None, "seq", None),
            P("exp", None, None, None, None),
            P("exp", "seq", None),
            P("exp", "seq", None),
        ),
        out_specs=(
            P(("seq", "exp"), None),
            P("exp", None, None, "seq", None),
            P("exp", None, None, None, None),
            P("exp", "seq", None),
        ),
        check_vma=False,
    )
```

```python
import functools

import jax
import jax.numpy as jnp
from jax import lax
from jax.experimental import pallas as pl
from jax.experimental.pallas import tpu as pltpu
from jax.sharding import PartitionSpec as P

SELECTED = 64
NPHM = 4
VMEM_LIMIT = 63 * 1024 * 1024
F32 = jnp.float32
BF16 = jnp.bfloat16


def iota(shape, dim):
    return lax.broadcasted_iota(jnp.int32, shape, dim)


def dot(left, right):
    return jnp.dot(left, right, preferred_element_type=F32)


def dot_tn(left, right):
    return lax.dot_general(left, right, (((0,), (0,)), ((), ())), preferred_element_type=F32)


def dot_nt(left, right):
    return lax.dot_general(left, right, (((1,), (1,)), ((), ())), preferred_element_type=F32)


HBM = pl.BlockSpec(memory_space=pltpu.HBM)
VMEM = pl.BlockSpec(memory_space=pltpu.VMEM)
SMEM = pl.BlockSpec(memory_space=pltpu.SMEM)


def call(body, outs, ins, name, flops, scratch=()):
    moved = sum(x.size * x.dtype.itemsize for x, _ in list(ins) + list(outs))
    return pl.pallas_call(
        body,
        out_shape=[x for x, _ in outs],
        in_specs=[place for _, place in ins],
        out_specs=[place for _, place in outs],
        scratch_shapes=list(scratch),
        compiler_params=pltpu.CompilerParams(vmem_limit_bytes=VMEM_LIMIT),
        cost_estimate=pl.CostEstimate(flops=flops, bytes_accessed=moved, transcendentals=0),
        name=name,
    )(*[x for x, _ in ins])


def begin(source, target, sem):
    copy = pltpu.make_async_copy(source, target, sem)
    copy.start()
    return copy


def shaped(shape, dtype):
    return jax.ShapeDtypeStruct(shape, dtype)


def scratch_like(shape, dtype):
    return pltpu.VMEM(shape, dtype)


def chunks_of(part):
    chunk = min(part, 512)
    return [slice(c * chunk, (c + 1) * chunk) for c in range(part // chunk)]


def front_body(cap, pieces, own_rows, block_len, half, cross, me_ref, chosen_hbm, *refs):
    chosen_ref, told_ref, slot_ref, small_sem = refs[-4:]
    small = begin(chosen_hbm, chosen_ref, small_sem.at[0])
    if cross:
        source_ref, told_hbm, slot_hbm, cross_ref, held_ref, sems = refs[:-4]
        width = cross_ref.shape[1]
        plane = lax.shift_right_logical(me_ref[0] & (half - 1), half.bit_length() - 2)
        at = pl.ds(pl.multiple_of((1 - plane) * width, width), width)
        load = begin(source_ref.at[:, at], held_ref, sems.at[0])
    else:
        told_hbm, slot_hbm = refs[:-4]
    small.wait()
    peers, rows = told_ref.shape[0] // 2, slot_ref.shape[1]
    blocks = [chosen_ref[b : b + 1, :] for b in range(chosen_ref.shape[0])]
    position = jnp.concatenate([x + b * block_len for b, x in enumerate(blocks)], axis=1)
    owner = lax.shift_right_logical(position, own_rows.bit_length() - 1)
    local = position & (own_rows - 1)
    peer = iota((peers, rows), 0)
    mine = (peer == owner).astype(F32)
    count = jnp.sum(mine, axis=1, keepdims=True)
    earlier = jnp.sum(jnp.where(peer < owner, count, 0.0), axis=0, keepdims=True).astype(jnp.int32)
    rank = iota((1, rows), 1) - earlier
    slot_ref[...] = owner * (cap * pieces) + rank
    lane = iota((rows, rows), 0)
    hit = jnp.zeros((rows, rows), F32)
    for j in range(pieces):
        hit = hit + (lane == rank + j * cap).astype(F32)
    twice = iota((2 * peers, rows), 0)
    marked = jnp.where(twice == 2 * owner, local + 1, 0).astype(F32)
    asked = dot_nt(marked.astype(BF16), hit.astype(BF16)).astype(jnp.int32)
    told_ref[...] = jnp.where((twice & 1) == 1, jnp.concatenate(blocks, axis=1), asked)
    stores = [
        begin(told_ref, told_hbm, small_sem.at[1]),
        begin(slot_ref, slot_hbm, small_sem.at[2]),
    ]
    if cross:
        load.wait()
        stores.append(begin(held_ref, cross_ref, sems.at[1]))
    for store in stores:
        store.wait()


def plane_columns(me, source, crossed, half):
    own_rows, width = source.shape
    part, count = width // half, half // 2

    def body(me_ref, source_ref, crossed_ref, *refs):
        outs, (held_ref, in_sem, out_sem) = refs[:count], refs[count:]
        low = me_ref[0] & (half - 1)
        plane = lax.shift_right_logical(low, half.bit_length() - 2)
        wide = count * part
        at = pl.ds(pl.multiple_of(plane * wide, wide), wide)
        loads = [
            begin(source_ref.at[:, at], held_ref.at[0], in_sem.at[0]),
            begin(crossed_ref, held_ref.at[1], in_sem.at[1]),
        ]
        copies = []
        for n, load in enumerate(loads):
            load.wait()
            for k in range(count):
                share = (low & (count - 1)) ^ k
                at = held_ref.at[n, :, pl.ds(pl.multiple_of(share * part, part), part)]
                rows = pl.ds(n * own_rows, own_rows)
                copies.append(begin(at, outs[k].at[rows], out_sem.at[n, k]))
        wait_all(copies)

    return call(
        body,
        [(shaped((2 * own_rows, part), BF16), HBM)] * count,
        [(me, SMEM), (source, HBM), (crossed, HBM)],
        "plane_columns",
        0,
        [
            scratch_like((2, own_rows, count * part), BF16),
            pltpu.SemaphoreType.DMA((2,)),
            pltpu.SemaphoreType.DMA((2, count)),
        ],
    )


def pick_matrix(cap, pieces, own_rows, requested):
    told, lanes = requested.shape
    peers = told // 2
    group = cap * pieces
    slots = peers * group
    peer = 2 * iota((peers, group, told), 0).reshape(slots, told)
    spread = dot(
        (peer == iota((slots, told), 1)).astype(BF16), requested.astype(F32).astype(BF16)
    )
    place = iota((peers, group, lanes), 1).reshape(slots, lanes)
    row = jnp.sum(
        jnp.where(place == iota((slots, lanes), 1), spread, 0.0), axis=1, keepdims=True
    ).astype(jnp.int32)
    piece = iota((peers, group, 1), 1).reshape(slots, 1)
    shift = jnp.zeros((slots, 1), jnp.int32)
    for j in range(1, pieces):
        shift = shift + jnp.where(piece >= j * cap, own_rows, 0)
    target = jnp.where(row > 0, row - 1 + shift, -1)
    return (target == iota((slots, pieces * own_rows), 1)).astype(BF16)


def pick_slots(cap, pieces, requested, source, after, name):
    own_rows, width = source.shape
    part = width // pieces
    slots = requested.shape[0] // 2 * cap * pieces
    columns = chunks_of(part)

    def body(requested_hbm, source_ref, *refs):
        out_ref, requested_ref, rows_ref, sent_ref, in_sem, out_sem = refs[len(after) :]
        asked = begin(requested_hbm, requested_ref, in_sem.at[len(columns), 0])
        loads = []
        for n, at in enumerate(columns):
            for j in range(pieces):
                wide = slice(j * part + at.start, j * part + at.stop)
                target = rows_ref.at[j * own_rows : (j + 1) * own_rows, at]
                loads.append(begin(source_ref.at[:, wide], target, in_sem.at[n, j]))
        asked.wait()
        pick = pick_matrix(cap, pieces, own_rows, requested_ref[...])
        stores = []
        for n, at in enumerate(columns):
            for load in loads[n * pieces : (n + 1) * pieces]:
                load.wait()
            sent_ref[:, at] = dot(pick, rows_ref[:, at]).astype(BF16)
            stores.append(begin(sent_ref.at[:, at], out_ref.at[:, at], out_sem.at[n]))
        for store in stores:
            store.wait()

    return call(
        body,
        [(shaped((slots, part), BF16), HBM)],
        [(requested, HBM), (source, HBM)] + [(x, HBM) for x in after],
        name,
        2 * slots * pieces * own_rows * part,
        [
            scratch_like(requested.shape, jnp.int32),
            scratch_like((pieces * own_rows, part), BF16),
            scratch_like((slots, part), BF16),
            pltpu.SemaphoreType.DMA((len(columns) + 1, pieces)),
            pltpu.SemaphoreType.DMA((len(columns),)),
        ],
    )[0]


def spread_columns(source, half):
    own_rows, width = source.shape
    part = width // half

    def body(source_ref, out_ref, held_ref, in_sem, out_sem):
        begin(source_ref, held_ref, in_sem).wait()
        copies = []
        for k in range(half):
            at = held_ref.at[:, k * part : (k + 1) * part]
            out = out_ref.at[k * own_rows : (k + 1) * own_rows]
            copies.append(begin(at, out, out_sem.at[k]))
        wait_all(copies)

    scratch = [
        scratch_like((own_rows, width), BF16),
        pltpu.SemaphoreType.DMA,
        pltpu.SemaphoreType.DMA((half,)),
    ]
    outs = [(shaped((half * own_rows, part), BF16), HBM)]
    return call(body, outs, [(source, HBM)], "spread_columns", 0, scratch)[0]


def cut_factors(factors, first):
    cuts = (slice(0, first), slice(first, factors.shape[0]))

    def body(factors_ref, *refs):
        outs, (held_ref, sems) = refs[:2], refs[2:]
        loads = [
            begin(factors_ref.at[at], held_ref.at[at], sems.at[0, n]) for n, at in enumerate(cuts)
        ]
        copies = []
        for n, at in enumerate(cuts):
            loads[n].wait()
            copies.append(begin(held_ref.at[at], outs[n], sems.at[1, n]))
        wait_all(copies)

    outs = [
        (shaped((at.stop - at.start,) + factors.shape[1:], BF16), HBM) for at in cuts
    ]
    scratch = [scratch_like(factors.shape, BF16), pltpu.SemaphoreType.DMA((2, 2))]
    return call(body, outs, [(factors, HBM)], "cut_factors", 0, scratch)


def pick_rows(me, half, own_rows, chosen, shares, after, name):
    peers, total = chosen.shape[0] // 2, chosen.shape[1]
    picks = total * half // peers
    part = shares[0].shape[1]
    block = half * own_rows
    batch = min(peers, 8)

    def body(me_ref, chosen_ref, *refs):
        refs = refs[len(after) :]
        parts, (out_ref, rows_ref, pick_ref, sent_ref, in_sem, out_sem) = (
            refs[: len(shares)],
            refs[len(shares) :],
        )
        loads = []
        for k in range(half):
            place = (me_ref[0] & (half - 1)) ^ k if len(parts) > 1 else k
            n, first = (k % len(parts), k // len(parts)) if len(parts) > 1 else (0, k)
            at = parts[n].at[first * own_rows : (first + 1) * own_rows]
            target = rows_ref.at[pl.ds(pl.multiple_of(place * own_rows, own_rows), own_rows)]
            loads.append(begin(at, target, in_sem.at[k]))
        block_at = lax.shift_right_logical(me_ref[0], half.bit_length() - 1)
        same = iota((picks, total), 0) + block_at * picks == iota((picks, total), 1)
        stores = []
        for first in range(0, peers, batch):
            for e in range(batch):
                wanted = chosen_ref[2 * (first + e) + 1 : 2 * (first + e) + 2, :]
                column = jnp.sum(jnp.where(same, wanted, 0), axis=1, keepdims=True)
                pick_ref[first // batch % 2, e * picks : (e + 1) * picks] = (
                    column == iota((picks, block), 1)
                ).astype(BF16)
            if first == 0:
                wait_all(loads)
            at = slice(first * picks, (first + batch) * picks)
            sent_ref[at] = dot(pick_ref[first // batch % 2], rows_ref[...]).astype(BF16)
            stores.append(begin(sent_ref.at[at], out_ref.at[at], out_sem.at[first // batch]))
        wait_all(stores)

    return call(
        body,
        [(shaped((peers * picks, part), BF16), HBM)],
        [(me, SMEM), (chosen, VMEM)] + [(x, HBM) for x in list(after) + list(shares)],
        name,
        2 * peers * picks * block * part,
        [
            scratch_like((block, part), BF16),
            scratch_like((2, batch * picks, block), BF16),
            scratch_like((peers * picks, part), BF16),
            pltpu.SemaphoreType.DMA((half,)),
            pltpu.SemaphoreType.DMA((peers // batch,)),
        ],
    )[0]


def place_rows(cap, pieces, own_rows, me, half, chosen):
    peers, total = chosen.shape[0] // 2, chosen.shape[1]
    picks = total * half // peers
    group = cap * pieces

    def body(me_ref, chosen_ref, out_ref, pick_ref):
        low = me_ref[0] & (half - 1)
        block_at = lax.shift_right_logical(me_ref[0], half.bit_length() - 1)
        lane = iota((2 * peers, total), 1) - block_at * picks
        here = (lane >= 0) & (lane < picks)
        local = jnp.where(here, chosen_ref[...] - low * own_rows, own_rows)
        before = jnp.sum((local < 0).astype(F32), axis=1, keepdims=True).astype(jnp.int32)
        ranks = lane - before
        owned = jnp.where((local >= 0) & (local < own_rows), local + 1, 0)
        place = iota((group, total), 0)
        for e in range(peers):
            at = slice(2 * e + 1, 2 * e + 2)
            rank, mine = ranks[at], owned[at]
            column = jnp.zeros((group, 1), jnp.int32)
            for j in range(pieces):
                hit = jnp.where((place == rank + j * cap) & (rank >= 0) & (rank < cap), mine, 0)
                row = jnp.sum(hit, axis=1, keepdims=True)
                column = column + jnp.where(row > 0, row + j * own_rows, 0)
            pick_ref[e * group : (e + 1) * group] = (
                column == iota((group, pieces * own_rows), 1) + 1
            ).astype(F32)
        out_ref[...] = jnp.transpose(pick_ref[...]).astype(BF16)

    return call(
        body,
        [(shaped((pieces * own_rows, peers * group), BF16), VMEM)],
        [(me, SMEM), (chosen, VMEM)],
        "place_rows",
        1 << 20,
        [scratch_like((peers * group, pieces * own_rows), F32)],
    )[0]


def sum_rows(pieces, placed, returned):
    slots, part = returned.shape
    own_rows = placed.shape[0] // pieces
    columns = chunks_of(part)

    def body(placed_hbm, returned_ref, out_ref, place_ref, got_ref, sum_ref, in_sem, out_sem):
        first = begin(placed_hbm, place_ref, in_sem.at[len(columns)])
        loads = [
            begin(returned_ref.at[:, at], got_ref.at[:, at], in_sem.at[n])
            for n, at in enumerate(columns)
        ]
        first.wait()
        stores = []
        for n, at in enumerate(columns):
            loads[n].wait()
            summed = dot(place_ref[...], got_ref[:, at]).astype(BF16)
            for j in range(pieces):
                wide = slice(j * part + at.start, j * part + at.stop)
                sum_ref[:, wide] = summed[j * own_rows : (j + 1) * own_rows]
                stores.append(
                    begin(sum_ref.at[:, wide], out_ref.at[:, wide], out_sem.at[n, j])
                )
        wait_all(stores)

    return call(
        body,
        [(shaped((own_rows, part * pieces), BF16), HBM)],
        [(placed, HBM), (returned, HBM)],
        "sum_rows",
        2 * slots * pieces * own_rows * part,
        [
            scratch_like(placed.shape, BF16),
            scratch_like((slots, part), BF16),
            scratch_like((own_rows, part * pieces), BF16),
            pltpu.SemaphoreType.DMA((len(columns) + 1,)),
            pltpu.SemaphoreType.DMA((len(columns), pieces)),
        ],
    )[0]


def load_factor(order_ref, parts, m, target, sems):
    copies = []
    _, count, rows, cols = parts[0].shape
    first = parts[1].shape[0] if len(parts) > 1 else 0
    for n in range(2 if len(parts) > 1 else 1):
        place = order_ref[0] ^ n if len(parts) > 1 else 0
        start = pl.multiple_of(place * rows, rows)
        for i in range(count):
            side = parts[0].at[m, i]
            if n == 1:
                flat = m * count + i
                side = parts[1].at[flat] if flat < first else parts[2].at[flat - first]
            at = target.at[pl.ds(start, rows), i * cols : (i + 1) * cols]
            copies.append(begin(side, at, sems.at[n, i]))
    return copies


def wait_all(copies):
    for copy in copies:
        copy.wait()


def place_matrix(cap, pieces, slots, slot):
    wide = jnp.concatenate([slot + j * cap for j in range(pieces)], axis=1)
    return (iota((slots, wide.shape[1]), 0) == wide).astype(BF16)


def load_rows(got_hbm, x_ref, sems):
    rows, depth = x_ref.shape[0] // NPHM, x_ref.shape[1]
    part = got_hbm.shape[1]
    shares = NPHM * depth // part
    picks = got_hbm.shape[0] * part // (NPHM * depth) // (rows // SELECTED)
    copies = []
    for n in range(got_hbm.shape[0] // picks):
        block, share = divmod(n, shares)
        a, start = share * part // depth, share * part % depth
        first = (block * NPHM + a) * picks
        at = x_ref.at[first : first + picks, start : start + part]
        copies.append(begin(got_hbm.at[n * picks : (n + 1) * picks], at, sems.at[n]))
    return copies


def load_slots(got_hbm, got_ref, sems):
    return [
        begin(got_hbm.at[:, at], got_ref.at[:, at], sems.at[n])
        for n, at in enumerate(chunks_of(got_ref.shape[1]))
    ]


def stack_rows(pieces, place, loads, got_ref, out_ref):
    part = got_ref.shape[1]
    rows, depth = out_ref.shape[0] // NPHM, out_ref.shape[1]
    for load, at in zip(loads, chunks_of(part)):
        load.wait()
        block = dot_tn(place, got_ref[:, at]).astype(BF16)
        for j in range(pieces):
            column = j * part + at.start
            a, start = column // depth, column % depth
            for n in range(rows // STRIP):
                first = (n * NPHM + a) * STRIP
                out_ref[first : first + STRIP, start : start + at.stop - at.start] = block[
                    j * rows + n * STRIP : j * rows + (n + 1) * STRIP
                ]


def store_parts(order_ref, source_ref, outs, sems):
    copies = []
    for n, out in enumerate(outs):
        size = out.shape[1]
        start = pl.multiple_of((order_ref[0] ^ n) * size if len(outs) > 1 else 0, size)
        copies.append(begin(source_ref.at[:, pl.ds(start, size)], out, sems.at[n]))
    return copies


STRIP = SELECTED


def rows_of(n, a):
    return slice((n * NPHM + a) * STRIP, (n * NPHM + a + 1) * STRIP)


def mix_in(mix_ref, m, y_ref, n):
    cols = y_ref.shape[1] // NPHM
    total = [jnp.zeros((STRIP, cols), F32)] * NPHM
    for a in range(NPHM):
        for i in range(NPHM):
            block = y_ref[rows_of(n, a), i * cols : (i + 1) * cols]
            for b in range(NPHM):
                total[b] = total[b] + mix_ref[m * 64 + i * 16 + a * 4 + b] * block
    return total


def mix_out(mix_ref, m, blocks, n, z_ref, offset=0):
    cols = blocks[0].shape[1]
    for a in range(NPHM):
        for i in range(NPHM):
            total = mix_ref[m * 64 + i * 16 + a * 4] * blocks[0]
            for b in range(1, NPHM):
                total = total + mix_ref[m * 64 + i * 16 + a * 4 + b] * blocks[b]
            z_ref[rows_of(n, a), offset + i * cols : offset + (i + 1) * cols] = total.astype(
                z_ref.dtype
            )


def blocks_of(d_ref, n):
    cols = d_ref.shape[1] // NPHM
    at = slice(n * STRIP, (n + 1) * STRIP)
    return [d_ref[at, b * cols : (b + 1) * cols].astype(F32) for b in range(NPHM)]


def join_factors(group, parts, first, stop, name):
    _, count, rows, cols = parts[0].shape
    depth, hidden = rows * (2 if len(parts) > 1 else 1), count * cols
    wide = (stop - first) * hidden

    def body(order_ref, *refs):
        ins, (out_ref, held_ref, sems, out_sem) = refs[: len(parts)], refs[len(parts) :]
        loads = []
        for m in range(first, stop):
            target = held_ref.at[:, (m - first) * hidden : (m - first + 1) * hidden]
            loads += load_factor(order_ref, ins, m, target, sems.at[m])
        wait_all(loads)
        begin(held_ref, out_ref, out_sem).wait()

    return call(
        body,
        [(shaped((depth, wide), BF16), HBM)],
        [(group, SMEM)] + [(x, HBM) for x in parts],
        name,
        0,
        [
            scratch_like((depth, wide), BF16),
            pltpu.SemaphoreType.DMA((stop, 2, count)),
            pltpu.SemaphoreType.DMA,
        ],
    )[0]


def order_body(cap, pieces, order_ref, slot_hbm, got_hbm, *refs):
    x_outs, (got_ref, x_ref, slot_ref, got_sem, out_sem) = refs[:-5], refs[-5:]
    small = begin(slot_hbm, slot_ref, got_sem.at[got_sem.shape[0] - 1])
    loads = load_slots(got_hbm, got_ref, got_sem)
    small.wait()
    place = place_matrix(cap, pieces, got_ref.shape[0], slot_ref[...])
    stack_rows(pieces, place, loads, got_ref, x_ref)
    wait_all(store_parts(order_ref, x_ref, x_outs, out_sem))


def forward_body(sides, order_ref, mix_ref, *refs):
    x_parts, side_hbm, refs = refs[:sides], refs[sides], refs[sides + 1 :]
    yg_hbm, yu_hbm, act_hbm, slope_hbm, hid_hbm = refs[:5]
    side_ref, x_ref, yg_ref, yu_ref, act_ref, slope_ref, hid_ref = refs[5:12]
    x_sem, side_sem, out_sem = refs[12:]
    loads = []
    for n, part in enumerate(x_parts):
        size = part.shape[1]
        start = pl.multiple_of((order_ref[0] ^ n) * size if sides > 1 else 0, size)
        loads.append(begin(part, x_ref.at[:, pl.ds(start, size)], x_sem.at[n]))
    side_in = begin(side_hbm, side_ref, side_sem)
    wait_all(loads)
    stores = []
    side_in.wait()
    hidden = yg_ref.shape[1]
    yg_ref[...] = dot(x_ref[...], side_ref[:, :hidden])
    stores.append(begin(yg_ref, yg_hbm, out_sem.at[2]))
    yu_ref[...] = dot(x_ref[...], side_ref[:, hidden:])
    stores.append(begin(yu_ref, yu_hbm, out_sem.at[3]))
    cols = yg_ref.shape[1] // NPHM
    for n in range(yg_ref.shape[0] // (NPHM * STRIP)):
        gates = mix_in(mix_ref, 0, yg_ref, n)
        ups = mix_in(mix_ref, 1, yu_ref, n)
        for b in range(NPHM):
            at = (slice(n * STRIP, (n + 1) * STRIP), slice(b * cols, (b + 1) * cols))
            sig = jax.nn.sigmoid(gates[b])
            act = gates[b] * sig
            act_ref[at] = act
            slope_ref[at] = ups[b] * (sig + act * (1.0 - sig))
            hid_ref[at] = act * ups[b]
    stores.append(begin(act_ref, act_hbm, out_sem.at[4]))
    stores.append(begin(slope_ref, slope_hbm, out_sem.at[5]))
    stores.append(begin(hid_ref, hid_hbm, out_sem.at[6]))
    wait_all(stores)


def backward_body(
    cap, pieces, sides, after, order_ref, mix_ref, slot_hbm, score_hbm, got_hbm, act_hbm, slope_hbm, hid_hbm,
    *refs,
):
    side_hbm, down_hbm, refs = refs[0], refs[1], refs[2 + after :]
    back_hbm, x_outs, refs = refs[0], refs[1 : 1 + sides], refs[1 + sides :]
    y_hbm, d_hbm, inner_hbm = refs[:3]
    (
        down_ref, side_ref, x_ref, y_ref, d_ref, act_ref, slope_ref, hid_ref, z_ref, grad_ref,
        back_ref, inner_ref, slot_ref, score_ref, got_sem, side_sem, in_sem, out_sem,
    ) = refs[3:]
    loads = load_rows(got_hbm, x_ref, got_sem)
    down_in = [begin(down_hbm, down_ref, side_sem.at[0])]
    small_in = [
        begin(source, target, in_sem.at[n])
        for n, (source, target) in enumerate(((score_hbm, score_ref), (slot_hbm, slot_ref)))
    ]
    flat_in = [
        begin(source, target, in_sem.at[2 + n])
        for n, (source, target) in enumerate(
            ((act_hbm, act_ref), (slope_hbm, slope_ref), (hid_hbm, hid_ref))
        )
    ]
    hidden = d_ref.shape[2]
    sides_in = [begin(side_hbm, side_ref, side_sem.at[1])]
    wait_all(small_in)
    score = jnp.concatenate([score_ref[b : b + 1, :] for b in range(score_ref.shape[0])], axis=1)
    rows = score.shape[1]
    same = iota((rows, rows), 0) == iota((rows, rows), 1)
    score = jnp.sum(jnp.where(same, score.astype(F32), 0.0), axis=1, keepdims=True)
    cols = hidden // NPHM
    gates = jnp.broadcast_to(jax.nn.sigmoid(score / 64.0), (rows, cols))
    place = place_matrix(cap, pieces, back_ref.shape[0], slot_ref[...])
    strips = rows // STRIP
    tall = NPHM * STRIP
    wait_all(loads)
    stores = store_parts(order_ref, x_ref, x_outs, out_sem)
    wait_all(down_in)
    for n in range(strips):
        y_ref[n * tall : (n + 1) * tall] = dot(x_ref[n * tall : (n + 1) * tall], down_ref[...])
    stores.append(begin(y_ref, y_hbm, out_sem.at[2]))
    wait_all(flat_in)
    wait_all(sides_in)
    for n in range(strips):
        down = mix_in(mix_ref, 2, y_ref, n)
        strip = slice(n * STRIP, (n + 1) * STRIP)
        gate = gates[strip]
        inner = jnp.zeros((STRIP, cols), F32)
        d_gate, d_up = [], []
        for b in range(NPHM):
            at = (strip, slice(b * cols, (b + 1) * cols))
            inner = inner + hid_ref[at] * down[b]
            hidden_grad = gate * down[b]
            d_gate.append(hidden_grad * slope_ref[at])
            d_up.append(hidden_grad * act_ref[at])
            d_ref[(0,) + at] = d_gate[b].astype(BF16)
            d_ref[(1,) + at] = d_up[b].astype(BF16)
            d_ref[(2,) + at] = (hid_ref[at] * gate).astype(BF16)
        inner_ref[strip] = inner
        mix_out(mix_ref, 0, d_gate, n, z_ref)
        mix_out(mix_ref, 1, d_up, n, z_ref, hidden)
        at = slice(n * tall, (n + 1) * tall)
        grad_ref[at] = dot_nt(z_ref[at], side_ref[...]).astype(BF16)
    stores.append(begin(d_ref, d_hbm, out_sem.at[3]))
    stores.append(begin(inner_ref, inner_hbm, out_sem.at[4]))
    part, depth = back_ref.shape[1], x_ref.shape[1]
    for k, at in enumerate(chunks_of(part)):
        blocks = []
        for j in range(pieces):
            column = j * part + at.start
            a, start = column // depth, column % depth
            wide = slice(start, start + at.stop - at.start)
            blocks += [grad_ref[rows_of(n, a), wide] for n in range(strips)]
        back_ref[:, at] = dot(place, jnp.concatenate(blocks, axis=0)).astype(BF16)
        stores.append(begin(back_ref.at[:, at], back_hbm.at[:, at], out_sem.at[5 + k]))
    wait_all(stores)


def factor_body(count_groups, mix_ref, *refs):
    rows_in, refs = refs[: 3 * count_groups], refs[3 * count_groups :]
    out_hbm, x_ref, g_ref, d_ref, z_ref, sum_ref, in_sem, out_sem = refs
    loads = []
    for n in range(count_groups):
        for k, target in enumerate((x_ref, g_ref, d_ref)):
            loads.append(begin(rows_in[3 * n + k], target.at[n], in_sem.at[n, k]))
    stores = []
    cols = out_hbm.shape[3]
    wait_all(loads)
    for m in (2, 0, 1):
        for n in range(count_groups):
            for strip in range(d_ref.shape[2] // STRIP):
                blocks = blocks_of(d_ref.at[n, m], strip)
                mix_out(mix_ref, m, blocks, strip, z_ref.at[n])
        left = g_ref if m == 2 else x_ref
        sum_ref[m] = sum(dot_tn(left[n], z_ref[n]) for n in range(count_groups))
        for i in range(NPHM):
            at = sum_ref.at[m, :, i * cols : (i + 1) * cols]
            stores.append(begin(at, out_hbm.at[m, i], out_sem.at[m, i]))
    wait_all(stores)


def mix_grad_body(yg_hbm, yu_hbm, yd_hbm, d_hbm, out_ref, y_ref, d_ref, sems):
    loads = [begin(d_hbm, d_ref, sems.at[3])]
    for m, source in enumerate((yg_hbm, yu_hbm, yd_hbm)):
        loads.append(begin(source, y_ref.at[m], sems.at[m]))
    wait_all(loads)
    rows, cols = d_ref.shape[1], d_ref.shape[2] // NPHM
    for m in range(3):
        for a in range(NPHM):
            for i in range(NPHM):
                at = slice(i * cols, (i + 1) * cols)
                strips = range(rows // STRIP)
                block = jnp.concatenate([y_ref[m, rows_of(n, a), at] for n in strips], axis=0)
                for b in range(NPHM):
                    at = m * 64 + i * 16 + a * 4 + b
                    other = d_ref[m, :, b * cols : (b + 1) * cols].astype(F32)
                    out_ref[at : at + 1, :] = jnp.sum(block * other, axis=0, keepdims=True)


def shards(tokens, cotangent, factors, mix, selection, scores):
    peers = lax.axis_size("exp")
    groups = lax.axis_size("seq")
    own_rows, width = tokens.shape
    _, weights, count, depth_own, cols = factors.shape
    depth = depth_own * groups
    hidden = count * cols
    cap = 3 * own_rows // (2 * peers)
    pieces = 1
    while (cap * pieces) % 8:
        pieces *= 2
    slots = peers * cap * pieces
    part = width // pieces
    steps = len(chunks_of(part))
    block_len = peers * SELECTED
    rows = selection.shape[1] * selection.shape[2]
    stacked = count * rows
    swap = groups == 2
    pair = [(0, 1), (1, 0)]
    mixing = mix.reshape(-1)
    dma = pltpu.SemaphoreType.DMA

    def across(array):
        return lax.ppermute(array, "seq", pair)

    half = peers // selection.shape[1]
    direct = half == 8
    me = lax.axis_index("exp").astype(jnp.int32).reshape(1)
    group = lax.axis_index("seq").astype(jnp.int32).reshape(1)
    halves = [list(range(h, h + half)) for h in range(0, peers, half)]
    if swap:
        flat_factors = factors[0].reshape(weights * count, depth_own, cols)
        cuts = [across(x) for x in cut_factors(flat_factors, 2 * count)]
        factor_parts = [factors[0]] + cuts
        sides = 2
    else:
        cuts = []
        factor_parts = [lax.all_gather(factors, "seq", axis=3, tiled=True)[0]]
        sides = 1
    cross = [(shaped((own_rows, width // 2), BF16), HBM)] if direct else []
    told, slot, *crossed = call(
        functools.partial(front_body, cap, pieces, own_rows, block_len, half, direct),
        [(shaped((2 * peers, rows), jnp.int32), HBM), (shaped((1, rows), jnp.int32), HBM)] + cross,
        [(me, SMEM), (selection[0], HBM)] + ([(cotangent, HBM)] if direct else []),
        "wanted_rows",
        1 << 20,
        ([scratch_like((own_rows, width // 2), BF16), dma((2,))] if direct else [])
        + [scratch_like(selection.shape[1:], jnp.int32)]
        + [scratch_like((2 * peers, rows), jnp.int32), scratch_like((1, rows), jnp.int32)]
        + [dma((3,))],
    )
    if direct:
        crossed = [lax.ppermute(crossed[0], "exp", [(n, n ^ (half // 2)) for n in range(peers)])]
    chosen = lax.all_to_all(told, "exp", split_axis=0, concat_axis=0, tiled=True)

    def to_peers(array):
        array = array.reshape(peers, -1, array.shape[1])
        array = lax.all_to_all(array, "exp", split_axis=0, concat_axis=0, tiled=True)
        return array.reshape(-1, array.shape[2])

    got_rows = to_peers(pick_slots(cap, pieces, chosen, tokens, crossed, "pick_tokens"))
    if direct:
        shares = plane_columns(me, cotangent, crossed[0], half)
        shares = [shares[0]] + [
            lax.ppermute(shares[k], "exp", [(n, n ^ k) for n in range(peers)])
            for k in range(1, half // 2)
        ]
    else:
        array = spread_columns(cotangent, half).reshape(half, own_rows, -1)
        array = lax.all_to_all(
            array, "exp", split_axis=0, concat_axis=0, axis_index_groups=halves, tiled=True
        )
        shares = [array.reshape(half * own_rows, -1)]
    picked = pick_rows(me, half, own_rows, chosen, shares, cuts[:1], "pick_cotangent")
    got_grads = to_peers(picked)
    placed = place_rows(cap, pieces, own_rows, me, half, chosen)
    gate = jax.nn.sigmoid(scores[0].reshape(-1).astype(F32) / 64.0)

    product = 2 * stacked * depth * hidden
    split = [(shaped((stacked, depth // sides), BF16), HBM)] * sides
    mixed = (shaped((stacked, hidden), F32), HBM)
    flat = (shaped((rows, hidden), F32), HBM)
    back_scratch = scratch_like((slots, part), BF16)
    pieces_in = got_grads.shape[0] // SELECTED
    stack_scratch = scratch_like((stacked, depth), BF16)
    mixed_scratch = scratch_like((stacked, hidden), F32)
    low_scratch = scratch_like((stacked, hidden), BF16)
    flat_scratch = scratch_like((rows, hidden), F32)
    gate_up = join_factors(group, factor_parts[:2], 0, 2, "join_gate_up")
    down = join_factors(group, factor_parts, 2, 3, "join_down")
    x_parts = call(
        functools.partial(order_body, cap, pieces),
        split,
        [(group, SMEM), (slot, HBM), (got_rows, HBM)],
        "order_rows",
        product // 4,
        [back_scratch, stack_scratch, scratch_like(slot.shape, jnp.int32)]
        + [dma((steps + 1,)), dma((2,))],
    )
    y_gate, y_up, act, slope, hid = call(
        functools.partial(forward_body, sides),
        [mixed, mixed, flat, flat, flat],
        [(group, SMEM), (mixing, SMEM)] + [(x, HBM) for x in x_parts] + [(gate_up, HBM)],
        "forward",
        2 * product,
        [scratch_like((depth, 2 * hidden), BF16), stack_scratch, mixed_scratch, mixed_scratch]
        + [flat_scratch] * 3
        + [dma((2,)), dma, dma((7,))],
    )
    x_rows = [x_parts[0]] + [across(x) for x in x_parts[1:]]
    after = x_rows[1:]
    outs = call(
        functools.partial(backward_body, cap, pieces, sides, len(after)),
        [(shaped((slots, part), BF16), HBM)]
        + split
        + [mixed, (shaped((weights, rows, hidden), BF16), HBM), (shaped((rows, cols), F32), HBM)],
        [(group, SMEM), (mixing, SMEM), (slot, HBM), (scores[0], HBM), (got_grads, HBM)]
        + [(x, HBM) for x in (act, slope, hid)]
        + [(x, HBM) for x in [gate_up, down] + after],
        "backward",
        3 * product,
        [scratch_like((depth, hidden), BF16), scratch_like((depth, 2 * hidden), BF16)]
        + [stack_scratch, mixed_scratch, scratch_like((weights, rows, hidden), BF16)]
        + [flat_scratch] * 3
        + [scratch_like((stacked, 2 * hidden), BF16), stack_scratch, back_scratch]
        + [scratch_like((rows, cols), F32), scratch_like(slot.shape, jnp.int32)]
        + [scratch_like(scores.shape[1:], jnp.int32)]
        + [dma((pieces_in,)), dma((2,)), dma((5,)), dma((5 + steps,))],
    )
    back, g_parts, (y_down, d_own, inner) = outs[0], outs[1 : 1 + sides], outs[1 + sides :]
    returned = to_peers(back)

    d_rows = [d_own] + [across(d_own) for _ in x_parts[1:]]
    g_rows = [g_parts[0]] + [across(x) for x in g_parts[1:]]
    depth_here = depth // sides
    factor_grad = call(
        functools.partial(factor_body, sides),
        [(shaped((weights, count, depth_here, cols), F32), HBM)],
        [(mixing, SMEM)]
        + [(x, HBM) for n in range(sides) for x in (x_rows[n], g_rows[n], d_rows[n])],
        "factor_grad",
        3 * product,
        [scratch_like((sides, stacked, depth_here), BF16)] * 2
        + [
            scratch_like((sides, weights, rows, hidden), BF16),
            scratch_like((sides, stacked, hidden), BF16),
            scratch_like((weights, depth_here, hidden), F32),
            dma((sides, 3)),
            dma((weights, count)),
        ],
    )[0]
    mix_rows = call(
        mix_grad_body,
        [(shaped((mixing.size, cols), F32), VMEM)],
        [(x, HBM) for x in (y_gate, y_up, y_down, d_own)],
        "mix_partials",
        weights * 64 * 2 * rows * cols,
        [
            scratch_like((weights, stacked, hidden), F32),
            scratch_like((weights, rows, hidden), BF16),
            dma((4,)),
        ],
    )[0]
    mix_part = jnp.sum(mix_rows, axis=1).reshape(mix.shape)
    if swap:
        mix_grad = mix_part + across(mix_part)
    else:
        factor_grad = lax.psum_scatter(
            factor_grad.astype(BF16), "seq", scatter_dimension=2, tiled=True
        ).astype(F32)
        mix_grad = lax.psum(mix_part, "seq")
    gate_grad = (jnp.sum(inner, axis=1) * gate * (1.0 - gate)).reshape(selection.shape)
    token_grad = sum_rows(pieces, placed, returned)
    return token_grad, factor_grad[None], mix_grad, gate_grad


def solution(mesh):
    return jax.shard_map(
        shards,
        mesh=mesh,
        in_specs=(
            P(("seq", "exp"), None),
            P(("seq", "exp"), None),
            P("exp", None, None, "seq", None),
            P("exp", None, None, None, None),
            P("exp", "seq", None),
            P("exp", "seq", None),
        ),
        out_specs=(
            P(("seq", "exp"), None),
            P("exp", None, None, "seq", None),
            P("exp", None, None, None, None),
            P("exp", "seq", None),
        ),
        check_vma=False,
    )
```

```python
import functools

import jax
import jax.numpy as jnp
from jax import lax
from jax.experimental import pallas as pl
from jax.experimental.pallas import tpu as pltpu
from jax.sharding import PartitionSpec as P

SELECTED = 64
NPHM = 4
VMEM_LIMIT = 65152 * 1024
F32 = jnp.float32
BF16 = jnp.bfloat16


def iota(shape, dim):
    return lax.broadcasted_iota(jnp.int32, shape, dim)


def dot(left, right):
    return jnp.dot(left, right, preferred_element_type=F32)


def dot_tn(left, right):
    return lax.dot_general(left, right, (((0,), (0,)), ((), ())), preferred_element_type=F32)


def dot_nt(left, right):
    return lax.dot_general(left, right, (((1,), (1,)), ((), ())), preferred_element_type=F32)


HBM = pl.BlockSpec(memory_space=pltpu.HBM)
VMEM = pl.BlockSpec(memory_space=pltpu.VMEM)
SMEM = pl.BlockSpec(memory_space=pltpu.SMEM)


def call(body, outs, ins, name, flops, scratch=()):
    moved = sum(x.size * x.dtype.itemsize for x, _ in list(ins) + list(outs))
    return pl.pallas_call(
        body,
        out_shape=[x for x, _ in outs],
        in_specs=[place for _, place in ins],
        out_specs=[place for _, place in outs],
        scratch_shapes=list(scratch),
        compiler_params=pltpu.CompilerParams(vmem_limit_bytes=VMEM_LIMIT),
        cost_estimate=pl.CostEstimate(flops=flops, bytes_accessed=moved, transcendentals=0),
        name=name,
    )(*[x for x, _ in ins])


def begin(source, target, sem):
    copy = pltpu.make_async_copy(source, target, sem)
    copy.start()
    return copy


def shaped(shape, dtype):
    return jax.ShapeDtypeStruct(shape, dtype)


def scratch_like(shape, dtype):
    return pltpu.VMEM(shape, dtype)


def chunks_of(part):
    chunk = min(part, 512)
    return [slice(c * chunk, (c + 1) * chunk) for c in range(part // chunk)]


def front_body(cap, pieces, own_rows, block_len, half, cross, me_ref, chosen_hbm, *refs):
    chosen_ref, told_ref, slot_ref, small_sem = refs[-4:]
    small = begin(chosen_hbm, chosen_ref, small_sem.at[0])
    if cross:
        source_ref, told_hbm, slot_hbm, cross_ref, held_ref, sems = refs[:-4]
        width = cross_ref.shape[1]
        plane = lax.shift_right_logical(me_ref[0] & (half - 1), half.bit_length() - 2)
        at = pl.ds(pl.multiple_of((1 - plane) * width, width), width)
        load = begin(source_ref.at[:, at], held_ref, sems.at[0])
    else:
        told_hbm, slot_hbm = refs[:-4]
    small.wait()
    peers, rows = told_ref.shape[0] // 2, slot_ref.shape[1]
    blocks = [chosen_ref[b : b + 1, :] for b in range(chosen_ref.shape[0])]
    position = jnp.concatenate([x + b * block_len for b, x in enumerate(blocks)], axis=1)
    owner = lax.shift_right_logical(position, own_rows.bit_length() - 1)
    local = position & (own_rows - 1)
    peer = iota((peers, rows), 0)
    mine = (peer == owner).astype(F32)
    count = jnp.sum(mine, axis=1, keepdims=True)
    earlier = jnp.sum(jnp.where(peer < owner, count, 0.0), axis=0, keepdims=True).astype(jnp.int32)
    rank = iota((1, rows), 1) - earlier
    slot_ref[...] = owner * (cap * pieces) + rank
    lane = iota((rows, rows), 0)
    hit = jnp.zeros((rows, rows), F32)
    for j in range(pieces):
        hit = hit + (lane == rank + j * cap).astype(F32)
    twice = iota((2 * peers, rows), 0)
    marked = jnp.where(twice == 2 * owner, local + 1, 0).astype(F32)
    asked = dot_nt(marked.astype(BF16), hit.astype(BF16)).astype(jnp.int32)
    told_ref[...] = jnp.where((twice & 1) == 1, jnp.concatenate(blocks, axis=1), asked)
    stores = [
        begin(told_ref, told_hbm, small_sem.at[1]),
        begin(slot_ref, slot_hbm, small_sem.at[2]),
    ]
    if cross:
        load.wait()
        stores.append(begin(held_ref, cross_ref, sems.at[1]))
    for store in stores:
        store.wait()


def plane_columns(me, source, crossed, half):
    own_rows, width = source.shape
    part, count = width // half, half // 2

    def body(me_ref, source_ref, crossed_ref, *refs):
        outs, (held_ref, in_sem, out_sem) = refs[:count], refs[count:]
        low = me_ref[0] & (half - 1)
        plane = lax.shift_right_logical(low, half.bit_length() - 2)
        wide = count * part
        at = pl.ds(pl.multiple_of(plane * wide, wide), wide)
        loads = [
            begin(source_ref.at[:, at], held_ref.at[0], in_sem.at[0]),
            begin(crossed_ref, held_ref.at[1], in_sem.at[1]),
        ]
        copies = []
        for n, load in enumerate(loads):
            load.wait()
            for k in range(count):
                share = (low & (count - 1)) ^ k
                at = held_ref.at[n, :, pl.ds(pl.multiple_of(share * part, part), part)]
                rows = pl.ds(n * own_rows, own_rows)
                copies.append(begin(at, outs[k].at[rows], out_sem.at[n, k]))
        wait_all(copies)

    return call(
        body,
        [(shaped((2 * own_rows, part), BF16), HBM)] * count,
        [(me, SMEM), (source, HBM), (crossed, HBM)],
        "plane_columns",
        0,
        [
            scratch_like((2, own_rows, count * part), BF16),
            pltpu.SemaphoreType.DMA((2,)),
            pltpu.SemaphoreType.DMA((2, count)),
        ],
    )


def pick_matrix(cap, pieces, own_rows, requested):
    told, lanes = requested.shape
    peers = told // 2
    group = cap * pieces
    slots = peers * group
    peer = 2 * iota((peers, group, told), 0).reshape(slots, told)
    spread = dot(
        (peer == iota((slots, told), 1)).astype(BF16), requested.astype(F32).astype(BF16)
    )
    place = iota((peers, group, lanes), 1).reshape(slots, lanes)
    row = jnp.sum(
        jnp.where(place == iota((slots, lanes), 1), spread, 0.0), axis=1, keepdims=True
    ).astype(jnp.int32)
    piece = iota((peers, group, 1), 1).reshape(slots, 1)
    shift = jnp.zeros((slots, 1), jnp.int32)
    for j in range(1, pieces):
        shift = shift + jnp.where(piece >= j * cap, own_rows, 0)
    target = jnp.where(row > 0, row - 1 + shift, -1)
    return (target == iota((slots, pieces * own_rows), 1)).astype(BF16)


def pick_slots(cap, pieces, requested, source, after, name):
    own_rows, width = source.shape
    part = width // pieces
    slots = requested.shape[0] // 2 * cap * pieces
    columns = chunks_of(part)

    def body(requested_hbm, source_ref, *refs):
        out_ref, requested_ref, rows_ref, sent_ref, in_sem, out_sem = refs[len(after) :]
        asked = begin(requested_hbm, requested_ref, in_sem.at[len(columns), 0])
        loads = []
        for n, at in enumerate(columns):
            for j in range(pieces):
                wide = slice(j * part + at.start, j * part + at.stop)
                target = rows_ref.at[j * own_rows : (j + 1) * own_rows, at]
                loads.append(begin(source_ref.at[:, wide], target, in_sem.at[n, j]))
        asked.wait()
        pick = pick_matrix(cap, pieces, own_rows, requested_ref[...])
        stores = []
        for n, at in enumerate(columns):
            for load in loads[n * pieces : (n + 1) * pieces]:
                load.wait()
            sent_ref[:, at] = dot(pick, rows_ref[:, at]).astype(BF16)
            stores.append(begin(sent_ref.at[:, at], out_ref.at[:, at], out_sem.at[n]))
        for store in stores:
            store.wait()

    return call(
        body,
        [(shaped((slots, part), BF16), HBM)],
        [(requested, HBM), (source, HBM)] + [(x, HBM) for x in after],
        name,
        2 * slots * pieces * own_rows * part,
        [
            scratch_like(requested.shape, jnp.int32),
            scratch_like((pieces * own_rows, part), BF16),
            scratch_like((slots, part), BF16),
            pltpu.SemaphoreType.DMA((len(columns) + 1, pieces)),
            pltpu.SemaphoreType.DMA((len(columns),)),
        ],
    )[0]


def spread_columns(source, half):
    own_rows, width = source.shape
    part = width // half

    def body(source_ref, out_ref, held_ref, in_sem, out_sem):
        begin(source_ref, held_ref, in_sem).wait()
        copies = []
        for k in range(half):
            at = held_ref.at[:, k * part : (k + 1) * part]
            out = out_ref.at[k * own_rows : (k + 1) * own_rows]
            copies.append(begin(at, out, out_sem.at[k]))
        wait_all(copies)

    scratch = [
        scratch_like((own_rows, width), BF16),
        pltpu.SemaphoreType.DMA,
        pltpu.SemaphoreType.DMA((half,)),
    ]
    outs = [(shaped((half * own_rows, part), BF16), HBM)]
    return call(body, outs, [(source, HBM)], "spread_columns", 0, scratch)[0]


def cut_factors(factors, first):
    cuts = (slice(0, first), slice(first, factors.shape[0]))

    def body(factors_ref, *refs):
        outs, (held_ref, sems) = refs[:2], refs[2:]
        loads = [
            begin(factors_ref.at[at], held_ref.at[at], sems.at[0, n]) for n, at in enumerate(cuts)
        ]
        copies = []
        for n, at in enumerate(cuts):
            loads[n].wait()
            copies.append(begin(held_ref.at[at], outs[n], sems.at[1, n]))
        wait_all(copies)

    outs = [
        (shaped((at.stop - at.start,) + factors.shape[1:], BF16), HBM) for at in cuts
    ]
    scratch = [scratch_like(factors.shape, BF16), pltpu.SemaphoreType.DMA((2, 2))]
    return call(body, outs, [(factors, HBM)], "cut_factors", 0, scratch)


def pick_rows(me, half, own_rows, chosen, shares, after, name):
    peers, total = chosen.shape[0] // 2, chosen.shape[1]
    picks = total * half // peers
    part = shares[0].shape[1]
    block = half * own_rows
    batch = min(peers, 8)

    def body(me_ref, chosen_ref, *refs):
        refs = refs[len(after) :]
        parts, (out_ref, rows_ref, pick_ref, sent_ref, in_sem, out_sem) = (
            refs[: len(shares)],
            refs[len(shares) :],
        )
        loads = []
        for k in range(half):
            place = (me_ref[0] & (half - 1)) ^ k if len(parts) > 1 else k
            n, first = (k % len(parts), k // len(parts)) if len(parts) > 1 else (0, k)
            at = parts[n].at[first * own_rows : (first + 1) * own_rows]
            target = rows_ref.at[pl.ds(pl.multiple_of(place * own_rows, own_rows), own_rows)]
            loads.append(begin(at, target, in_sem.at[k]))
        block_at = lax.shift_right_logical(me_ref[0], half.bit_length() - 1)
        same = iota((picks, total), 0) + block_at * picks == iota((picks, total), 1)
        stores = []
        for first in range(0, peers, batch):
            for e in range(batch):
                wanted = chosen_ref[2 * (first + e) + 1 : 2 * (first + e) + 2, :]
                column = jnp.sum(jnp.where(same, wanted, 0), axis=1, keepdims=True)
                pick_ref[first // batch % 2, e * picks : (e + 1) * picks] = (
                    column == iota((picks, block), 1)
                ).astype(BF16)
            if first == 0:
                wait_all(loads)
            at = slice(first * picks, (first + batch) * picks)
            sent_ref[at] = dot(pick_ref[first // batch % 2], rows_ref[...]).astype(BF16)
            stores.append(begin(sent_ref.at[at], out_ref.at[at], out_sem.at[first // batch]))
        wait_all(stores)

    return call(
        body,
        [(shaped((peers * picks, part), BF16), HBM)],
        [(me, SMEM), (chosen, VMEM)] + [(x, HBM) for x in list(after) + list(shares)],
        name,
        2 * peers * picks * block * part,
        [
            scratch_like((block, part), BF16),
            scratch_like((2, batch * picks, block), BF16),
            scratch_like((peers * picks, part), BF16),
            pltpu.SemaphoreType.DMA((half,)),
            pltpu.SemaphoreType.DMA((peers // batch,)),
        ],
    )[0]


def place_rows(cap, pieces, own_rows, me, half, chosen):
    peers, total = chosen.shape[0] // 2, chosen.shape[1]
    picks = total * half // peers
    group = cap * pieces

    def body(me_ref, chosen_ref, out_ref, pick_ref):
        low = me_ref[0] & (half - 1)
        block_at = lax.shift_right_logical(me_ref[0], half.bit_length() - 1)
        lane = iota((2 * peers, total), 1) - block_at * picks
        here = (lane >= 0) & (lane < picks)
        local = jnp.where(here, chosen_ref[...] - low * own_rows, own_rows)
        before = jnp.sum((local < 0).astype(F32), axis=1, keepdims=True).astype(jnp.int32)
        ranks = lane - before
        owned = jnp.where((local >= 0) & (local < own_rows), local + 1, 0)
        place = iota((group, total), 0)
        for e in range(peers):
            at = slice(2 * e + 1, 2 * e + 2)
            rank, mine = ranks[at], owned[at]
            column = jnp.zeros((group, 1), jnp.int32)
            for j in range(pieces):
                hit = jnp.where((place == rank + j * cap) & (rank >= 0) & (rank < cap), mine, 0)
                row = jnp.sum(hit, axis=1, keepdims=True)
                column = column + jnp.where(row > 0, row + j * own_rows, 0)
            pick_ref[e * group : (e + 1) * group] = (
                column == iota((group, pieces * own_rows), 1) + 1
            ).astype(F32)
        out_ref[...] = jnp.transpose(pick_ref[...]).astype(BF16)

    return call(
        body,
        [(shaped((pieces * own_rows, peers * group), BF16), VMEM)],
        [(me, SMEM), (chosen, VMEM)],
        "place_rows",
        1 << 20,
        [scratch_like((peers * group, pieces * own_rows), F32)],
    )[0]


def sum_rows(pieces, placed, returned):
    slots, part = returned.shape
    own_rows = placed.shape[0] // pieces
    columns = chunks_of(part)

    def body(placed_hbm, returned_ref, out_ref, place_ref, got_ref, sum_ref, in_sem, out_sem):
        first = begin(placed_hbm, place_ref, in_sem.at[len(columns)])
        loads = [
            begin(returned_ref.at[:, at], got_ref.at[:, at], in_sem.at[n])
            for n, at in enumerate(columns)
        ]
        first.wait()
        stores = []
        for n, at in enumerate(columns):
            loads[n].wait()
            summed = dot(place_ref[...], got_ref[:, at]).astype(BF16)
            for j in range(pieces):
                wide = slice(j * part + at.start, j * part + at.stop)
                sum_ref[:, wide] = summed[j * own_rows : (j + 1) * own_rows]
                stores.append(
                    begin(sum_ref.at[:, wide], out_ref.at[:, wide], out_sem.at[n, j])
                )
        wait_all(stores)

    return call(
        body,
        [(shaped((own_rows, part * pieces), BF16), HBM)],
        [(placed, HBM), (returned, HBM)],
        "sum_rows",
        2 * slots * pieces * own_rows * part,
        [
            scratch_like(placed.shape, BF16),
            scratch_like((slots, part), BF16),
            scratch_like((own_rows, part * pieces), BF16),
            pltpu.SemaphoreType.DMA((len(columns) + 1,)),
            pltpu.SemaphoreType.DMA((len(columns), pieces)),
        ],
    )[0]


def load_factor(order_ref, parts, m, target, sems):
    copies = []
    _, count, rows, cols = parts[0].shape
    first = parts[1].shape[0] if len(parts) > 1 else 0
    for n in range(2 if len(parts) > 1 else 1):
        place = order_ref[0] ^ n if len(parts) > 1 else 0
        start = pl.multiple_of(place * rows, rows)
        for i in range(count):
            side = parts[0].at[m, i]
            if n == 1:
                flat = m * count + i
                side = parts[1].at[flat] if flat < first else parts[2].at[flat - first]
            at = target.at[pl.ds(start, rows), i * cols : (i + 1) * cols]
            copies.append(begin(side, at, sems.at[n, i]))
    return copies


def wait_all(copies):
    for copy in copies:
        copy.wait()


def place_matrix(cap, pieces, slots, slot):
    wide = jnp.concatenate([slot + j * cap for j in range(pieces)], axis=1)
    return (iota((slots, wide.shape[1]), 0) == wide).astype(BF16)


def load_rows(got_hbm, x_ref, sems):
    rows, depth = x_ref.shape[0] // NPHM, x_ref.shape[1]
    part = got_hbm.shape[1]
    shares = NPHM * depth // part
    picks = got_hbm.shape[0] * part // (NPHM * depth) // (rows // SELECTED)
    copies = []
    for n in range(got_hbm.shape[0] // picks):
        block, share = divmod(n, shares)
        a, start = share * part // depth, share * part % depth
        first = (block * NPHM + a) * picks
        at = x_ref.at[first : first + picks, start : start + part]
        copies.append(begin(got_hbm.at[n * picks : (n + 1) * picks], at, sems.at[n]))
    return copies


def load_slots(got_hbm, got_ref, sems):
    return [
        begin(got_hbm.at[:, at], got_ref.at[:, at], sems.at[n])
        for n, at in enumerate(chunks_of(got_ref.shape[1]))
    ]


def stack_rows(pieces, place, loads, got_ref, out_ref):
    part = got_ref.shape[1]
    rows, depth = out_ref.shape[0] // NPHM, out_ref.shape[1]
    for load, at in zip(loads, chunks_of(part)):
        load.wait()
        block = dot_tn(place, got_ref[:, at]).astype(BF16)
        for j in range(pieces):
            column = j * part + at.start
            a, start = column // depth, column % depth
            for n in range(rows // STRIP):
                first = (n * NPHM + a) * STRIP
                out_ref[first : first + STRIP, start : start + at.stop - at.start] = block[
                    j * rows + n * STRIP : j * rows + (n + 1) * STRIP
                ]


def store_parts(order_ref, source_ref, outs, sems):
    copies = []
    for n, out in enumerate(outs):
        size = out.shape[1]
        start = pl.multiple_of((order_ref[0] ^ n) * size if len(outs) > 1 else 0, size)
        copies.append(begin(source_ref.at[:, pl.ds(start, size)], out, sems.at[n]))
    return copies


STRIP = SELECTED


def rows_of(n, a):
    return slice((n * NPHM + a) * STRIP, (n * NPHM + a + 1) * STRIP)


def mix_in(mix_ref, m, y_ref, n):
    cols = y_ref.shape[1] // NPHM
    total = [jnp.zeros((STRIP, cols), F32)] * NPHM
    for a in range(NPHM):
        for i in range(NPHM):
            block = y_ref[rows_of(n, a), i * cols : (i + 1) * cols]
            for b in range(NPHM):
                total[b] = total[b] + mix_ref[m * 64 + i * 16 + a * 4 + b] * block
    return total


def mix_out(mix_ref, m, blocks, n, z_ref, offset=0):
    cols = blocks[0].shape[1]
    for a in range(NPHM):
        for i in range(NPHM):
            total = mix_ref[m * 64 + i * 16 + a * 4] * blocks[0]
            for b in range(1, NPHM):
                total = total + mix_ref[m * 64 + i * 16 + a * 4 + b] * blocks[b]
            z_ref[rows_of(n, a), offset + i * cols : offset + (i + 1) * cols] = total.astype(
                z_ref.dtype
            )


def blocks_of(d_ref, n):
    cols = d_ref.shape[1] // NPHM
    at = slice(n * STRIP, (n + 1) * STRIP)
    return [d_ref[at, b * cols : (b + 1) * cols].astype(F32) for b in range(NPHM)]


def join_factors(group, parts, first, stop, name):
    _, count, rows, cols = parts[0].shape
    depth, hidden = rows * (2 if len(parts) > 1 else 1), count * cols
    wide = (stop - first) * hidden

    def body(order_ref, *refs):
        ins, (out_ref, held_ref, sems, out_sem) = refs[: len(parts)], refs[len(parts) :]
        loads = []
        for m in range(first, stop):
            target = held_ref.at[:, (m - first) * hidden : (m - first + 1) * hidden]
            loads += load_factor(order_ref, ins, m, target, sems.at[m])
        wait_all(loads)
        begin(held_ref, out_ref, out_sem).wait()

    return call(
        body,
        [(shaped((depth, wide), BF16), HBM)],
        [(group, SMEM)] + [(x, HBM) for x in parts],
        name,
        0,
        [
            scratch_like((depth, wide), BF16),
            pltpu.SemaphoreType.DMA((stop, 2, count)),
            pltpu.SemaphoreType.DMA,
        ],
    )[0]


def order_body(cap, pieces, order_ref, slot_hbm, got_hbm, *refs):
    x_outs, (got_ref, x_ref, slot_ref, got_sem, out_sem) = refs[:-5], refs[-5:]
    small = begin(slot_hbm, slot_ref, got_sem.at[got_sem.shape[0] - 1])
    loads = load_slots(got_hbm, got_ref, got_sem)
    small.wait()
    place = place_matrix(cap, pieces, got_ref.shape[0], slot_ref[...])
    stack_rows(pieces, place, loads, got_ref, x_ref)
    wait_all(store_parts(order_ref, x_ref, x_outs, out_sem))


def forward_body(sides, order_ref, mix_ref, *refs):
    x_parts, side_hbm, refs = refs[:sides], refs[sides], refs[sides + 1 :]
    yg_hbm, yu_hbm, act_hbm, slope_hbm, hid_hbm = refs[:5]
    side_ref, x_ref, yg_ref, yu_ref, act_ref, slope_ref, hid_ref = refs[5:12]
    x_sem, side_sem, out_sem = refs[12:]
    loads = []
    for n, part in enumerate(x_parts):
        size = part.shape[1]
        start = pl.multiple_of((order_ref[0] ^ n) * size if sides > 1 else 0, size)
        loads.append(begin(part, x_ref.at[:, pl.ds(start, size)], x_sem.at[n]))
    side_in = begin(side_hbm, side_ref, side_sem)
    wait_all(loads)
    stores = []
    side_in.wait()
    hidden = yg_ref.shape[1]
    yg_ref[...] = dot(x_ref[...], side_ref[:, :hidden])
    stores.append(begin(yg_ref, yg_hbm, out_sem.at[2]))
    yu_ref[...] = dot(x_ref[...], side_ref[:, hidden:])
    stores.append(begin(yu_ref, yu_hbm, out_sem.at[3]))
    cols = yg_ref.shape[1] // NPHM
    for n in range(yg_ref.shape[0] // (NPHM * STRIP)):
        gates = mix_in(mix_ref, 0, yg_ref, n)
        ups = mix_in(mix_ref, 1, yu_ref, n)
        for b in range(NPHM):
            at = (slice(n * STRIP, (n + 1) * STRIP), slice(b * cols, (b + 1) * cols))
            sig = jax.nn.sigmoid(gates[b])
            act = gates[b] * sig
            act_ref[at] = act
            slope_ref[at] = ups[b] * (sig + act * (1.0 - sig))
            hid_ref[at] = act * ups[b]
    stores.append(begin(act_ref, act_hbm, out_sem.at[4]))
    stores.append(begin(slope_ref, slope_hbm, out_sem.at[5]))
    stores.append(begin(hid_ref, hid_hbm, out_sem.at[6]))
    wait_all(stores)


def backward_body(
    cap, pieces, sides, after, order_ref, mix_ref, slot_hbm, score_hbm, got_hbm, act_hbm, slope_hbm, hid_hbm,
    *refs,
):
    side_hbm, down_hbm, refs = refs[0], refs[1], refs[2 + after :]
    back_hbm, x_outs, refs = refs[0], refs[1 : 1 + sides], refs[1 + sides :]
    y_hbm, d_hbm, inner_hbm = refs[:3]
    (
        down_ref, side_ref, x_ref, y_ref, d_ref, act_ref, slope_ref, hid_ref, z_ref, grad_ref,
        back_ref, inner_ref, slot_ref, score_ref, got_sem, side_sem, in_sem, out_sem,
    ) = refs[3:]
    loads = load_rows(got_hbm, x_ref, got_sem)
    down_in = [begin(down_hbm, down_ref, side_sem.at[0])]
    small_in = [
        begin(source, target, in_sem.at[n])
        for n, (source, target) in enumerate(((score_hbm, score_ref), (slot_hbm, slot_ref)))
    ]
    flat_in = [
        begin(source, target, in_sem.at[2 + n])
        for n, (source, target) in enumerate(
            ((act_hbm, act_ref), (slope_hbm, slope_ref), (hid_hbm, hid_ref))
        )
    ]
    hidden = d_ref.shape[2]
    sides_in = [begin(side_hbm, side_ref, side_sem.at[1])]
    wait_all(small_in)
    score = jnp.concatenate([score_ref[b : b + 1, :] for b in range(score_ref.shape[0])], axis=1)
    rows = score.shape[1]
    same = iota((rows, rows), 0) == iota((rows, rows), 1)
    score = jnp.sum(jnp.where(same, score.astype(F32), 0.0), axis=1, keepdims=True)
    cols = hidden // NPHM
    gates = jnp.broadcast_to(jax.nn.sigmoid(score / 64.0), (rows, cols))
    place = place_matrix(cap, pieces, back_ref.shape[0], slot_ref[...])
    strips = rows // STRIP
    tall = NPHM * STRIP
    wait_all(loads)
    stores = store_parts(order_ref, x_ref, x_outs, out_sem)
    wait_all(down_in)
    for n in range(strips):
        y_ref[n * tall : (n + 1) * tall] = dot(x_ref[n * tall : (n + 1) * tall], down_ref[...])
    stores.append(begin(y_ref, y_hbm, out_sem.at[2]))
    wait_all(flat_in)
    wait_all(sides_in)
    for n in range(strips):
        down = mix_in(mix_ref, 2, y_ref, n)
        strip = slice(n * STRIP, (n + 1) * STRIP)
        gate = gates[strip]
        inner = jnp.zeros((STRIP, cols), F32)
        d_gate, d_up = [], []
        for b in range(NPHM):
            at = (strip, slice(b * cols, (b + 1) * cols))
            inner = inner + hid_ref[at] * down[b]
            hidden_grad = gate * down[b]
            d_gate.append(hidden_grad * slope_ref[at])
            d_up.append(hidden_grad * act_ref[at])
            d_ref[(0,) + at] = d_gate[b].astype(BF16)
            d_ref[(1,) + at] = d_up[b].astype(BF16)
            d_ref[(2,) + at] = (hid_ref[at] * gate).astype(BF16)
        inner_ref[strip] = inner
        mix_out(mix_ref, 0, d_gate, n, z_ref)
        mix_out(mix_ref, 1, d_up, n, z_ref, hidden)
        at = slice(n * tall, (n + 1) * tall)
        grad_ref[at] = dot_nt(z_ref[at], side_ref[...]).astype(BF16)
    stores.append(begin(d_ref, d_hbm, out_sem.at[3]))
    stores.append(begin(inner_ref, inner_hbm, out_sem.at[4]))
    part, depth = back_ref.shape[1], x_ref.shape[1]
    for k, at in enumerate(chunks_of(part)):
        blocks = []
        for j in range(pieces):
            column = j * part + at.start
            a, start = column // depth, column % depth
            wide = slice(start, start + at.stop - at.start)
            blocks += [grad_ref[rows_of(n, a), wide] for n in range(strips)]
        back_ref[:, at] = dot(place, jnp.concatenate(blocks, axis=0)).astype(BF16)
        stores.append(begin(back_ref.at[:, at], back_hbm.at[:, at], out_sem.at[5 + k]))
    wait_all(stores)


def factor_body(count_groups, mix_ref, *refs):
    rows_in, refs = refs[: 3 * count_groups], refs[3 * count_groups :]
    out_hbm, x_ref, g_ref, d_ref, z_ref, sum_ref, in_sem, out_sem = refs
    loads = []
    for n in range(count_groups):
        for k, target in enumerate((x_ref, g_ref, d_ref)):
            loads.append(begin(rows_in[3 * n + k], target.at[n], in_sem.at[n, k]))
    stores = []
    cols = out_hbm.shape[3]
    wait_all(loads)
    for m in (2, 0, 1):
        for n in range(count_groups):
            for strip in range(d_ref.shape[2] // STRIP):
                blocks = blocks_of(d_ref.at[n, m], strip)
                mix_out(mix_ref, m, blocks, strip, z_ref.at[n])
        left = g_ref if m == 2 else x_ref
        sum_ref[m] = sum(dot_tn(left[n], z_ref[n]) for n in range(count_groups))
        for i in range(NPHM):
            at = sum_ref.at[m, :, i * cols : (i + 1) * cols]
            stores.append(begin(at, out_hbm.at[m, i], out_sem.at[m, i]))
    wait_all(stores)


def mix_grad_body(yg_hbm, yu_hbm, yd_hbm, d_hbm, out_ref, y_ref, d_ref, sems):
    loads = [begin(d_hbm, d_ref, sems.at[3])]
    for m, source in enumerate((yg_hbm, yu_hbm, yd_hbm)):
        loads.append(begin(source, y_ref.at[m], sems.at[m]))
    wait_all(loads)
    rows, cols = d_ref.shape[1], d_ref.shape[2] // NPHM
    for m in range(3):
        for a in range(NPHM):
            for i in range(NPHM):
                at = slice(i * cols, (i + 1) * cols)
                strips = range(rows // STRIP)
                block = jnp.concatenate([y_ref[m, rows_of(n, a), at] for n in strips], axis=0)
                for b in range(NPHM):
                    at = m * 64 + i * 16 + a * 4 + b
                    other = d_ref[m, :, b * cols : (b + 1) * cols].astype(F32)
                    out_ref[at : at + 1, :] = jnp.sum(block * other, axis=0, keepdims=True)


def shards(tokens, cotangent, factors, mix, selection, scores):
    peers = lax.axis_size("exp")
    groups = lax.axis_size("seq")
    own_rows, width = tokens.shape
    _, weights, count, depth_own, cols = factors.shape
    depth = depth_own * groups
    hidden = count * cols
    cap = 3 * own_rows // (2 * peers)
    pieces = 1
    while (cap * pieces) % 8:
        pieces *= 2
    slots = peers * cap * pieces
    part = width // pieces
    steps = len(chunks_of(part))
    block_len = peers * SELECTED
    rows = selection.shape[1] * selection.shape[2]
    stacked = count * rows
    swap = groups == 2
    pair = [(0, 1), (1, 0)]
    mixing = mix.reshape(-1)
    dma = pltpu.SemaphoreType.DMA

    def across(array):
        return lax.ppermute(array, "seq", pair)

    half = peers // selection.shape[1]
    direct = half == 8
    me = lax.axis_index("exp").astype(jnp.int32).reshape(1)
    group = lax.axis_index("seq").astype(jnp.int32).reshape(1)
    halves = [list(range(h, h + half)) for h in range(0, peers, half)]
    if swap:
        flat_factors = factors[0].reshape(weights * count, depth_own, cols)
        cuts = [across(x) for x in cut_factors(flat_factors, 2 * count)]
        factor_parts = [factors[0]] + cuts
        sides = 2
    else:
        cuts = []
        factor_parts = [lax.all_gather(factors, "seq", axis=3, tiled=True)[0]]
        sides = 1
    cross = [(shaped((own_rows, width // 2), BF16), HBM)] if direct else []
    told, slot, *crossed = call(
        functools.partial(front_body, cap, pieces, own_rows, block_len, half, direct),
        [(shaped((2 * peers, rows), jnp.int32), HBM), (shaped((1, rows), jnp.int32), HBM)] + cross,
        [(me, SMEM), (selection[0], HBM)] + ([(cotangent, HBM)] if direct else []),
        "wanted_rows",
        1 << 20,
        ([scratch_like((own_rows, width // 2), BF16), dma((2,))] if direct else [])
        + [scratch_like(selection.shape[1:], jnp.int32)]
        + [scratch_like((2 * peers, rows), jnp.int32), scratch_like((1, rows), jnp.int32)]
        + [dma((3,))],
    )
    if direct:
        crossed = [lax.ppermute(crossed[0], "exp", [(n, n ^ (half // 2)) for n in range(peers)])]
    chosen = lax.all_to_all(told, "exp", split_axis=0, concat_axis=0, tiled=True)

    def to_peers(array):
        array = array.reshape(peers, -1, array.shape[1])
        array = lax.all_to_all(array, "exp", split_axis=0, concat_axis=0, tiled=True)
        return array.reshape(-1, array.shape[2])

    got_rows = to_peers(pick_slots(cap, pieces, chosen, tokens, crossed, "pick_tokens"))
    if direct:
        shares = plane_columns(me, cotangent, crossed[0], half)
        shares = [shares[0]] + [
            lax.ppermute(shares[k], "exp", [(n, n ^ k) for n in range(peers)])
            for k in range(1, half // 2)
        ]
    else:
        array = spread_columns(cotangent, half).reshape(half, own_rows, -1)
        array = lax.all_to_all(
            array, "exp", split_axis=0, concat_axis=0, axis_index_groups=halves, tiled=True
        )
        shares = [array.reshape(half * own_rows, -1)]
    picked = pick_rows(me, half, own_rows, chosen, shares, cuts[:1], "pick_cotangent")
    got_grads = to_peers(picked)
    placed = place_rows(cap, pieces, own_rows, me, half, chosen)
    gate = jax.nn.sigmoid(scores[0].reshape(-1).astype(F32) / 64.0)

    product = 2 * stacked * depth * hidden
    split = [(shaped((stacked, depth // sides), BF16), HBM)] * sides
    mixed = (shaped((stacked, hidden), F32), HBM)
    flat = (shaped((rows, hidden), F32), HBM)
    back_scratch = scratch_like((slots, part), BF16)
    pieces_in = got_grads.shape[0] // SELECTED
    stack_scratch = scratch_like((stacked, depth), BF16)
    mixed_scratch = scratch_like((stacked, hidden), F32)
    low_scratch = scratch_like((stacked, hidden), BF16)
    flat_scratch = scratch_like((rows, hidden), F32)
    gate_up = join_factors(group, factor_parts[:2], 0, 2, "join_gate_up")
    down = join_factors(group, factor_parts, 2, 3, "join_down")
    x_parts = call(
        functools.partial(order_body, cap, pieces),
        split,
        [(group, SMEM), (slot, HBM), (got_rows, HBM)],
        "order_rows",
        product // 4,
        [back_scratch, stack_scratch, scratch_like(slot.shape, jnp.int32)]
        + [dma((steps + 1,)), dma((2,))],
    )
    y_gate, y_up, act, slope, hid = call(
        functools.partial(forward_body, sides),
        [mixed, mixed, flat, flat, flat],
        [(group, SMEM), (mixing, SMEM)] + [(x, HBM) for x in x_parts] + [(gate_up, HBM)],
        "forward",
        2 * product,
        [scratch_like((depth, 2 * hidden), BF16), stack_scratch, mixed_scratch, mixed_scratch]
        + [flat_scratch] * 3
        + [dma((2,)), dma, dma((7,))],
    )
    x_rows = [x_parts[0]] + [across(x) for x in x_parts[1:]]
    after = x_rows[1:]
    outs = call(
        functools.partial(backward_body, cap, pieces, sides, len(after)),
        [(shaped((slots, part), BF16), HBM)]
        + split
        + [mixed, (shaped((weights, rows, hidden), BF16), HBM), (shaped((rows, cols), F32), HBM)],
        [(group, SMEM), (mixing, SMEM), (slot, HBM), (scores[0], HBM), (got_grads, HBM)]
        + [(x, HBM) for x in (act, slope, hid)]
        + [(x, HBM) for x in [gate_up, down] + after],
        "backward",
        3 * product,
        [scratch_like((depth, hidden), BF16), scratch_like((depth, 2 * hidden), BF16)]
        + [stack_scratch, mixed_scratch, scratch_like((weights, rows, hidden), BF16)]
        + [flat_scratch] * 3
        + [scratch_like((stacked, 2 * hidden), BF16), stack_scratch, back_scratch]
        + [scratch_like((rows, cols), F32), scratch_like(slot.shape, jnp.int32)]
        + [scratch_like(scores.shape[1:], jnp.int32)]
        + [dma((pieces_in,)), dma((2,)), dma((5,)), dma((5 + steps,))],
    )
    back, g_parts, (y_down, d_own, inner) = outs[0], outs[1 : 1 + sides], outs[1 + sides :]
    returned = to_peers(back)

    d_rows = [d_own] + [across(d_own) for _ in x_parts[1:]]
    g_rows = [g_parts[0]] + [across(x) for x in g_parts[1:]]
    depth_here = depth // sides
    factor_grad = call(
        functools.partial(factor_body, sides),
        [(shaped((weights, count, depth_here, cols), F32), HBM)],
        [(mixing, SMEM)]
        + [(x, HBM) for n in range(sides) for x in (x_rows[n], g_rows[n], d_rows[n])],
        "factor_grad",
        3 * product,
        [scratch_like((sides, stacked, depth_here), BF16)] * 2
        + [
            scratch_like((sides, weights, rows, hidden), BF16),
            scratch_like((sides, stacked, hidden), BF16),
            scratch_like((weights, depth_here, hidden), F32),
            dma((sides, 3)),
            dma((weights, count)),
        ],
    )[0]
    mix_rows = call(
        mix_grad_body,
        [(shaped((mixing.size, cols), F32), VMEM)],
        [(x, HBM) for x in (y_gate, y_up, y_down, d_own)],
        "mix_partials",
        weights * 64 * 2 * rows * cols,
        [
            scratch_like((weights, stacked, hidden), F32),
            scratch_like((weights, rows, hidden), BF16),
            dma((4,)),
        ],
    )[0]
    mix_part = jnp.sum(mix_rows, axis=1).reshape(mix.shape)
    if swap:
        mix_grad = mix_part + across(mix_part)
    else:
        factor_grad = lax.psum_scatter(
            factor_grad.astype(BF16), "seq", scatter_dimension=2, tiled=True
        ).astype(F32)
        mix_grad = lax.psum(mix_part, "seq")
    gate_grad = (jnp.sum(inner, axis=1) * gate * (1.0 - gate)).reshape(selection.shape)
    token_grad = sum_rows(pieces, placed, returned)
    return token_grad, factor_grad[None], mix_grad, gate_grad


def solution(mesh):
    return jax.shard_map(
        shards,
        mesh=mesh,
        in_specs=(
            P(("seq", "exp"), None),
            P(("seq", "exp"), None),
            P("exp", None, None, "seq", None),
            P("exp", None, None, None, None),
            P("exp", "seq", None),
            P("exp", "seq", None),
        ),
        out_specs=(
            P(("seq", "exp"), None),
            P("exp", None, None, "seq", None),
            P("exp", None, None, None, None),
            P("exp", "seq", None),
        ),
        check_vma=False,
    )
```
